32 devices in a mesh: group: 4 (over y, x), cluster: 8 (over z, core).
Axes of the slice: x: 2, y: 2, z: 4, core: 2. Of those that a mesh axis runs over, the one named last changes fastest.
Arguments:
- charges: float32 [262144, 128], P(('group', 'cluster')), may hold values from -6 to 6
- leaf_size: int32 [1024], P(('group', 'cluster')), may hold values from 1 to 256, 196608 in all
- leaf_basis: float32 [1024, 64, 256], P(('group', 'cluster')), may hold values from -0.375 to 0.375
- leaf_transfer: float32 [1024, 64, 64], P(('group', 'cluster')), may hold values from -0.375 to 0.375
- mid_transfer: float32 [256, 64, 64], P(('group', 'cluster')), may hold values from -0.25 to 0.25
- leaf_parent: int32 [1024], P(('group', 'cluster')), may hold values from 0 to 7, as said below
- send_leaf: int32 [2048], P(('group', 'cluster')), may hold values from 0 to 32, as said below
- pair_leaf: int32 [1024, 12], P(('group', 'cluster')), may hold values from 0 to 64, as said below
- leaf_coupling: float32 [1024, 64, 768], P(('group', 'cluster')), may hold values from -0.21875 to 0.21875
- send_mid: int32 [2048], P(('group', 'cluster')), may hold values from 0 to 8, as said below
- pair_mid: int32 [256, 32], P(('group', 'cluster')), may hold values from 0 to 64, as said below
- mid_coupling: float32 [256, 64, 2048], P(('group', 'cluster')), may hold values from -0.125 to 0.125
- top_pairs: int32 [32, 4], P('group'), may hold values from 0 to 32, as said below
- top_coupling: float32 [32, 64, 256], P('group'), may hold values from -0.375 to 0.375
Outputs:
- far_field: float32 [262144, 128], P(('group', 'cluster'))
The draws below stay inside these ranges and needn't reach their ends.
Inputs may be any that keep to these rules, and one draw needn't show every extreme that they name: `send_leaf`: entry (d * 32 + r) * 2 + j is the leaf, local to device d, whose block d puts in slot j for device r, or 32 for an empty slot; the leaves in one sender's slots to one receiver are distinct; some receiver has every slot from every sender filled. `pair_leaf`: row t names leaf t's admissible partners as positions 2 * d + j among the slots its owner receives, filled slots only and distinct within a row, or 64 for no partner; every filled slot is named by some row of its receiver. `send_mid`: as send_leaf, for level-one clusters: local indices below 8, 8 for an empty slot; some receiver has every slot from every sender filled. `pair_mid`: as pair_leaf, for level-one clusters; every filled slot is named by some row of its receiver. `leaf_parent`: every level-one cluster of a device is the parent of at least one of its leaves. `top_pairs`: row o names coarse clusters other than o, distinct within a row, at least one a row, or 32 for no partner.
All inputs are finite; a program needn't handle non-finite values. No bound on the sum of `leaf_size` on one device may be relied on, other than what follows from the above.
Results may differ from the reference program's by a relative error of at most 0.000062.
Values sent between devices are 32-bit elements; how exact they have to be, the bound alone decides.
No kernel may reach another device: no remote copies, remote signals or barrier semaphores. Data moves between devices by JAX's collectives and lax.ppermute only.
A program may use at most 128 MiB of HBM per device.

```python
import math
import jax
import jax.numpy as jnp
import numpy as np
from jax import lax

PORTS = 128
RANK = 64
LEAF = 256
SLOTS = 2
LIST_LEAF = 12
LIST_MID = 32
LIST_TOP = 4
LEAVES_DEV = 32
MIDS_DEV = 8
OWNERS = 32
LEAVES = 1024
MIDS = 256
COARSE = 32
UNKNOWNS = 262144


def distinct_order(key, row_count, width):
    scores = jax.random.randint(key, (row_count, width), 0, 1 << 20) * width + jnp.arange(width, dtype=jnp.int32)[None, :]
    return jnp.argsort(scores, axis=1).astype(jnp.int32)


def routing_plan(key, per_owner, listed):
    streams = jax.random.split(key, 6)
    heavy_row = jax.random.randint(streams[0], (OWNERS, 1), 0, 2)
    counts = jax.random.randint(streams[1], (OWNERS, OWNERS), 0, SLOTS // 2 + 1) + heavy_row * (SLOTS - SLOTS // 2)
    full_row = jax.random.randint(streams[2], (), 0, OWNERS)
    counts = jnp.where(jnp.arange(OWNERS, dtype=jnp.int32)[:, None] == full_row, SLOTS, counts)
    ordering = distinct_order(streams[3], OWNERS * OWNERS, per_owner).reshape(OWNERS, OWNERS, per_owner)
    chosen = ordering[:, :, :SLOTS]
    slot_ids = jnp.arange(SLOTS, dtype=jnp.int32)
    is_live = slot_ids[None, None, :] < counts[:, :, None]
    send_table = jnp.where(is_live, chosen, per_owner)
    send_table = jnp.transpose(send_table, (1, 0, 2)).reshape(-1).astype(jnp.int32)
    flat_live = is_live.reshape(OWNERS, OWNERS * SLOTS)
    position = jnp.arange(OWNERS * SLOTS, dtype=jnp.int32)
    sort_value = jnp.where(flat_live, 0, 1) * (OWNERS * SLOTS) + position[None, :]
    live_list = jnp.argsort(sort_value, axis=1).astype(jnp.int32)
    live_total = jnp.sum(flat_live.astype(jnp.int32), axis=1)
    need_each = (live_total + per_owner - 1) // per_owner
    low_fill = jnp.minimum(need_each, listed)
    drawn_fill = jax.random.randint(streams[4], (OWNERS, per_owner), 0, listed + 1)
    filled = jnp.minimum(jnp.maximum(drawn_fill, low_fill[:, None]), jnp.minimum(live_total, listed)[:, None])
    first_spot = jnp.cumsum(filled, axis=1) - filled
    rotation = jax.random.randint(streams[5], (OWNERS, 1, 1), 0, OWNERS * SLOTS)
    column = jnp.arange(listed, dtype=jnp.int32)
    spot_index = first_spot[:, :, None] + column[None, None, :] + rotation
    safe_total = jnp.maximum(live_total, 1)
    wrapped = (spot_index % safe_total[:, None, None]).reshape(OWNERS, per_owner * listed)
    picked = jnp.take_along_axis(live_list, wrapped, axis=1).reshape(OWNERS, per_owner, listed)
    pair_table = jnp.where(column[None, None, :] < filled[:, :, None], picked, OWNERS * SLOTS)
    return (send_table, pair_table.reshape(OWNERS * per_owner, listed).astype(jnp.int32))


def draw_send_leaf(key, part):
    return routing_plan(jax.random.fold_in(key, 11), LEAVES_DEV, LIST_LEAF)[0]


def draw_pair_leaf(key, part):
    return routing_plan(jax.random.fold_in(key, 11), LEAVES_DEV, LIST_LEAF)[1]


def draw_send_mid(key, part):
    return routing_plan(jax.random.fold_in(key, 12), MIDS_DEV, LIST_MID)[0]


def draw_pair_mid(key, part):
    return routing_plan(jax.random.fold_in(key, 12), MIDS_DEV, LIST_MID)[1]


def draw_leaf_parent(key, part):
    streams = jax.random.split(jax.random.fold_in(key, 13), 2)
    local_index = jnp.arange(LEAVES_DEV, dtype=jnp.int32)
    spare_parent = jax.random.randint(streams[0], (OWNERS, LEAVES_DEV), 0, MIDS_DEV)
    base_parent = jnp.where(local_index[None, :] < MIDS_DEV, local_index[None, :], spare_parent)
    ordering = distinct_order(streams[1], OWNERS, LEAVES_DEV)
    return jnp.take_along_axis(base_parent, ordering, axis=1).reshape(-1).astype(jnp.int32)


def draw_top_pairs(key, part):
    streams = jax.random.split(jax.random.fold_in(key, 14), 3)
    ordering = distinct_order(streams[0], COARSE, COARSE - 1)[:, :LIST_TOP]
    target = jnp.arange(COARSE, dtype=jnp.int32)[:, None]
    sources = (target + 1 + ordering) % COARSE
    filled = jax.random.randint(streams[1], (COARSE, 1), 1, LIST_TOP + 1)
    full_row = jax.random.randint(streams[2], (), 0, COARSE)
    filled = jnp.where(target == full_row, LIST_TOP, filled)
    column = jnp.arange(LIST_TOP, dtype=jnp.int32)[None, :]
    return jnp.where(column < filled, sources, COARSE).astype(jnp.int32)


def level_of(key, extent, cuts, smallest, top_value):
    def one(dim, shards_of):
        draws = jax.random.uniform(jax.random.fold_in(jax.random.fold_in(key, 6), dim), (shards_of,), jnp.float32, smallest / len(cuts), top_value / len(cuts))
        return jnp.repeat(jnp.exp(draws), extent[dim] // shards_of).reshape((-1,) + (1,) * (len(extent) - dim - 1))

    gain = one(*cuts[0])
    for cut in cuts[1:]:
        gain = gain * one(*cut)
    return gain


def split_up(amount, total, bound, skew):
    loads = [(1 << 20) // math.isqrt(standing ** skew) + 1 for standing in range(2, amount + 1)]
    surplus, holding = total - bound - (amount - 1), [1] * (amount - 1)
    while surplus > 0:
        free = [i for i in range(amount - 1) if holding[i] < bound]
        pool, left = sum([loads[i] for i in free]), surplus
        for i in free:
            extra = min(bound - holding[i], max(1, left * loads[i] // pool), surplus)
            holding[i] = holding[i] + extra
            surplus = surplus - extra
    return np.array([bound] + holding)


def uneven_parts(own_key, number_of, total, limit, skew):
    if number_of == 2:
        one = jax.random.randint(own_key, (), max(1, total - limit), min(limit, total - 1) + 1)
        return jnp.stack([one, total - one])
    tallies = jnp.asarray(split_up(number_of, total, limit, skew), jnp.int32)
    twos = (number_of - 1) // 2
    giver, taker = tallies[1:1 + 2 * twos:2], tallies[2:2 + 2 * twos:2]
    margin = jnp.minimum(giver - 1, limit - taker)
    moved = jax.random.randint(jax.random.fold_in(own_key, 1), (twos,), 0, 1 << 20) % (margin + 1)
    tallies = tallies.at[1:1 + 2 * twos:2].set(giver - moved).at[2:2 + 2 * twos:2].set(taker + moved)
    return tallies[jax.random.permutation(jax.random.fold_in(own_key, 2), number_of)]


def bell_draw(own_key, dims, deviation, limit, shards=(), kind=jnp.bfloat16):
    values = deviation * jax.random.normal(own_key, dims, jnp.float32)
    if shards:
        values = values * level_of(own_key, dims, shards, -0.22, 0.18)
    return jnp.clip(values, -limit, limit).astype(kind)


def setup_inputs(seed: int = 0) -> dict:
    keys = jax.random.split(jax.random.key(seed), 15)
    charges = bell_draw(keys[0], (UNKNOWNS, PORTS), 1.0, 6.0, ((0, 32),), jnp.float32)
    leaf_size = uneven_parts(keys[1], LEAVES, LEAVES * (LEAF * 3 // 4), LEAF, 1).astype(jnp.int32)
    leaf_basis = bell_draw(keys[2], (LEAVES, RANK, LEAF), LEAF ** -0.5, 0.375, ((0, 32),), jnp.float32)
    leaf_transfer = bell_draw(keys[3], (LEAVES, RANK, RANK), (4 * RANK) ** -0.5, 0.375, ((0, 32),), jnp.float32)
    mid_transfer = bell_draw(keys[4], (MIDS, RANK, RANK), (MIDS_DEV * RANK) ** -0.5, 0.25, ((0, 32),), jnp.float32)
    leaf_parent = draw_leaf_parent(jax.random.fold_in(keys[14], 71), 0)
    send_leaf = draw_send_leaf(jax.random.fold_in(keys[14], 71), 0)
    pair_leaf = draw_pair_leaf(jax.random.fold_in(keys[14], 71), 0)
    leaf_coupling = bell_draw(keys[8], (LEAVES, RANK, LIST_LEAF * RANK), (LIST_LEAF * RANK) ** -0.5, 0.21875, ((0, 32),), jnp.float32)
    send_mid = draw_send_mid(jax.random.fold_in(keys[14], 71), 0)
    pair_mid = draw_pair_mid(jax.random.fold_in(keys[14], 71), 0)
    mid_coupling = bell_draw(keys[11], (MIDS, RANK, LIST_MID * RANK), (LIST_MID * RANK) ** -0.5, 0.125, ((0, 32),), jnp.float32)
    top_pairs = draw_top_pairs(jax.random.fold_in(keys[14], 71), 0)
    top_coupling = bell_draw(keys[13], (COARSE, RANK, LIST_TOP * RANK), (LIST_TOP * RANK) ** -0.5, 0.375, ((0, 4),), jnp.float32)
    return dict(charges=charges, leaf_size=leaf_size, leaf_basis=leaf_basis, leaf_transfer=leaf_transfer, mid_transfer=mid_transfer, leaf_parent=leaf_parent, send_leaf=send_leaf, pair_leaf=pair_leaf, leaf_coupling=leaf_coupling, send_mid=send_mid, pair_mid=pair_mid, mid_coupling=mid_coupling, top_pairs=top_pairs, top_coupling=top_coupling)


exact_mode = lax.Precision.HIGHEST


def couple(coupling, coef, index):
    stacked = jnp.take(coef, index, axis=0, mode="fill", fill_value=0.0)
    stacked = stacked.reshape(index.shape[0], index.shape[1] * coef.shape[1], coef.shape[2])
    return jnp.einsum("nkq,nqp->nkp", coupling, stacked, precision=exact_mode)


def couple_blocks(coupling, coef, index):
    per_owner = coupling.shape[0] // OWNERS

    def apply_block(pieces):
        return couple(pieces[0], coef, pieces[1])

    coupled = lax.map(apply_block, (coupling.reshape(OWNERS, per_owner, coupling.shape[1], coupling.shape[2]), index.reshape(OWNERS, per_owner, index.shape[1])))
    return coupled.reshape(coupling.shape[0], coef.shape[1], coef.shape[2])


def source_index(send_table, pair_table, per_owner):
    slot_table = send_table.reshape(OWNERS, OWNERS, SLOTS)
    receiver = (jnp.arange(pair_table.shape[0], dtype=jnp.int32) // per_owner)[:, None]
    is_live = pair_table < OWNERS * SLOTS
    sender = jnp.minimum(pair_table // SLOTS, OWNERS - 1).astype(jnp.int32)
    slot_index = (pair_table % SLOTS).astype(jnp.int32)
    local_index = slot_table[sender, receiver, slot_index]
    found = sender * per_owner + local_index
    return jnp.where(is_live & (local_index < per_owner), found, OWNERS * per_owner).astype(jnp.int32)


def reference(charges, leaf_size, leaf_basis, leaf_transfer, mid_transfer, leaf_parent, send_leaf, pair_leaf, leaf_coupling, send_mid, pair_mid, mid_coupling, top_pairs, top_coupling):
    point_mask = (jnp.arange(LEAF, dtype=jnp.int32)[None, :] < leaf_size[:, None]).astype(jnp.float32)
    blocks = charges.reshape(LEAVES, LEAF, PORTS) * point_mask[:, :, None]
    coef_leaf = jnp.einsum("lkm,lmp->lkp", leaf_basis, blocks, precision=exact_mode)
    parent_global = ((jnp.arange(LEAVES, dtype=jnp.int32) // LEAVES_DEV) * MIDS_DEV + leaf_parent).astype(jnp.int32)
    moved_up = jnp.einsum("ljk,lkp->ljp", leaf_transfer, coef_leaf, precision=exact_mode)
    coef_mid = jax.ops.segment_sum(moved_up, parent_global, num_segments=MIDS)
    moved_mid = jnp.einsum("mjk,mkp->mjp", mid_transfer, coef_mid, precision=exact_mode)
    coef_top = jnp.sum(moved_mid.reshape(OWNERS, MIDS_DEV, RANK, PORTS), axis=1)
    near_leaf = couple_blocks(leaf_coupling, coef_leaf, source_index(send_leaf, pair_leaf, LEAVES_DEV))
    near_mid = couple_blocks(mid_coupling, coef_mid, source_index(send_mid, pair_mid, MIDS_DEV))
    near_top = couple(top_coupling, coef_top, top_pairs)
    top_spread = jnp.repeat(near_top, MIDS_DEV, axis=0)
    down_mid = near_mid + jnp.einsum("mjk,mjp->mkp", mid_transfer, top_spread, precision=exact_mode)
    from_parent = jnp.take(down_mid, parent_global, axis=0)
    down_leaf = near_leaf + jnp.einsum("ljk,ljp->lkp", leaf_transfer, from_parent, precision=exact_mode)
    far_field = jnp.einsum("lkm,lkp->lmp", leaf_basis, down_leaf, precision=exact_mode) * point_mask[:, :, None]
    return far_field.reshape(UNKNOWNS, PORTS)
```

```python
import functools

import jax
import jax.numpy as jnp
from jax import lax
from jax.experimental import pallas as pl
from jax.experimental.pallas import tpu as pltpu
from jax.sharding import PartitionSpec as P

AXES = ("group", "cluster")
VMEM_LIMIT = 48 * 1024 * 1024


def split(x):
    high = x.astype(jnp.bfloat16)
    low = (x - high.astype(jnp.float32)).astype(jnp.bfloat16)
    return high, low


def rows_of(x):
    return jnp.concatenate(split(x), axis=0)


def lanes_of(x):
    return jnp.concatenate(split(x), axis=1)


def dot(a, b):
    return lax.dot_general(a, b, (((1,), (0,)), ((), ())), preferred_element_type=jnp.float32)


def fold(product):
    m, n = product.shape[0] // 2, product.shape[1] // 2
    return product[:m, :n] + (product[:m, n:] + product[m:, :n] + product[m:, n:])


def up_kernel(
    size, parent, send, charges, basis, transfer, mid_transfer, table, out_leaf, out_up, coef
):
    step = pl.program_id(0)
    group, rank, points = basis.shape
    mids = mid_transfer.shape[0]
    leaves = coef.shape[0]

    @pl.when(step == 0)
    def _():
        out_up[: mids * rank, :] = jnp.zeros((mids * rank, out_up.shape[1]), jnp.float32)
        out_up[(mids + 1) * rank :, :] = table[...]

    point = lax.broadcasted_iota(jnp.int32, (points, charges.shape[1]), 0)
    for g in range(group):
        leaf = step * group + g
        block = jnp.where(point < size[leaf], charges[g * points : (g + 1) * points, :], 0.0)
        value = fold(dot(rows_of(basis[g]), lanes_of(block)))
        coef[leaf] = value
        moved = fold(dot(rows_of(transfer[g]), lanes_of(value)))
        where = pl.ds(pl.multiple_of(parent[leaf] * rank, rank), rank)
        out_up[where, :] += moved

    @pl.when(step == pl.num_programs(0) - 1)
    def _():
        top = jnp.zeros((rank, out_up.shape[1]), jnp.float32)
        for c in range(mids):
            mid = out_up[c * rank : (c + 1) * rank, :]
            top += fold(dot(rows_of(mid_transfer[c]), lanes_of(mid)))
        out_up[mids * rank : (mids + 1) * rank, :] = top

        @pl.loop(0, out_leaf.shape[0], unroll=8)
        def _(slot):
            out_leaf[slot] = coef[jnp.minimum(send[slot], leaves - 1)]


def up_sweep(charges, leaf_size, basis, transfer, mid_transfer, leaf_parent, send_leaf, table):
    leaves, rank, points = basis.shape
    ports = charges.shape[1]
    mids = mid_transfer.shape[0]
    slots = send_leaf.shape[0]
    group = 8
    up_rows = (mids + 1) * rank + table.shape[0]
    whole = lambda shape: pl.BlockSpec(shape, lambda i, *_: (0,) * len(shape))
    return pl.pallas_call(
        up_kernel,
        grid_spec=pltpu.PrefetchScalarGridSpec(
            num_scalar_prefetch=3,
            grid=(leaves // group,),
            in_specs=[
                pl.BlockSpec((group * points, ports), lambda i, *_: (i, 0)),
                pl.BlockSpec((group, rank, points), lambda i, *_: (i, 0, 0)),
                pl.BlockSpec((group, rank, rank), lambda i, *_: (i, 0, 0)),
                whole(mid_transfer.shape),
                whole(table.shape),
            ],
            out_specs=[whole((slots, rank, ports)), whole((up_rows, ports))],
            scratch_shapes=[pltpu.VMEM((leaves, rank, ports), jnp.float32)],
        ),
        out_shape=[
            jax.ShapeDtypeStruct((slots, rank, ports), jnp.float32),
            jax.ShapeDtypeStruct((up_rows, ports), jnp.float32),
        ],
        compiler_params=pltpu.CompilerParams(vmem_limit_bytes=VMEM_LIMIT),
        cost_estimate=pl.CostEstimate(flops=10**9, bytes_accessed=10**7, transcendentals=0),
        name="up_sweep",
    )(leaf_size, leaf_parent, send_leaf, charges, basis, transfer, mid_transfer, table)


def mid_kernel(
    up_rows, first, pair, position, top_pairs, gathered, coupling, top_coupling, mid_transfer,
    down, arrived, parts, top_parts, near_top, sem, top_sem
):
    step = pl.program_id(0)
    group, rank, width = coupling.shape
    slots = parts.shape[0] - 1
    listed_top = top_pairs.shape[1]
    owners = gathered.shape[0] // up_rows
    mids = pair.shape[0]

    @pl.when(step == 0)
    def _():
        @pl.loop(0, slots, unroll=4)
        def _(slot):
            start = pl.multiple_of(first[slot], 8)
            pltpu.make_async_copy(
                gathered.at[pl.ds(start, rank), :],
                arrived.at[pl.ds(pl.multiple_of(slot * rank, rank), rank), :],
                sem,
            ).start()

        for k in range(listed_top):
            source = jnp.clip(top_pairs[position[0], k], 0, owners - 1)
            start = pl.multiple_of(source * up_rows + mids * rank, 8)
            pltpu.make_async_copy(
                gathered.at[pl.ds(start, rank), :],
                top_parts.at[pl.ds(k * rank, rank), :],
                top_sem,
            ).start()
        pltpu.make_async_copy(
            gathered.at[pl.ds(0, listed_top * rank), :], top_parts, top_sem
        ).wait()
        pltpu.make_async_copy(gathered.at[pl.ds(0, slots * rank), :], arrived, sem).wait()

        pieces = []
        for k in range(listed_top):
            live = top_pairs[position[0], k] < owners
            pieces.append(jnp.where(live, top_parts[k * rank : (k + 1) * rank, :], 0.0))
        near_top[...] = fold(
            dot(rows_of(top_coupling[0]), lanes_of(jnp.concatenate(pieces, axis=0)))
        )

        @pl.loop(0, slots, unroll=4)
        def _(slot):
            block = arrived[pl.ds(pl.multiple_of(slot * rank, rank), rank), :]
            parts[slot] = lanes_of(block)

        parts[slots] = jnp.zeros(parts.shape[1:], jnp.bfloat16)

    top = lanes_of(near_top[...])
    for g in range(group):
        c = step * group + g
        stacked = jnp.concatenate([parts[pair[c, k]] for k in range(width // rank)], axis=0)
        near = fold(dot(rows_of(coupling[g]), stacked))
        back = fold(dot(rows_of(mid_transfer[g].T), top))
        down[g] = near + back


def mid_level(up_rows, first, pair, position, top_pairs, gathered, coupling, top_coupling, mid_transfer):
    mids, rank, width = coupling.shape
    ports = gathered.shape[1]
    slots = first.shape[0]
    listed_top = top_pairs.shape[1]
    group = 2
    return pl.pallas_call(
        functools.partial(mid_kernel, up_rows),
        grid_spec=pltpu.PrefetchScalarGridSpec(
            num_scalar_prefetch=4,
            grid=(mids // group,),
            in_specs=[
                pl.BlockSpec(memory_space=pl.ANY),
                pl.BlockSpec((group, rank, width), lambda i, *_: (i, 0, 0)),
                pl.BlockSpec(
                    (1,) + top_coupling.shape[1:], lambda i, first, pair, position, tops: (position[0], 0, 0)
                ),
                pl.BlockSpec((group, rank, rank), lambda i, *_: (i, 0, 0)),
            ],
            out_specs=pl.BlockSpec((group, rank, ports), lambda i, *_: (i, 0, 0)),
            scratch_shapes=[
                pltpu.VMEM((slots * rank, ports), jnp.float32),
                pltpu.VMEM((slots + 1, rank, 2 * ports), jnp.bfloat16),
                pltpu.VMEM((listed_top * rank, ports), jnp.float32),
                pltpu.VMEM((rank, ports), jnp.float32),
                pltpu.SemaphoreType.DMA,
                pltpu.SemaphoreType.DMA,
            ],
        ),
        out_shape=jax.ShapeDtypeStruct((mids, rank, ports), jnp.float32),
        compiler_params=pltpu.CompilerParams(vmem_limit_bytes=VMEM_LIMIT),
        cost_estimate=pl.CostEstimate(flops=2 * 10**9, bytes_accessed=10**7, transcendentals=0),
        name="mid_level",
    )(first, pair, position, top_pairs, gathered, coupling, top_coupling, mid_transfer)


def leaf_kernel(
    size, parent, pair, arrived, coupling, basis, transfer, down_mid, out, parts
):
    step = pl.program_id(0)
    group, rank, width = coupling.shape
    points = basis.shape[2]
    slots = arrived.shape[0]

    @pl.when(step == 0)
    def _():
        @pl.loop(0, slots, unroll=4)
        def _(slot):
            parts[slot] = lanes_of(arrived[slot])

        parts[slots] = jnp.zeros(parts.shape[1:], jnp.bfloat16)

    point = lax.broadcasted_iota(jnp.int32, (points, out.shape[1]), 0)
    for g in range(group):
        leaf = step * group + g
        stacked = jnp.concatenate([parts[pair[leaf, k]] for k in range(width // rank)], axis=0)
        near = fold(dot(rows_of(coupling[g]), stacked))
        back = fold(dot(rows_of(transfer[g].T), lanes_of(down_mid[parent[leaf]])))
        value = near + back
        far = fold(dot(rows_of(basis[g].T), lanes_of(value)))
        out[g * points : (g + 1) * points, :] = jnp.where(point < size[leaf], far, 0.0)


def leaf_level(leaf_size, leaf_parent, pair_leaf, arrived, coupling, basis, transfer, down_mid):
    leaves, rank, width = coupling.shape
    points = basis.shape[2]
    ports = arrived.shape[2]
    slots = arrived.shape[0]
    group = 4
    whole = lambda shape: pl.BlockSpec(shape, lambda i, *_: (0,) * len(shape))
    return pl.pallas_call(
        leaf_kernel,
        grid_spec=pltpu.PrefetchScalarGridSpec(
            num_scalar_prefetch=3,
            grid=(leaves // group,),
            in_specs=[
                whole(arrived.shape),
                pl.BlockSpec((group, rank, width), lambda i, *_: (i, 0, 0)),
                pl.BlockSpec((group, rank, points), lambda i, *_: (i, 0, 0)),
                pl.BlockSpec((group, rank, rank), lambda i, *_: (i, 0, 0)),
                whole(down_mid.shape),
            ],
            out_specs=pl.BlockSpec((group * points, ports), lambda i, *_: (i, 0)),
            scratch_shapes=[pltpu.VMEM((slots + 1, rank, 2 * ports), jnp.bfloat16)],
        ),
        out_shape=jax.ShapeDtypeStruct((leaves * points, ports), jnp.float32),
        compiler_params=pltpu.CompilerParams(vmem_limit_bytes=VMEM_LIMIT),
        cost_estimate=pl.CostEstimate(flops=4 * 10**9, bytes_accessed=2 * 10**7, transcendentals=0),
        name="leaf_level",
    )(leaf_size, leaf_parent, pair_leaf, arrived, coupling, basis, transfer, down_mid)


def body(
    charges, leaf_size, leaf_basis, leaf_transfer, mid_transfer, leaf_parent, send_leaf, pair_leaf,
    leaf_coupling, send_mid, pair_mid, mid_coupling, top_pairs, top_coupling,
):
    rank = leaf_basis.shape[1]
    ports = charges.shape[1]
    mids = mid_transfer.shape[0]
    slots = send_mid.shape[0]
    owners = lax.axis_size(AXES)
    per_pair = slots // owners
    tile = 8 * ports
    table_rows = -(-slots // tile) * 8
    table = jnp.pad(send_mid.astype(jnp.float32), (0, table_rows * ports - slots))
    table = table.reshape(table_rows, ports)
    outgoing, lifted = up_sweep(
        charges, leaf_size, leaf_basis, leaf_transfer, mid_transfer, leaf_parent, send_leaf, table
    )
    up_rows = lifted.shape[0]
    arrived = lax.all_to_all(outgoing, AXES, split_axis=0, concat_axis=0, tiled=True)
    gathered = lax.all_gather(lifted, AXES, axis=0, tiled=True)
    me = lax.axis_index(AXES)
    tables = gathered.reshape(owners, up_rows, ports)[:, (mids + 1) * rank :, :]
    tables = tables.reshape(owners, table_rows * ports)
    mine = lax.dynamic_slice_in_dim(tables, me * per_pair, per_pair, 1).astype(jnp.int32)
    sender = jnp.arange(owners, dtype=jnp.int32)[:, None]
    first = (sender * up_rows + jnp.clip(mine, 0, mids - 1) * rank).reshape(-1)
    position = lax.axis_index("cluster").astype(jnp.int32)[None]
    down_mid = mid_level(
        up_rows, first, pair_mid, position, top_pairs, gathered, mid_coupling, top_coupling,
        mid_transfer,
    )
    return leaf_level(
        leaf_size, leaf_parent, pair_leaf, arrived, leaf_coupling, leaf_basis, leaf_transfer,
        down_mid,
    )


def solution(mesh):
    both = P(AXES)
    in_specs = (
        P(AXES, None),
        both,
        P(AXES, None, None),
        P(AXES, None, None),
        P(AXES, None, None),
        both,
        both,
        P(AXES, None),
        P(AXES, None, None),
        both,
        P(AXES, None),
        P(AXES, None, None),
        P("group", None),
        P("group", None, None),
    )
    return jax.shard_map(
        body, mesh=mesh, in_specs=in_specs, out_specs=P(AXES, None), check_vma=False
    )
```

```python
import functools

import jax
import jax.numpy as jnp
from jax import lax
from jax.experimental import pallas as pl
from jax.experimental.pallas import tpu as pltpu
from jax.sharding import PartitionSpec as P

AXES = ("group", "cluster")
VMEM_LIMIT = 60 * 1024 * 1024


def split(x):
    high = x.astype(jnp.bfloat16)
    low = (x - high.astype(jnp.float32)).astype(jnp.bfloat16)
    return high, low


def rows_of(x):
    return jnp.concatenate(split(x), axis=0)


def lanes_of(x):
    return jnp.concatenate(split(x), axis=1)


def dot(a, b):
    return lax.dot_general(a, b, (((1,), (0,)), ((), ())), preferred_element_type=jnp.float32)


def fold(product):
    m, n = product.shape[0] // 2, product.shape[1] // 2
    return product[:m, :n] + (product[:m, n:] + product[m:, :n] + product[m:, n:])


def up_kernel(
    size, parent, send, charges, basis, transfer, mid_transfer, table, out_leaf, out_up, coef
):
    step = pl.program_id(0)
    group, rank, points = basis.shape
    mids = mid_transfer.shape[0]
    leaves = coef.shape[0]

    @pl.when(step == 0)
    def _():
        out_up[: mids * rank, :] = jnp.zeros((mids * rank, out_up.shape[1]), jnp.float32)
        out_up[(mids + 1) * rank :, :] = table[...]

    point = lax.broadcasted_iota(jnp.int32, (points, charges.shape[1]), 0)
    for g in range(group):
        leaf = step * group + g
        block = jnp.where(point < size[leaf], charges[g * points : (g + 1) * points, :], 0.0)
        value = fold(dot(rows_of(basis[g]), lanes_of(block)))
        coef[leaf] = value
        moved = fold(dot(rows_of(transfer[g]), lanes_of(value)))
        where = pl.ds(pl.multiple_of(parent[leaf] * rank, rank), rank)
        out_up[where, :] += moved

    @pl.when(step == pl.num_programs(0) - 1)
    def _():
        top = jnp.zeros((rank, out_up.shape[1]), jnp.float32)
        for c in range(mids):
            mid = out_up[c * rank : (c + 1) * rank, :]
            top += fold(dot(rows_of(mid_transfer[c]), lanes_of(mid)))
        out_up[mids * rank : (mids + 1) * rank, :] = top

        @pl.loop(0, out_leaf.shape[0], unroll=8)
        def _(slot):
            out_leaf[slot] = coef[jnp.minimum(send[slot], leaves - 1)]


def up_sweep(charges, leaf_size, basis, transfer, mid_transfer, leaf_parent, send_leaf, table):
    leaves, rank, points = basis.shape
    ports = charges.shape[1]
    mids = mid_transfer.shape[0]
    slots = send_leaf.shape[0]
    group = 8
    up_rows = (mids + 1) * rank + table.shape[0]
    whole = lambda shape: pl.BlockSpec(shape, lambda i, *_: (0,) * len(shape))
    return pl.pallas_call(
        up_kernel,
        grid_spec=pltpu.PrefetchScalarGridSpec(
            num_scalar_prefetch=3,
            grid=(leaves // group,),
            in_specs=[
                pl.BlockSpec((group * points, ports), lambda i, *_: (i, 0)),
                pl.BlockSpec((group, rank, points), lambda i, *_: (i, 0, 0)),
                pl.BlockSpec((group, rank, rank), lambda i, *_: (i, 0, 0)),
                whole(mid_transfer.shape),
                whole(table.shape),
            ],
            out_specs=[whole((slots, rank, ports)), whole((up_rows, ports))],
            scratch_shapes=[pltpu.VMEM((leaves, rank, ports), jnp.float32)],
        ),
        out_shape=[
            jax.ShapeDtypeStruct((slots, rank, ports), jnp.float32),
            jax.ShapeDtypeStruct((up_rows, ports), jnp.float32),
        ],
        compiler_params=pltpu.CompilerParams(vmem_limit_bytes=VMEM_LIMIT),
        cost_estimate=pl.CostEstimate(flops=10**9, bytes_accessed=10**7, transcendentals=0),
        name="up_sweep",
    )(leaf_size, leaf_parent, send_leaf, charges, basis, transfer, mid_transfer, table)


def select_kernel(sizes, place, own, other, *refs):
    messages, tables, sem = refs[:-2], refs[-2], refs[-1]
    lines, per_cluster, up_rows, mids, rank, per_pair = sizes
    group, lane = place[0], place[1]
    core = lax.rem(lane, 2)
    table_rows = up_rows - (mids + 1) * rank
    ports = own.shape[1]
    copies = []
    for side, ref in enumerate((own, other)):
        for line in range(lines):
            start = (lines - 1 - line) * up_rows + (mids + 1) * rank
            copies.append(
                pltpu.make_async_copy(
                    ref.at[pl.ds(start, table_rows), :], tables.at[side, line], sem.at[side, line]
                )
            )
    for copy in copies:
        copy.start()
    for copy in copies:
        copy.wait()
    for side, ref in enumerate((own, other)):
        at_core = core if side == 0 else 1 - core
        for line in range(lines):
            base = (lines - 1 - line) * up_rows
            sender = line * 2 + at_core
            for d, message in enumerate(messages):
                receiver = (group ^ d) * per_cluster + lane
                for j in range(per_pair):
                    entry = receiver * per_pair + j
                    listed = tables[side, line, lax.div(entry, ports), lax.rem(entry, ports)]
                    block = jnp.clip(listed.astype(jnp.int32), 0, mids - 1)
                    source = pl.ds(pl.multiple_of(base + block * rank, 8), rank)
                    target = pl.multiple_of((sender * per_pair + j) * rank, rank)
                    message[pl.ds(target, rank), :] = ref[source, :]
                target = pl.multiple_of((per_cluster * per_pair + sender) * rank, rank)
                message[pl.ds(target, rank), :] = ref[base + mids * rank : base + (mids + 1) * rank, :]


def select(sizes, groups, place, own, other):
    lines, per_cluster, up_rows, mids, rank, per_pair = sizes
    ports = own.shape[1]
    table_rows = up_rows - (mids + 1) * rank
    shape = jax.ShapeDtypeStruct((per_cluster * (per_pair + 1) * rank, ports), jnp.float32)
    vmem = pl.BlockSpec(memory_space=pltpu.VMEM)
    return pl.pallas_call(
        functools.partial(select_kernel, sizes),
        in_specs=[pl.BlockSpec(memory_space=pltpu.SMEM), vmem, vmem],
        out_specs=[vmem] * groups,
        out_shape=[shape] * groups,
        scratch_shapes=[
            pltpu.SMEM((2, lines, table_rows, ports), jnp.float32),
            pltpu.SemaphoreType.DMA((2, lines)),
        ],
        compiler_params=pltpu.CompilerParams(vmem_limit_bytes=VMEM_LIMIT),
        cost_estimate=pl.CostEstimate(flops=0, bytes_accessed=6 * 10**6, transcendentals=0),
        name="select",
    )(place, own, other)


def mid_kernel(pair, position, tops, *refs):
    (*messages, coupling, top_coupling, mid_transfer, down, parts, top_parts, near_top) = refs
    step = pl.program_id(0)
    group, rank, width = coupling.shape
    slots = parts.shape[0] - 1
    top_count = top_parts.shape[0] - 1
    per_message, tops_message = slots // len(messages), top_count // len(messages)

    @pl.when(step == 0)
    def _():
        for d, message in enumerate(messages):
            @pl.loop(0, per_message, unroll=4)
            def _(slot):
                block = message[pl.ds(pl.multiple_of(slot * rank, rank), rank), :]
                parts[d * per_message + slot] = lanes_of(block)

            @pl.loop(0, tops_message, unroll=4)
            def _(slot):
                start = pl.multiple_of((per_message + slot) * rank, rank)
                top_parts[d * tops_message + slot] = lanes_of(message[pl.ds(start, rank), :])

        parts[slots] = jnp.zeros(parts.shape[1:], jnp.bfloat16)
        top_parts[top_count] = jnp.zeros(top_parts.shape[1:], jnp.bfloat16)
        stacked = jnp.concatenate([top_parts[tops[k]] for k in range(tops.shape[0])], axis=0)
        near_top[...] = fold(dot(rows_of(top_coupling[0]), stacked))

    top = lanes_of(near_top[...])
    for g in range(group):
        c = step * group + g
        stacked = jnp.concatenate([parts[pair[c, k]] for k in range(width // rank)], axis=0)
        near = fold(dot(rows_of(coupling[g]), stacked))
        back = fold(dot(rows_of(mid_transfer[g].T), top))
        down[g] = near + back


def mid_level(slots, owners, pair, position, tops, messages, coupling, top_coupling, mid_transfer):
    mids, rank, width = coupling.shape
    ports = messages[0].shape[1]
    group = 2
    whole = lambda shape: pl.BlockSpec(shape, lambda i, *_: (0,) * len(shape))
    return pl.pallas_call(
        mid_kernel,
        grid_spec=pltpu.PrefetchScalarGridSpec(
            num_scalar_prefetch=3,
            grid=(mids // group,),
            in_specs=[whole(m.shape) for m in messages]
            + [
                pl.BlockSpec((group, rank, width), lambda i, *_: (i, 0, 0)),
                pl.BlockSpec(
                    (1,) + top_coupling.shape[1:], lambda i, pair, position, tops: (position[0], 0, 0)
                ),
                pl.BlockSpec((group, rank, rank), lambda i, *_: (i, 0, 0)),
            ],
            out_specs=pl.BlockSpec((group, rank, ports), lambda i, *_: (i, 0, 0)),
            scratch_shapes=[
                pltpu.VMEM((slots + 1, rank, 2 * ports), jnp.bfloat16),
                pltpu.VMEM((owners + 1, rank, 2 * ports), jnp.bfloat16),
                pltpu.VMEM((rank, ports), jnp.float32),
            ],
        ),
        out_shape=jax.ShapeDtypeStruct((mids, rank, ports), jnp.float32),
        compiler_params=pltpu.CompilerParams(vmem_limit_bytes=VMEM_LIMIT),
        cost_estimate=pl.CostEstimate(flops=2 * 10**9, bytes_accessed=10**7, transcendentals=0),
        name="mid_level",
    )(pair, position, tops, *messages, coupling, top_coupling, mid_transfer)


def leaf_kernel(
    size, parent, pair, arrived, coupling, basis, transfer, down_mid, out, parts
):
    step = pl.program_id(0)
    group, rank, width = coupling.shape
    points = basis.shape[2]
    slots = arrived.shape[0]

    @pl.when(step == 0)
    def _():
        @pl.loop(0, slots, unroll=4)
        def _(slot):
            parts[slot] = lanes_of(arrived[slot])

        parts[slots] = jnp.zeros(parts.shape[1:], jnp.bfloat16)

    point = lax.broadcasted_iota(jnp.int32, (points, out.shape[1]), 0)
    for g in range(group):
        leaf = step * group + g
        stacked = jnp.concatenate([parts[pair[leaf, k]] for k in range(width // rank)], axis=0)
        near = fold(dot(rows_of(coupling[g]), stacked))
        back = fold(dot(rows_of(transfer[g].T), lanes_of(down_mid[parent[leaf]])))
        value = near + back
        far = fold(dot(rows_of(basis[g].T), lanes_of(value)))
        out[g * points : (g + 1) * points, :] = jnp.where(point < size[leaf], far, 0.0)


def leaf_level(leaf_size, leaf_parent, pair_leaf, arrived, coupling, basis, transfer, down_mid):
    leaves, rank, width = coupling.shape
    points = basis.shape[2]
    ports = arrived.shape[2]
    slots = arrived.shape[0]
    group = 4
    whole = lambda shape: pl.BlockSpec(shape, lambda i, *_: (0,) * len(shape))
    return pl.pallas_call(
        leaf_kernel,
        grid_spec=pltpu.PrefetchScalarGridSpec(
            num_scalar_prefetch=3,
            grid=(leaves // group,),
            in_specs=[
                whole(arrived.shape),
                pl.BlockSpec((group, rank, width), lambda i, *_: (i, 0, 0)),
                pl.BlockSpec((group, rank, points), lambda i, *_: (i, 0, 0)),
                pl.BlockSpec((group, rank, rank), lambda i, *_: (i, 0, 0)),
                whole(down_mid.shape),
            ],
            out_specs=pl.BlockSpec((group * points, ports), lambda i, *_: (i, 0)),
            scratch_shapes=[pltpu.VMEM((slots + 1, rank, 2 * ports), jnp.bfloat16)],
        ),
        out_shape=jax.ShapeDtypeStruct((leaves * points, ports), jnp.float32),
        compiler_params=pltpu.CompilerParams(vmem_limit_bytes=VMEM_LIMIT),
        cost_estimate=pl.CostEstimate(flops=4 * 10**9, bytes_accessed=2 * 10**7, transcendentals=0),
        name="leaf_level",
    )(leaf_size, leaf_parent, pair_leaf, arrived, coupling, basis, transfer, down_mid)


def body(
    charges, leaf_size, leaf_basis, leaf_transfer, mid_transfer, leaf_parent, send_leaf, pair_leaf,
    leaf_coupling, send_mid, pair_mid, mid_coupling, top_pairs, top_coupling,
):
    rank = leaf_basis.shape[1]
    ports = charges.shape[1]
    mids = mid_transfer.shape[0]
    slots = send_mid.shape[0]
    owners = lax.axis_size(AXES)
    groups, per_cluster = lax.axis_size("group"), lax.axis_size("cluster")
    lines = per_cluster // 2
    per_pair = slots // owners
    tile = 8 * ports
    table_rows = -(-slots // tile) * 8
    table = jnp.pad(send_mid.astype(jnp.float32), (0, table_rows * ports - slots))
    table = table.reshape(table_rows, ports)
    outgoing, lifted = up_sweep(
        charges, leaf_size, leaf_basis, leaf_transfer, mid_transfer, leaf_parent, send_leaf, table
    )
    up_rows = lifted.shape[0]
    arrived = lax.all_to_all(outgoing, AXES, split_axis=0, concat_axis=0, tiled=True)

    group, lane = lax.axis_index("group"), lax.axis_index("cluster")
    from_below, from_above = [lifted], [lifted]
    for step in range(1, lines):
        below = [(c, c + 2) for c in range(2 * (step - 1), per_cluster - 2)]
        above = [(c, c - 2) for c in range(2, per_cluster - 2 * (step - 1))]
        from_below.append(lax.ppermute(from_below[-1], "cluster", below))
        from_above.append(lax.ppermute(from_above[-1], "cluster", above))
    line = jnp.concatenate(from_above[:0:-1] + from_below, axis=0)
    own = lax.dynamic_slice_in_dim(line, (lane // 2) * up_rows, lines * up_rows, 0)
    other = lax.ppermute(own, "cluster", [(c, c ^ 1) for c in range(per_cluster)])
    place = jnp.stack([group, lane]).astype(jnp.int32)
    sizes = (lines, per_cluster, up_rows, mids, rank, per_pair)
    messages = select(sizes, groups, place, own, other)
    messages = [
        messages[d] if d == 0 else lax.ppermute(messages[d], "group", [(g, g ^ d) for g in range(groups)])
        for d in range(groups)
    ]

    per_message = per_cluster * per_pair
    spot = ((pair_mid // per_message) ^ group) * per_message + pair_mid % per_message
    spot = jnp.where((pair_mid >= 0) & (pair_mid < slots), spot, slots)
    wanted = lax.dynamic_slice_in_dim(top_pairs, lane, 1, 0)[0]
    tops = ((wanted // per_cluster) ^ group) * per_cluster + wanted % per_cluster
    tops = jnp.where((wanted >= 0) & (wanted < owners), tops, owners)
    position = lane.astype(jnp.int32)[None]
    down_mid = mid_level(
        slots, owners, spot, position, tops, messages, mid_coupling, top_coupling, mid_transfer
    )
    return leaf_level(
        leaf_size, leaf_parent, pair_leaf, arrived, leaf_coupling, leaf_basis, leaf_transfer,
        down_mid,
    )


def solution(mesh):
    both = P(AXES)
    in_specs = (
        P(AXES, None),
        both,
        P(AXES, None, None),
        P(AXES, None, None),
        P(AXES, None, None),
        both,
        both,
        P(AXES, None),
        P(AXES, None, None),
        both,
        P(AXES, None),
        P(AXES, None, None),
        P("group", None),
        P("group", None, None),
    )
    return jax.shard_map(
        body, mesh=mesh, in_specs=in_specs, out_specs=P(AXES, None), check_vma=False
    )
```

```python
import functools

import jax
import jax.numpy as jnp
from jax import lax
from jax.experimental import pallas as pl
from jax.experimental.pallas import tpu as pltpu
from jax.sharding import PartitionSpec as P

AXES = ("group", "cluster")
VMEM_LIMIT = 60 * 1024 * 1024


def params():
    return pltpu.CompilerParams(vmem_limit_bytes=VMEM_LIMIT)


def cost(flops, size):
    return pl.CostEstimate(flops=flops, bytes_accessed=size, transcendentals=0)


def whole(shape):
    return pl.BlockSpec(shape, lambda i, *_: (0,) * len(shape))


def first(group, *rest):
    return pl.BlockSpec((group,) + rest, lambda i, *_: (i,) + (0,) * len(rest))


def split(x):
    high = x.astype(jnp.bfloat16)
    low = (x - high.astype(jnp.float32)).astype(jnp.bfloat16)
    return high, low


def rows_of(x):
    return jnp.concatenate(split(x), axis=0)


def lanes_of(x):
    return jnp.concatenate(split(x), axis=1)


def dot(a, b):
    return lax.dot_general(a, b, (((1,), (0,)), ((), ())), preferred_element_type=jnp.float32)


def fold(product):
    m, n = product.shape[0] // 2, product.shape[1] // 2
    return product[:m, :n] + (product[:m, n:] + product[m:, :n] + product[m:, n:])


def deep_dot(a, b):
    high, low = split(b)
    return dot(jnp.concatenate([a, a], axis=1), jnp.concatenate([high, high, low, low], axis=0))


def up_kernel(size, parent, charges, basis, transfer, mid_transfer, send, coef, up):
    step = pl.program_id(0)
    group, rank, points = basis.shape
    mids = mid_transfer.shape[0]
    ports = up.shape[1]

    @pl.when(step == 0)
    def _():
        up[: mids * rank, :] = jnp.zeros((mids * rank, ports), jnp.float32)
        up[(mids + 1) * rank :, :] = jnp.zeros((up.shape[0] - (mids + 1) * rank, ports), jnp.float32)
        for row in range(send.shape[0]):
            spot = (mids + 1) * rank + row
            up[spot : spot + 1, : send.shape[1]] = send[row : row + 1, :].astype(jnp.float32)

    point = lax.broadcasted_iota(jnp.int32, (points, ports), 0)
    values = []
    for g in range(group):
        block = jnp.where(
            point < size[step * group + g], charges[g * points : (g + 1) * points, :], 0.0
        )
        values.append(fold(dot(rows_of(basis[g]), lanes_of(block))))
    for g in range(group):
        coef[g] = values[g]
    moved = [fold(dot(rows_of(transfer[g]), lanes_of(values[g]))) for g in range(group)]
    for g in range(group):
        where = pl.ds(pl.multiple_of(parent[step * group + g] * rank, rank), rank)
        up[where, :] += moved[g]

    @pl.when(step == pl.num_programs(0) - 1)
    def _():
        terms = [
            fold(dot(rows_of(mid_transfer[c]), lanes_of(up[c * rank : (c + 1) * rank, :])))
            for c in range(mids)
        ]
        while len(terms) > 1:
            terms = [sum(terms[i : i + 2]) for i in range(0, len(terms), 2)]
        up[mids * rank : (mids + 1) * rank, :] = terms[0]


def up_sweep(charges, leaf_size, basis, transfer, mid_transfer, leaf_parent, send_mid):
    leaves, rank, points = basis.shape
    ports = charges.shape[1]
    mids = mid_transfer.shape[0]
    group = 8
    up_rows = (mids + 1) * rank + -(-send_mid.shape[0] // 8) * 8
    return pl.pallas_call(
        up_kernel,
        grid_spec=pltpu.PrefetchScalarGridSpec(
            num_scalar_prefetch=2,
            grid=(leaves // group,),
            in_specs=[
                first(group * points, ports),
                first(group, rank, points),
                first(group, rank, rank),
                whole(mid_transfer.shape),
                whole(send_mid.shape),
            ],
            out_specs=[first(group, rank, ports), whole((up_rows, ports))],
        ),
        out_shape=[
            jax.ShapeDtypeStruct((leaves, rank, ports), jnp.float32),
            jax.ShapeDtypeStruct((up_rows, ports), jnp.float32),
        ],
        compiler_params=params(),
        cost_estimate=cost(10**9, 10**7),
        name="up_sweep",
    )(leaf_size, leaf_parent, charges, basis, transfer, mid_transfer, send_mid)


def spread_kernel(send, coef, out):
    leaves = coef.shape[0]

    @pl.loop(0, out.shape[0], unroll=8)
    def _(slot):
        out[slot] = coef[jnp.minimum(send[slot], leaves - 1)]


def spread(send_leaf, coef):
    vmem = pl.BlockSpec(memory_space=pltpu.VMEM)
    shape = (send_leaf.shape[0],) + coef.shape[1:]
    return pl.pallas_call(
        spread_kernel,
        in_specs=[pl.BlockSpec(memory_space=pltpu.SMEM), vmem],
        out_specs=vmem,
        out_shape=jax.ShapeDtypeStruct(shape, jnp.float32),
        compiler_params=params(),
        cost_estimate=cost(0, 4 * 10**6),
        name="spread",
    )(send_leaf, coef)


def select_kernel(sizes, place, *refs):
    lines, per_cluster, up_rows, mids, rank, per_pair, groups = sizes
    received, messages = refs[: 2 * lines - 1], refs[2 * lines - 1 : 2 * lines - 1 + groups]
    line_buffer, tables, sem, table_sem = refs[2 * lines - 1 + groups :]
    group, lane = place[0], place[1]
    at_line, core = lax.div(lane, 2), lax.rem(lane, 2)
    table_rows = up_rows - (mids + 1) * rank
    ports = line_buffer.shape[2]

    def each(act):
        for index, ref in enumerate(received):
            line = at_line + (lines - 1) - index

            @pl.when((line >= 0) & (line < lines))
            def _():
                spot = jnp.clip(line, 0, lines - 1)
                table = ref.at[pl.ds((mids + 1) * rank, table_rows), :]
                act(pltpu.make_async_copy(table, tables.at[spot], table_sem.at[index]))
                act(pltpu.make_async_copy(ref, line_buffer.at[spot], sem.at[index]))

    each(lambda copy: copy.start())
    each(lambda copy: copy.wait())
    for d, message in enumerate(messages):
        for side in range(2):
            receiver = (group ^ d) * per_cluster + at_line * 2 + (core ^ side)

            @pl.loop(0, lines, unroll=min(lines, 4))
            def _(line):
                for j in range(per_pair):
                    entry = receiver * per_pair + j
                    listed = tables[line, lax.div(entry, ports), lax.rem(entry, ports)]
                    block = jnp.clip(listed.astype(jnp.int32), 0, mids - 1)
                    target = (side * lines + line) * per_pair + j
                    message[target] = line_buffer[line, pl.ds(pl.multiple_of(block * rank, 8), rank), :]

        for line in range(lines):
            message[2 * lines * per_pair + line] = line_buffer[line, mids * rank : (mids + 1) * rank, :]


def select(sizes, place, received):
    lines, per_cluster, up_rows, mids, rank, per_pair, groups = sizes
    ports = received[0].shape[1]
    table_rows = up_rows - (mids + 1) * rank
    shape = jax.ShapeDtypeStruct((lines * (2 * per_pair + 1), rank, ports), jnp.float32)
    return pl.pallas_call(
        functools.partial(select_kernel, sizes),
        in_specs=[pl.BlockSpec(memory_space=pltpu.SMEM)]
        + [pl.BlockSpec(memory_space=pl.ANY)] * len(received),
        out_specs=[pl.BlockSpec(memory_space=pltpu.VMEM)] * groups,
        out_shape=[shape] * groups,
        scratch_shapes=[
            pltpu.VMEM((lines, up_rows, ports), jnp.float32),
            pltpu.SMEM((lines, table_rows, ports), jnp.float32),
            pltpu.SemaphoreType.DMA((2 * lines - 1,)),
            pltpu.SemaphoreType.DMA((2 * lines - 1,)),
        ],
        compiler_params=params(),
        cost_estimate=cost(0, 4 * 10**6),
        name="select",
    )(place, *received)


def prepare_kernel(after, coupling, basis, transfer, mid_coupling, mid_transfer, *out):
    wide, basis_t, transfer_t, mid_wide, mid_transfer_t = out
    for g in range(coupling.shape[0]):
        wide[g] = rows_of(coupling[g])
        basis_t[g] = rows_of(basis[g]).T
        transfer_t[g] = rows_of(transfer[g]).T
    for g in range(mid_coupling.shape[0]):
        mid_wide[g] = rows_of(mid_coupling[g])
        mid_transfer_t[g] = rows_of(mid_transfer[g]).T


def prepare(after, coupling, basis, transfer, mid_coupling, mid_transfer):
    leaves, rank, width = coupling.shape
    points = basis.shape[2]
    mids, _, mid_width = mid_coupling.shape
    steps = mids
    group = leaves // steps
    shapes = [
        (leaves, 2 * rank, width),
        (leaves, points, 2 * rank),
        (leaves, rank, 2 * rank),
        (mids, 2 * rank, mid_width),
        (mids, rank, 2 * rank),
    ]
    return pl.pallas_call(
        prepare_kernel,
        grid=(steps,),
        in_specs=[
            pl.BlockSpec(memory_space=pl.ANY),
            first(group, rank, width),
            first(group, rank, points),
            first(group, rank, rank),
            first(1, rank, mid_width),
            first(1, rank, rank),
        ],
        out_specs=[first(s[0] // steps, *s[1:]) for s in shapes],
        out_shape=[jax.ShapeDtypeStruct(s, jnp.bfloat16) for s in shapes],
        compiler_params=params(),
        cost_estimate=cost(0, 3 * 10**7),
        name="prepare",
    )(after, coupling, basis, transfer, mid_coupling, mid_transfer)


def mid_kernel(sizes, parent, pair, position, tops, *refs):
    lines, per_pair, groups = sizes
    near_side, far_side = refs[:groups], refs[groups : 2 * groups]
    coupling, top_coupling, mid_transfer, transfer, back, parts, top_parts, near_top, down = refs[2 * groups :]
    step = pl.program_id(0)
    leaves = back.shape[0]
    group, _, width = coupling.shape
    rank = near_top.shape[0]
    slots, top_count = parts.shape[0] - 1, top_parts.shape[0] - 1
    piece = lines * per_pair

    @pl.when(step == 0)
    def _():
        for d in range(groups):
            for side, (ref, skip) in enumerate(((near_side[d], 2 * piece), (far_side[d], piece))):
                @pl.loop(0, piece, unroll=4)
                def _(slot):
                    parts[(2 * d + side) * piece + slot] = lanes_of(ref[slot])

                @pl.loop(0, lines, unroll=4)
                def _(line):
                    top_parts[(2 * d + side) * lines + line] = lanes_of(ref[skip + line])

        parts[slots] = jnp.zeros(parts.shape[1:], jnp.bfloat16)
        top_parts[top_count] = jnp.zeros(top_parts.shape[1:], jnp.bfloat16)
        stacked = jnp.concatenate([top_parts[tops[k]] for k in range(tops.shape[0])], axis=0)
        near_top[...] = fold(dot(rows_of(top_coupling[0]), stacked))

    near = []
    for g in range(group):
        c = step * group + g
        stacked = jnp.concatenate([parts[pair[c, k]] for k in range(width // rank)], axis=0)
        near.append(fold(dot(coupling[g], stacked)) + deep_dot(mid_transfer[g], near_top[...]))
    for g in range(group):
        down[step * group + g] = near[g]

    @pl.when(step == pl.num_programs(0) - 1)
    def _():
        @pl.loop(0, leaves, unroll=8)
        def _(leaf):
            back[leaf] = deep_dot(transfer[leaf], down[parent[leaf]])


def mid_level(sizes, parent, pair, position, tops, near_side, far_side, coupling, top_coupling, mid_transfer, transfer):
    lines, per_pair, groups = sizes
    mids, _, width = coupling.shape
    rank, ports = near_side[0].shape[1:]
    leaves = transfer.shape[0]
    owners = 2 * lines * groups
    group = 2
    return pl.pallas_call(
        functools.partial(mid_kernel, sizes),
        grid_spec=pltpu.PrefetchScalarGridSpec(
            num_scalar_prefetch=4,
            grid=(mids // group,),
            in_specs=[whole(m.shape) for m in near_side + far_side]
            + [
                first(group, 2 * rank, width),
                pl.BlockSpec(
                    (1,) + top_coupling.shape[1:],
                    lambda i, parent, pair, position, tops: (position[0], 0, 0),
                ),
                first(group, rank, 2 * rank),
                whole(transfer.shape),
            ],
            out_specs=whole((leaves, rank, ports)),
            scratch_shapes=[
                pltpu.VMEM((owners * per_pair + 1, rank, 2 * ports), jnp.bfloat16),
                pltpu.VMEM((owners + 1, rank, 2 * ports), jnp.bfloat16),
                pltpu.VMEM((rank, ports), jnp.float32),
                pltpu.VMEM((mids, rank, ports), jnp.float32),
            ],
        ),
        out_shape=jax.ShapeDtypeStruct((leaves, rank, ports), jnp.float32),
        compiler_params=params(),
        cost_estimate=cost(2 * 10**9, 10**7),
        name="mid_level",
    )(parent, pair, position, tops, *near_side, *far_side, coupling, top_coupling, mid_transfer, transfer)


def leaf_kernel(size, pair, arrived, coupling, basis, back, out, parts):
    step = pl.program_id(0)
    group, rank, _ = back.shape
    points = basis.shape[1]
    slots = arrived.shape[0]

    @pl.when(step == 0)
    def _():
        @pl.loop(0, slots, unroll=8)
        def _(slot):
            parts[slot] = lanes_of(arrived[slot])

        parts[slots] = jnp.zeros(parts.shape[1:], jnp.bfloat16)

    point = lax.broadcasted_iota(jnp.int32, (points, out.shape[1]), 0)
    values = []
    for g in range(group):
        leaf = step * group + g
        stacked = jnp.concatenate([parts[pair[leaf, k]] for k in range(coupling.shape[2] // rank)], axis=0)
        values.append(fold(dot(coupling[g], stacked)) + back[g])
    for g in range(group):
        far = deep_dot(basis[g], values[g])
        out[g * points : (g + 1) * points, :] = jnp.where(point < size[step * group + g], far, 0.0)


def leaf_level(leaf_size, pair_leaf, arrived, coupling, basis, back):
    leaves, _, width = coupling.shape
    points = basis.shape[1]
    slots, rank, ports = arrived.shape
    group = 4
    return pl.pallas_call(
        leaf_kernel,
        grid_spec=pltpu.PrefetchScalarGridSpec(
            num_scalar_prefetch=2,
            grid=(leaves // group,),
            in_specs=[
                whole(arrived.shape),
                first(group, 2 * rank, width),
                first(group, points, 2 * rank),
                first(group, rank, ports),
            ],
            out_specs=first(group * points, ports),
            scratch_shapes=[pltpu.VMEM((slots + 1, rank, 2 * ports), jnp.bfloat16)],
        ),
        out_shape=jax.ShapeDtypeStruct((leaves * points, ports), jnp.float32),
        compiler_params=params(),
        cost_estimate=cost(4 * 10**9, 2 * 10**7),
        name="leaf_level",
    )(leaf_size, pair_leaf, arrived, coupling, basis, back)


def body(
    charges, leaf_size, leaf_basis, leaf_transfer, mid_transfer, leaf_parent, send_leaf, pair_leaf,
    leaf_coupling, send_mid, pair_mid, mid_coupling, top_pairs, top_coupling,
):
    rank = leaf_basis.shape[1]
    ports = charges.shape[1]
    mids = mid_transfer.shape[0]
    slots = send_mid.shape[0]
    groups, per_cluster = lax.axis_size("group"), lax.axis_size("cluster")
    owners = groups * per_cluster
    lines = per_cluster // 2
    per_pair = slots // owners
    group, lane = lax.axis_index("group"), lax.axis_index("cluster")

    table = send_mid.reshape(-1, min(slots, ports))
    coef, lifted = up_sweep(
        charges, leaf_size, leaf_basis, leaf_transfer, mid_transfer, leaf_parent, table
    )
    up_rows = lifted.shape[0]
    outgoing = spread(send_leaf, coef)

    from_below, from_above = [lifted], [lifted]
    for step in range(1, lines):
        below = [(c, c + 2) for c in range(2 * (step - 1), per_cluster - 2)]
        above = [(c, c - 2) for c in range(2, per_cluster - 2 * (step - 1))]
        if step == lines - 1:
            outgoing, from_below[-1], from_above[-1] = lax.optimization_barrier(
                (outgoing, from_below[-1], from_above[-1])
            )
        from_below.append(lax.ppermute(from_below[-1], "cluster", below))
        from_above.append(lax.ppermute(from_above[-1], "cluster", above))
    arrived = lax.all_to_all(outgoing, AXES, split_axis=0, concat_axis=0, tiled=True)

    wide, basis_t, transfer_t, mid_wide, mid_transfer_t = prepare(
        from_below[1], leaf_coupling, leaf_basis, leaf_transfer, mid_coupling, mid_transfer
    )

    place = jnp.stack([group, lane]).astype(jnp.int32)
    sizes = (lines, per_cluster, up_rows, mids, rank, per_pair, groups)
    messages = select(sizes, place, from_above[:0:-1] + from_below)
    near_side, far_side = [], []
    for d in range(groups):
        message = messages[d]
        if d:
            message = lax.ppermute(message, "group", [(g, g ^ d) for g in range(groups)])
        near_side.append(message)
        far_side.append(
            lax.ppermute(
                message[lines * per_pair :], "cluster", [(c, c ^ 1) for c in range(per_cluster)]
            )
        )

    def spot_of(sender):
        at_group, at_lane = sender // per_cluster, sender % per_cluster
        return ((at_group ^ group) * 2 + ((at_lane ^ lane) & 1)) * lines + at_lane // 2

    spot = spot_of(pair_mid // per_pair) * per_pair + pair_mid % per_pair
    spot = jnp.where((pair_mid >= 0) & (pair_mid < slots), spot, slots)
    wanted = lax.dynamic_slice_in_dim(top_pairs, lane, 1, 0)[0]
    tops = jnp.where((wanted >= 0) & (wanted < owners), spot_of(wanted), owners)
    position = lane.astype(jnp.int32)[None]
    back = mid_level(
        (lines, per_pair, groups), leaf_parent, spot, position, tops, near_side, far_side,
        mid_wide, top_coupling, mid_transfer_t, transfer_t,
    )
    return leaf_level(leaf_size, pair_leaf, arrived, wide, basis_t, back)


def solution(mesh):
    both = P(AXES)
    in_specs = (
        P(AXES, None),
        both,
        P(AXES, None, None),
        P(AXES, None, None),
        P(AXES, None, None),
        both,
        both,
        P(AXES, None),
        P(AXES, None, None),
        both,
        P(AXES, None),
        P(AXES, None, None),
        P("group", None),
        P("group", None, None),
    )
    return jax.shard_map(
        body, mesh=mesh, in_specs=in_specs, out_specs=P(AXES, None), check_vma=False
    )
```

```python
import functools

import jax
import jax.numpy as jnp
from jax import lax
from jax.experimental import pallas as pl
from jax.experimental.pallas import tpu as pltpu
from jax.sharding import PartitionSpec as P

AXES = ("group", "cluster")
VMEM_LIMIT = 60 * 1024 * 1024


def params():
    return pltpu.CompilerParams(vmem_limit_bytes=VMEM_LIMIT)


def cost(flops, size):
    return pl.CostEstimate(flops=flops, bytes_accessed=size, transcendentals=0)


def whole(shape):
    return pl.BlockSpec(shape, lambda i, *_: (0,) * len(shape))


def first(group, *rest):
    return pl.BlockSpec((group,) + rest, lambda i, *_: (i,) + (0,) * len(rest))


def split(x):
    high = x.astype(jnp.bfloat16)
    low = (x - high.astype(jnp.float32)).astype(jnp.bfloat16)
    return high, low


def rows_of(x):
    return jnp.concatenate(split(x), axis=0)


def lanes_of(x):
    return jnp.concatenate(split(x), axis=1)


def dot(a, b):
    return lax.dot_general(a, b, (((1,), (0,)), ((), ())), preferred_element_type=jnp.float32)


def fold(product):
    m, n = product.shape[0] // 2, product.shape[1] // 2
    return product[:m, :n] + (product[:m, n:] + product[m:, :n] + product[m:, n:])


def deep_dot(a, b):
    high, low = split(b)
    return dot(jnp.concatenate([a, a], axis=1), jnp.concatenate([high, high, low, low], axis=0))


def up_kernel(size, parent, charges, basis, transfer, mid_transfer, send, coef, up):
    step = pl.program_id(0)
    group, rank, points = basis.shape
    mids = mid_transfer.shape[0]
    ports = up.shape[1]

    @pl.when(step == 0)
    def _():
        up[: mids * rank, :] = jnp.zeros((mids * rank, ports), jnp.float32)
        up[(mids + 1) * rank :, :] = jnp.zeros((up.shape[0] - (mids + 1) * rank, ports), jnp.float32)
        for row in range(send.shape[0]):
            spot = (mids + 1) * rank + row
            up[spot : spot + 1, : send.shape[1]] = send[row : row + 1, :].astype(jnp.float32)

    point = lax.broadcasted_iota(jnp.int32, (points, ports), 0)
    values = []
    for g in range(group):
        block = jnp.where(
            point < size[step * group + g], charges[g * points : (g + 1) * points, :], 0.0
        )
        values.append(fold(dot(rows_of(basis[g]), lanes_of(block))))
    for g in range(group):
        coef[g] = values[g]
    moved = [fold(dot(rows_of(transfer[g]), lanes_of(values[g]))) for g in range(group)]
    for g in range(group):
        where = pl.ds(pl.multiple_of(parent[step * group + g] * rank, rank), rank)
        up[where, :] += moved[g]

    @pl.when(step == pl.num_programs(0) - 1)
    def _():
        terms = [
            fold(dot(rows_of(mid_transfer[c]), lanes_of(up[c * rank : (c + 1) * rank, :])))
            for c in range(mids)
        ]
        while len(terms) > 1:
            terms = [sum(terms[i : i + 2]) for i in range(0, len(terms), 2)]
        up[mids * rank : (mids + 1) * rank, :] = terms[0]


def up_sweep(charges, leaf_size, basis, transfer, mid_transfer, leaf_parent, send_mid):
    leaves, rank, points = basis.shape
    ports = charges.shape[1]
    mids = mid_transfer.shape[0]
    group = 8
    up_rows = (mids + 1) * rank + -(-send_mid.shape[0] // 8) * 8
    return pl.pallas_call(
        up_kernel,
        grid_spec=pltpu.PrefetchScalarGridSpec(
            num_scalar_prefetch=2,
            grid=(leaves // group,),
            in_specs=[
                first(group * points, ports),
                first(group, rank, points),
                first(group, rank, rank),
                whole(mid_transfer.shape),
                whole(send_mid.shape),
            ],
            out_specs=[first(group, rank, ports), whole((up_rows, ports))],
        ),
        out_shape=[
            jax.ShapeDtypeStruct((leaves, rank, ports), jnp.float32),
            jax.ShapeDtypeStruct((up_rows, ports), jnp.float32),
        ],
        compiler_params=params(),
        cost_estimate=cost(10**9, 10**7),
        name="up_sweep",
    )(leaf_size, leaf_parent, charges, basis, transfer, mid_transfer, send_mid)


def spread_kernel(send, coef, out):
    leaves = coef.shape[0]

    @pl.loop(0, out.shape[0], unroll=8)
    def _(slot):
        out[slot] = coef[jnp.minimum(send[slot], leaves - 1)]


def spread(send_leaf, coef):
    vmem = pl.BlockSpec(memory_space=pltpu.VMEM)
    shape = (send_leaf.shape[0],) + coef.shape[1:]
    return pl.pallas_call(
        spread_kernel,
        in_specs=[pl.BlockSpec(memory_space=pltpu.SMEM), vmem],
        out_specs=vmem,
        out_shape=jax.ShapeDtypeStruct(shape, jnp.float32),
        compiler_params=params(),
        cost_estimate=cost(0, 4 * 10**6),
        name="spread",
    )(send_leaf, coef)


def select_kernel(sizes, place, *refs):
    lines, per_cluster, up_rows, mids, rank, per_pair, groups = sizes
    received, messages = refs[:lines], refs[lines : lines + groups]
    line_buffer, tables, sem, table_sem = refs[lines + groups :]
    group, lane = place[0], place[1]
    at_line, core = lax.div(lane, 2), lax.rem(lane, 2)
    table_rows = up_rows - (mids + 1) * rank
    ports = line_buffer.shape[2]
    copies = []
    for d, ref in enumerate(received):
        table = ref.at[pl.ds((mids + 1) * rank, table_rows), :]
        copies.append(pltpu.make_async_copy(table, tables.at[at_line ^ d], table_sem.at[d]))
        copies.append(pltpu.make_async_copy(ref, line_buffer.at[at_line ^ d], sem.at[d]))
    for copy in copies:
        copy.start()
    for copy in copies:
        copy.wait()
    for d, message in enumerate(messages):
        for side in range(2):
            receiver = (group ^ d) * per_cluster + at_line * 2 + (core ^ side)

            @pl.loop(0, lines, unroll=min(lines, 4))
            def _(line):
                for j in range(per_pair):
                    entry = receiver * per_pair + j
                    listed = tables[line, lax.div(entry, ports), lax.rem(entry, ports)]
                    block = jnp.clip(listed.astype(jnp.int32), 0, mids - 1)
                    target = (side * lines + line) * per_pair + j
                    message[target] = line_buffer[line, pl.ds(pl.multiple_of(block * rank, 8), rank), :]

        for line in range(lines):
            message[2 * lines * per_pair + line] = line_buffer[line, mids * rank : (mids + 1) * rank, :]


def select(sizes, place, received):
    lines, per_cluster, up_rows, mids, rank, per_pair, groups = sizes
    ports = received[0].shape[1]
    table_rows = up_rows - (mids + 1) * rank
    shape = jax.ShapeDtypeStruct((lines * (2 * per_pair + 1), rank, ports), jnp.float32)
    return pl.pallas_call(
        functools.partial(select_kernel, sizes),
        in_specs=[pl.BlockSpec(memory_space=pltpu.SMEM)]
        + [pl.BlockSpec(memory_space=pl.ANY)] * len(received),
        out_specs=[pl.BlockSpec(memory_space=pltpu.VMEM)] * groups,
        out_shape=[shape] * groups,
        scratch_shapes=[
            pltpu.VMEM((lines, up_rows, ports), jnp.float32),
            pltpu.SMEM((lines, table_rows, ports), jnp.float32),
            pltpu.SemaphoreType.DMA((lines,)),
            pltpu.SemaphoreType.DMA((lines,)),
        ],
        compiler_params=params(),
        cost_estimate=cost(0, 4 * 10**6),
        name="select",
    )(place, *received)


def prepare_kernel(after, coupling, basis, transfer, mid_coupling, mid_transfer, *out):
    wide, basis_t, transfer_t, mid_wide, mid_transfer_t = out
    for g in range(coupling.shape[0]):
        wide[g] = rows_of(coupling[g])
        basis_t[g] = rows_of(basis[g]).T
        transfer_t[g] = rows_of(transfer[g]).T
    for g in range(mid_coupling.shape[0]):
        mid_wide[g] = rows_of(mid_coupling[g])
        mid_transfer_t[g] = rows_of(mid_transfer[g]).T


def prepare(after, coupling, basis, transfer, mid_coupling, mid_transfer):
    leaves, rank, width = coupling.shape
    points = basis.shape[2]
    mids, _, mid_width = mid_coupling.shape
    steps = mids
    group = leaves // steps
    shapes = [
        (leaves, 2 * rank, width),
        (leaves, points, 2 * rank),
        (leaves, rank, 2 * rank),
        (mids, 2 * rank, mid_width),
        (mids, rank, 2 * rank),
    ]
    return pl.pallas_call(
        prepare_kernel,
        grid=(steps,),
        in_specs=[
            pl.BlockSpec(memory_space=pl.ANY),
            first(group, rank, width),
            first(group, rank, points),
            first(group, rank, rank),
            first(1, rank, mid_width),
            first(1, rank, rank),
        ],
        out_specs=[first(s[0] // steps, *s[1:]) for s in shapes],
        out_shape=[jax.ShapeDtypeStruct(s, jnp.bfloat16) for s in shapes],
        compiler_params=params(),
        cost_estimate=cost(0, 3 * 10**7),
        name="prepare",
    )(after, coupling, basis, transfer, mid_coupling, mid_transfer)


def mid_kernel(sizes, parent, pair, position, tops, *refs):
    lines, per_pair, groups = sizes
    near_side, far_side = refs[:groups], refs[groups : 2 * groups]
    coupling, top_coupling, mid_transfer, transfer, back, parts, top_parts, near_top, down = refs[2 * groups :]
    step = pl.program_id(0)
    leaves = back.shape[0]
    group, _, width = coupling.shape
    rank = near_top.shape[0]
    slots, top_count = parts.shape[0] - 1, top_parts.shape[0] - 1
    piece = lines * per_pair

    @pl.when(step == 0)
    def _():
        for d in range(groups):
            for side, (ref, skip) in enumerate(((near_side[d], 2 * piece), (far_side[d], piece))):
                @pl.loop(0, piece, unroll=4)
                def _(slot):
                    parts[(2 * d + side) * piece + slot] = lanes_of(ref[slot])

                @pl.loop(0, lines, unroll=4)
                def _(line):
                    top_parts[(2 * d + side) * lines + line] = lanes_of(ref[skip + line])

        parts[slots] = jnp.zeros(parts.shape[1:], jnp.bfloat16)
        top_parts[top_count] = jnp.zeros(top_parts.shape[1:], jnp.bfloat16)
        stacked = jnp.concatenate([top_parts[tops[k]] for k in range(tops.shape[0])], axis=0)
        near_top[...] = fold(dot(rows_of(top_coupling[0]), stacked))

    near = []
    for g in range(group):
        c = step * group + g
        stacked = jnp.concatenate([parts[pair[c, k]] for k in range(width // rank)], axis=0)
        near.append(fold(dot(coupling[g], stacked)) + deep_dot(mid_transfer[g], near_top[...]))
    for g in range(group):
        down[step * group + g] = near[g]

    @pl.when(step == pl.num_programs(0) - 1)
    def _():
        @pl.loop(0, leaves, unroll=8)
        def _(leaf):
            back[leaf] = deep_dot(transfer[leaf], down[parent[leaf]])


def mid_level(sizes, parent, pair, position, tops, near_side, far_side, coupling, top_coupling, mid_transfer, transfer):
    lines, per_pair, groups = sizes
    mids, _, width = coupling.shape
    rank, ports = near_side[0].shape[1:]
    leaves = transfer.shape[0]
    owners = 2 * lines * groups
    group = 2
    return pl.pallas_call(
        functools.partial(mid_kernel, sizes),
        grid_spec=pltpu.PrefetchScalarGridSpec(
            num_scalar_prefetch=4,
            grid=(mids // group,),
            in_specs=[whole(m.shape) for m in near_side + far_side]
            + [
                first(group, 2 * rank, width),
                pl.BlockSpec(
                    (1,) + top_coupling.shape[1:],
                    lambda i, parent, pair, position, tops: (position[0], 0, 0),
                ),
                first(group, rank, 2 * rank),
                whole(transfer.shape),
            ],
            out_specs=whole((leaves, rank, ports)),
            scratch_shapes=[
                pltpu.VMEM((owners * per_pair + 1, rank, 2 * ports), jnp.bfloat16),
                pltpu.VMEM((owners + 1, rank, 2 * ports), jnp.bfloat16),
                pltpu.VMEM((rank, ports), jnp.float32),
                pltpu.VMEM((mids, rank, ports), jnp.float32),
            ],
        ),
        out_shape=jax.ShapeDtypeStruct((leaves, rank, ports), jnp.float32),
        compiler_params=params(),
        cost_estimate=cost(2 * 10**9, 10**7),
        name="mid_level",
    )(parent, pair, position, tops, *near_side, *far_side, coupling, top_coupling, mid_transfer, transfer)


def leaf_kernel(size, pair, arrived, coupling, basis, back, out, parts):
    step = pl.program_id(0)
    group, rank, _ = back.shape
    points = basis.shape[1]
    slots = arrived.shape[0]

    @pl.when(step == 0)
    def _():
        @pl.loop(0, slots, unroll=8)
        def _(slot):
            parts[slot] = lanes_of(arrived[slot])

        parts[slots] = jnp.zeros(parts.shape[1:], jnp.bfloat16)

    point = lax.broadcasted_iota(jnp.int32, (points, out.shape[1]), 0)
    values = []
    for g in range(group):
        leaf = step * group + g
        stacked = jnp.concatenate([parts[pair[leaf, k]] for k in range(coupling.shape[2] // rank)], axis=0)
        values.append(fold(dot(coupling[g], stacked)) + back[g])
    for g in range(group):
        far = deep_dot(basis[g], values[g])
        out[g * points : (g + 1) * points, :] = jnp.where(point < size[step * group + g], far, 0.0)


def leaf_level(leaf_size, pair_leaf, arrived, coupling, basis, back):
    leaves, _, width = coupling.shape
    points = basis.shape[1]
    slots, rank, ports = arrived.shape
    group = 4
    return pl.pallas_call(
        leaf_kernel,
        grid_spec=pltpu.PrefetchScalarGridSpec(
            num_scalar_prefetch=2,
            grid=(leaves // group,),
            in_specs=[
                whole(arrived.shape),
                first(group, 2 * rank, width),
                first(group, points, 2 * rank),
                first(group, rank, ports),
            ],
            out_specs=first(group * points, ports),
            scratch_shapes=[pltpu.VMEM((slots + 1, rank, 2 * ports), jnp.bfloat16)],
        ),
        out_shape=jax.ShapeDtypeStruct((leaves * points, ports), jnp.float32),
        compiler_params=params(),
        cost_estimate=cost(4 * 10**9, 2 * 10**7),
        name="leaf_level",
    )(leaf_size, pair_leaf, arrived, coupling, basis, back)


def body(
    charges, leaf_size, leaf_basis, leaf_transfer, mid_transfer, leaf_parent, send_leaf, pair_leaf,
    leaf_coupling, send_mid, pair_mid, mid_coupling, top_pairs, top_coupling,
):
    rank = leaf_basis.shape[1]
    ports = charges.shape[1]
    mids = mid_transfer.shape[0]
    slots = send_mid.shape[0]
    groups, per_cluster = lax.axis_size("group"), lax.axis_size("cluster")
    owners = groups * per_cluster
    lines = per_cluster // 2
    per_pair = slots // owners
    group, lane = lax.axis_index("group"), lax.axis_index("cluster")

    table = send_mid.reshape(-1, min(slots, ports))
    coef, lifted = up_sweep(
        charges, leaf_size, leaf_basis, leaf_transfer, mid_transfer, leaf_parent, table
    )
    up_rows = lifted.shape[0]
    outgoing = spread(send_leaf, coef)

    received = [lifted]
    for d in range(1, lines):
        received.append(
            lax.ppermute(lifted, "cluster", [(c, c ^ (2 * d)) for c in range(per_cluster)])
        )
    outgoing, received[1] = lax.optimization_barrier((outgoing, received[1]))
    arrived = lax.all_to_all(outgoing, AXES, split_axis=0, concat_axis=0, tiled=True)

    wide, basis_t, transfer_t, mid_wide, mid_transfer_t = prepare(
        lifted, leaf_coupling, leaf_basis, leaf_transfer, mid_coupling, mid_transfer
    )

    place = jnp.stack([group, lane]).astype(jnp.int32)
    sizes = (lines, per_cluster, up_rows, mids, rank, per_pair, groups)
    messages = select(sizes, place, received)
    near_side, far_side = [], []
    for d in range(groups):
        message = messages[d]
        if d:
            message = lax.ppermute(message, "group", [(g, g ^ d) for g in range(groups)])
            message, mid_wide = lax.optimization_barrier((message, mid_wide))
        near_side.append(message)
        far_side.append(
            lax.ppermute(
                message[lines * per_pair :], "cluster", [(c, c ^ 1) for c in range(per_cluster)]
            )
        )

    def spot_of(sender):
        at_group, at_lane = sender // per_cluster, sender % per_cluster
        return ((at_group ^ group) * 2 + ((at_lane ^ lane) & 1)) * lines + at_lane // 2

    spot = spot_of(pair_mid // per_pair) * per_pair + pair_mid % per_pair
    spot = jnp.where((pair_mid >= 0) & (pair_mid < slots), spot, slots)
    wanted = lax.dynamic_slice_in_dim(top_pairs, lane, 1, 0)[0]
    tops = jnp.where((wanted >= 0) & (wanted < owners), spot_of(wanted), owners)
    position = lane.astype(jnp.int32)[None]
    back = mid_level(
        (lines, per_pair, groups), leaf_parent, spot, position, tops, near_side, far_side,
        mid_wide, top_coupling, mid_transfer_t, transfer_t,
    )
    return leaf_level(leaf_size, pair_leaf, arrived, wide, basis_t, back)


def solution(mesh):
    both = P(AXES)
    in_specs = (
        P(AXES, None),
        both,
        P(AXES, None, None),
        P(AXES, None, None),
        P(AXES, None, None),
        both,
        both,
        P(AXES, None),
        P(AXES, None, None),
        both,
        P(AXES, None),
        P(AXES, None, None),
        P("group", None),
        P("group", None, None),
    )
    return jax.shard_map(
        body, mesh=mesh, in_specs=in_specs, out_specs=P(AXES, None), check_vma=False
    )
```

```python
import functools

import jax
import jax.numpy as jnp
from jax import lax
from jax.experimental import pallas as pl
from jax.experimental.pallas import tpu as pltpu
from jax.sharding import PartitionSpec as P

AXES = ("group", "cluster")
VMEM_LIMIT = 60 * 1024 * 1024


def params():
    return pltpu.CompilerParams(vmem_limit_bytes=VMEM_LIMIT)


def cost(flops, size):
    return pl.CostEstimate(flops=flops, bytes_accessed=size, transcendentals=0)


def whole(shape):
    return pl.BlockSpec(shape, lambda i, *_: (0,) * len(shape))


def first(group, *rest):
    return pl.BlockSpec((group,) + rest, lambda i, *_: (i,) + (0,) * len(rest))


def split(x):
    high = x.astype(jnp.bfloat16)
    low = (x - high.astype(jnp.float32)).astype(jnp.bfloat16)
    return high, low


def rows_of(x):
    return jnp.concatenate(split(x), axis=0)


def lanes_of(x):
    return jnp.concatenate(split(x), axis=1)


def dot(a, b):
    return lax.dot_general(a, b, (((1,), (0,)), ((), ())), preferred_element_type=jnp.float32)


def fold(product):
    m, n = product.shape[0] // 2, product.shape[1] // 2
    return product[:m, :n] + (product[:m, n:] + product[m:, :n] + product[m:, n:])


def deep_dot(a, b):
    high, low = split(b)
    return dot(jnp.concatenate([a, a], axis=1), jnp.concatenate([high, high, low, low], axis=0))


def up_kernel(size, parent, charges, basis, transfer, mid_transfer, send, coef, up):
    step = pl.program_id(0)
    group, rank, points = basis.shape
    mids = mid_transfer.shape[0]
    ports = up.shape[1]

    @pl.when(step == 0)
    def _():
        up[: mids * rank, :] = jnp.zeros((mids * rank, ports), jnp.float32)
        up[(mids + 1) * rank :, :] = jnp.zeros((up.shape[0] - (mids + 1) * rank, ports), jnp.float32)
        for row in range(send.shape[0]):
            spot = (mids + 1) * rank + row
            up[spot : spot + 1, : send.shape[1]] = send[row : row + 1, :].astype(jnp.float32)

    point = lax.broadcasted_iota(jnp.int32, (points, ports), 0)
    values = []
    for g in range(group):
        block = jnp.where(
            point < size[step * group + g], charges[g * points : (g + 1) * points, :], 0.0
        )
        values.append(fold(dot(rows_of(basis[g]), lanes_of(block))))
    for g in range(group):
        coef[g] = values[g]
    moved = [fold(dot(rows_of(transfer[g]), lanes_of(values[g]))) for g in range(group)]
    for g in range(group):
        where = pl.ds(pl.multiple_of(parent[step * group + g] * rank, rank), rank)
        up[where, :] += moved[g]

    @pl.when(step == pl.num_programs(0) - 1)
    def _():
        terms = [
            fold(dot(rows_of(mid_transfer[c]), lanes_of(up[c * rank : (c + 1) * rank, :])))
            for c in range(mids)
        ]
        while len(terms) > 1:
            terms = [sum(terms[i : i + 2]) for i in range(0, len(terms), 2)]
        up[mids * rank : (mids + 1) * rank, :] = terms[0]


def up_sweep(charges, leaf_size, basis, transfer, mid_transfer, leaf_parent, send_mid):
    leaves, rank, points = basis.shape
    ports = charges.shape[1]
    mids = mid_transfer.shape[0]
    group = 8
    up_rows = (mids + 1) * rank + -(-send_mid.shape[0] // 8) * 8
    return pl.pallas_call(
        up_kernel,
        grid_spec=pltpu.PrefetchScalarGridSpec(
            num_scalar_prefetch=2,
            grid=(leaves // group,),
            in_specs=[
                first(group * points, ports),
                first(group, rank, points),
                first(group, rank, rank),
                whole(mid_transfer.shape),
                whole(send_mid.shape),
            ],
            out_specs=[first(group, rank, ports), whole((up_rows, ports))],
        ),
        out_shape=[
            jax.ShapeDtypeStruct((leaves, rank, ports), jnp.float32),
            jax.ShapeDtypeStruct((up_rows, ports), jnp.float32),
        ],
        compiler_params=params(),
        cost_estimate=cost(10**9, 10**7),
        name="up_sweep",
    )(leaf_size, leaf_parent, charges, basis, transfer, mid_transfer, send_mid)


def spread_kernel(send, coef, out):
    leaves = coef.shape[0]

    @pl.loop(0, out.shape[0], unroll=8)
    def _(slot):
        out[slot] = coef[jnp.minimum(send[slot], leaves - 1)]


def spread(send_leaf, coef):
    vmem = pl.BlockSpec(memory_space=pltpu.VMEM)
    shape = (send_leaf.shape[0],) + coef.shape[1:]
    return pl.pallas_call(
        spread_kernel,
        in_specs=[pl.BlockSpec(memory_space=pltpu.SMEM), vmem],
        out_specs=vmem,
        out_shape=jax.ShapeDtypeStruct(shape, jnp.float32),
        compiler_params=params(),
        cost_estimate=cost(0, 4 * 10**6),
        name="spread",
    )(send_leaf, coef)


def select_kernel(sizes, place, *refs):
    lines, per_cluster, up_rows, mids, rank, per_pair, groups = sizes
    received, messages = refs[:lines], refs[lines : lines + groups]
    line_buffer, tables, sem, table_sem = refs[lines + groups :]
    group, lane = place[0], place[1]
    at_line, core = lax.div(lane, 2), lax.rem(lane, 2)
    table_rows = up_rows - (mids + 1) * rank
    ports = line_buffer.shape[2]
    copies = []
    for d, ref in enumerate(received):
        table = ref.at[pl.ds((mids + 1) * rank, table_rows), :]
        copies.append(pltpu.make_async_copy(table, tables.at[at_line ^ d], table_sem.at[d]))
        copies.append(pltpu.make_async_copy(ref, line_buffer.at[at_line ^ d], sem.at[d]))
    for copy in copies:
        copy.start()
    for copy in copies:
        copy.wait()
    for d, message in enumerate(messages):
        for side in range(2):
            receiver = (group ^ d) * per_cluster + at_line * 2 + (core ^ side)

            @pl.loop(0, lines, unroll=min(lines, 4))
            def _(line):
                for j in range(per_pair):
                    entry = receiver * per_pair + j
                    listed = tables[line, lax.div(entry, ports), lax.rem(entry, ports)]
                    block = jnp.clip(listed.astype(jnp.int32), 0, mids - 1)
                    target = (side * lines + line) * per_pair + j
                    message[target] = line_buffer[line, pl.ds(pl.multiple_of(block * rank, 8), rank), :]

        for line in range(lines):
            message[2 * lines * per_pair + line] = line_buffer[line, mids * rank : (mids + 1) * rank, :]


def select(sizes, place, received):
    lines, per_cluster, up_rows, mids, rank, per_pair, groups = sizes
    ports = received[0].shape[1]
    table_rows = up_rows - (mids + 1) * rank
    shape = jax.ShapeDtypeStruct((lines * (2 * per_pair + 1), rank, ports), jnp.float32)
    return pl.pallas_call(
        functools.partial(select_kernel, sizes),
        in_specs=[pl.BlockSpec(memory_space=pltpu.SMEM)]
        + [pl.BlockSpec(memory_space=pl.ANY)] * len(received),
        out_specs=[pl.BlockSpec(memory_space=pltpu.VMEM)] * groups,
        out_shape=[shape] * groups,
        scratch_shapes=[
            pltpu.VMEM((lines, up_rows, ports), jnp.float32),
            pltpu.SMEM((lines, table_rows, ports), jnp.float32),
            pltpu.SemaphoreType.DMA((lines,)),
            pltpu.SemaphoreType.DMA((lines,)),
        ],
        compiler_params=params(),
        cost_estimate=cost(0, 4 * 10**6),
        name="select",
    )(place, *received)


def prepare_kernel(after, coupling, basis, transfer, mid_coupling, mid_transfer, *out):
    wide, basis_t, transfer_t, mid_wide, mid_transfer_t = out
    for g in range(coupling.shape[0]):
        wide[g] = rows_of(coupling[g])
        basis_t[g] = rows_of(basis[g]).T
        transfer_t[g] = rows_of(transfer[g]).T
    for g in range(mid_coupling.shape[0]):
        mid_wide[g] = rows_of(mid_coupling[g])
        mid_transfer_t[g] = rows_of(mid_transfer[g]).T


def prepare(after, coupling, basis, transfer, mid_coupling, mid_transfer):
    leaves, rank, width = coupling.shape
    points = basis.shape[2]
    mids, _, mid_width = mid_coupling.shape
    steps = mids
    group = leaves // steps
    shapes = [
        (leaves, 2 * rank, width),
        (leaves, points, 2 * rank),
        (leaves, rank, 2 * rank),
        (mids, 2 * rank, mid_width),
        (mids, rank, 2 * rank),
    ]
    return pl.pallas_call(
        prepare_kernel,
        grid=(steps,),
        in_specs=[
            pl.BlockSpec(memory_space=pl.ANY),
            first(group, rank, width),
            first(group, rank, points),
            first(group, rank, rank),
            first(1, rank, mid_width),
            first(1, rank, rank),
        ],
        out_specs=[first(s[0] // steps, *s[1:]) for s in shapes],
        out_shape=[jax.ShapeDtypeStruct(s, jnp.bfloat16) for s in shapes],
        compiler_params=params(),
        cost_estimate=cost(0, 3 * 10**7),
        name="prepare",
    )(after, coupling, basis, transfer, mid_coupling, mid_transfer)


def mid_kernel(sizes, parent, pair, position, tops, *refs):
    lines, per_pair, groups = sizes
    near_side, far_side = refs[:groups], refs[groups : 2 * groups]
    coupling, top_coupling, mid_transfer, transfer, back, parts, top_parts, near_top, down = refs[2 * groups :]
    step = pl.program_id(0)
    leaves = back.shape[0]
    group, _, width = coupling.shape
    rank = near_top.shape[0]
    slots, top_count = parts.shape[0] - 1, top_parts.shape[0] - 1
    piece = lines * per_pair

    @pl.when(step == 0)
    def _():
        for d in range(groups):
            for side, (ref, skip) in enumerate(((near_side[d], 2 * piece), (far_side[d], piece))):
                @pl.loop(0, piece, unroll=4)
                def _(slot):
                    parts[(2 * d + side) * piece + slot] = lanes_of(ref[slot])

                @pl.loop(0, lines, unroll=4)
                def _(line):
                    top_parts[(2 * d + side) * lines + line] = lanes_of(ref[skip + line])

        parts[slots] = jnp.zeros(parts.shape[1:], jnp.bfloat16)
        top_parts[top_count] = jnp.zeros(top_parts.shape[1:], jnp.bfloat16)
        stacked = jnp.concatenate([top_parts[tops[k]] for k in range(tops.shape[0])], axis=0)
        near_top[...] = fold(dot(rows_of(top_coupling[0]), stacked))

    near = []
    for g in range(group):
        c = step * group + g
        stacked = jnp.concatenate([parts[pair[c, k]] for k in range(width // rank)], axis=0)
        near.append(fold(dot(coupling[g], stacked)) + deep_dot(mid_transfer[g], near_top[...]))
    for g in range(group):
        down[step * group + g] = near[g]

    @pl.when(step == pl.num_programs(0) - 1)
    def _():
        @pl.loop(0, leaves, unroll=8)
        def _(leaf):
            back[leaf] = deep_dot(transfer[leaf], down[parent[leaf]])


def mid_level(sizes, parent, pair, position, tops, near_side, far_side, coupling, top_coupling, mid_transfer, transfer):
    lines, per_pair, groups = sizes
    mids, _, width = coupling.shape
    rank, ports = near_side[0].shape[1:]
    leaves = transfer.shape[0]
    owners = 2 * lines * groups
    group = 2
    return pl.pallas_call(
        functools.partial(mid_kernel, sizes),
        grid_spec=pltpu.PrefetchScalarGridSpec(
            num_scalar_prefetch=4,
            grid=(mids // group,),
            in_specs=[whole(m.shape) for m in near_side + far_side]
            + [
                first(group, 2 * rank, width),
                pl.BlockSpec(
                    (1,) + top_coupling.shape[1:],
                    lambda i, parent, pair, position, tops: (position[0], 0, 0),
                ),
                first(group, rank, 2 * rank),
                whole(transfer.shape),
            ],
            out_specs=whole((leaves, rank, ports)),
            scratch_shapes=[
                pltpu.VMEM((owners * per_pair + 1, rank, 2 * ports), jnp.bfloat16),
                pltpu.VMEM((owners + 1, rank, 2 * ports), jnp.bfloat16),
                pltpu.VMEM((rank, ports), jnp.float32),
                pltpu.VMEM((mids, rank, ports), jnp.float32),
            ],
        ),
        out_shape=jax.ShapeDtypeStruct((leaves, rank, ports), jnp.float32),
        compiler_params=params(),
        cost_estimate=cost(2 * 10**9, 10**7),
        name="mid_level",
    )(parent, pair, position, tops, *near_side, *far_side, coupling, top_coupling, mid_transfer, transfer)


def leaf_kernel(size, pair, arrived, coupling, basis, back, out, parts):
    step = pl.program_id(0)
    group, rank, _ = back.shape
    points = basis.shape[1]
    slots = arrived.shape[0]

    @pl.when(step == 0)
    def _():
        @pl.loop(0, slots, unroll=8)
        def _(slot):
            parts[slot] = lanes_of(arrived[slot])

        parts[slots] = jnp.zeros(parts.shape[1:], jnp.bfloat16)

    point = lax.broadcasted_iota(jnp.int32, (points, out.shape[1]), 0)
    values = []
    for g in range(group):
        leaf = step * group + g
        stacked = jnp.concatenate([parts[pair[leaf, k]] for k in range(coupling.shape[2] // rank)], axis=0)
        values.append(fold(dot(coupling[g], stacked)) + back[g])
    for g in range(group):
        far = deep_dot(basis[g], values[g])
        out[g * points : (g + 1) * points, :] = jnp.where(point < size[step * group + g], far, 0.0)


def leaf_level(leaf_size, pair_leaf, arrived, coupling, basis, back):
    leaves, _, width = coupling.shape
    points = basis.shape[1]
    slots, rank, ports = arrived.shape
    group = 4
    return pl.pallas_call(
        leaf_kernel,
        grid_spec=pltpu.PrefetchScalarGridSpec(
            num_scalar_prefetch=2,
            grid=(leaves // group,),
            in_specs=[
                whole(arrived.shape),
                first(group, 2 * rank, width),
                first(group, points, 2 * rank),
                first(group, rank, ports),
            ],
            out_specs=first(group * points, ports),
            scratch_shapes=[pltpu.VMEM((slots + 1, rank, 2 * ports), jnp.bfloat16)],
        ),
        out_shape=jax.ShapeDtypeStruct((leaves * points, ports), jnp.float32),
        compiler_params=params(),
        cost_estimate=cost(4 * 10**9, 2 * 10**7),
        name="leaf_level",
    )(leaf_size, pair_leaf, arrived, coupling, basis, back)


def body(
    charges, leaf_size, leaf_basis, leaf_transfer, mid_transfer, leaf_parent, send_leaf, pair_leaf,
    leaf_coupling, send_mid, pair_mid, mid_coupling, top_pairs, top_coupling,
):
    rank = leaf_basis.shape[1]
    ports = charges.shape[1]
    mids = mid_transfer.shape[0]
    slots = send_mid.shape[0]
    groups, per_cluster = lax.axis_size("group"), lax.axis_size("cluster")
    owners = groups * per_cluster
    lines = per_cluster // 2
    per_pair = slots // owners
    group, lane = lax.axis_index("group"), lax.axis_index("cluster")

    table = send_mid.reshape(-1, min(slots, ports))
    coef, lifted = up_sweep(
        charges, leaf_size, leaf_basis, leaf_transfer, mid_transfer, leaf_parent, table
    )
    up_rows = lifted.shape[0]
    outgoing = spread(send_leaf, coef)

    received = [lifted]
    for d in range(1, lines):
        received.append(
            lax.ppermute(lifted, "cluster", [(c, c ^ (2 * d)) for c in range(per_cluster)])
        )
    outgoing, *received[1:] = lax.optimization_barrier((outgoing, *received[1:]))
    arrived = lax.all_to_all(outgoing, AXES, split_axis=0, concat_axis=0, tiled=True)

    wide, basis_t, transfer_t, mid_wide, mid_transfer_t = prepare(
        lifted, leaf_coupling, leaf_basis, leaf_transfer, mid_coupling, mid_transfer
    )

    place = jnp.stack([group, lane]).astype(jnp.int32)
    sizes = (lines, per_cluster, up_rows, mids, rank, per_pair, groups)
    messages = select(sizes, place, received)
    near_side, far_side = [], []
    for d in range(groups):
        message = messages[d]
        if d:
            message = lax.ppermute(message, "group", [(g, g ^ d) for g in range(groups)])
            message, mid_wide = lax.optimization_barrier((message, mid_wide))
        near_side.append(message)
        far_side.append(
            lax.ppermute(
                message[lines * per_pair :], "cluster", [(c, c ^ 1) for c in range(per_cluster)]
            )
        )

    def spot_of(sender):
        at_group, at_lane = sender // per_cluster, sender % per_cluster
        return ((at_group ^ group) * 2 + ((at_lane ^ lane) & 1)) * lines + at_lane // 2

    spot = spot_of(pair_mid // per_pair) * per_pair + pair_mid % per_pair
    spot = jnp.where((pair_mid >= 0) & (pair_mid < slots), spot, slots)
    wanted = lax.dynamic_slice_in_dim(top_pairs, lane, 1, 0)[0]
    tops = jnp.where((wanted >= 0) & (wanted < owners), spot_of(wanted), owners)
    position = lane.astype(jnp.int32)[None]
    back = mid_level(
        (lines, per_pair, groups), leaf_parent, spot, position, tops, near_side, far_side,
        mid_wide, top_coupling, mid_transfer_t, transfer_t,
    )
    return leaf_level(leaf_size, pair_leaf, arrived, wide, basis_t, back)


def solution(mesh):
    both = P(AXES)
    in_specs = (
        P(AXES, None),
        both,
        P(AXES, None, None),
        P(AXES, None, None),
        P(AXES, None, None),
        both,
        both,
        P(AXES, None),
        P(AXES, None, None),
        both,
        P(AXES, None),
        P(AXES, None, None),
        P("group", None),
        P("group", None, None),
    )
    return jax.shard_map(
        body, mesh=mesh, in_specs=in_specs, out_specs=P(AXES, None), check_vma=False
    )
```

```python
import functools

import jax
import jax.numpy as jnp
from jax import lax
from jax.experimental import pallas as pl
from jax.experimental.pallas import tpu as pltpu
from jax.sharding import PartitionSpec as P

AXES = ("group", "cluster")
VMEM_LIMIT = 60 * 1024 * 1024


def params():
    return pltpu.CompilerParams(vmem_limit_bytes=VMEM_LIMIT)


def cost(flops, size):
    return pl.CostEstimate(flops=flops, bytes_accessed=size, transcendentals=0)


def whole(shape):
    return pl.BlockSpec(shape, lambda i, *_: (0,) * len(shape))


def first(group, *rest):
    return pl.BlockSpec((group,) + rest, lambda i, *_: (i,) + (0,) * len(rest))


def split(x):
    high = x.astype(jnp.bfloat16)
    low = (x - high.astype(jnp.float32)).astype(jnp.bfloat16)
    return high, low


def rows_of(x):
    return jnp.concatenate(split(x), axis=0)


def lanes_of(x):
    return jnp.concatenate(split(x), axis=1)


def dot(a, b):
    return lax.dot_general(a, b, (((1,), (0,)), ((), ())), preferred_element_type=jnp.float32)


def fold(product):
    m, n = product.shape[0] // 2, product.shape[1] // 2
    return product[:m, :n] + (product[:m, n:] + product[m:, :n] + product[m:, n:])


def deep_dot(a, b):
    high, low = split(b)
    return dot(jnp.concatenate([a, a], axis=1), jnp.concatenate([high, high, low, low], axis=0))


def up_kernel(size, parent, charges, basis, transfer, mid_transfer, send, coef, up):
    step = pl.program_id(0)
    group, rank, points = basis.shape
    mids = mid_transfer.shape[0]
    ports = up.shape[1]

    @pl.when(step == 0)
    def _():
        up[: mids * rank, :] = jnp.zeros((mids * rank, ports), jnp.float32)
        up[(mids + 1) * rank :, :] = jnp.zeros((up.shape[0] - (mids + 1) * rank, ports), jnp.float32)
        for row in range(send.shape[0]):
            spot = (mids + 1) * rank + row
            up[spot : spot + 1, : send.shape[1]] = send[row : row + 1, :].astype(jnp.float32)

    point = lax.broadcasted_iota(jnp.int32, (points, ports), 0)
    values = []
    for g in range(group):
        block = jnp.where(
            point < size[step * group + g], charges[g * points : (g + 1) * points, :], 0.0
        )
        values.append(fold(dot(rows_of(basis[g]), lanes_of(block))))
    for g in range(group):
        coef[g] = values[g]
    moved = [fold(dot(rows_of(transfer[g]), lanes_of(values[g]))) for g in range(group)]
    for g in range(group):
        where = pl.ds(pl.multiple_of(parent[step * group + g] * rank, rank), rank)
        up[where, :] += moved[g]

    @pl.when(step == pl.num_programs(0) - 1)
    def _():
        terms = [
            fold(dot(rows_of(mid_transfer[c]), lanes_of(up[c * rank : (c + 1) * rank, :])))
            for c in range(mids)
        ]
        while len(terms) > 1:
            terms = [sum(terms[i : i + 2]) for i in range(0, len(terms), 2)]
        up[mids * rank : (mids + 1) * rank, :] = terms[0]


def up_sweep(charges, leaf_size, basis, transfer, mid_transfer, leaf_parent, send_mid):
    leaves, rank, points = basis.shape
    ports = charges.shape[1]
    mids = mid_transfer.shape[0]
    group = 8
    up_rows = (mids + 1) * rank + -(-send_mid.shape[0] // 8) * 8
    return pl.pallas_call(
        up_kernel,
        grid_spec=pltpu.PrefetchScalarGridSpec(
            num_scalar_prefetch=2,
            grid=(leaves // group,),
            in_specs=[
                first(group * points, ports),
                first(group, rank, points),
                first(group, rank, rank),
                whole(mid_transfer.shape),
                whole(send_mid.shape),
            ],
            out_specs=[first(group, rank, ports), whole((up_rows, ports))],
        ),
        out_shape=[
            jax.ShapeDtypeStruct((leaves, rank, ports), jnp.float32),
            jax.ShapeDtypeStruct((up_rows, ports), jnp.float32),
        ],
        compiler_params=params(),
        cost_estimate=cost(10**9, 10**7),
        name="up_sweep",
    )(leaf_size, leaf_parent, charges, basis, transfer, mid_transfer, send_mid)


def spread_kernel(send, coef, out):
    leaves = coef.shape[0]

    @pl.loop(0, out.shape[0], unroll=8)
    def _(slot):
        out[slot] = coef[jnp.minimum(send[slot], leaves - 1)]


def spread(send_leaf, coef):
    vmem = pl.BlockSpec(memory_space=pltpu.VMEM)
    shape = (send_leaf.shape[0],) + coef.shape[1:]
    return pl.pallas_call(
        spread_kernel,
        in_specs=[pl.BlockSpec(memory_space=pltpu.SMEM), vmem],
        out_specs=vmem,
        out_shape=jax.ShapeDtypeStruct(shape, jnp.float32),
        compiler_params=params(),
        cost_estimate=cost(0, 4 * 10**6),
        name="spread",
    )(send_leaf, coef)


def select_kernel(sizes, place, *refs):
    lines, per_cluster, up_rows, mids, rank, per_pair, groups = sizes
    received, messages = refs[:lines], refs[lines : lines + groups]
    line_buffer, tables, sem, table_sem = refs[lines + groups :]
    group, lane = place[0], place[1]
    at_line, core = lax.div(lane, 2), lax.rem(lane, 2)
    table_rows = up_rows - (mids + 1) * rank
    ports = line_buffer.shape[2]
    copies = []
    for d, ref in enumerate(received):
        table = ref.at[pl.ds((mids + 1) * rank, table_rows), :]
        copies.append(pltpu.make_async_copy(table, tables.at[at_line ^ d], table_sem.at[d]))
        copies.append(pltpu.make_async_copy(ref, line_buffer.at[at_line ^ d], sem.at[d]))
    for copy in copies:
        copy.start()
    for copy in copies:
        copy.wait()
    for d, message in enumerate(messages):
        for side in range(2):
            receiver = (group ^ d) * per_cluster + at_line * 2 + (core ^ side)

            @pl.loop(0, lines, unroll=min(lines, 4))
            def _(line):
                for j in range(per_pair):
                    entry = receiver * per_pair + j
                    listed = tables[line, lax.div(entry, ports), lax.rem(entry, ports)]
                    block = jnp.clip(listed.astype(jnp.int32), 0, mids - 1)
                    target = (side * lines + line) * per_pair + j
                    message[target] = line_buffer[line, pl.ds(pl.multiple_of(block * rank, 8), rank), :]

        for line in range(lines):
            message[2 * lines * per_pair + line] = line_buffer[line, mids * rank : (mids + 1) * rank, :]


def select(sizes, place, received):
    lines, per_cluster, up_rows, mids, rank, per_pair, groups = sizes
    ports = received[0].shape[1]
    table_rows = up_rows - (mids + 1) * rank
    shape = jax.ShapeDtypeStruct((lines * (2 * per_pair + 1), rank, ports), jnp.float32)
    return pl.pallas_call(
        functools.partial(select_kernel, sizes),
        in_specs=[pl.BlockSpec(memory_space=pltpu.SMEM)]
        + [pl.BlockSpec(memory_space=pl.ANY)] * len(received),
        out_specs=[pl.BlockSpec(memory_space=pltpu.VMEM)] * groups,
        out_shape=[shape] * groups,
        scratch_shapes=[
            pltpu.VMEM((lines, up_rows, ports), jnp.float32),
            pltpu.SMEM((lines, table_rows, ports), jnp.float32),
            pltpu.SemaphoreType.DMA((lines,)),
            pltpu.SemaphoreType.DMA((lines,)),
        ],
        compiler_params=params(),
        cost_estimate=cost(0, 4 * 10**6),
        name="select",
    )(place, *received)


def prepare_kernel(after, coupling, basis, transfer, mid_coupling, mid_transfer, *out):
    wide, basis_t, transfer_t, mid_wide, mid_transfer_t = out
    for g in range(coupling.shape[0]):
        wide[g] = rows_of(coupling[g])
        basis_t[g] = rows_of(basis[g]).T
        transfer_t[g] = rows_of(transfer[g]).T
    for g in range(mid_coupling.shape[0]):
        mid_wide[g] = rows_of(mid_coupling[g])
        mid_transfer_t[g] = rows_of(mid_transfer[g]).T


def prepare(after, coupling, basis, transfer, mid_coupling, mid_transfer):
    leaves, rank, width = coupling.shape
    points = basis.shape[2]
    mids, _, mid_width = mid_coupling.shape
    steps = mids
    group = leaves // steps
    shapes = [
        (leaves, 2 * rank, width),
        (leaves, points, 2 * rank),
        (leaves, rank, 2 * rank),
        (mids, 2 * rank, mid_width),
        (mids, rank, 2 * rank),
    ]
    return pl.pallas_call(
        prepare_kernel,
        grid=(steps,),
        in_specs=[
            pl.BlockSpec(memory_space=pl.ANY),
            first(group, rank, width),
            first(group, rank, points),
            first(group, rank, rank),
            first(1, rank, mid_width),
            first(1, rank, rank),
        ],
        out_specs=[first(s[0] // steps, *s[1:]) for s in shapes],
        out_shape=[jax.ShapeDtypeStruct(s, jnp.bfloat16) for s in shapes],
        compiler_params=params(),
        cost_estimate=cost(0, 3 * 10**7),
        name="prepare",
    )(after, coupling, basis, transfer, mid_coupling, mid_transfer)


def mid_kernel(sizes, parent, pair, position, tops, *refs):
    lines, per_pair, groups = sizes
    near_side, far_side = refs[:groups], refs[groups : 2 * groups]
    coupling, top_coupling, mid_transfer, transfer, back, parts, top_parts, near_top, down = refs[2 * groups :]
    step = pl.program_id(0)
    leaves = back.shape[0]
    group, _, width = coupling.shape
    rank = near_top.shape[0]
    slots, top_count = parts.shape[0] - 1, top_parts.shape[0] - 1
    piece = lines * per_pair

    @pl.when(step == 0)
    def _():
        for d in range(groups):
            for side, (ref, skip) in enumerate(((near_side[d], 2 * piece), (far_side[d], piece))):
                @pl.loop(0, piece, unroll=4)
                def _(slot):
                    parts[(2 * d + side) * piece + slot] = lanes_of(ref[slot])

                @pl.loop(0, lines, unroll=4)
                def _(line):
                    top_parts[(2 * d + side) * lines + line] = lanes_of(ref[skip + line])

        parts[slots] = jnp.zeros(parts.shape[1:], jnp.bfloat16)
        top_parts[top_count] = jnp.zeros(top_parts.shape[1:], jnp.bfloat16)
        stacked = jnp.concatenate([top_parts[tops[k]] for k in range(tops.shape[0])], axis=0)
        near_top[...] = fold(dot(rows_of(top_coupling[0]), stacked))

    near = []
    for g in range(group):
        c = step * group + g
        stacked = jnp.concatenate([parts[pair[c, k]] for k in range(width // rank)], axis=0)
        near.append(fold(dot(coupling[g], stacked)) + deep_dot(mid_transfer[g], near_top[...]))
    for g in range(group):
        down[step * group + g] = near[g]

    @pl.when(step == pl.num_programs(0) - 1)
    def _():
        @pl.loop(0, leaves, unroll=8)
        def _(leaf):
            back[leaf] = deep_dot(transfer[leaf], down[parent[leaf]])


def mid_level(sizes, parent, pair, position, tops, near_side, far_side, coupling, top_coupling, mid_transfer, transfer):
    lines, per_pair, groups = sizes
    mids, _, width = coupling.shape
    rank, ports = near_side[0].shape[1:]
    leaves = transfer.shape[0]
    owners = 2 * lines * groups
    group = 4
    return pl.pallas_call(
        functools.partial(mid_kernel, sizes),
        grid_spec=pltpu.PrefetchScalarGridSpec(
            num_scalar_prefetch=4,
            grid=(mids // group,),
            in_specs=[whole(m.shape) for m in near_side + far_side]
            + [
                first(group, 2 * rank, width),
                pl.BlockSpec(
                    (1,) + top_coupling.shape[1:],
                    lambda i, parent, pair, position, tops: (position[0], 0, 0),
                ),
                first(group, rank, 2 * rank),
                whole(transfer.shape),
            ],
            out_specs=whole((leaves, rank, ports)),
            scratch_shapes=[
                pltpu.VMEM((owners * per_pair + 1, rank, 2 * ports), jnp.bfloat16),
                pltpu.VMEM((owners + 1, rank, 2 * ports), jnp.bfloat16),
                pltpu.VMEM((rank, ports), jnp.float32),
                pltpu.VMEM((mids, rank, ports), jnp.float32),
            ],
        ),
        out_shape=jax.ShapeDtypeStruct((leaves, rank, ports), jnp.float32),
        compiler_params=params(),
        cost_estimate=cost(2 * 10**9, 10**7),
        name="mid_level",
    )(parent, pair, position, tops, *near_side, *far_side, coupling, top_coupling, mid_transfer, transfer)


def leaf_kernel(size, pair, arrived, coupling, basis, back, out, parts):
    step = pl.program_id(0)
    group, rank, _ = back.shape
    points = basis.shape[1]
    slots = arrived.shape[0]

    @pl.when(step == 0)
    def _():
        @pl.loop(0, slots, unroll=8)
        def _(slot):
            parts[slot] = lanes_of(arrived[slot])

        parts[slots] = jnp.zeros(parts.shape[1:], jnp.bfloat16)

    point = lax.broadcasted_iota(jnp.int32, (points, out.shape[1]), 0)
    values = []
    for g in range(group):
        leaf = step * group + g
        stacked = jnp.concatenate([parts[pair[leaf, k]] for k in range(coupling.shape[2] // rank)], axis=0)
        values.append(fold(dot(coupling[g], stacked)) + back[g])
    for g in range(group):
        far = deep_dot(basis[g], values[g])
        out[g * points : (g + 1) * points, :] = jnp.where(point < size[step * group + g], far, 0.0)


def leaf_level(leaf_size, pair_leaf, arrived, coupling, basis, back):
    leaves, _, width = coupling.shape
    points = basis.shape[1]
    slots, rank, ports = arrived.shape
    group = 8
    return pl.pallas_call(
        leaf_kernel,
        grid_spec=pltpu.PrefetchScalarGridSpec(
            num_scalar_prefetch=2,
            grid=(leaves // group,),
            in_specs=[
                whole(arrived.shape),
                first(group, 2 * rank, width),
                first(group, points, 2 * rank),
                first(group, rank, ports),
            ],
            out_specs=first(group * points, ports),
            scratch_shapes=[pltpu.VMEM((slots + 1, rank, 2 * ports), jnp.bfloat16)],
        ),
        out_shape=jax.ShapeDtypeStruct((leaves * points, ports), jnp.float32),
        compiler_params=params(),
        cost_estimate=cost(4 * 10**9, 2 * 10**7),
        name="leaf_level",
    )(leaf_size, pair_leaf, arrived, coupling, basis, back)


def body(
    charges, leaf_size, leaf_basis, leaf_transfer, mid_transfer, leaf_parent, send_leaf, pair_leaf,
    leaf_coupling, send_mid, pair_mid, mid_coupling, top_pairs, top_coupling,
):
    rank = leaf_basis.shape[1]
    ports = charges.shape[1]
    mids = mid_transfer.shape[0]
    slots = send_mid.shape[0]
    groups, per_cluster = lax.axis_size("group"), lax.axis_size("cluster")
    owners = groups * per_cluster
    lines = per_cluster // 2
    per_pair = slots // owners
    group, lane = lax.axis_index("group"), lax.axis_index("cluster")

    table = send_mid.reshape(-1, min(slots, ports))
    coef, lifted = up_sweep(
        charges, leaf_size, leaf_basis, leaf_transfer, mid_transfer, leaf_parent, table
    )
    up_rows = lifted.shape[0]
    outgoing = spread(send_leaf, coef)

    received = [lifted]
    for d in range(1, lines):
        received.append(
            lax.ppermute(lifted, "cluster", [(c, c ^ (2 * d)) for c in range(per_cluster)])
        )
    wide, basis_t, transfer_t, mid_wide, mid_transfer_t = prepare(
        lifted, leaf_coupling, leaf_basis, leaf_transfer, mid_coupling, mid_transfer
    )

    place = jnp.stack([group, lane]).astype(jnp.int32)
    sizes = (lines, per_cluster, up_rows, mids, rank, per_pair, groups)
    place, mid_wide = lax.optimization_barrier((place, mid_wide))
    messages = list(select(sizes, place, received))
    outgoing, messages[0] = lax.optimization_barrier((outgoing, messages[0]))
    arrived = lax.all_to_all(outgoing, AXES, split_axis=0, concat_axis=0, tiled=True)
    near_side, far_side = [], []
    for d in range(groups):
        message = messages[d]
        if d:
            message = lax.ppermute(message, "group", [(g, g ^ d) for g in range(groups)])
        near_side.append(message)
        far_side.append(
            lax.ppermute(
                message[lines * per_pair :], "cluster", [(c, c ^ 1) for c in range(per_cluster)]
            )
        )

    def spot_of(sender):
        at_group, at_lane = sender // per_cluster, sender % per_cluster
        return ((at_group ^ group) * 2 + ((at_lane ^ lane) & 1)) * lines + at_lane // 2

    spot = spot_of(pair_mid // per_pair) * per_pair + pair_mid % per_pair
    spot = jnp.where((pair_mid >= 0) & (pair_mid < slots), spot, slots)
    wanted = lax.dynamic_slice_in_dim(top_pairs, lane, 1, 0)[0]
    tops = jnp.where((wanted >= 0) & (wanted < owners), spot_of(wanted), owners)
    position = lane.astype(jnp.int32)[None]
    back = mid_level(
        (lines, per_pair, groups), leaf_parent, spot, position, tops, near_side, far_side,
        mid_wide, top_coupling, mid_transfer_t, transfer_t,
    )
    return leaf_level(leaf_size, pair_leaf, arrived, wide, basis_t, back)


def solution(mesh):
    both = P(AXES)
    in_specs = (
        P(AXES, None),
        both,
        P(AXES, None, None),
        P(AXES, None, None),
        P(AXES, None, None),
        both,
        both,
        P(AXES, None),
        P(AXES, None, None),
        both,
        P(AXES, None),
        P(AXES, None, None),
        P("group", None),
        P("group", None, None),
    )
    return jax.shard_map(
        body, mesh=mesh, in_specs=in_specs, out_specs=P(AXES, None), check_vma=False
    )
```

```python
import functools

import jax
import jax.numpy as jnp
from jax import lax
from jax.experimental import pallas as pl
from jax.experimental.pallas import tpu as pltpu
from jax.sharding import PartitionSpec as P

AXES = ("group", "cluster")
VMEM_LIMIT = 60 * 1024 * 1024


def params(limit=VMEM_LIMIT):
    return pltpu.CompilerParams(vmem_limit_bytes=limit)


def cost(flops, size):
    return pl.CostEstimate(flops=flops, bytes_accessed=size, transcendentals=0)


def whole(shape):
    return pl.BlockSpec(shape, lambda i, *_: (0,) * len(shape))


def first(group, *rest):
    return pl.BlockSpec((group,) + rest, lambda i, *_: (i,) + (0,) * len(rest))


def split(x):
    high = x.astype(jnp.bfloat16)
    low = (x - high.astype(jnp.float32)).astype(jnp.bfloat16)
    return high, low


def rows_of(x):
    return jnp.concatenate(split(x), axis=0)


def lanes_of(x):
    return jnp.concatenate(split(x), axis=1)


def dot(a, b):
    return lax.dot_general(a, b, (((1,), (0,)), ((), ())), preferred_element_type=jnp.float32)


def fold(product):
    m, n = product.shape[0] // 2, product.shape[1] // 2
    return product[:m, :n] + (product[:m, n:] + product[m:, :n] + product[m:, n:])


def deep_dot(a, b):
    high, low = split(b)
    return dot(jnp.concatenate([a, a], axis=1), jnp.concatenate([high, high, low, low], axis=0))


def up_kernel(size, parent, charges, basis, transfer, mid_transfer, send, coef, up):
    step = pl.program_id(0)
    group, rank, points = basis.shape
    mids = mid_transfer.shape[0]
    ports = up.shape[1]

    @pl.when(step == 0)
    def _():
        up[: mids * rank, :] = jnp.zeros((mids * rank, ports), jnp.float32)
        up[(mids + 1) * rank :, :] = jnp.zeros((up.shape[0] - (mids + 1) * rank, ports), jnp.float32)
        for row in range(send.shape[0]):
            spot = (mids + 1) * rank + row
            up[spot : spot + 1, : send.shape[1]] = send[row : row + 1, :].astype(jnp.float32)

    point = lax.broadcasted_iota(jnp.int32, (points, ports), 0)
    values = []
    for g in range(group):
        block = jnp.where(
            point < size[step * group + g], charges[g * points : (g + 1) * points, :], 0.0
        )
        values.append(fold(dot(rows_of(basis[g]), lanes_of(block))))
    for g in range(group):
        coef[g] = values[g]
    moved = [fold(dot(rows_of(transfer[g]), lanes_of(values[g]))) for g in range(group)]
    for g in range(group):
        where = pl.ds(pl.multiple_of(parent[step * group + g] * rank, rank), rank)
        up[where, :] += moved[g]

    @pl.when(step == pl.num_programs(0) - 1)
    def _():
        terms = [
            fold(dot(rows_of(mid_transfer[c]), lanes_of(up[c * rank : (c + 1) * rank, :])))
            for c in range(mids)
        ]
        while len(terms) > 1:
            terms = [sum(terms[i : i + 2]) for i in range(0, len(terms), 2)]
        up[mids * rank : (mids + 1) * rank, :] = terms[0]


def up_sweep(charges, leaf_size, basis, transfer, mid_transfer, leaf_parent, send_mid):
    leaves, rank, points = basis.shape
    ports = charges.shape[1]
    mids = mid_transfer.shape[0]
    group = 8
    up_rows = (mids + 1) * rank + -(-send_mid.shape[0] // 8) * 8
    return pl.pallas_call(
        up_kernel,
        grid_spec=pltpu.PrefetchScalarGridSpec(
            num_scalar_prefetch=2,
            grid=(leaves // group,),
            in_specs=[
                first(group * points, ports),
                first(group, rank, points),
                first(group, rank, rank),
                whole(mid_transfer.shape),
                whole(send_mid.shape),
            ],
            out_specs=[first(group, rank, ports), whole((up_rows, ports))],
        ),
        out_shape=[
            jax.ShapeDtypeStruct((leaves, rank, ports), jnp.float32),
            jax.ShapeDtypeStruct((up_rows, ports), jnp.float32),
        ],
        compiler_params=params(),
        cost_estimate=cost(10**9, 10**7),
        name="up_sweep",
    )(leaf_size, leaf_parent, charges, basis, transfer, mid_transfer, send_mid)


def spread_kernel(send, coef, out):
    leaves = coef.shape[0]

    @pl.loop(0, out.shape[0], unroll=8)
    def _(slot):
        out[slot] = coef[jnp.minimum(send[slot], leaves - 1)]


def spread(send_leaf, coef):
    vmem = pl.BlockSpec(memory_space=pltpu.VMEM)
    shape = (send_leaf.shape[0],) + coef.shape[1:]
    return pl.pallas_call(
        spread_kernel,
        in_specs=[pl.BlockSpec(memory_space=pltpu.SMEM), vmem],
        out_specs=vmem,
        out_shape=jax.ShapeDtypeStruct(shape, jnp.float32),
        compiler_params=params(),
        cost_estimate=cost(0, 4 * 10**6),
        name="spread",
    )(send_leaf, coef)


def select_kernel(sizes, place, *refs):
    lines, per_cluster, up_rows, mids, rank, per_pair, groups = sizes
    received, messages = refs[:lines], refs[lines : lines + groups]
    payloads, tables, sem, table_sem = refs[lines + groups :]
    group, lane = place[0], place[1]
    table_rows = up_rows - (mids + 1) * rank
    ports = payloads.shape[2]
    copies = []
    for line, ref in enumerate(received):
        table = ref.at[pl.ds((mids + 1) * rank, table_rows), :]
        copies.append(pltpu.make_async_copy(table, tables.at[line], table_sem.at[line]))
        copies.append(pltpu.make_async_copy(ref, payloads.at[line], sem.at[line]))
    for copy in copies:
        copy.start()
    for copy in copies:
        copy.wait()
    for d, message in enumerate(messages):
        for side in range(2):
            receiver = (group ^ d) * per_cluster + (lane ^ side)

            @pl.loop(0, lines, unroll=min(lines, 4))
            def _(line):
                for j in range(per_pair):
                    entry = receiver * per_pair + j
                    listed = tables[line, lax.div(entry, ports), lax.rem(entry, ports)]
                    block = jnp.clip(listed.astype(jnp.int32), 0, mids - 1)
                    target = (side * lines + line) * per_pair + j
                    message[target] = payloads[line, pl.ds(pl.multiple_of(block * rank, 8), rank), :]

        for line in range(lines):
            message[2 * lines * per_pair + line] = payloads[line, mids * rank : (mids + 1) * rank, :]


def select(sizes, place, received):
    lines, per_cluster, up_rows, mids, rank, per_pair, groups = sizes
    ports = received[0].shape[1]
    table_rows = up_rows - (mids + 1) * rank
    shape = jax.ShapeDtypeStruct((lines * (2 * per_pair + 1), rank, ports), jnp.float32)
    return pl.pallas_call(
        functools.partial(select_kernel, sizes),
        in_specs=[pl.BlockSpec(memory_space=pltpu.SMEM)]
        + [pl.BlockSpec(memory_space=pl.ANY)] * len(received),
        out_specs=[pl.BlockSpec(memory_space=pltpu.VMEM)] * groups,
        out_shape=[shape] * groups,
        scratch_shapes=[
            pltpu.VMEM((lines, up_rows, ports), jnp.float32),
            pltpu.SMEM((lines, table_rows, ports), jnp.float32),
            pltpu.SemaphoreType.DMA((lines,)),
            pltpu.SemaphoreType.DMA((lines,)),
        ],
        compiler_params=params(),
        cost_estimate=cost(0, 4 * 10**6),
        name="select",
    )(place, *received)


def prepare_kernel(after, coupling, basis, transfer, mid_coupling, mid_transfer, *out):
    wide, basis_t, transfer_t, mid_wide, mid_transfer_t = out
    for g in range(coupling.shape[0]):
        wide[g] = rows_of(coupling[g])
        basis_t[g] = rows_of(basis[g]).T
        transfer_t[g] = rows_of(transfer[g]).T
    for g in range(mid_coupling.shape[0]):
        mid_wide[g] = rows_of(mid_coupling[g])
        mid_transfer_t[g] = rows_of(mid_transfer[g]).T


def prepare(after, coupling, basis, transfer, mid_coupling, mid_transfer):
    leaves, rank, width = coupling.shape
    points = basis.shape[2]
    mids, _, mid_width = mid_coupling.shape
    steps = mids
    group = leaves // steps
    shapes = [
        (leaves, 2 * rank, width),
        (leaves, points, 2 * rank),
        (leaves, rank, 2 * rank),
        (mids, 2 * rank, mid_width),
        (mids, rank, 2 * rank),
    ]
    return pl.pallas_call(
        prepare_kernel,
        grid=(steps,),
        in_specs=[
            pl.BlockSpec(memory_space=pl.ANY),
            first(group, rank, width),
            first(group, rank, points),
            first(group, rank, rank),
            first(1, rank, mid_width),
            first(1, rank, rank),
        ],
        out_specs=[first(s[0] // steps, *s[1:]) for s in shapes],
        out_shape=[jax.ShapeDtypeStruct(s, jnp.bfloat16) for s in shapes],
        compiler_params=params(),
        cost_estimate=cost(0, 3 * 10**7),
        name="prepare",
    )(after, coupling, basis, transfer, mid_coupling, mid_transfer)


def mid_kernel(sizes, parent, pair, position, tops, *refs):
    batches, lines, per_pair, groups = sizes
    count = batches * groups
    near_side, far_side = refs[:count], refs[count : 2 * count]
    coupling, top_coupling, mid_transfer, transfer, back, parts, top_parts, near_top, down = refs[2 * count :]
    step = pl.program_id(0)
    leaves = back.shape[0]
    group, _, width = coupling.shape
    rank = near_top.shape[0]
    slots, top_count = parts.shape[0] - 1, top_parts.shape[0] - 1
    piece = lines * per_pair

    @pl.when(step == 0)
    def _():
        for message in range(count):
            sides = ((near_side[message], 2 * piece), (far_side[message], piece))
            for side, (ref, skip) in enumerate(sides):
                first_line = (message * 2 + side) * lines

                @pl.loop(0, piece, unroll=4)
                def _(slot):
                    parts[first_line * per_pair + slot] = lanes_of(ref[slot])

                for line in range(lines):
                    top_parts[first_line + line] = lanes_of(ref[skip + line])

        parts[slots] = jnp.zeros(parts.shape[1:], jnp.bfloat16)
        top_parts[top_count] = jnp.zeros(top_parts.shape[1:], jnp.bfloat16)
        stacked = jnp.concatenate([top_parts[tops[k]] for k in range(tops.shape[0])], axis=0)
        near_top[...] = fold(dot(rows_of(top_coupling[0]), stacked))

    near = []
    for g in range(group):
        c = step * group + g
        stacked = jnp.concatenate([parts[pair[c, k]] for k in range(width // rank)], axis=0)
        near.append(fold(dot(coupling[g], stacked)) + deep_dot(mid_transfer[g], near_top[...]))
    for g in range(group):
        down[step * group + g] = near[g]

    @pl.when(step == pl.num_programs(0) - 1)
    def _():
        @pl.loop(0, leaves, unroll=8)
        def _(leaf):
            back[leaf] = deep_dot(transfer[leaf], down[parent[leaf]])


def mid_level(sizes, parent, pair, position, tops, near_side, far_side, coupling, top_coupling, mid_transfer, transfer):
    batches, lines, per_pair, groups = sizes
    mids, _, width = coupling.shape
    rank, ports = near_side[0].shape[1:]
    leaves = transfer.shape[0]
    owners = 2 * batches * lines * groups
    group = 4
    return pl.pallas_call(
        functools.partial(mid_kernel, sizes),
        grid_spec=pltpu.PrefetchScalarGridSpec(
            num_scalar_prefetch=4,
            grid=(mids // group,),
            in_specs=[whole(m.shape) for m in near_side + far_side]
            + [
                first(group, 2 * rank, width),
                pl.BlockSpec(
                    (1,) + top_coupling.shape[1:],
                    lambda i, parent, pair, position, tops: (position[0], 0, 0),
                ),
                first(group, rank, 2 * rank),
                whole(transfer.shape),
            ],
            out_specs=whole((leaves, rank, ports)),
            scratch_shapes=[
                pltpu.VMEM((owners * per_pair + 1, rank, 2 * ports), jnp.bfloat16),
                pltpu.VMEM((owners + 1, rank, 2 * ports), jnp.bfloat16),
                pltpu.VMEM((rank, ports), jnp.float32),
                pltpu.VMEM((mids, rank, ports), jnp.float32),
            ],
        ),
        out_shape=jax.ShapeDtypeStruct((leaves, rank, ports), jnp.float32),
        compiler_params=params(),
        cost_estimate=cost(2 * 10**9, 10**7),
        name="mid_level",
    )(parent, pair, position, tops, *near_side, *far_side, coupling, top_coupling, mid_transfer, transfer)


def leaf_kernel(size, pair, arrived, coupling, basis, back, out, parts):
    step = pl.program_id(0)
    group, rank, _ = back.shape
    points = basis.shape[1]
    slots = arrived.shape[0]

    @pl.when(step == 0)
    def _():
        @pl.loop(0, slots, unroll=8)
        def _(slot):
            parts[slot] = lanes_of(arrived[slot])

        parts[slots] = jnp.zeros(parts.shape[1:], jnp.bfloat16)

    point = lax.broadcasted_iota(jnp.int32, (points, out.shape[1]), 0)
    values = []
    for g in range(group):
        leaf = step * group + g
        stacked = jnp.concatenate([parts[pair[leaf, k]] for k in range(coupling.shape[2] // rank)], axis=0)
        values.append(fold(dot(coupling[g], stacked)) + back[g])
    for g in range(group):
        far = deep_dot(basis[g], values[g])
        out[g * points : (g + 1) * points, :] = jnp.where(point < size[step * group + g], far, 0.0)


def leaf_level(leaf_size, pair_leaf, arrived, coupling, basis, back):
    leaves, _, width = coupling.shape
    points = basis.shape[1]
    slots, rank, ports = arrived.shape
    group = 8
    return pl.pallas_call(
        leaf_kernel,
        grid_spec=pltpu.PrefetchScalarGridSpec(
            num_scalar_prefetch=2,
            grid=(leaves // group,),
            in_specs=[
                whole(arrived.shape),
                first(group, 2 * rank, width),
                first(group, points, 2 * rank),
                first(group, rank, ports),
            ],
            out_specs=first(group * points, ports),
            scratch_shapes=[pltpu.VMEM((slots + 1, rank, 2 * ports), jnp.bfloat16)],
        ),
        out_shape=jax.ShapeDtypeStruct((leaves * points, ports), jnp.float32),
        compiler_params=params(36 * 1024 * 1024),
        cost_estimate=cost(4 * 10**9, 2 * 10**7),
        name="leaf_level",
    )(leaf_size, pair_leaf, arrived, coupling, basis, back)


def body(
    charges, leaf_size, leaf_basis, leaf_transfer, mid_transfer, leaf_parent, send_leaf, pair_leaf,
    leaf_coupling, send_mid, pair_mid, mid_coupling, top_pairs, top_coupling,
):
    rank = leaf_basis.shape[1]
    ports = charges.shape[1]
    mids = mid_transfer.shape[0]
    slots = send_mid.shape[0]
    groups, per_cluster = lax.axis_size("group"), lax.axis_size("cluster")
    owners = groups * per_cluster
    lines = per_cluster // 2
    per_pair = slots // owners
    group, lane = lax.axis_index("group"), lax.axis_index("cluster")

    table = send_mid.reshape(-1, min(slots, ports))
    coef, lifted = up_sweep(
        charges, leaf_size, leaf_basis, leaf_transfer, mid_transfer, leaf_parent, table
    )
    up_rows = lifted.shape[0]
    outgoing = spread(send_leaf, coef)

    received = [lifted]
    for d in range(1, lines):
        received.append(
            lax.ppermute(lifted, "cluster", [(c, c ^ (2 * d)) for c in range(per_cluster)])
        )
    near_payloads = received[: lines // 2]
    wide, basis_t, transfer_t, mid_wide, mid_transfer_t = prepare(
        lifted, leaf_coupling, leaf_basis, leaf_transfer, mid_coupling, mid_transfer
    )

    place = jnp.stack([group, lane]).astype(jnp.int32)
    outgoing, *received[1:] = lax.optimization_barrier((outgoing, *received[1:]))
    arrived = lax.all_to_all(outgoing, AXES, split_axis=0, concat_axis=0, tiled=True)
    batches = 2
    half = lines // batches
    sizes = (half, per_cluster, up_rows, mids, rank, per_pair, groups)
    near_side, far_side = [], []
    for batch in range(batches):
        payloads = near_payloads if batch == 0 else received[half:]
        messages = select(sizes, place, payloads)
        for d in range(groups):
            message = messages[d]
            if d:
                message = lax.ppermute(message, "group", [(g, g ^ d) for g in range(groups)])
                if batch:
                    message, mid_wide = lax.optimization_barrier((message, mid_wide))
            near_side.append(message)
            far_side.append(
                lax.ppermute(
                    message[half * per_pair :], "cluster", [(c, c ^ 1) for c in range(per_cluster)]
                )
            )

    def spot_of(sender):
        at_group, at_lane = sender // per_cluster, sender % per_cluster
        line = (at_lane // 2) ^ (lane // 2)
        message = (line // half) * groups + (at_group ^ group)
        return (message * 2 + ((at_lane ^ lane) & 1)) * half + line % half

    spot = spot_of(pair_mid // per_pair) * per_pair + pair_mid % per_pair
    spot = jnp.where((pair_mid >= 0) & (pair_mid < slots), spot, slots)
    wanted = lax.dynamic_slice_in_dim(top_pairs, lane, 1, 0)[0]
    tops = jnp.where((wanted >= 0) & (wanted < owners), spot_of(wanted), owners)
    position = lane.astype(jnp.int32)[None]
    back = mid_level(
        (batches, half, per_pair, groups), leaf_parent, spot, position, tops, near_side, far_side,
        mid_wide, top_coupling, mid_transfer_t, transfer_t,
    )
    return leaf_level(leaf_size, pair_leaf, arrived, wide, basis_t, back)


def solution(mesh):
    both = P(AXES)
    in_specs = (
        P(AXES, None),
        both,
        P(AXES, None, None),
        P(AXES, None, None),
        P(AXES, None, None),
        both,
        both,
        P(AXES, None),
        P(AXES, None, None),
        both,
        P(AXES, None),
        P(AXES, None, None),
        P("group", None),
        P("group", None, None),
    )
    return jax.shard_map(
        body, mesh=mesh, in_specs=in_specs, out_specs=P(AXES, None), check_vma=False
    )
```

```python
import functools

import jax
import jax.numpy as jnp
from jax import lax
from jax.experimental import pallas as pl
from jax.experimental.pallas import tpu as pltpu
from jax.sharding import PartitionSpec as P

AXES = ("group", "cluster")
VMEM_LIMIT = 60 * 1024 * 1024


def params(limit=VMEM_LIMIT):
    return pltpu.CompilerParams(vmem_limit_bytes=limit)


def cost(flops, size):
    return pl.CostEstimate(flops=flops, bytes_accessed=size, transcendentals=0)


def whole(shape):
    return pl.BlockSpec(shape, lambda i, *_: (0,) * len(shape), pipeline_mode=pl.Buffered(1))


def first(group, *rest):
    return pl.BlockSpec((group,) + rest, lambda i, *_: (i,) + (0,) * len(rest))


def split(x):
    high = x.astype(jnp.bfloat16)
    low = (x - high.astype(jnp.float32)).astype(jnp.bfloat16)
    return high, low


def rows_of(x):
    return jnp.concatenate(split(x), axis=0)


def lanes_of(x):
    return jnp.concatenate(split(x), axis=1)


def dot(a, b):
    return lax.dot_general(a, b, (((1,), (0,)), ((), ())), preferred_element_type=jnp.float32)


def fold(product):
    m, n = product.shape[0] // 2, product.shape[1] // 2
    return product[:m, :n] + (product[:m, n:] + product[m:, :n] + product[m:, n:])


def deep_dot(a, b):
    high, low = split(b)
    return dot(jnp.concatenate([a, a], axis=1), jnp.concatenate([high, high, low, low], axis=0))


def up_kernel(size, parent, charges, basis, transfer, mid_transfer, send, coef, up):
    step = pl.program_id(0)
    group, rank, points = basis.shape
    mids = mid_transfer.shape[0]
    ports = up.shape[1]

    @pl.when(step == 0)
    def _():
        up[: mids * rank, :] = jnp.zeros((mids * rank, ports), jnp.float32)
        up[(mids + 1) * rank :, :] = jnp.zeros((up.shape[0] - (mids + 1) * rank, ports), jnp.float32)
        for row in range(send.shape[0]):
            spot = (mids + 1) * rank + row
            up[spot : spot + 1, : send.shape[1]] = send[row : row + 1, :].astype(jnp.float32)

    point = lax.broadcasted_iota(jnp.int32, (points, ports), 0)
    values = []
    for g in range(group):
        block = jnp.where(
            point < size[step * group + g], charges[g * points : (g + 1) * points, :], 0.0
        )
        values.append(fold(dot(rows_of(basis[g]), lanes_of(block))))
    for g in range(group):
        coef[g] = values[g]
    moved = [fold(dot(rows_of(transfer[g]), lanes_of(values[g]))) for g in range(group)]
    for g in range(group):
        where = pl.ds(pl.multiple_of(parent[step * group + g] * rank, rank), rank)
        up[where, :] += moved[g]

    @pl.when(step == pl.num_programs(0) - 1)
    def _():
        terms = [
            fold(dot(rows_of(mid_transfer[c]), lanes_of(up[c * rank : (c + 1) * rank, :])))
            for c in range(mids)
        ]
        while len(terms) > 1:
            terms = [sum(terms[i : i + 2]) for i in range(0, len(terms), 2)]
        up[mids * rank : (mids + 1) * rank, :] = terms[0]


def up_sweep(charges, leaf_size, basis, transfer, mid_transfer, leaf_parent, send_mid):
    leaves, rank, points = basis.shape
    ports = charges.shape[1]
    mids = mid_transfer.shape[0]
    group = 8
    up_rows = (mids + 1) * rank + -(-send_mid.shape[0] // 8) * 8
    return pl.pallas_call(
        up_kernel,
        grid_spec=pltpu.PrefetchScalarGridSpec(
            num_scalar_prefetch=2,
            grid=(leaves // group,),
            in_specs=[
                first(group * points, ports),
                first(group, rank, points),
                first(group, rank, rank),
                whole(mid_transfer.shape),
                whole(send_mid.shape),
            ],
            out_specs=[first(group, rank, ports), whole((up_rows, ports))],
        ),
        out_shape=[
            jax.ShapeDtypeStruct((leaves, rank, ports), jnp.float32),
            jax.ShapeDtypeStruct((up_rows, ports), jnp.float32),
        ],
        compiler_params=params(),
        cost_estimate=cost(10**9, 10**7),
        name="up_sweep",
    )(leaf_size, leaf_parent, charges, basis, transfer, mid_transfer, send_mid)


def spread_kernel(send, coef, out):
    leaves = coef.shape[0]

    @pl.loop(0, out.shape[0], unroll=8)
    def _(slot):
        out[slot] = coef[jnp.minimum(send[slot], leaves - 1)]


def spread(send_leaf, coef):
    vmem = pl.BlockSpec(memory_space=pltpu.VMEM)
    shape = (send_leaf.shape[0],) + coef.shape[1:]
    return pl.pallas_call(
        spread_kernel,
        in_specs=[pl.BlockSpec(memory_space=pltpu.SMEM), vmem],
        out_specs=vmem,
        out_shape=jax.ShapeDtypeStruct(shape, jnp.float32),
        compiler_params=params(),
        cost_estimate=cost(0, 4 * 10**6),
        name="spread",
    )(send_leaf, coef)


def select_kernel(sizes, place, *refs):
    lines, per_cluster, up_rows, mids, rank, per_pair, groups = sizes
    received, messages = refs[:lines], refs[lines : lines + groups]
    payloads, tables, sem, table_sem = refs[lines + groups :]
    group, lane = place[0], place[1]
    table_rows = up_rows - (mids + 1) * rank
    ports = payloads.shape[2]
    copies = []
    for line, ref in enumerate(received):
        table = ref.at[pl.ds((mids + 1) * rank, table_rows), :]
        copies.append(pltpu.make_async_copy(table, tables.at[line], table_sem.at[line]))
        copies.append(pltpu.make_async_copy(ref, payloads.at[line], sem.at[line]))
    for copy in copies:
        copy.start()
    for copy in copies:
        copy.wait()
    for d, message in enumerate(messages):
        for side in range(2):
            receiver = (group ^ d) * per_cluster + (lane ^ side)

            @pl.loop(0, lines, unroll=min(lines, 4))
            def _(line):
                for j in range(per_pair):
                    entry = receiver * per_pair + j
                    listed = tables[line, lax.div(entry, ports), lax.rem(entry, ports)]
                    block = jnp.clip(listed.astype(jnp.int32), 0, mids - 1)
                    target = (side * lines + line) * per_pair + j
                    message[target] = payloads[line, pl.ds(pl.multiple_of(block * rank, 8), rank), :]

        for line in range(lines):
            message[2 * lines * per_pair + line] = payloads[line, mids * rank : (mids + 1) * rank, :]


def select(sizes, place, received):
    lines, per_cluster, up_rows, mids, rank, per_pair, groups = sizes
    ports = received[0].shape[1]
    table_rows = up_rows - (mids + 1) * rank
    shape = jax.ShapeDtypeStruct((lines * (2 * per_pair + 1), rank, ports), jnp.float32)
    return pl.pallas_call(
        functools.partial(select_kernel, sizes),
        in_specs=[pl.BlockSpec(memory_space=pltpu.SMEM)]
        + [pl.BlockSpec(memory_space=pl.ANY)] * len(received),
        out_specs=[pl.BlockSpec(memory_space=pltpu.VMEM)] * groups,
        out_shape=[shape] * groups,
        scratch_shapes=[
            pltpu.VMEM((lines, up_rows, ports), jnp.float32),
            pltpu.SMEM((lines, table_rows, ports), jnp.float32),
            pltpu.SemaphoreType.DMA((lines,)),
            pltpu.SemaphoreType.DMA((lines,)),
        ],
        compiler_params=params(),
        cost_estimate=cost(0, 4 * 10**6),
        name="select",
    )(place, *received)


def prepare_kernel(after, coupling, basis, transfer, mid_coupling, mid_transfer, *out):
    wide, basis_t, transfer_t, mid_wide, mid_transfer_t = out
    for g in range(coupling.shape[0]):
        wide[g] = rows_of(coupling[g])
        basis_t[g] = rows_of(basis[g]).T
        transfer_t[g] = rows_of(transfer[g]).T
    for g in range(mid_coupling.shape[0]):
        mid_wide[g] = rows_of(mid_coupling[g])
        mid_transfer_t[g] = rows_of(mid_transfer[g]).T


def prepare(after, coupling, basis, transfer, mid_coupling, mid_transfer):
    leaves, rank, width = coupling.shape
    points = basis.shape[2]
    mids, _, mid_width = mid_coupling.shape
    steps = mids
    group = leaves // steps
    shapes = [
        (leaves, 2 * rank, width),
        (leaves, points, 2 * rank),
        (leaves, rank, 2 * rank),
        (mids, 2 * rank, mid_width),
        (mids, rank, 2 * rank),
    ]
    return pl.pallas_call(
        prepare_kernel,
        grid=(steps,),
        in_specs=[
            pl.BlockSpec(memory_space=pl.ANY),
            first(group, rank, width),
            first(group, rank, points),
            first(group, rank, rank),
            first(1, rank, mid_width),
            first(1, rank, rank),
        ],
        out_specs=[first(s[0] // steps, *s[1:]) for s in shapes],
        out_shape=[jax.ShapeDtypeStruct(s, jnp.bfloat16) for s in shapes],
        compiler_params=params(),
        cost_estimate=cost(0, 3 * 10**7),
        name="prepare",
    )(after, coupling, basis, transfer, mid_coupling, mid_transfer)


def mid_kernel(sizes, parent, pair, position, tops, *refs):
    bounds, per_pair, groups = sizes
    lines = bounds[-1]
    count = (len(bounds) - 1) * groups
    near_side, far_side = refs[:count], refs[count : 2 * count]
    coupling, top_coupling, mid_transfer, transfer, back, parts, top_parts, near_top, down = refs[2 * count :]
    step = pl.program_id(0)
    leaves = back.shape[0]
    group, _, width = coupling.shape
    rank = near_top.shape[0]
    slots, top_count = parts.shape[0] - 1, top_parts.shape[0] - 1

    @pl.when(step == 0)
    def _():
        for message in range(count):
            batch, d = divmod(message, groups)
            held = bounds[batch + 1] - bounds[batch]
            piece = held * per_pair
            sides = ((near_side[message], 2 * piece), (far_side[message], piece))
            for side, (ref, skip) in enumerate(sides):
                base = (d * 2 + side) * lines + bounds[batch]

                @pl.loop(0, piece, unroll=min(piece, 6))
                def _(slot):
                    parts[base * per_pair + slot] = lanes_of(ref[slot])

                for line in range(held):
                    top_parts[base + line] = lanes_of(ref[skip + line])

        parts[slots] = jnp.zeros(parts.shape[1:], jnp.bfloat16)
        top_parts[top_count] = jnp.zeros(top_parts.shape[1:], jnp.bfloat16)
        stacked = jnp.concatenate([top_parts[tops[k]] for k in range(tops.shape[0])], axis=0)
        near_top[...] = fold(dot(rows_of(top_coupling[0]), stacked))

    near = []
    for g in range(group):
        c = step * group + g
        stacked = jnp.concatenate([parts[pair[c, k]] for k in range(width // rank)], axis=0)
        near.append(fold(dot(coupling[g], stacked)) + deep_dot(mid_transfer[g], near_top[...]))
    for g in range(group):
        down[step * group + g] = near[g]

    @pl.when(step == pl.num_programs(0) - 1)
    def _():
        @pl.loop(0, leaves, unroll=8)
        def _(leaf):
            back[leaf] = deep_dot(transfer[leaf], down[parent[leaf]])


def mid_level(sizes, parent, pair, position, tops, near_side, far_side, coupling, top_coupling, mid_transfer, transfer):
    bounds, per_pair, groups = sizes
    mids, _, width = coupling.shape
    rank, ports = near_side[0].shape[1:]
    leaves = transfer.shape[0]
    owners = 2 * bounds[-1] * groups
    group = 4
    return pl.pallas_call(
        functools.partial(mid_kernel, sizes),
        grid_spec=pltpu.PrefetchScalarGridSpec(
            num_scalar_prefetch=4,
            grid=(mids // group,),
            in_specs=[whole(m.shape) for m in near_side + far_side]
            + [
                first(group, 2 * rank, width),
                pl.BlockSpec(
                    (1,) + top_coupling.shape[1:],
                    lambda i, parent, pair, position, tops: (position[0], 0, 0),
                ),
                first(group, rank, 2 * rank),
                whole(transfer.shape),
            ],
            out_specs=whole((leaves, rank, ports)),
            scratch_shapes=[
                pltpu.VMEM((owners * per_pair + 1, rank, 2 * ports), jnp.bfloat16),
                pltpu.VMEM((owners + 1, rank, 2 * ports), jnp.bfloat16),
                pltpu.VMEM((rank, ports), jnp.float32),
                pltpu.VMEM((mids, rank, ports), jnp.float32),
            ],
        ),
        out_shape=jax.ShapeDtypeStruct((leaves, rank, ports), jnp.float32),
        compiler_params=params(40 * 1024 * 1024),
        cost_estimate=cost(2 * 10**9, 10**7),
        name="mid_level",
    )(parent, pair, position, tops, *near_side, *far_side, coupling, top_coupling, mid_transfer, transfer)


def leaf_kernel(size, pair, arrived, coupling, basis, back, out, parts):
    step = pl.program_id(0)
    group, rank, _ = back.shape
    points = basis.shape[1]
    slots = arrived.shape[0]

    @pl.when(step == 0)
    def _():
        @pl.loop(0, slots, unroll=8)
        def _(slot):
            parts[slot] = lanes_of(arrived[slot])

        parts[slots] = jnp.zeros(parts.shape[1:], jnp.bfloat16)

    point = lax.broadcasted_iota(jnp.int32, (points, out.shape[1]), 0)
    values = []
    for g in range(group):
        leaf = step * group + g
        stacked = jnp.concatenate([parts[pair[leaf, k]] for k in range(coupling.shape[2] // rank)], axis=0)
        values.append(fold(dot(coupling[g], stacked)) + back[g])
    for g in range(group):
        far = deep_dot(basis[g], values[g])
        out[g * points : (g + 1) * points, :] = jnp.where(point < size[step * group + g], far, 0.0)


def leaf_level(leaf_size, pair_leaf, arrived, coupling, basis, back):
    leaves, _, width = coupling.shape
    points = basis.shape[1]
    slots, rank, ports = arrived.shape
    group = 8
    return pl.pallas_call(
        leaf_kernel,
        grid_spec=pltpu.PrefetchScalarGridSpec(
            num_scalar_prefetch=2,
            grid=(leaves // group,),
            in_specs=[
                whole(arrived.shape),
                first(group, 2 * rank, width),
                first(group, points, 2 * rank),
                first(group, rank, ports),
            ],
            out_specs=first(group * points, ports),
            scratch_shapes=[pltpu.VMEM((slots + 1, rank, 2 * ports), jnp.bfloat16)],
        ),
        out_shape=jax.ShapeDtypeStruct((leaves * points, ports), jnp.float32),
        compiler_params=params(36 * 1024 * 1024),
        cost_estimate=cost(4 * 10**9, 2 * 10**7),
        name="leaf_level",
    )(leaf_size, pair_leaf, arrived, coupling, basis, back)


def body(
    charges, leaf_size, leaf_basis, leaf_transfer, mid_transfer, leaf_parent, send_leaf, pair_leaf,
    leaf_coupling, send_mid, pair_mid, mid_coupling, top_pairs, top_coupling,
):
    rank = leaf_basis.shape[1]
    ports = charges.shape[1]
    mids = mid_transfer.shape[0]
    slots = send_mid.shape[0]
    groups, per_cluster = lax.axis_size("group"), lax.axis_size("cluster")
    owners = groups * per_cluster
    lines = per_cluster // 2
    per_pair = slots // owners
    group, lane = lax.axis_index("group"), lax.axis_index("cluster")

    table = send_mid.reshape(-1, min(slots, ports))
    coef, lifted = up_sweep(
        charges, leaf_size, leaf_basis, leaf_transfer, mid_transfer, leaf_parent, table
    )
    up_rows = lifted.shape[0]
    outgoing = spread(send_leaf, coef)

    received = [lifted]
    for d in range(1, lines):
        received.append(
            lax.ppermute(lifted, "cluster", [(c, c ^ (2 * d)) for c in range(per_cluster)])
        )
    wide, basis_t, transfer_t, mid_wide, mid_transfer_t = prepare(
        lifted, leaf_coupling, leaf_basis, leaf_transfer, mid_coupling, mid_transfer
    )

    place = jnp.stack([group, lane]).astype(jnp.int32)
    bounds = (0, 1, lines)
    near_side, far_side = [], []
    for low, high in zip(bounds[:-1], bounds[1:]):
        held = high - low
        sizes = (held, per_cluster, up_rows, mids, rank, per_pair, groups)
        messages = select(sizes, place, received[low:high])
        moved = [messages[0]]
        for d in range(1, groups):
            moved.append(lax.ppermute(messages[d], "group", [(g, g ^ d) for g in range(groups)]))
        if low == 0:
            outgoing, moved, received[1:] = lax.optimization_barrier((outgoing, moved, received[1:]))
            arrived = lax.all_to_all(outgoing, AXES, split_axis=0, concat_axis=0, tiled=True)
        else:
            moved, mid_wide = lax.optimization_barrier((moved, mid_wide))
        near_side += moved
        swap = [(c, c ^ 1) for c in range(per_cluster)]
        far_side += [lax.ppermute(m[held * per_pair :], "cluster", swap) for m in moved]

    def spot_of(sender):
        at_group, at_lane = sender // per_cluster, sender % per_cluster
        line = (at_lane // 2) ^ (lane // 2)
        return ((at_group ^ group) * 2 + ((at_lane ^ lane) & 1)) * lines + line

    spot = spot_of(pair_mid // per_pair) * per_pair + pair_mid % per_pair
    spot = jnp.where((pair_mid >= 0) & (pair_mid < slots), spot, slots)
    wanted = lax.dynamic_slice_in_dim(top_pairs, lane, 1, 0)[0]
    tops = jnp.where((wanted >= 0) & (wanted < owners), spot_of(wanted), owners)
    position = lane.astype(jnp.int32)[None]
    back = mid_level(
        (bounds, per_pair, groups), leaf_parent, spot, position, tops, near_side, far_side,
        mid_wide, top_coupling, mid_transfer_t, transfer_t,
    )
    return leaf_level(leaf_size, pair_leaf, arrived, wide, basis_t, back)


def solution(mesh):
    both = P(AXES)
    in_specs = (
        P(AXES, None),
        both,
        P(AXES, None, None),
        P(AXES, None, None),
        P(AXES, None, None),
        both,
        both,
        P(AXES, None),
        P(AXES, None, None),
        both,
        P(AXES, None),
        P(AXES, None, None),
        P("group", None),
        P("group", None, None),
    )
    return jax.shard_map(
        body, mesh=mesh, in_specs=in_specs, out_specs=P(AXES, None), check_vma=False
    )
```

```python
import functools
import math

import jax
import jax.numpy as jnp
from jax import lax
from jax.experimental import pallas as pl
from jax.experimental.pallas import tpu as pltpu
from jax.sharding import PartitionSpec as P

AXES = ("group", "cluster")
MIB = 1024 * 1024


def params(size):
    return pltpu.CompilerParams(vmem_limit_bytes=size)


def room(*blocks):
    size = sum(buffers * itemsize * math.prod(shape) for buffers, itemsize, shape in blocks)
    return size + size // 8 + 4 * MIB


def cost(flops, size):
    return pl.CostEstimate(flops=flops, bytes_accessed=size, transcendentals=0)


def whole(shape):
    return pl.BlockSpec(shape, lambda i, *_: (0,) * len(shape), pipeline_mode=pl.Buffered(1))


def first(group, *rest):
    return pl.BlockSpec((group,) + rest, lambda i, *_: (i,) + (0,) * len(rest))


def split(x):
    high = x.astype(jnp.bfloat16)
    low = (x - high.astype(jnp.float32)).astype(jnp.bfloat16)
    return high, low


def rows_of(x):
    return jnp.concatenate(split(x), axis=0)


def lanes_of(x):
    return jnp.concatenate(split(x), axis=1)


def dot(a, b):
    return lax.dot_general(a, b, (((1,), (0,)), ((), ())), preferred_element_type=jnp.float32)


def fold(product):
    m, n = product.shape[0] // 2, product.shape[1] // 2
    return product[:m, :n] + (product[:m, n:] + product[m:, :n] + product[m:, n:])


def deep_dot(a, b):
    high, low = split(b)
    return dot(jnp.concatenate([a, a], axis=1), jnp.concatenate([high, high, low, low], axis=0))


def up_kernel(
    sizes, size, parent, slots, group_at, lane_at, charges, basis, transfer, mid_transfer, send, coef, up,
    *messages
):
    step = pl.program_id(0)
    group, rank, points = basis.shape
    mids = mid_transfer.shape[0]
    ports = up.shape[1]

    @pl.when(step == 0)
    def _():
        up[: mids * rank, :] = jnp.zeros((mids * rank, ports), jnp.float32)
        up[(mids + 1) * rank :, :] = jnp.zeros((up.shape[0] - (mids + 1) * rank, ports), jnp.float32)
        for row in range(send.shape[0]):
            spot = (mids + 1) * rank + row
            up[spot : spot + 1, : send.shape[1]] = send[row : row + 1, :].astype(jnp.float32)

    point = lax.broadcasted_iota(jnp.int32, (points, ports), 0)
    values = []
    for g in range(group):
        block = jnp.where(
            point < size[step * group + g], charges[g * points : (g + 1) * points, :], 0.0
        )
        values.append(fold(dot(rows_of(basis[g]), lanes_of(block))))
    for g in range(group):
        coef[g] = values[g]
    moved = [fold(dot(rows_of(transfer[g]), lanes_of(values[g]))) for g in range(group)]
    for g in range(group):
        where = pl.ds(pl.multiple_of(parent[step * group + g] * rank, rank), rank)
        up[where, :] += moved[g]

    @pl.when(step == pl.num_programs(0) - 1)
    def _():
        terms = [
            fold(dot(rows_of(mid_transfer[c]), lanes_of(up[c * rank : (c + 1) * rank, :])))
            for c in range(mids)
        ]
        while len(terms) > 1:
            terms = [sum(terms[i : i + 2]) for i in range(0, len(terms), 2)]
        up[mids * rank : (mids + 1) * rank, :] = terms[0]
        per_cluster, per_pair = sizes
        for d, message in enumerate(messages):
            for side in range(2):
                receiver = (group_at[0] ^ d) * per_cluster + (lane_at[0] ^ side)
                for j in range(per_pair):
                    block = jnp.clip(slots[receiver * per_pair + j], 0, mids - 1)
                    source = pl.ds(pl.multiple_of(block * rank, rank), rank)
                    message[side * per_pair + j] = up[source, :]
            message[2 * per_pair] = terms[0]


def up_sweep(
    sizes, groups, group_at, lane_at, charges, leaf_size, basis, transfer, mid_transfer, leaf_parent, slots
):
    leaves, rank, points = basis.shape
    ports = charges.shape[1]
    mids = mid_transfer.shape[0]
    group = 8
    send_mid = slots.reshape(-1, min(slots.shape[0], ports))
    up_rows = (mids + 1) * rank + -(-send_mid.shape[0] // 8) * 8
    message = (2 * sizes[1] + 1, rank, ports)
    return pl.pallas_call(
        functools.partial(up_kernel, sizes),
        grid_spec=pltpu.PrefetchScalarGridSpec(
            num_scalar_prefetch=5,
            grid=(leaves // group,),
            in_specs=[
                first(group * points, ports),
                first(group, rank, points),
                first(group, rank, rank),
                whole(mid_transfer.shape),
                whole(send_mid.shape),
            ],
            out_specs=[first(group, rank, ports), whole((up_rows, ports))] + [whole(message)] * groups,
        ),
        out_shape=[
            jax.ShapeDtypeStruct((leaves, rank, ports), jnp.float32),
            jax.ShapeDtypeStruct((up_rows, ports), jnp.float32),
        ]
        + [jax.ShapeDtypeStruct(message, jnp.float32)] * groups,
        compiler_params=params(60 * MIB),
        cost_estimate=cost(10**9, 10**7),
        name="up_sweep",
    )(
        leaf_size, leaf_parent, slots, group_at, lane_at, charges, basis, transfer, mid_transfer, send_mid
    )


def spread_kernel(send, coef, out):
    leaves = coef.shape[0]

    @pl.loop(0, out.shape[0], unroll=8)
    def _(slot):
        out[slot] = coef[jnp.minimum(send[slot], leaves - 1)]


def spread(send_leaf, coef):
    vmem = pl.BlockSpec(memory_space=pltpu.VMEM)
    shape = (send_leaf.shape[0],) + coef.shape[1:]
    return pl.pallas_call(
        spread_kernel,
        in_specs=[pl.BlockSpec(memory_space=pltpu.SMEM), vmem],
        out_specs=vmem,
        out_shape=jax.ShapeDtypeStruct(shape, jnp.float32),
        compiler_params=params(room((1, 4, coef.shape), (1, 4, shape))),
        cost_estimate=cost(0, 4 * 10**6),
        name="spread",
    )(send_leaf, coef)


def select_kernel(sizes, group_at, lane_at, *refs):
    lines, per_cluster, up_rows, mids, rank, per_pair, groups = sizes
    received, messages = refs[:lines], refs[lines : lines + groups]
    payloads, tables, sem, table_sem = refs[lines + groups :]
    group, lane = group_at[0], lane_at[0]
    table_rows = up_rows - (mids + 1) * rank
    ports = payloads.shape[2]
    copies = []
    for line, ref in enumerate(received):
        table = ref.at[pl.ds((mids + 1) * rank, table_rows), :]
        copies.append(pltpu.make_async_copy(table, tables.at[line], table_sem.at[line]))
        copies.append(pltpu.make_async_copy(ref, payloads.at[line], sem.at[line]))
    for copy in copies:
        copy.start()
    for copy in copies:
        copy.wait()
    for d, message in enumerate(messages):
        for side in range(2):
            receiver = (group ^ d) * per_cluster + (lane ^ side)

            @pl.loop(0, lines, unroll=min(lines, 4))
            def _(line):
                for j in range(per_pair):
                    entry = receiver * per_pair + j
                    listed = tables[line, lax.div(entry, ports), lax.rem(entry, ports)]
                    block = jnp.clip(listed.astype(jnp.int32), 0, mids - 1)
                    target = (side * lines + line) * per_pair + j
                    message[target] = payloads[line, pl.ds(pl.multiple_of(block * rank, 8), rank), :]

        for line in range(lines):
            message[2 * lines * per_pair + line] = payloads[line, mids * rank : (mids + 1) * rank, :]


def select(sizes, group_at, lane_at, received):
    lines, per_cluster, up_rows, mids, rank, per_pair, groups = sizes
    ports = received[0].shape[1]
    table_rows = up_rows - (mids + 1) * rank
    payloads = (lines, up_rows, ports)
    shape = jax.ShapeDtypeStruct((lines * (2 * per_pair + 1), rank, ports), jnp.float32)
    return pl.pallas_call(
        functools.partial(select_kernel, sizes),
        in_specs=[pl.BlockSpec(memory_space=pltpu.SMEM)] * 2
        + [pl.BlockSpec(memory_space=pl.ANY)] * len(received),
        out_specs=[pl.BlockSpec(memory_space=pltpu.VMEM)] * groups,
        out_shape=[shape] * groups,
        scratch_shapes=[
            pltpu.VMEM(payloads, jnp.float32),
            pltpu.SMEM((lines, table_rows, ports), jnp.float32),
            pltpu.SemaphoreType.DMA((lines,)),
            pltpu.SemaphoreType.DMA((lines,)),
        ],
        compiler_params=params(room((1, 4, payloads), (groups, 4, shape.shape))),
        cost_estimate=cost(0, 4 * 10**6),
        name="select",
    )(group_at, lane_at, *received)


def prepare_kernel(after, coupling, basis, transfer, mid_coupling, mid_transfer, *out):
    wide, basis_t, transfer_t, mid_wide, mid_transfer_t = out
    for g in range(coupling.shape[0]):
        wide[g] = rows_of(coupling[g])
        basis_t[g] = rows_of(basis[g]).T
        transfer_t[g] = rows_of(transfer[g]).T
    for g in range(mid_coupling.shape[0]):
        mid_wide[g] = rows_of(mid_coupling[g])
        mid_transfer_t[g] = rows_of(mid_transfer[g]).T


def prepare(after, coupling, basis, transfer, mid_coupling, mid_transfer):
    leaves, rank, width = coupling.shape
    points = basis.shape[2]
    mids, _, mid_width = mid_coupling.shape
    steps = mids
    group = leaves // steps
    shapes = [
        (leaves, 2 * rank, width),
        (leaves, points, 2 * rank),
        (leaves, rank, 2 * rank),
        (mids, 2 * rank, mid_width),
        (mids, rank, 2 * rank),
    ]
    return pl.pallas_call(
        prepare_kernel,
        grid=(steps,),
        in_specs=[
            pl.BlockSpec(memory_space=pl.ANY),
            first(group, rank, width),
            first(group, rank, points),
            first(group, rank, rank),
            first(1, rank, mid_width),
            first(1, rank, rank),
        ],
        out_specs=[first(s[0] // steps, *s[1:]) for s in shapes],
        out_shape=[jax.ShapeDtypeStruct(s, jnp.bfloat16) for s in shapes],
        compiler_params=params(16 * MIB),
        cost_estimate=cost(0, 3 * 10**7),
        name="prepare",
    )(after, coupling, basis, transfer, mid_coupling, mid_transfer)


def mid_kernel(sizes, parent, pair, position, tops, *refs):
    bounds, per_pair, groups = sizes
    lines = bounds[-1]
    count = (len(bounds) - 1) * groups
    near_side, far_side = refs[:count], refs[count : 2 * count]
    coupling, top_coupling, mid_transfer, transfer, back, parts, top_parts, near_top, down = refs[2 * count :]
    step = pl.program_id(0)
    leaves = back.shape[0]
    group, _, width = coupling.shape
    rank = near_top.shape[0]
    slots, top_count = parts.shape[0] - 1, top_parts.shape[0] - 1

    @pl.when(step == 0)
    def _():
        for message in range(count):
            batch, d = divmod(message, groups)
            held = bounds[batch + 1] - bounds[batch]
            piece = held * per_pair
            for side, ref in enumerate((near_side[message], far_side[message])):
                base = (d * 2 + side) * lines + bounds[batch]

                @pl.loop(0, piece, unroll=min(piece, 6))
                def _(slot):
                    parts[base * per_pair + slot] = lanes_of(ref[side * piece + slot])

                for line in range(held):
                    top_parts[base + line] = lanes_of(ref[2 * piece + line])

        parts[slots] = jnp.zeros(parts.shape[1:], jnp.bfloat16)
        top_parts[top_count] = jnp.zeros(top_parts.shape[1:], jnp.bfloat16)
        stacked = jnp.concatenate([top_parts[tops[k]] for k in range(tops.shape[0])], axis=0)
        near_top[...] = fold(dot(rows_of(top_coupling[0]), stacked))

    near = []
    for g in range(group):
        c = step * group + g
        stacked = jnp.concatenate([parts[pair[c, k]] for k in range(width // rank)], axis=0)
        near.append(fold(dot(coupling[g], stacked)) + deep_dot(mid_transfer[g], near_top[...]))
    for g in range(group):
        down[step * group + g] = near[g]

    @pl.when(step == pl.num_programs(0) - 1)
    def _():
        @pl.loop(0, leaves, unroll=8)
        def _(leaf):
            back[leaf] = deep_dot(transfer[leaf], down[parent[leaf]])


def mid_level(sizes, parent, pair, position, tops, near_side, far_side, coupling, top_coupling, mid_transfer, transfer):
    bounds, per_pair, groups = sizes
    mids, _, width = coupling.shape
    rank, ports = near_side[0].shape[1:]
    leaves = transfer.shape[0]
    owners = 2 * bounds[-1] * groups
    group = 4
    parts = (owners * per_pair + 1, rank, 2 * ports)
    top_parts = (owners + 1, rank, 2 * ports)
    size = room(
        *((1, 4, m.shape) for m in near_side + far_side),
        (2, 2, (group, 2 * rank, width)),
        (1, 2, parts),
        (1, 2, top_parts),
        (1, 2, transfer.shape),
        (2, 4, (leaves, rank, ports)),
    )
    return pl.pallas_call(
        functools.partial(mid_kernel, sizes),
        grid_spec=pltpu.PrefetchScalarGridSpec(
            num_scalar_prefetch=4,
            grid=(mids // group,),
            in_specs=[whole(m.shape) for m in near_side + far_side]
            + [
                first(group, 2 * rank, width),
                pl.BlockSpec(
                    (1,) + top_coupling.shape[1:],
                    lambda i, parent, pair, position, tops: (position[0], 0, 0),
                ),
                first(group, rank, 2 * rank),
                whole(transfer.shape),
            ],
            out_specs=whole((leaves, rank, ports)),
            scratch_shapes=[
                pltpu.VMEM(parts, jnp.bfloat16),
                pltpu.VMEM(top_parts, jnp.bfloat16),
                pltpu.VMEM((rank, ports), jnp.float32),
                pltpu.VMEM((mids, rank, ports), jnp.float32),
            ],
        ),
        out_shape=jax.ShapeDtypeStruct((leaves, rank, ports), jnp.float32),
        compiler_params=params(size),
        cost_estimate=cost(2 * 10**9, 10**7),
        name="mid_level",
    )(parent, pair, position, tops, *near_side, *far_side, coupling, top_coupling, mid_transfer, transfer)


def leaf_kernel(size, pair, arrived, coupling, basis, back, out, parts):
    step = pl.program_id(0)
    group, rank, _ = back.shape
    points = basis.shape[1]
    slots = arrived.shape[0]

    @pl.when(step == 0)
    def _():
        @pl.loop(0, slots, unroll=8)
        def _(slot):
            parts[slot] = lanes_of(arrived[slot])

        parts[slots] = jnp.zeros(parts.shape[1:], jnp.bfloat16)

    point = lax.broadcasted_iota(jnp.int32, (points, out.shape[1]), 0)
    values = []
    for g in range(group):
        leaf = step * group + g
        stacked = jnp.concatenate([parts[pair[leaf, k]] for k in range(coupling.shape[2] // rank)], axis=0)
        values.append(fold(dot(coupling[g], stacked)) + back[g])
    for g in range(group):
        far = deep_dot(basis[g], values[g])
        out[g * points : (g + 1) * points, :] = jnp.where(point < size[step * group + g], far, 0.0)


def leaf_level(leaf_size, pair_leaf, arrived, coupling, basis, back):
    leaves, _, width = coupling.shape
    points = basis.shape[1]
    slots, rank, ports = arrived.shape
    group = 8
    parts = (slots + 1, rank, 2 * ports)
    size = room(
        (1, 4, arrived.shape),
        (1, 2, parts),
        (2, 2, (group, 2 * rank, width)),
        (2, 2, (group, points, 2 * rank)),
        (2, 4, (group, rank, ports)),
        (2, 4, (group * points, ports)),
    )
    return pl.pallas_call(
        leaf_kernel,
        grid_spec=pltpu.PrefetchScalarGridSpec(
            num_scalar_prefetch=2,
            grid=(leaves // group,),
            in_specs=[
                whole(arrived.shape),
                first(group, 2 * rank, width),
                first(group, points, 2 * rank),
                first(group, rank, ports),
            ],
            out_specs=first(group * points, ports),
            scratch_shapes=[pltpu.VMEM(parts, jnp.bfloat16)],
        ),
        out_shape=jax.ShapeDtypeStruct((leaves * points, ports), jnp.float32),
        compiler_params=params(size),
        cost_estimate=cost(4 * 10**9, 2 * 10**7),
        name="leaf_level",
    )(leaf_size, pair_leaf, arrived, coupling, basis, back)


def body(
    charges, leaf_size, leaf_basis, leaf_transfer, mid_transfer, leaf_parent, send_leaf, pair_leaf,
    leaf_coupling, send_mid, pair_mid, mid_coupling, top_pairs, top_coupling,
):
    rank = leaf_basis.shape[1]
    ports = charges.shape[1]
    mids = mid_transfer.shape[0]
    slots = send_mid.shape[0]
    groups, per_cluster = lax.axis_size("group"), lax.axis_size("cluster")
    owners = groups * per_cluster
    lines = per_cluster // 2
    per_pair = slots // owners
    group, lane = lax.axis_index("group"), lax.axis_index("cluster")

    group_at, lane_at = group.astype(jnp.int32)[None], lane.astype(jnp.int32)[None]
    coef, lifted, *own_messages = up_sweep(
        (per_cluster, per_pair), groups, group_at, lane_at, charges, leaf_size, leaf_basis,
        leaf_transfer, mid_transfer, leaf_parent, send_mid,
    )
    up_rows = lifted.shape[0]
    outgoing = spread(send_leaf, coef)

    received = [lifted]
    for d in range(1, lines):
        received.append(
            lax.ppermute(lifted, "cluster", [(c, c ^ (2 * d)) for c in range(per_cluster)])
        )
    wide, basis_t, transfer_t, mid_wide, mid_transfer_t = prepare(
        lifted, leaf_coupling, leaf_basis, leaf_transfer, mid_coupling, mid_transfer
    )

    bounds = (0, 1, lines)
    near_side, far_side = [], []
    for low, high in zip(bounds[:-1], bounds[1:]):
        held = high - low
        sizes = (held, per_cluster, up_rows, mids, rank, per_pair, groups)
        messages = own_messages if low == 0 else select(sizes, group_at, lane_at, received[low:high])
        moved = [messages[0]]
        for d in range(1, groups):
            moved.append(lax.ppermute(messages[d], "group", [(g, g ^ d) for g in range(groups)]))
        if low == 0:
            outgoing, moved, received[1:] = lax.optimization_barrier((outgoing, moved, received[1:]))
            arrived = lax.all_to_all(outgoing, AXES, split_axis=0, concat_axis=0, tiled=True)
        else:
            moved, mid_wide = lax.optimization_barrier((moved, mid_wide))
        near_side += moved
        swap = [(c, c ^ 1) for c in range(per_cluster)]
        far_side += [lax.ppermute(m, "cluster", swap) for m in moved]

    def spot_of(sender):
        at_group, at_lane = sender // per_cluster, sender % per_cluster
        line = (at_lane // 2) ^ (lane // 2)
        return ((at_group ^ group) * 2 + ((at_lane ^ lane) & 1)) * lines + line

    spot = spot_of(pair_mid // per_pair) * per_pair + pair_mid % per_pair
    spot = jnp.where((pair_mid >= 0) & (pair_mid < slots), spot, slots)
    wanted = lax.dynamic_slice_in_dim(top_pairs, lane, 1, 0)[0]
    tops = jnp.where((wanted >= 0) & (wanted < owners), spot_of(wanted), owners)
    back = mid_level(
        (bounds, per_pair, groups), leaf_parent, spot, lane_at, tops, near_side, far_side,
        mid_wide, top_coupling, mid_transfer_t, transfer_t,
    )
    return leaf_level(leaf_size, pair_leaf, arrived, wide, basis_t, back)


def solution(mesh):
    both = P(AXES)
    in_specs = (
        P(AXES, None),
        both,
        P(AXES, None, None),
        P(AXES, None, None),
        P(AXES, None, None),
        both,
        both,
        P(AXES, None),
        P(AXES, None, None),
        both,
        P(AXES, None),
        P(AXES, None, None),
        P("group", None),
        P("group", None, None),
    )
    return jax.shard_map(
        body, mesh=mesh, in_specs=in_specs, out_specs=P(AXES, None), check_vma=False
    )
```

```python
import functools

import jax
import jax.numpy as jnp
from jax import lax
from jax.experimental import pallas as pl
from jax.experimental.pallas import tpu as pltpu
from jax.sharding import PartitionSpec as P

AXES = ("group", "cluster")
MIB = 1024 * 1024


def params(size):
    return pltpu.CompilerParams(vmem_limit_bytes=size)


def cost(flops, size):
    return pl.CostEstimate(flops=flops, bytes_accessed=size, transcendentals=0)


def whole(shape):
    return pl.BlockSpec(shape, lambda i, *_: (0,) * len(shape), pipeline_mode=pl.Buffered(1))


def first(group, *rest):
    return pl.BlockSpec((group,) + rest, lambda i, *_: (i,) + (0,) * len(rest))


def split(x):
    high = x.astype(jnp.bfloat16)
    low = (x - high.astype(jnp.float32)).astype(jnp.bfloat16)
    return high, low


def rows_of(x):
    return jnp.concatenate(split(x), axis=0)


def lanes_of(x):
    return jnp.concatenate(split(x), axis=1)


def dot(a, b):
    return lax.dot_general(a, b, (((1,), (0,)), ((), ())), preferred_element_type=jnp.float32)


def fold(product):
    m, n = product.shape[0] // 2, product.shape[1] // 2
    return product[:m, :n] + (product[:m, n:] + product[m:, :n] + product[m:, n:])


def deep_dot(a, b):
    high, low = split(b)
    return dot(jnp.concatenate([a, a], axis=1), jnp.concatenate([high, high, low, low], axis=0))


def up_kernel(
    sizes, size, parent, slots, group_at, lane_at, charges, basis, transfer, mid_transfer, send, coef, up,
    *messages
):
    step = pl.program_id(0)
    group, rank, points = basis.shape
    mids = mid_transfer.shape[0]
    ports = up.shape[1]

    @pl.when(step == 0)
    def _():
        up[: mids * rank, :] = jnp.zeros((mids * rank, ports), jnp.float32)
        up[(mids + 1) * rank :, :] = jnp.zeros((up.shape[0] - (mids + 1) * rank, ports), jnp.float32)
        for row in range(send.shape[0]):
            spot = (mids + 1) * rank + row
            up[spot : spot + 1, : send.shape[1]] = send[row : row + 1, :].astype(jnp.float32)

    point = lax.broadcasted_iota(jnp.int32, (points, ports), 0)
    values = []
    for g in range(group):
        block = jnp.where(
            point < size[step * group + g], charges[g * points : (g + 1) * points, :], 0.0
        )
        values.append(fold(dot(rows_of(basis[g]), lanes_of(block))))
    for g in range(group):
        coef[g] = values[g]
    moved = [fold(dot(rows_of(transfer[g]), lanes_of(values[g]))) for g in range(group)]
    for g in range(group):
        where = pl.ds(pl.multiple_of(parent[step * group + g] * rank, rank), rank)
        up[where, :] += moved[g]

    @pl.when(step == pl.num_programs(0) - 1)
    def _():
        terms = [
            fold(dot(rows_of(mid_transfer[c]), lanes_of(up[c * rank : (c + 1) * rank, :])))
            for c in range(mids)
        ]
        while len(terms) > 1:
            terms = [sum(terms[i : i + 2]) for i in range(0, len(terms), 2)]
        up[mids * rank : (mids + 1) * rank, :] = terms[0]
        per_cluster, per_pair = sizes
        for d, message in enumerate(messages):
            for side in range(2):
                receiver = (group_at[0] ^ d) * per_cluster + (lane_at[0] ^ side)
                for j in range(per_pair):
                    block = jnp.clip(slots[receiver * per_pair + j], 0, mids - 1)
                    source = pl.ds(pl.multiple_of(block * rank, rank), rank)
                    message[(1 - side) * (per_pair + 1) + j] = up[source, :]
            message[per_pair] = terms[0]


def up_sweep(
    sizes, groups, group_at, lane_at, charges, leaf_size, basis, transfer, mid_transfer, leaf_parent, slots
):
    leaves, rank, points = basis.shape
    ports = charges.shape[1]
    mids = mid_transfer.shape[0]
    group = 8
    send_mid = slots.reshape(-1, min(slots.shape[0], ports))
    up_rows = (mids + 1) * rank + -(-send_mid.shape[0] // 8) * 8
    message = (2 * sizes[1] + 1, rank, ports)
    return pl.pallas_call(
        functools.partial(up_kernel, sizes),
        grid_spec=pltpu.PrefetchScalarGridSpec(
            num_scalar_prefetch=5,
            grid=(leaves // group,),
            in_specs=[
                first(group * points, ports),
                first(group, rank, points),
                first(group, rank, rank),
                whole(mid_transfer.shape),
                whole(send_mid.shape),
            ],
            out_specs=[first(group, rank, ports), whole((up_rows, ports))] + [whole(message)] * groups,
        ),
        out_shape=[
            jax.ShapeDtypeStruct((leaves, rank, ports), jnp.float32),
            jax.ShapeDtypeStruct((up_rows, ports), jnp.float32),
        ]
        + [jax.ShapeDtypeStruct(message, jnp.float32)] * groups,
        compiler_params=params(60 * MIB),
        cost_estimate=cost(10**9, 10**7),
        name="up_sweep",
    )(
        leaf_size, leaf_parent, slots, group_at, lane_at, charges, basis, transfer, mid_transfer, send_mid
    )


def spread_kernel(send, coef, out):
    leaves = coef.shape[0]

    @pl.loop(0, out.shape[0], unroll=8)
    def _(slot):
        out[slot] = coef[jnp.minimum(send[slot], leaves - 1)]


def spread(send_leaf, coef):
    vmem = pl.BlockSpec(memory_space=pltpu.VMEM)
    shape = (send_leaf.shape[0],) + coef.shape[1:]
    return pl.pallas_call(
        spread_kernel,
        in_specs=[pl.BlockSpec(memory_space=pltpu.SMEM), vmem],
        out_specs=vmem,
        out_shape=jax.ShapeDtypeStruct(shape, jnp.float32),
        compiler_params=params(60 * MIB),
        cost_estimate=cost(0, 4 * 10**6),
        name="spread",
    )(send_leaf, coef)


def select_kernel(sizes, group_at, lane_at, *refs):
    lines, per_cluster, up_rows, mids, rank, per_pair, groups = sizes
    received, messages = refs[:lines], refs[lines : lines + groups]
    payloads, tables, sem, table_sem = refs[lines + groups :]
    group, lane = group_at[0], lane_at[0]
    table_rows = up_rows - (mids + 1) * rank
    ports = payloads.shape[2]
    copies = []
    for line, ref in enumerate(received):
        table = ref.at[pl.ds((mids + 1) * rank, table_rows), :]
        copies.append(pltpu.make_async_copy(table, tables.at[line], table_sem.at[line]))
        copies.append(pltpu.make_async_copy(ref, payloads.at[line], sem.at[line]))
    for copy in copies:
        copy.start()
    for copy in copies:
        copy.wait()
    for d, message in enumerate(messages):
        for side in range(2):
            receiver = (group ^ d) * per_cluster + (lane ^ side)

            @pl.loop(0, lines, unroll=min(lines, 4))
            def _(line):
                for j in range(per_pair):
                    entry = receiver * per_pair + j
                    listed = tables[line, lax.div(entry, ports), lax.rem(entry, ports)]
                    block = jnp.clip(listed.astype(jnp.int32), 0, mids - 1)
                    target = (1 - side) * (per_pair + 1) * lines + line * per_pair + j
                    message[target] = payloads[line, pl.ds(pl.multiple_of(block * rank, 8), rank), :]

        for line in range(lines):
            message[lines * per_pair + line] = payloads[line, mids * rank : (mids + 1) * rank, :]


def select(sizes, group_at, lane_at, received):
    lines, per_cluster, up_rows, mids, rank, per_pair, groups = sizes
    ports = received[0].shape[1]
    table_rows = up_rows - (mids + 1) * rank
    payloads = (lines, up_rows, ports)
    shape = jax.ShapeDtypeStruct((lines * (2 * per_pair + 1), rank, ports), jnp.float32)
    return pl.pallas_call(
        functools.partial(select_kernel, sizes),
        in_specs=[pl.BlockSpec(memory_space=pltpu.SMEM)] * 2
        + [pl.BlockSpec(memory_space=pl.ANY)] * len(received),
        out_specs=[pl.BlockSpec(memory_space=pltpu.VMEM)] * groups,
        out_shape=[shape] * groups,
        scratch_shapes=[
            pltpu.VMEM(payloads, jnp.float32),
            pltpu.SMEM((lines, table_rows, ports), jnp.float32),
            pltpu.SemaphoreType.DMA((lines,)),
            pltpu.SemaphoreType.DMA((lines,)),
        ],
        compiler_params=params(60 * MIB),
        cost_estimate=cost(0, 4 * 10**6),
        name="select",
    )(group_at, lane_at, *received)


def prepare_kernel(after, coupling, basis, transfer, mid_coupling, mid_transfer, *out):
    wide, basis_t, transfer_t, mid_wide, mid_transfer_t = out
    for g in range(coupling.shape[0]):
        wide[g] = rows_of(coupling[g])
        basis_t[g] = rows_of(basis[g]).T
        transfer_t[g] = rows_of(transfer[g]).T
    for g in range(mid_coupling.shape[0]):
        mid_wide[g] = rows_of(mid_coupling[g])
        mid_transfer_t[g] = rows_of(mid_transfer[g]).T


def prepare(after, coupling, basis, transfer, mid_coupling, mid_transfer):
    leaves, rank, width = coupling.shape
    points = basis.shape[2]
    mids, _, mid_width = mid_coupling.shape
    steps = mids
    group = leaves // steps
    shapes = [
        (leaves, 2 * rank, width),
        (leaves, points, 2 * rank),
        (leaves, rank, 2 * rank),
        (mids, 2 * rank, mid_width),
        (mids, rank, 2 * rank),
    ]
    return pl.pallas_call(
        prepare_kernel,
        grid=(steps,),
        in_specs=[
            pl.BlockSpec(memory_space=pl.ANY),
            first(group, rank, width),
            first(group, rank, points),
            first(group, rank, rank),
            first(1, rank, mid_width),
            first(1, rank, rank),
        ],
        out_specs=[first(s[0] // steps, *s[1:]) for s in shapes],
        out_shape=[jax.ShapeDtypeStruct(s, jnp.bfloat16) for s in shapes],
        compiler_params=params(60 * MIB),
        cost_estimate=cost(0, 3 * 10**7),
        name="prepare",
    )(after, coupling, basis, transfer, mid_coupling, mid_transfer)


def tail_kernel(
    sizes, parent, pair, position, tops, size, pair_leaf, *refs
):
    bounds, per_pair, groups, chunk, group = sizes
    lines, count = bounds[-1], (len(bounds) - 1) * groups
    messages = refs[: 2 * count]
    (arrived, mid_wide, mid_transfer, transfer, top_coupling, wide, basis, out) = refs[2 * count : 2 * count + 8]
    scratch = refs[2 * count + 8 :]
    held_messages, scratch = scratch[: 2 * count], scratch[2 * count :]
    (
        arrived_held, mid_wide_held, mid_transfer_held, transfer_held, top_held, wide_held, basis_held,
        parts, top_parts, leaf_parts, near_top, down, back, out_held,
        message_sem, arrived_sem, mid_sem, small_sem, wide_sem, basis_sem, out_sem,
    ) = scratch
    mids, leaves = mid_wide.shape[0], wide.shape[0]
    rank, ports = back.shape[1:]
    slots, top_count = parts.shape[0] - 1, top_parts.shape[0] - 1
    points = basis.shape[1]

    def fetch_message(index):
        held = held_messages[index]
        start = 0 if index >= count else messages[index].shape[0] - held.shape[0]
        source = messages[index].at[pl.ds(start, held.shape[0])]
        return pltpu.make_async_copy(source, held, message_sem.at[index])

    def fetch_arrived(index):
        source = arrived.at[pl.ds(index * chunk, chunk)]
        return pltpu.make_async_copy(source, arrived_held.at[index % 2], arrived_sem.at[index % 2])

    def fetch_mid(c):
        return pltpu.make_async_copy(mid_wide.at[c], mid_wide_held.at[c], mid_sem.at[c])

    def fetch_leaves(index):
        some = pl.ds(index * group, group)
        return (
            pltpu.make_async_copy(wide.at[some], wide_held.at[some], wide_sem.at[index]),
            pltpu.make_async_copy(basis.at[some], basis_held.at[some], basis_sem.at[index]),
        )

    small = (
        pltpu.make_async_copy(top_coupling.at[position[0]], top_held, small_sem.at[0]),
        pltpu.make_async_copy(mid_transfer, mid_transfer_held, small_sem.at[1]),
        pltpu.make_async_copy(transfer, transfer_held, small_sem.at[2]),
    )
    chunks = slots // chunk
    for index in range(min(2, chunks)):
        fetch_arrived(index).start()
    for index in range(2 * count):
        fetch_message(index).start()
    for copy in small:
        copy.start()
    for c in range(mids):
        fetch_mid(c).start()
    for index in range(leaves // group):
        for copy in fetch_leaves(index):
            copy.start()

    leaf_parts[slots] = jnp.zeros(leaf_parts.shape[1:], jnp.bfloat16)
    parts[slots] = jnp.zeros(parts.shape[1:], jnp.bfloat16)
    top_parts[top_count] = jnp.zeros(top_parts.shape[1:], jnp.bfloat16)
    for index in range(chunks):
        fetch_arrived(index).wait()

        @pl.loop(0, chunk, unroll=8)
        def _(slot):
            leaf_parts[index * chunk + slot] = lanes_of(arrived_held[index % 2, slot])

        if index + 2 < chunks:
            fetch_arrived(index + 2).start()

    for index in range(2 * count):
        side, message = divmod(index, count)
        batch, d = divmod(message, groups)
        lines_held = bounds[batch + 1] - bounds[batch]
        piece = lines_held * per_pair
        base = (d * 2 + side) * lines + bounds[batch]
        held = held_messages[index]
        first_slot, first_top = (lines_held, 0) if side == 0 else (0, piece)
        fetch_message(index).wait()

        @pl.loop(0, piece, unroll=min(piece, 6))
        def _(slot):
            parts[base * per_pair + slot] = lanes_of(held[first_slot + slot])

        for line in range(lines_held):
            top_parts[base + line] = lanes_of(held[first_top + line])

    for copy in small:
        copy.wait()
    stacked = jnp.concatenate([top_parts[tops[k]] for k in range(tops.shape[0])], axis=0)
    near_top[...] = fold(dot(rows_of(top_held[...]), stacked))
    for c in range(mids):
        fetch_mid(c).wait()

    @pl.loop(0, mids, step=4)
    def _(start):
        near = []
        for g in range(4):
            c = start + g
            stacked = jnp.concatenate([parts[pair[c, k]] for k in range(pair.shape[1])], axis=0)
            value = fold(dot(mid_wide_held[c], stacked))
            near.append(value + deep_dot(mid_transfer_held[c], near_top[...]))
        for g in range(4):
            down[start + g] = near[g]

    @pl.loop(0, leaves, step=8)
    def _(start):
        terms = [deep_dot(transfer_held[start + g], down[parent[start + g]]) for g in range(8)]
        for g in range(8):
            back[start + g] = terms[g]

    point = lax.broadcasted_iota(jnp.int32, (points, ports), 0)

    def send(index):
        rows = group * points
        target = out.at[pl.ds(pl.multiple_of(index * rows, rows), rows), :]
        return pltpu.make_async_copy(out_held.at[index % 2], target, out_sem.at[index % 2])

    for index in range(leaves // group):
        for copy in fetch_leaves(index):
            copy.wait()
        values = []
        for g in range(group):
            leaf = index * group + g
            stacked = jnp.concatenate(
                [leaf_parts[pair_leaf[leaf, k]] for k in range(pair_leaf.shape[1])], axis=0
            )
            values.append(fold(dot(wide_held[leaf], stacked)) + back[leaf])
        if index >= 2:
            send(index - 2).wait()
        for g in range(group):
            far = deep_dot(basis_held[index * group + g], values[g])
            far = jnp.where(point < size[index * group + g], far, 0.0)
            out_held[index % 2, g * points : (g + 1) * points, :] = far
        send(index).start()
    for index in range(max(0, leaves // group - 2), leaves // group):
        send(index).wait()


def tail(
    bounds, per_pair, groups, parent, pair, position, tops, size, pair_leaf, near_side, far_side, arrived,
    mid_wide, mid_transfer, transfer, top_coupling, wide, basis
):
    mids, _, mid_width = mid_wide.shape
    leaves, points, _ = basis.shape
    slots, rank, ports = arrived.shape
    owners = slots // per_pair
    group, chunk = 4, min(slots, 32)
    held = []
    for message in range(len(near_side)):
        batch = message // groups
        held.append((bounds[batch + 1] - bounds[batch]) * (per_pair + 1))
    full, half = jnp.float32, jnp.bfloat16
    scratch = [((h, rank, ports), full) for h in held + held] + [
        ((2, chunk, rank, ports), full),
        (mid_wide.shape, half),
        (mid_transfer.shape, half),
        (transfer.shape, half),
        (top_coupling.shape[1:], full),
        (wide.shape, half),
        (basis.shape, half),
        ((slots + 1, rank, 2 * ports), half),
        ((owners + 1, rank, 2 * ports), half),
        ((slots + 1, rank, 2 * ports), half),
        ((rank, ports), full),
        ((mids, rank, ports), full),
        ((leaves, rank, ports), full),
        ((2, group * points, ports), full),
    ]
    semaphores = [2 * len(near_side), 2, mids, 3, leaves // group, leaves // group, 2]
    scalars = (parent, pair, position, tops, size, pair_leaf)
    arrays = (*near_side, *far_side, arrived, mid_wide, mid_transfer, transfer, top_coupling, wide, basis)
    return pl.pallas_call(
        functools.partial(tail_kernel, (bounds, per_pair, groups, chunk, group)),
        in_specs=[pl.BlockSpec(memory_space=pltpu.SMEM)] * len(scalars)
        + [pl.BlockSpec(memory_space=pl.ANY)] * len(arrays),
        out_specs=pl.BlockSpec(memory_space=pl.ANY),
        out_shape=jax.ShapeDtypeStruct((leaves * points, ports), full),
        scratch_shapes=[pltpu.VMEM(shape, dtype) for shape, dtype in scratch]
        + [pltpu.SemaphoreType.DMA((n,)) for n in semaphores],
        compiler_params=params(60 * MIB),
        cost_estimate=cost(6 * 10**9, 2 * 10**7),
        name="tail",
    )(*scalars, *arrays)


def body(
    charges, leaf_size, leaf_basis, leaf_transfer, mid_transfer, leaf_parent, send_leaf, pair_leaf,
    leaf_coupling, send_mid, pair_mid, mid_coupling, top_pairs, top_coupling,
):
    rank = leaf_basis.shape[1]
    ports = charges.shape[1]
    mids = mid_transfer.shape[0]
    slots = send_mid.shape[0]
    groups, per_cluster = lax.axis_size("group"), lax.axis_size("cluster")
    owners = groups * per_cluster
    lines = per_cluster // 2
    per_pair = slots // owners
    group, lane = lax.axis_index("group"), lax.axis_index("cluster")

    group_at, lane_at = group.astype(jnp.int32)[None], lane.astype(jnp.int32)[None]
    coef, lifted, *own_messages = up_sweep(
        (per_cluster, per_pair), groups, group_at, lane_at, charges, leaf_size, leaf_basis,
        leaf_transfer, mid_transfer, leaf_parent, send_mid,
    )
    up_rows = lifted.shape[0]
    outgoing = spread(send_leaf, coef)

    received = [lifted]
    for d in range(1, lines):
        received.append(
            lax.ppermute(lifted, "cluster", [(c, c ^ (2 * d)) for c in range(per_cluster)])
        )
    wide, basis_t, transfer_t, mid_wide, mid_transfer_t = prepare(
        lifted, leaf_coupling, leaf_basis, leaf_transfer, mid_coupling, mid_transfer
    )

    bounds = (0, 1, lines)
    near_side, far_side = [], []
    for low, high in zip(bounds[:-1], bounds[1:]):
        held = high - low
        sizes = (held, per_cluster, up_rows, mids, rank, per_pair, groups)
        messages = own_messages if low == 0 else select(sizes, group_at, lane_at, received[low:high])
        moved = [messages[0]]
        for d in range(1, groups):
            moved.append(lax.ppermute(messages[d], "group", [(g, g ^ d) for g in range(groups)]))
        if low == 0:
            outgoing, moved, received[1:] = lax.optimization_barrier((outgoing, moved, received[1:]))
            arrived = lax.all_to_all(outgoing, AXES, split_axis=0, concat_axis=0, tiled=True)
        else:
            moved, mid_wide = lax.optimization_barrier((moved, mid_wide))
        near_side += moved
        swap = [(c, c ^ 1) for c in range(per_cluster)]
        far_side += [lax.ppermute(m, "cluster", swap) for m in moved]

    def spot_of(sender):
        at_group, at_lane = sender // per_cluster, sender % per_cluster
        line = (at_lane // 2) ^ (lane // 2)
        return ((at_group ^ group) * 2 + ((at_lane ^ lane) & 1)) * lines + line

    spot = spot_of(pair_mid // per_pair) * per_pair + pair_mid % per_pair
    spot = jnp.where((pair_mid >= 0) & (pair_mid < slots), spot, slots)
    wanted = lax.dynamic_slice_in_dim(top_pairs, lane, 1, 0)[0]
    tops = jnp.where((wanted >= 0) & (wanted < owners), spot_of(wanted), owners)
    return tail(
        bounds, per_pair, groups, leaf_parent, spot, lane_at, tops, leaf_size, pair_leaf, near_side,
        far_side, arrived, mid_wide, mid_transfer_t, transfer_t, top_coupling, wide, basis_t,
    )


def solution(mesh):
    both = P(AXES)
    in_specs = (
        P(AXES, None),
        both,
        P(AXES, None, None),
        P(AXES, None, None),
        P(AXES, None, None),
        both,
        both,
        P(AXES, None),
        P(AXES, None, None),
        both,
        P(AXES, None),
        P(AXES, None, None),
        P("group", None),
        P("group", None, None),
    )
    return jax.shard_map(
        body, mesh=mesh, in_specs=in_specs, out_specs=P(AXES, None), check_vma=False
    )
```

```python
import functools

import jax
import jax.numpy as jnp
from jax import lax
from jax.experimental import pallas as pl
from jax.experimental.pallas import tpu as pltpu
from jax.sharding import PartitionSpec as P

AXES = ("group", "cluster")
MIB = 1024 * 1024


def params(size):
    return pltpu.CompilerParams(vmem_limit_bytes=size)


def cost(flops, size):
    return pl.CostEstimate(flops=flops, bytes_accessed=size, transcendentals=0)


def whole(shape):
    return pl.BlockSpec(shape, lambda i, *_: (0,) * len(shape), pipeline_mode=pl.Buffered(1))


def first(group, *rest):
    return pl.BlockSpec((group,) + rest, lambda i, *_: (i,) + (0,) * len(rest))


def split(x):
    high = x.astype(jnp.bfloat16)
    low = (x - high.astype(jnp.float32)).astype(jnp.bfloat16)
    return high, low


def rows_of(x):
    return jnp.concatenate(split(x), axis=0)


def lanes_of(x):
    return jnp.concatenate(split(x), axis=1)


def dot(a, b):
    return lax.dot_general(a, b, (((1,), (0,)), ((), ())), preferred_element_type=jnp.float32)


def fold(product):
    m, n = product.shape[0] // 2, product.shape[1] // 2
    return product[:m, :n] + (product[:m, n:] + product[m:, :n] + product[m:, n:])


def deep_dot(a, b):
    high, low = split(b)
    return dot(jnp.concatenate([a, a], axis=1), jnp.concatenate([high, high, low, low], axis=0))


def up_kernel(
    sizes, size, parent, slots, group_at, lane_at, charges, basis, transfer, mid_transfer, send, coef, up,
    *messages
):
    step = pl.program_id(0)
    group, rank, points = basis.shape
    mids = mid_transfer.shape[0]
    ports = up.shape[1]

    @pl.when(step == 0)
    def _():
        up[: mids * rank, :] = jnp.zeros((mids * rank, ports), jnp.float32)
        up[(mids + 1) * rank :, :] = jnp.zeros((up.shape[0] - (mids + 1) * rank, ports), jnp.float32)
        for row in range(send.shape[0]):
            spot = (mids + 1) * rank + row
            up[spot : spot + 1, : send.shape[1]] = send[row : row + 1, :].astype(jnp.float32)

    point = lax.broadcasted_iota(jnp.int32, (points, ports), 0)
    values = []
    for g in range(group):
        block = jnp.where(
            point < size[step * group + g], charges[g * points : (g + 1) * points, :], 0.0
        )
        values.append(fold(dot(rows_of(basis[g]), lanes_of(block))))
    for g in range(group):
        coef[g] = values[g]
    moved = [fold(dot(rows_of(transfer[g]), lanes_of(values[g]))) for g in range(group)]
    for g in range(group):
        where = pl.ds(pl.multiple_of(parent[step * group + g] * rank, rank), rank)
        up[where, :] += moved[g]

    @pl.when(step == pl.num_programs(0) - 1)
    def _():
        terms = [
            fold(dot(rows_of(mid_transfer[c]), lanes_of(up[c * rank : (c + 1) * rank, :])))
            for c in range(mids)
        ]
        while len(terms) > 1:
            terms = [sum(terms[i : i + 2]) for i in range(0, len(terms), 2)]
        up[mids * rank : (mids + 1) * rank, :] = terms[0]
        per_cluster, per_pair = sizes
        for d, message in enumerate(messages):
            for side in range(2):
                receiver = (group_at[0] ^ d) * per_cluster + (lane_at[0] ^ side)
                for j in range(per_pair):
                    block = jnp.clip(slots[receiver * per_pair + j], 0, mids - 1)
                    source = pl.ds(pl.multiple_of(block * rank, rank), rank)
                    message[(1 - side) * (per_pair + 1) + j] = up[source, :]
            message[per_pair] = terms[0]


def up_sweep(
    sizes, groups, group_at, lane_at, charges, leaf_size, basis, transfer, mid_transfer, leaf_parent, slots
):
    leaves, rank, points = basis.shape
    ports = charges.shape[1]
    mids = mid_transfer.shape[0]
    group = 8
    send_mid = slots.reshape(-1, min(slots.shape[0], ports))
    up_rows = (mids + 1) * rank + -(-send_mid.shape[0] // 8) * 8
    message = (2 * sizes[1] + 1, rank, ports)
    return pl.pallas_call(
        functools.partial(up_kernel, sizes),
        grid_spec=pltpu.PrefetchScalarGridSpec(
            num_scalar_prefetch=5,
            grid=(leaves // group,),
            in_specs=[
                first(group * points, ports),
                first(group, rank, points),
                first(group, rank, rank),
                whole(mid_transfer.shape),
                whole(send_mid.shape),
            ],
            out_specs=[first(group, rank, ports), whole((up_rows, ports))] + [whole(message)] * groups,
        ),
        out_shape=[
            jax.ShapeDtypeStruct((leaves, rank, ports), jnp.float32),
            jax.ShapeDtypeStruct((up_rows, ports), jnp.float32),
        ]
        + [jax.ShapeDtypeStruct(message, jnp.float32)] * groups,
        compiler_params=params(60 * MIB),
        cost_estimate=cost(10**9, 10**7),
        name="up_sweep",
    )(
        leaf_size, leaf_parent, slots, group_at, lane_at, charges, basis, transfer, mid_transfer, send_mid
    )


def spread_kernel(send, coef, out):
    leaves = coef.shape[0]

    @pl.loop(0, out.shape[0], unroll=8)
    def _(slot):
        out[slot] = coef[jnp.minimum(send[slot], leaves - 1)]


def spread(send_leaf, coef):
    vmem = pl.BlockSpec(memory_space=pltpu.VMEM)
    shape = (send_leaf.shape[0],) + coef.shape[1:]
    return pl.pallas_call(
        spread_kernel,
        in_specs=[pl.BlockSpec(memory_space=pltpu.SMEM), vmem],
        out_specs=vmem,
        out_shape=jax.ShapeDtypeStruct(shape, jnp.float32),
        compiler_params=params(60 * MIB),
        cost_estimate=cost(0, 4 * 10**6),
        name="spread",
    )(send_leaf, coef)


def select_kernel(sizes, group_at, lane_at, *refs):
    lines, per_cluster, up_rows, mids, rank, per_pair, groups = sizes
    received, messages = refs[:lines], refs[lines : lines + groups]
    payloads, tables, sem, table_sem = refs[lines + groups :]
    group, lane = group_at[0], lane_at[0]
    table_rows = up_rows - (mids + 1) * rank
    ports = payloads.shape[2]
    copies = []
    for line, ref in enumerate(received):
        table = ref.at[pl.ds((mids + 1) * rank, table_rows), :]
        copies.append(pltpu.make_async_copy(table, tables.at[line], table_sem.at[line]))
        copies.append(pltpu.make_async_copy(ref, payloads.at[line], sem.at[line]))
    for copy in copies:
        copy.start()
    for copy in copies:
        copy.wait()
    for d, message in enumerate(messages):
        for side in range(2):
            receiver = (group ^ d) * per_cluster + (lane ^ side)

            @pl.loop(0, lines, unroll=min(lines, 4))
            def _(line):
                for j in range(per_pair):
                    entry = receiver * per_pair + j
                    listed = tables[line, lax.div(entry, ports), lax.rem(entry, ports)]
                    block = jnp.clip(listed.astype(jnp.int32), 0, mids - 1)
                    target = (1 - side) * (per_pair + 1) * lines + line * per_pair + j
                    message[target] = payloads[line, pl.ds(pl.multiple_of(block * rank, 8), rank), :]

        for line in range(lines):
            message[lines * per_pair + line] = payloads[line, mids * rank : (mids + 1) * rank, :]


def select(sizes, group_at, lane_at, received):
    lines, per_cluster, up_rows, mids, rank, per_pair, groups = sizes
    ports = received[0].shape[1]
    table_rows = up_rows - (mids + 1) * rank
    payloads = (lines, up_rows, ports)
    shape = jax.ShapeDtypeStruct((lines * (2 * per_pair + 1), rank, ports), jnp.float32)
    return pl.pallas_call(
        functools.partial(select_kernel, sizes),
        in_specs=[pl.BlockSpec(memory_space=pltpu.SMEM)] * 2
        + [pl.BlockSpec(memory_space=pl.ANY)] * len(received),
        out_specs=[pl.BlockSpec(memory_space=pltpu.VMEM)] * groups,
        out_shape=[shape] * groups,
        scratch_shapes=[
            pltpu.VMEM(payloads, jnp.float32),
            pltpu.SMEM((lines, table_rows, ports), jnp.float32),
            pltpu.SemaphoreType.DMA((lines,)),
            pltpu.SemaphoreType.DMA((lines,)),
        ],
        compiler_params=params(60 * MIB),
        cost_estimate=cost(0, 4 * 10**6),
        name="select",
    )(group_at, lane_at, *received)


def prepare_kernel(after, coupling, basis, transfer, mid_coupling, mid_transfer, *out):
    wide, basis_t, transfer_t, mid_wide, mid_transfer_t = out
    for g in range(coupling.shape[0]):
        wide[g] = rows_of(coupling[g])
        basis_t[g] = rows_of(basis[g]).T
        transfer_t[g] = rows_of(transfer[g]).T
    for g in range(mid_coupling.shape[0]):
        mid_wide[g] = rows_of(mid_coupling[g])
        mid_transfer_t[g] = rows_of(mid_transfer[g]).T


def prepare(after, coupling, basis, transfer, mid_coupling, mid_transfer):
    leaves, rank, width = coupling.shape
    points = basis.shape[2]
    mids, _, mid_width = mid_coupling.shape
    steps = mids
    group = leaves // steps
    shapes = [
        (leaves, 2 * rank, width),
        (leaves, points, 2 * rank),
        (leaves, rank, 2 * rank),
        (mids, 2 * rank, mid_width),
        (mids, rank, 2 * rank),
    ]
    return pl.pallas_call(
        prepare_kernel,
        grid=(steps,),
        in_specs=[
            pl.BlockSpec(memory_space=pl.ANY),
            first(group, rank, width),
            first(group, rank, points),
            first(group, rank, rank),
            first(1, rank, mid_width),
            first(1, rank, rank),
        ],
        out_specs=[first(s[0] // steps, *s[1:]) for s in shapes],
        out_shape=[jax.ShapeDtypeStruct(s, jnp.bfloat16) for s in shapes],
        compiler_params=params(60 * MIB),
        cost_estimate=cost(0, 3 * 10**7),
        name="prepare",
    )(after, coupling, basis, transfer, mid_coupling, mid_transfer)


def mid_kernel(sizes, parent, pair, position, tops, *refs):
    bounds, per_pair, groups = sizes
    lines, count = bounds[-1], (len(bounds) - 1) * groups
    messages = refs[: 2 * count]
    mid_wide, mid_transfer, transfer, top_coupling, out = refs[2 * count : 2 * count + 5]
    scratch = refs[2 * count + 5 :]
    held_messages, scratch = scratch[: 2 * count], scratch[2 * count :]
    (
        mid_wide_held, mid_transfer_held, transfer_held, top_held, parts, top_parts, near_top, down,
        message_sem, mid_sem, small_sem,
    ) = scratch
    mids, leaves = mid_wide.shape[0], transfer.shape[0]
    slots, top_count = parts.shape[0] - 1, top_parts.shape[0] - 1

    def fetch_message(index):
        held = held_messages[index]
        start = 0 if index >= count else messages[index].shape[0] - held.shape[0]
        source = messages[index].at[pl.ds(start, held.shape[0])]
        return pltpu.make_async_copy(source, held, message_sem.at[index])

    def fetch_mid(c):
        return pltpu.make_async_copy(mid_wide.at[c], mid_wide_held.at[c], mid_sem.at[c])

    small = (
        pltpu.make_async_copy(top_coupling.at[position[0]], top_held, small_sem.at[0]),
        pltpu.make_async_copy(mid_transfer, mid_transfer_held, small_sem.at[1]),
        pltpu.make_async_copy(transfer, transfer_held, small_sem.at[2]),
    )
    for index in range(2 * count):
        fetch_message(index).start()
    for copy in small:
        copy.start()
    for c in range(mids):
        fetch_mid(c).start()

    parts[slots] = jnp.zeros(parts.shape[1:], jnp.bfloat16)
    top_parts[top_count] = jnp.zeros(top_parts.shape[1:], jnp.bfloat16)
    for index in range(2 * count):
        side, message = divmod(index, count)
        batch, d = divmod(message, groups)
        lines_held = bounds[batch + 1] - bounds[batch]
        piece = lines_held * per_pair
        base = (d * 2 + side) * lines + bounds[batch]
        held = held_messages[index]
        first_slot, first_top = (lines_held, 0) if side == 0 else (0, piece)
        fetch_message(index).wait()

        @pl.loop(0, piece, unroll=min(piece, 4))
        def _(slot):
            parts[base * per_pair + slot] = lanes_of(held[first_slot + slot])

        for line in range(lines_held):
            top_parts[base + line] = lanes_of(held[first_top + line])

    for copy in small:
        copy.wait()
    stacked = jnp.concatenate([top_parts[tops[k]] for k in range(tops.shape[0])], axis=0)
    near_top[...] = fold(dot(rows_of(top_held[...]), stacked))
    for c in range(mids):
        fetch_mid(c).wait()

    @pl.loop(0, mids, step=4)
    def _(start):
        near = []
        for g in range(4):
            c = start + g
            stacked = jnp.concatenate([parts[pair[c, k]] for k in range(pair.shape[1])], axis=0)
            value = fold(dot(mid_wide_held[c], stacked))
            near.append(value + deep_dot(mid_transfer_held[c], near_top[...]))
        for g in range(4):
            down[start + g] = near[g]

    @pl.loop(0, leaves, step=8)
    def _(start):
        terms = [deep_dot(transfer_held[start + g], down[parent[start + g]]) for g in range(8)]
        for g in range(8):
            out[start + g] = terms[g]


def mid_level(
    bounds, per_pair, groups, parent, pair, position, tops, near_side, far_side, mid_wide, mid_transfer,
    transfer, top_coupling
):
    mids = mid_wide.shape[0]
    leaves = transfer.shape[0]
    rank, ports = near_side[0].shape[1:]
    owners = 2 * bounds[-1] * groups
    held = []
    for message in range(len(near_side)):
        batch = message // groups
        held.append((bounds[batch + 1] - bounds[batch]) * (per_pair + 1))
    full, half = jnp.float32, jnp.bfloat16
    scratch = [((h, rank, ports), full) for h in held + held] + [
        (mid_wide.shape, half),
        (mid_transfer.shape, half),
        (transfer.shape, half),
        (top_coupling.shape[1:], full),
        ((owners * per_pair + 1, rank, 2 * ports), half),
        ((owners + 1, rank, 2 * ports), half),
        ((rank, ports), full),
        ((mids, rank, ports), full),
    ]
    semaphores = [2 * len(near_side), mids, 3]
    scalars = (parent, pair, position, tops)
    arrays = (*near_side, *far_side, mid_wide, mid_transfer, transfer, top_coupling)
    return pl.pallas_call(
        functools.partial(mid_kernel, (bounds, per_pair, groups)),
        in_specs=[pl.BlockSpec(memory_space=pltpu.SMEM)] * len(scalars)
        + [pl.BlockSpec(memory_space=pl.ANY)] * len(arrays),
        out_specs=pl.BlockSpec(memory_space=pltpu.VMEM),
        out_shape=jax.ShapeDtypeStruct((leaves, rank, ports), full),
        scratch_shapes=[pltpu.VMEM(shape, dtype) for shape, dtype in scratch]
        + [pltpu.SemaphoreType.DMA((n,)) for n in semaphores],
        compiler_params=params(60 * MIB),
        cost_estimate=cost(2 * 10**9, 10**7),
        name="mid_level",
    )(*scalars, *arrays)


def leaf_kernel(
    sizes, size, pair, arrived, wide, basis, back, out,
    arrived_held, wide_held, basis_held, back_held, parts, out_held,
    arrived_sem, wide_sem, basis_sem, back_sem, out_sem,
):
    chunk, group = sizes
    leaves, points, _ = basis.shape
    slots, _, ports = arrived.shape

    def fetch_arrived(index):
        source = arrived.at[pl.ds(index * chunk, chunk)]
        return pltpu.make_async_copy(source, arrived_held.at[index % 2], arrived_sem.at[index % 2])

    def fetch_leaves(index):
        some = pl.ds(index * group, group)
        return (
            pltpu.make_async_copy(wide.at[some], wide_held.at[some], wide_sem.at[index]),
            pltpu.make_async_copy(basis.at[some], basis_held.at[some], basis_sem.at[index]),
        )

    def send(index):
        rows = group * points
        target = out.at[pl.ds(index * rows, rows), :]
        return pltpu.make_async_copy(out_held.at[index % 2], target, out_sem.at[index % 2])

    fetch_back = pltpu.make_async_copy(back, back_held, back_sem)
    chunks = slots // chunk
    for index in range(min(2, chunks)):
        fetch_arrived(index).start()
    for index in range(leaves // group):
        for copy in fetch_leaves(index):
            copy.start()
        if index == 0:
            fetch_back.start()

    parts[slots] = jnp.zeros(parts.shape[1:], jnp.bfloat16)
    for index in range(chunks):
        fetch_arrived(index).wait()

        @pl.loop(0, chunk, unroll=8)
        def _(slot):
            parts[index * chunk + slot] = lanes_of(arrived_held[index % 2, slot])

        if index + 2 < chunks:
            fetch_arrived(index + 2).start()

    point = lax.broadcasted_iota(jnp.int32, (points, ports), 0)
    fetch_back.wait()
    for index in range(leaves // group):
        for copy in fetch_leaves(index):
            copy.wait()
        values = []
        for g in range(group):
            leaf = index * group + g
            stacked = jnp.concatenate([parts[pair[leaf, k]] for k in range(pair.shape[1])], axis=0)
            values.append(fold(dot(wide_held[leaf], stacked)) + back_held[leaf])
        if index >= 2:
            send(index - 2).wait()
        for g in range(group):
            far = deep_dot(basis_held[index * group + g], values[g])
            far = jnp.where(point < size[index * group + g], far, 0.0)
            out_held[index % 2, g * points : (g + 1) * points, :] = far
        send(index).start()
    for index in range(max(0, leaves // group - 2), leaves // group):
        send(index).wait()


def leaf_level(size, pair, arrived, wide, basis, back):
    leaves, points, _ = basis.shape
    slots, rank, ports = arrived.shape
    group, chunk = 4, min(slots, 32)
    full, half = jnp.float32, jnp.bfloat16
    scratch = [
        ((2, chunk, rank, ports), full),
        (wide.shape, half),
        (basis.shape, half),
        (back.shape, full),
        ((slots + 1, rank, 2 * ports), half),
        ((2, group * points, ports), full),
    ]
    semaphores = [(2,), (leaves // group,), (leaves // group,), (), (2,)]
    return pl.pallas_call(
        functools.partial(leaf_kernel, (chunk, group)),
        in_specs=[pl.BlockSpec(memory_space=pltpu.SMEM)] * 2 + [pl.BlockSpec(memory_space=pl.ANY)] * 4,
        out_specs=pl.BlockSpec(memory_space=pl.ANY),
        out_shape=jax.ShapeDtypeStruct((leaves * points, ports), full),
        scratch_shapes=[pltpu.VMEM(shape, dtype) for shape, dtype in scratch]
        + [pltpu.SemaphoreType.DMA(n) for n in semaphores],
        compiler_params=params(60 * MIB),
        cost_estimate=cost(4 * 10**9, 2 * 10**7),
        name="leaf_level",
    )(size, pair, arrived, wide, basis, back)


def body(
    charges, leaf_size, leaf_basis, leaf_transfer, mid_transfer, leaf_parent, send_leaf, pair_leaf,
    leaf_coupling, send_mid, pair_mid, mid_coupling, top_pairs, top_coupling,
):
    rank = leaf_basis.shape[1]
    ports = charges.shape[1]
    mids = mid_transfer.shape[0]
    slots = send_mid.shape[0]
    groups, per_cluster = lax.axis_size("group"), lax.axis_size("cluster")
    owners = groups * per_cluster
    lines = per_cluster // 2
    per_pair = slots // owners
    group, lane = lax.axis_index("group"), lax.axis_index("cluster")

    group_at, lane_at = group.astype(jnp.int32)[None], lane.astype(jnp.int32)[None]
    coef, lifted, *own_messages = up_sweep(
        (per_cluster, per_pair), groups, group_at, lane_at, charges, leaf_size, leaf_basis,
        leaf_transfer, mid_transfer, leaf_parent, send_mid,
    )
    up_rows = lifted.shape[0]
    outgoing, own_messages = lax.optimization_barrier((spread(send_leaf, coef), own_messages))

    received = [lifted]
    for d in range(1, lines):
        received.append(
            lax.ppermute(lifted, "cluster", [(c, c ^ (2 * d)) for c in range(per_cluster)])
        )
    wide, basis_t, transfer_t, mid_wide, mid_transfer_t = prepare(
        lifted, leaf_coupling, leaf_basis, leaf_transfer, mid_coupling, mid_transfer
    )

    def spot_of(sender):
        at_group, at_lane = sender // per_cluster, sender % per_cluster
        line = (at_lane // 2) ^ (lane // 2)
        return ((at_group ^ group) * 2 + ((at_lane ^ lane) & 1)) * lines + line

    spot = spot_of(pair_mid // per_pair) * per_pair + pair_mid % per_pair
    spot = jnp.where((pair_mid >= 0) & (pair_mid < slots), spot, slots)
    wanted = lax.dynamic_slice_in_dim(top_pairs, lane, 1, 0)[0]
    tops = jnp.where((wanted >= 0) & (wanted < owners), spot_of(wanted), owners)

    bounds = (0, 1, 2, lines)
    swap = [(c, c ^ 1) for c in range(per_cluster)]
    near_side, far_side = [], []
    for low, high in zip(bounds[:-1], bounds[1:]):
        sizes = (high - low, per_cluster, up_rows, mids, rank, per_pair, groups)
        messages = own_messages if low == 0 else select(sizes, group_at, lane_at, received[low:high])
        moved = [messages[0]]
        for d in range(1, groups):
            moved.append(lax.ppermute(messages[d], "group", [(g, g ^ d) for g in range(groups)]))
        if high < lines:
            near_side += moved
        if low == 1:
            outgoing, near_side, received[2:] = lax.optimization_barrier(
                (outgoing, near_side, received[2:])
            )
            arrived = lax.all_to_all(outgoing, AXES, split_axis=0, concat_axis=0, tiled=True)
            far_side = [lax.ppermute(m, "cluster", swap) for m in near_side]
        if high == lines:
            ready = (moved, far_side, mid_wide, spot, tops, pair_leaf)
            moved, far_side, mid_wide, spot, tops, pair_leaf = lax.optimization_barrier(ready)
            near_side += moved
            far_side += [lax.ppermute(m, "cluster", swap) for m in moved]

    back = mid_level(
        bounds, per_pair, groups, leaf_parent, spot, lane_at, tops, near_side, far_side, mid_wide,
        mid_transfer_t, transfer_t, top_coupling,
    )
    return leaf_level(leaf_size, pair_leaf, arrived, wide, basis_t, back)


def solution(mesh):
    both = P(AXES)
    in_specs = (
        P(AXES, None),
        both,
        P(AXES, None, None),
        P(AXES, None, None),
        P(AXES, None, None),
        both,
        both,
        P(AXES, None),
        P(AXES, None, None),
        both,
        P(AXES, None),
        P(AXES, None, None),
        P("group", None),
        P("group", None, None),
    )
    return jax.shard_map(
        body, mesh=mesh, in_specs=in_specs, out_specs=P(AXES, None), check_vma=False
    )
```

```python
import functools
import math

import jax
import jax.numpy as jnp
from jax import lax
from jax.experimental import pallas as pl
from jax.experimental.pallas import tpu as pltpu
from jax.sharding import PartitionSpec as P

AXES = ("group", "cluster")
MIB = 1024 * 1024


def params(size):
    return pltpu.CompilerParams(vmem_limit_bytes=size)


def room(*blocks):
    size = sum(buffers * itemsize * math.prod(shape) for buffers, itemsize, shape in blocks)
    return size + size // 8 + 4 * MIB


def cost(flops, size):
    return pl.CostEstimate(flops=flops, bytes_accessed=size, transcendentals=0)


def whole(shape):
    return pl.BlockSpec(shape, lambda i, *_: (0,) * len(shape), pipeline_mode=pl.Buffered(1))


def first(group, *rest):
    return pl.BlockSpec((group,) + rest, lambda i, *_: (i,) + (0,) * len(rest))


def split(x):
    high = x.astype(jnp.bfloat16)
    low = (x - high.astype(jnp.float32)).astype(jnp.bfloat16)
    return high, low


def rows_of(x):
    return jnp.concatenate(split(x), axis=0)


def lanes_of(x):
    return jnp.concatenate(split(x), axis=1)


def dot(a, b):
    return lax.dot_general(a, b, (((1,), (0,)), ((), ())), preferred_element_type=jnp.float32)


def fold(product):
    m, n = product.shape[0] // 2, product.shape[1] // 2
    return product[:m, :n] + (product[:m, n:] + product[m:, :n] + product[m:, n:])


def deep_dot(a, b):
    high, low = split(b)
    return dot(jnp.concatenate([a, a], axis=1), jnp.concatenate([high, high, low, low], axis=0))


def up_kernel(
    sizes, size, parent, slots, group_at, lane_at, charges, basis, transfer, mid_transfer, send, coef, up,
    *messages
):
    step = pl.program_id(0)
    group, rank, points = basis.shape
    mids = mid_transfer.shape[0]
    ports = up.shape[1]

    @pl.when(step == 0)
    def _():
        up[: mids * rank, :] = jnp.zeros((mids * rank, ports), jnp.float32)
        up[(mids + 1) * rank :, :] = jnp.zeros((up.shape[0] - (mids + 1) * rank, ports), jnp.float32)
        for row in range(send.shape[0]):
            spot = (mids + 1) * rank + row
            up[spot : spot + 1, : send.shape[1]] = send[row : row + 1, :].astype(jnp.float32)

    point = lax.broadcasted_iota(jnp.int32, (points, ports), 0)
    values = []
    for g in range(group):
        block = jnp.where(
            point < size[step * group + g], charges[g * points : (g + 1) * points, :], 0.0
        )
        values.append(fold(dot(rows_of(basis[g]), lanes_of(block))))
    for g in range(group):
        coef[g] = values[g]
    moved = [fold(dot(rows_of(transfer[g]), lanes_of(values[g]))) for g in range(group)]
    for g in range(group):
        where = pl.ds(pl.multiple_of(parent[step * group + g] * rank, rank), rank)
        up[where, :] += moved[g]

    @pl.when(step == pl.num_programs(0) - 1)
    def _():
        terms = [
            fold(dot(rows_of(mid_transfer[c]), lanes_of(up[c * rank : (c + 1) * rank, :])))
            for c in range(mids)
        ]
        while len(terms) > 1:
            terms = [sum(terms[i : i + 2]) for i in range(0, len(terms), 2)]
        up[mids * rank : (mids + 1) * rank, :] = terms[0]
        per_cluster, per_pair = sizes
        for d, message in enumerate(messages):
            for side in range(2):
                receiver = (group_at[0] ^ d) * per_cluster + (lane_at[0] ^ side)
                for j in range(per_pair):
                    block = jnp.clip(slots[receiver * per_pair + j], 0, mids - 1)
                    source = pl.ds(pl.multiple_of(block * rank, rank), rank)
                    message[(1 - side) * (per_pair + 1) + j] = up[source, :]
            message[per_pair] = terms[0]


def up_sweep(
    sizes, groups, group_at, lane_at, charges, leaf_size, basis, transfer, mid_transfer, leaf_parent, slots
):
    leaves, rank, points = basis.shape
    ports = charges.shape[1]
    mids = mid_transfer.shape[0]
    group = 8
    send_mid = slots.reshape(-1, min(slots.shape[0], ports))
    up_rows = (mids + 1) * rank + -(-send_mid.shape[0] // 8) * 8
    message = (2 * sizes[1] + 1, rank, ports)
    return pl.pallas_call(
        functools.partial(up_kernel, sizes),
        grid_spec=pltpu.PrefetchScalarGridSpec(
            num_scalar_prefetch=5,
            grid=(leaves // group,),
            in_specs=[
                first(group * points, ports),
                first(group, rank, points),
                first(group, rank, rank),
                whole(mid_transfer.shape),
                whole(send_mid.shape),
            ],
            out_specs=[first(group, rank, ports), whole((up_rows, ports))] + [whole(message)] * groups,
        ),
        out_shape=[
            jax.ShapeDtypeStruct((leaves, rank, ports), jnp.float32),
            jax.ShapeDtypeStruct((up_rows, ports), jnp.float32),
        ]
        + [jax.ShapeDtypeStruct(message, jnp.float32)] * groups,
        compiler_params=params(60 * MIB),
        cost_estimate=cost(10**9, 10**7),
        name="up_sweep",
    )(
        leaf_size, leaf_parent, slots, group_at, lane_at, charges, basis, transfer, mid_transfer, send_mid
    )


def spread_kernel(send, coef, out):
    leaves = coef.shape[0]

    @pl.loop(0, out.shape[0], unroll=8)
    def _(slot):
        out[slot] = coef[jnp.minimum(send[slot], leaves - 1)]


def spread(send_leaf, coef):
    vmem = pl.BlockSpec(memory_space=pltpu.VMEM)
    shape = (send_leaf.shape[0],) + coef.shape[1:]
    return pl.pallas_call(
        spread_kernel,
        in_specs=[pl.BlockSpec(memory_space=pltpu.SMEM), vmem],
        out_specs=vmem,
        out_shape=jax.ShapeDtypeStruct(shape, jnp.float32),
        compiler_params=params(room((1, 4, coef.shape), (1, 4, shape))),
        cost_estimate=cost(0, 4 * 10**6),
        name="spread",
    )(send_leaf, coef)


def select_kernel(sizes, group_at, lane_at, *refs):
    lines, per_cluster, up_rows, mids, rank, per_pair, groups = sizes
    received, messages = refs[:lines], refs[lines : lines + groups]
    payloads, tables, sem, table_sem = refs[lines + groups :]
    group, lane = group_at[0], lane_at[0]
    table_rows = up_rows - (mids + 1) * rank
    ports = payloads.shape[2]
    copies = []
    for line, ref in enumerate(received):
        table = ref.at[pl.ds((mids + 1) * rank, table_rows), :]
        copies.append(pltpu.make_async_copy(table, tables.at[line], table_sem.at[line]))
        copies.append(pltpu.make_async_copy(ref, payloads.at[line], sem.at[line]))
    for copy in copies:
        copy.start()
    for copy in copies:
        copy.wait()
    for d, message in enumerate(messages):
        for side in range(2):
            receiver = (group ^ d) * per_cluster + (lane ^ side)

            @pl.loop(0, lines, unroll=min(lines, 4))
            def _(line):
                for j in range(per_pair):
                    entry = receiver * per_pair + j
                    listed = tables[line, lax.div(entry, ports), lax.rem(entry, ports)]
                    block = jnp.clip(listed.astype(jnp.int32), 0, mids - 1)
                    target = (1 - side) * (per_pair + 1) * lines + line * per_pair + j
                    message[target] = payloads[line, pl.ds(pl.multiple_of(block * rank, 8), rank), :]

        for line in range(lines):
            message[lines * per_pair + line] = payloads[line, mids * rank : (mids + 1) * rank, :]


def select(sizes, group_at, lane_at, received):
    lines, per_cluster, up_rows, mids, rank, per_pair, groups = sizes
    ports = received[0].shape[1]
    table_rows = up_rows - (mids + 1) * rank
    payloads = (lines, up_rows, ports)
    shape = jax.ShapeDtypeStruct((lines * (2 * per_pair + 1), rank, ports), jnp.float32)
    return pl.pallas_call(
        functools.partial(select_kernel, sizes),
        in_specs=[pl.BlockSpec(memory_space=pltpu.SMEM)] * 2
        + [pl.BlockSpec(memory_space=pl.ANY)] * len(received),
        out_specs=[pl.BlockSpec(memory_space=pltpu.VMEM)] * groups,
        out_shape=[shape] * groups,
        scratch_shapes=[
            pltpu.VMEM(payloads, jnp.float32),
            pltpu.SMEM((lines, table_rows, ports), jnp.float32),
            pltpu.SemaphoreType.DMA((lines,)),
            pltpu.SemaphoreType.DMA((lines,)),
        ],
        compiler_params=params(room((1, 4, payloads), (groups, 4, shape.shape))),
        cost_estimate=cost(0, 4 * 10**6),
        name="select",
    )(group_at, lane_at, *received)


def prepare_kernel(after, coupling, basis, transfer, mid_coupling, mid_transfer, *out):
    wide, basis_t, transfer_t, mid_wide, mid_transfer_t = out
    for g in range(coupling.shape[0]):
        wide[g] = rows_of(coupling[g])
        basis_t[g] = rows_of(basis[g]).T
        transfer_t[g] = rows_of(transfer[g]).T
    for g in range(mid_coupling.shape[0]):
        mid_wide[g] = rows_of(mid_coupling[g])
        mid_transfer_t[g] = rows_of(mid_transfer[g]).T


def prepare(after, coupling, basis, transfer, mid_coupling, mid_transfer):
    leaves, rank, width = coupling.shape
    points = basis.shape[2]
    mids, _, mid_width = mid_coupling.shape
    steps = mids
    group = leaves // steps
    shapes = [
        (leaves, 2 * rank, width),
        (leaves, points, 2 * rank),
        (leaves, rank, 2 * rank),
        (mids, 2 * rank, mid_width),
        (mids, rank, 2 * rank),
    ]
    return pl.pallas_call(
        prepare_kernel,
        grid=(steps,),
        in_specs=[
            pl.BlockSpec(memory_space=pl.ANY),
            first(group, rank, width),
            first(group, rank, points),
            first(group, rank, rank),
            first(1, rank, mid_width),
            first(1, rank, rank),
        ],
        out_specs=[first(s[0] // steps, *s[1:]) for s in shapes],
        out_shape=[pltpu.VMEM(s, jnp.bfloat16) for s in shapes],
        compiler_params=params(20 * MIB),
        cost_estimate=cost(0, 3 * 10**7),
        name="prepare",
    )(after, coupling, basis, transfer, mid_coupling, mid_transfer)


def mid_kernel(sizes, parent, pair, position, tops, *refs):
    bounds, per_pair, groups = sizes
    lines, count = bounds[-1], (len(bounds) - 1) * groups
    messages = refs[: 2 * count]
    mid_wide, mid_transfer, transfer, top_coupling, out = refs[2 * count : 2 * count + 5]
    scratch = refs[2 * count + 5 :]
    held_messages, scratch = scratch[: 2 * count], scratch[2 * count :]
    (
        mid_wide_held, mid_transfer_held, transfer_held, top_held, parts, top_parts, near_top, down,
        message_sem, mid_sem, small_sem,
    ) = scratch
    mids, leaves = mid_wide.shape[0], transfer.shape[0]
    slots, top_count = parts.shape[0] - 1, top_parts.shape[0] - 1

    def fetch_message(index):
        held = held_messages[index]
        start = 0 if index >= count else messages[index].shape[0] - held.shape[0]
        source = messages[index].at[pl.ds(start, held.shape[0])]
        return pltpu.make_async_copy(source, held, message_sem.at[index])

    def fetch_mid(c):
        return pltpu.make_async_copy(mid_wide.at[c], mid_wide_held.at[c], mid_sem.at[c])

    small = (
        pltpu.make_async_copy(top_coupling.at[position[0]], top_held, small_sem.at[0]),
        pltpu.make_async_copy(mid_transfer, mid_transfer_held, small_sem.at[1]),
        pltpu.make_async_copy(transfer, transfer_held, small_sem.at[2]),
    )
    for index in range(2 * count):
        fetch_message(index).start()
    for copy in small:
        copy.start()
    for c in range(mids):
        fetch_mid(c).start()

    parts[slots] = jnp.zeros(parts.shape[1:], jnp.bfloat16)
    top_parts[top_count] = jnp.zeros(top_parts.shape[1:], jnp.bfloat16)
    for index in range(2 * count):
        side, message = divmod(index, count)
        batch, d = divmod(message, groups)
        lines_held = bounds[batch + 1] - bounds[batch]
        piece = lines_held * per_pair
        base = (d * 2 + side) * lines + bounds[batch]
        held = held_messages[index]
        first_slot, first_top = (lines_held, 0) if side == 0 else (0, piece)
        fetch_message(index).wait()

        @pl.loop(0, piece, unroll=min(piece, 4))
        def _(slot):
            parts[base * per_pair + slot] = lanes_of(held[first_slot + slot])

        for line in range(lines_held):
            top_parts[base + line] = lanes_of(held[first_top + line])

    for copy in small:
        copy.wait()
    stacked = jnp.concatenate([top_parts[tops[k]] for k in range(tops.shape[0])], axis=0)
    near_top[...] = fold(dot(rows_of(top_held[...]), stacked))
    for c in range(mids):
        fetch_mid(c).wait()

    @pl.loop(0, mids, step=4)
    def _(start):
        near = []
        for g in range(4):
            c = start + g
            stacked = jnp.concatenate([parts[pair[c, k]] for k in range(pair.shape[1])], axis=0)
            value = fold(dot(mid_wide_held[c], stacked))
            near.append(value + deep_dot(mid_transfer_held[c], near_top[...]))
        for g in range(4):
            down[start + g] = near[g]

    @pl.loop(0, leaves, step=8)
    def _(start):
        terms = [deep_dot(transfer_held[start + g], down[parent[start + g]]) for g in range(8)]
        for g in range(8):
            out[start + g] = terms[g]


def mid_level(
    bounds, per_pair, groups, parent, pair, position, tops, near_side, far_side, mid_wide, mid_transfer,
    transfer, top_coupling
):
    mids = mid_wide.shape[0]
    leaves = transfer.shape[0]
    rank, ports = near_side[0].shape[1:]
    owners = 2 * bounds[-1] * groups
    held = []
    for message in range(len(near_side)):
        batch = message // groups
        held.append((bounds[batch + 1] - bounds[batch]) * (per_pair + 1))
    full, half = jnp.float32, jnp.bfloat16
    scratch = [((h, rank, ports), full) for h in held + held] + [
        (mid_wide.shape, half),
        (mid_transfer.shape, half),
        (transfer.shape, half),
        (top_coupling.shape[1:], full),
        ((owners * per_pair + 1, rank, 2 * ports), half),
        ((owners + 1, rank, 2 * ports), half),
        ((rank, ports), full),
        ((mids, rank, ports), full),
    ]
    semaphores = [2 * len(near_side), mids, 3]
    sizes = [(1, jnp.dtype(dtype).itemsize, shape) for shape, dtype in scratch]
    size = room((1, 4, (leaves, rank, ports)), *sizes)
    scalars = (parent, pair, position, tops)
    arrays = (*near_side, *far_side, mid_wide, mid_transfer, transfer, top_coupling)
    return pl.pallas_call(
        functools.partial(mid_kernel, (bounds, per_pair, groups)),
        in_specs=[pl.BlockSpec(memory_space=pltpu.SMEM)] * len(scalars)
        + [pl.BlockSpec(memory_space=pl.ANY)] * len(arrays),
        out_specs=pl.BlockSpec(memory_space=pltpu.VMEM),
        out_shape=jax.ShapeDtypeStruct((leaves, rank, ports), full),
        scratch_shapes=[pltpu.VMEM(shape, dtype) for shape, dtype in scratch]
        + [pltpu.SemaphoreType.DMA((n,)) for n in semaphores],
        compiler_params=params(size),
        cost_estimate=cost(2 * 10**9, 10**7),
        name="mid_level",
    )(*scalars, *arrays)


def leaf_kernel(size, pair, arrived, coupling, basis, back, out, parts):
    step = pl.program_id(0)
    group, rank, _ = back.shape
    points = basis.shape[1]
    slots = arrived.shape[0]

    @pl.when(step == 0)
    def _():
        @pl.loop(0, slots, unroll=8)
        def _(slot):
            parts[slot] = lanes_of(arrived[slot])

        parts[slots] = jnp.zeros(parts.shape[1:], jnp.bfloat16)

    point = lax.broadcasted_iota(jnp.int32, (points, out.shape[1]), 0)
    values = []
    for g in range(group):
        leaf = step * group + g
        stacked = jnp.concatenate([parts[pair[leaf, k]] for k in range(coupling.shape[2] // rank)], axis=0)
        values.append(fold(dot(coupling[g], stacked)) + back[g])
    for g in range(group):
        far = deep_dot(basis[g], values[g])
        out[g * points : (g + 1) * points, :] = jnp.where(point < size[step * group + g], far, 0.0)


def leaf_level(leaf_size, pair_leaf, arrived, coupling, basis, back):
    leaves, _, width = coupling.shape
    points = basis.shape[1]
    slots, rank, ports = arrived.shape
    group = 8
    parts = (slots + 1, rank, 2 * ports)
    size = room(
        (1, 4, arrived.shape),
        (1, 2, parts),
        (2, 2, (group, 2 * rank, width)),
        (2, 2, (group, points, 2 * rank)),
        (2, 4, (group, rank, ports)),
        (2, 4, (group * points, ports)),
    )
    return pl.pallas_call(
        leaf_kernel,
        grid_spec=pltpu.PrefetchScalarGridSpec(
            num_scalar_prefetch=2,
            grid=(leaves // group,),
            in_specs=[
                whole(arrived.shape),
                first(group, 2 * rank, width),
                first(group, points, 2 * rank),
                first(group, rank, ports),
            ],
            out_specs=first(group * points, ports),
            scratch_shapes=[pltpu.VMEM(parts, jnp.bfloat16)],
        ),
        out_shape=jax.ShapeDtypeStruct((leaves * points, ports), jnp.float32),
        compiler_params=params(size),
        cost_estimate=cost(4 * 10**9, 2 * 10**7),
        name="leaf_level",
    )(leaf_size, pair_leaf, arrived, coupling, basis, back)


def body(
    charges, leaf_size, leaf_basis, leaf_transfer, mid_transfer, leaf_parent, send_leaf, pair_leaf,
    leaf_coupling, send_mid, pair_mid, mid_coupling, top_pairs, top_coupling,
):
    rank = leaf_basis.shape[1]
    ports = charges.shape[1]
    mids = mid_transfer.shape[0]
    slots = send_mid.shape[0]
    groups, per_cluster = lax.axis_size("group"), lax.axis_size("cluster")
    owners = groups * per_cluster
    lines = per_cluster // 2
    per_pair = slots // owners
    group, lane = lax.axis_index("group"), lax.axis_index("cluster")

    group_at, lane_at = group.astype(jnp.int32)[None], lane.astype(jnp.int32)[None]
    coef, lifted, *own_messages = up_sweep(
        (per_cluster, per_pair), groups, group_at, lane_at, charges, leaf_size, leaf_basis,
        leaf_transfer, mid_transfer, leaf_parent, send_mid,
    )
    up_rows = lifted.shape[0]
    outgoing = spread(send_leaf, coef)

    received = [lifted]
    for d in range(1, lines):
        received.append(
            lax.ppermute(lifted, "cluster", [(c, c ^ (2 * d)) for c in range(per_cluster)])
        )
    wide, basis_t, transfer_t, mid_wide, mid_transfer_t = prepare(
        lifted, leaf_coupling, leaf_basis, leaf_transfer, mid_coupling, mid_transfer
    )

    def spot_of(sender):
        at_group, at_lane = sender // per_cluster, sender % per_cluster
        line = (at_lane // 2) ^ (lane // 2)
        return ((at_group ^ group) * 2 + ((at_lane ^ lane) & 1)) * lines + line

    spot = spot_of(pair_mid // per_pair) * per_pair + pair_mid % per_pair
    spot = jnp.where((pair_mid >= 0) & (pair_mid < slots), spot, slots)
    wanted = lax.dynamic_slice_in_dim(top_pairs, lane, 1, 0)[0]
    tops = jnp.where((wanted >= 0) & (wanted < owners), spot_of(wanted), owners)

    own_messages, received[1] = lax.optimization_barrier((own_messages, received[1]))
    bounds = (0, 1, lines)
    swap = [(c, c ^ 1) for c in range(per_cluster)]
    near_side, far_side = [], []
    for low, high in zip(bounds[:-1], bounds[1:]):
        sizes = (high - low, per_cluster, up_rows, mids, rank, per_pair, groups)
        messages = own_messages if low == 0 else select(sizes, group_at, lane_at, received[low:high])
        moved = [messages[0]]
        for d in range(1, groups):
            moved.append(lax.ppermute(messages[d], "group", [(g, g ^ d) for g in range(groups)]))
        if high < lines:
            near_side += moved
        if low == 0:
            outgoing, near_side, received[1:] = lax.optimization_barrier(
                (outgoing, near_side, received[1:])
            )
            arrived = lax.all_to_all(outgoing, AXES, split_axis=0, concat_axis=0, tiled=True)
            far_side = [lax.ppermute(m, "cluster", swap) for m in near_side]
        if high == lines:
            ready = (moved, far_side, mid_wide, spot, tops, pair_leaf)
            moved, far_side, mid_wide, spot, tops, pair_leaf = lax.optimization_barrier(ready)
            near_side += moved
            far_side += [lax.ppermute(m, "cluster", swap) for m in moved]

    back = mid_level(
        bounds, per_pair, groups, leaf_parent, spot, lane_at, tops, near_side, far_side, mid_wide,
        mid_transfer_t, transfer_t, top_coupling,
    )
    return leaf_level(leaf_size, pair_leaf, arrived, wide, basis_t, back)


def solution(mesh):
    both = P(AXES)
    in_specs = (
        P(AXES, None),
        both,
        P(AXES, None, None),
        P(AXES, None, None),
        P(AXES, None, None),
        both,
        both,
        P(AXES, None),
        P(AXES, None, None),
        both,
        P(AXES, None),
        P(AXES, None, None),
        P("group", None),
        P("group", None, None),
    )
    return jax.shard_map(
        body, mesh=mesh, in_specs=in_specs, out_specs=P(AXES, None), check_vma=False
    )
```

```python
import functools

import jax
import jax.numpy as jnp
from jax import lax
from jax.experimental import pallas as pl
from jax.experimental.pallas import tpu as pltpu
from jax.sharding import PartitionSpec as P

AXES = ("group", "cluster")
MIB = 1024 * 1024


def params(size):
    return pltpu.CompilerParams(vmem_limit_bytes=size)


def cost(flops, size):
    return pl.CostEstimate(flops=flops, bytes_accessed=size, transcendentals=0)


def whole(shape):
    return pl.BlockSpec(shape, lambda i, *_: (0,) * len(shape), pipeline_mode=pl.Buffered(1))


def first(group, *rest):
    return pl.BlockSpec((group,) + rest, lambda i, *_: (i,) + (0,) * len(rest))


def split(x):
    high = x.astype(jnp.bfloat16)
    low = (x - high.astype(jnp.float32)).astype(jnp.bfloat16)
    return high, low


def rows_of(x):
    return jnp.concatenate(split(x), axis=0)


def lanes_of(x):
    return jnp.concatenate(split(x), axis=1)


def dot(a, b):
    return lax.dot_general(a, b, (((1,), (0,)), ((), ())), preferred_element_type=jnp.float32)


def fold(product):
    m, n = product.shape[0] // 2, product.shape[1] // 2
    return product[:m, :n] + (product[:m, n:] + product[m:, :n] + product[m:, n:])


def deep_dot(a, b):
    high, low = split(b)
    return dot(jnp.concatenate([a, a], axis=1), jnp.concatenate([high, high, low, low], axis=0))


def up_kernel(size, parent, charges, basis, transfer, mid_transfer, send, coef, up):
    step = pl.program_id(0)
    group, rank, points = basis.shape
    mids = mid_transfer.shape[0]
    ports = up.shape[1]

    @pl.when(step == 0)
    def _():
        up[: mids * rank, :] = jnp.zeros((mids * rank, ports), jnp.float32)
        up[(mids + 1) * rank :, :] = jnp.zeros((up.shape[0] - (mids + 1) * rank, ports), jnp.float32)
        for row in range(send.shape[0]):
            spot = (mids + 1) * rank + row
            up[spot : spot + 1, : send.shape[1]] = send[row : row + 1, :].astype(jnp.float32)

    point = lax.broadcasted_iota(jnp.int32, (points, ports), 0)
    values = []
    for g in range(group):
        block = jnp.where(
            point < size[step * group + g], charges[g * points : (g + 1) * points, :], 0.0
        )
        values.append(fold(dot(rows_of(basis[g]), lanes_of(block))))
    for g in range(group):
        coef[g] = values[g]
    moved = [fold(dot(rows_of(transfer[g]), lanes_of(values[g]))) for g in range(group)]
    for g in range(group):
        where = pl.ds(pl.multiple_of(parent[step * group + g] * rank, rank), rank)
        up[where, :] += moved[g]

    @pl.when(step == pl.num_programs(0) - 1)
    def _():
        terms = [
            fold(dot(rows_of(mid_transfer[c]), lanes_of(up[c * rank : (c + 1) * rank, :])))
            for c in range(mids)
        ]
        while len(terms) > 1:
            terms = [sum(terms[i : i + 2]) for i in range(0, len(terms), 2)]
        up[mids * rank : (mids + 1) * rank, :] = terms[0]


def up_sweep(charges, leaf_size, basis, transfer, mid_transfer, leaf_parent, slots):
    leaves, rank, points = basis.shape
    ports = charges.shape[1]
    mids = mid_transfer.shape[0]
    group = 8
    send_mid = slots.reshape(-1, min(slots.shape[0], ports))
    up_rows = (mids + 1) * rank + -(-send_mid.shape[0] // 8) * 8
    return pl.pallas_call(
        up_kernel,
        grid_spec=pltpu.PrefetchScalarGridSpec(
            num_scalar_prefetch=2,
            grid=(leaves // group,),
            in_specs=[
                first(group * points, ports),
                first(group, rank, points),
                first(group, rank, rank),
                whole(mid_transfer.shape),
                whole(send_mid.shape),
            ],
            out_specs=[first(group, rank, ports), whole((up_rows, ports))],
        ),
        out_shape=[
            jax.ShapeDtypeStruct((leaves, rank, ports), jnp.float32),
            jax.ShapeDtypeStruct((up_rows, ports), jnp.float32),
        ],
        compiler_params=params(60 * MIB),
        cost_estimate=cost(10**9, 10**7),
        name="up_sweep",
    )(leaf_size, leaf_parent, charges, basis, transfer, mid_transfer, send_mid)


def spread_kernel(send, coef, out):
    leaves = coef.shape[0]

    @pl.loop(0, out.shape[0], unroll=8)
    def _(slot):
        out[slot] = coef[jnp.minimum(send[slot], leaves - 1)]


def spread(send_leaf, coef):
    vmem = pl.BlockSpec(memory_space=pltpu.VMEM)
    shape = (send_leaf.shape[0],) + coef.shape[1:]
    return pl.pallas_call(
        spread_kernel,
        in_specs=[pl.BlockSpec(memory_space=pltpu.SMEM), vmem],
        out_specs=vmem,
        out_shape=jax.ShapeDtypeStruct(shape, jnp.float32),
        compiler_params=params(60 * MIB),
        cost_estimate=cost(0, 4 * 10**6),
        name="spread",
    )(send_leaf, coef)


def select_kernel(sizes, group_at, lane_at, *refs):
    lines, per_cluster, up_rows, mids, rank, per_pair, groups = sizes
    received, messages = refs[:lines], refs[lines : lines + groups]
    payloads, tables, sem, table_sem = refs[lines + groups :]
    group, lane = group_at[0], lane_at[0]
    table_rows = up_rows - (mids + 1) * rank
    ports = payloads.shape[2]
    copies = []
    for line, ref in enumerate(received):
        table = ref.at[pl.ds((mids + 1) * rank, table_rows), :]
        copies.append(pltpu.make_async_copy(table, tables.at[line], table_sem.at[line]))
        copies.append(pltpu.make_async_copy(ref, payloads.at[line], sem.at[line]))
    for copy in copies:
        copy.start()
    for copy in copies:
        copy.wait()
    for d, message in enumerate(messages):
        for side in range(2):
            receiver = (group ^ d) * per_cluster + (lane ^ side)

            @pl.loop(0, lines, unroll=min(lines, 4))
            def _(line):
                for j in range(per_pair):
                    entry = receiver * per_pair + j
                    listed = tables[line, lax.div(entry, ports), lax.rem(entry, ports)]
                    block = jnp.clip(listed.astype(jnp.int32), 0, mids - 1)
                    target = (1 - side) * (per_pair + 1) * lines + line * per_pair + j
                    message[target] = payloads[line, pl.ds(pl.multiple_of(block * rank, 8), rank), :]

        for line in range(lines):
            message[lines * per_pair + line] = payloads[line, mids * rank : (mids + 1) * rank, :]


def select(sizes, group_at, lane_at, received):
    lines, per_cluster, up_rows, mids, rank, per_pair, groups = sizes
    ports = received[0].shape[1]
    table_rows = up_rows - (mids + 1) * rank
    payloads = (lines, up_rows, ports)
    shape = jax.ShapeDtypeStruct((lines * (2 * per_pair + 1), rank, ports), jnp.float32)
    return pl.pallas_call(
        functools.partial(select_kernel, sizes),
        in_specs=[pl.BlockSpec(memory_space=pltpu.SMEM)] * 2
        + [pl.BlockSpec(memory_space=pl.ANY)] * len(received),
        out_specs=[pl.BlockSpec(memory_space=pltpu.VMEM)] * groups,
        out_shape=[shape] * groups,
        scratch_shapes=[
            pltpu.VMEM(payloads, jnp.float32),
            pltpu.SMEM((lines, table_rows, ports), jnp.float32),
            pltpu.SemaphoreType.DMA((lines,)),
            pltpu.SemaphoreType.DMA((lines,)),
        ],
        compiler_params=params(60 * MIB),
        cost_estimate=cost(0, 4 * 10**6),
        name="select",
    )(group_at, lane_at, *received)


def prepare_kernel(after, coupling, basis, transfer, mid_coupling, mid_transfer, *out):
    wide, basis_t, transfer_t, mid_wide, mid_transfer_t = out
    for g in range(coupling.shape[0]):
        wide[g] = rows_of(coupling[g])
        basis_t[g] = rows_of(basis[g]).T
        transfer_t[g] = rows_of(transfer[g]).T
    for g in range(mid_coupling.shape[0]):
        mid_wide[g] = rows_of(mid_coupling[g])
        mid_transfer_t[g] = rows_of(mid_transfer[g]).T


def prepare(after, coupling, basis, transfer, mid_coupling, mid_transfer):
    leaves, rank, width = coupling.shape
    points = basis.shape[2]
    mids, _, mid_width = mid_coupling.shape
    steps = mids
    group = leaves // steps
    shapes = [
        (leaves, 2 * rank, width),
        (leaves, points, 2 * rank),
        (leaves, rank, 2 * rank),
        (mids, 2 * rank, mid_width),
        (mids, rank, 2 * rank),
    ]
    return pl.pallas_call(
        prepare_kernel,
        grid=(steps,),
        in_specs=[
            pl.BlockSpec(memory_space=pl.ANY),
            first(group, rank, width),
            first(group, rank, points),
            first(group, rank, rank),
            first(1, rank, mid_width),
            first(1, rank, rank),
        ],
        out_specs=[first(s[0] // steps, *s[1:]) for s in shapes],
        out_shape=[jax.ShapeDtypeStruct(s, jnp.bfloat16) for s in shapes],
        compiler_params=params(60 * MIB),
        cost_estimate=cost(0, 3 * 10**7),
        name="prepare",
    )(after, coupling, basis, transfer, mid_coupling, mid_transfer)


def mid_kernel(sizes, parent, pair, position, tops, *refs):
    bounds, per_pair, groups = sizes
    lines, count = bounds[-1], (len(bounds) - 1) * groups
    messages = refs[: 2 * count]
    mid_wide, mid_transfer, transfer, top_coupling, out = refs[2 * count : 2 * count + 5]
    scratch = refs[2 * count + 5 :]
    held_messages, scratch = scratch[: 2 * count], scratch[2 * count :]
    (
        mid_wide_held, mid_transfer_held, transfer_held, top_held, parts, top_parts, near_top, down,
        message_sem, mid_sem, small_sem,
    ) = scratch
    mids, leaves = mid_wide.shape[0], transfer.shape[0]
    slots, top_count = parts.shape[0] - 1, top_parts.shape[0] - 1

    def fetch_message(index):
        held = held_messages[index]
        start = 0 if index >= count else messages[index].shape[0] - held.shape[0]
        source = messages[index].at[pl.ds(start, held.shape[0])]
        return pltpu.make_async_copy(source, held, message_sem.at[index])

    def fetch_mid(c):
        return pltpu.make_async_copy(mid_wide.at[c], mid_wide_held.at[c], mid_sem.at[c])

    small = (
        pltpu.make_async_copy(top_coupling.at[position[0]], top_held, small_sem.at[0]),
        pltpu.make_async_copy(mid_transfer, mid_transfer_held, small_sem.at[1]),
        pltpu.make_async_copy(transfer, transfer_held, small_sem.at[2]),
    )
    for index in range(2 * count):
        fetch_message(index).start()
    for copy in small:
        copy.start()

    parts[slots] = jnp.zeros(parts.shape[1:], jnp.bfloat16)
    top_parts[top_count] = jnp.zeros(top_parts.shape[1:], jnp.bfloat16)
    for index in range(2 * count):
        side, message = divmod(index, count)
        batch, d = divmod(message, groups)
        lines_held = bounds[batch + 1] - bounds[batch]
        piece = lines_held * per_pair
        base = (d * 2 + side) * lines + bounds[batch]
        held = held_messages[index]
        first_slot, first_top = (lines_held, 0) if side == 0 else (0, piece)
        fetch_message(index).wait()
        if index == count:
            for c in range(mids):
                fetch_mid(c).start()

        @pl.loop(0, piece, unroll=min(piece, 4))
        def _(slot):
            parts[base * per_pair + slot] = lanes_of(held[first_slot + slot])

        for line in range(lines_held):
            top_parts[base + line] = lanes_of(held[first_top + line])

    for copy in small:
        copy.wait()
    stacked = jnp.concatenate([top_parts[tops[k]] for k in range(tops.shape[0])], axis=0)
    near_top[...] = fold(dot(rows_of(top_held[...]), stacked))
    for c in range(mids):
        fetch_mid(c).wait()

    @pl.loop(0, mids, step=4)
    def _(start):
        near = []
        for g in range(4):
            c = start + g
            stacked = jnp.concatenate([parts[pair[c, k]] for k in range(pair.shape[1])], axis=0)
            value = fold(dot(mid_wide_held[c], stacked))
            near.append(value + deep_dot(mid_transfer_held[c], near_top[...]))
        for g in range(4):
            down[start + g] = near[g]

    @pl.loop(0, leaves, step=8)
    def _(start):
        terms = [deep_dot(transfer_held[start + g], down[parent[start + g]]) for g in range(8)]
        for g in range(8):
            out[start + g] = terms[g]


def mid_level(
    bounds, per_pair, groups, parent, pair, position, tops, near_side, far_side, mid_wide, mid_transfer,
    transfer, top_coupling
):
    mids = mid_wide.shape[0]
    leaves = transfer.shape[0]
    rank, ports = near_side[0].shape[1:]
    owners = 2 * bounds[-1] * groups
    held = []
    for message in range(len(near_side)):
        batch = message // groups
        held.append((bounds[batch + 1] - bounds[batch]) * (per_pair + 1))
    full, half = jnp.float32, jnp.bfloat16
    scratch = [((h, rank, ports), full) for h in held + held] + [
        (mid_wide.shape, half),
        (mid_transfer.shape, half),
        (transfer.shape, half),
        (top_coupling.shape[1:], full),
        ((owners * per_pair + 1, rank, 2 * ports), half),
        ((owners + 1, rank, 2 * ports), half),
        ((rank, ports), full),
        ((mids, rank, ports), full),
    ]
    semaphores = [2 * len(near_side), mids, 3]
    scalars = (parent, pair, position, tops)
    arrays = (*near_side, *far_side, mid_wide, mid_transfer, transfer, top_coupling)
    return pl.pallas_call(
        functools.partial(mid_kernel, (bounds, per_pair, groups)),
        in_specs=[pl.BlockSpec(memory_space=pltpu.SMEM)] * len(scalars)
        + [pl.BlockSpec(memory_space=pl.ANY)] * len(arrays),
        out_specs=pl.BlockSpec(memory_space=pltpu.VMEM),
        out_shape=jax.ShapeDtypeStruct((leaves, rank, ports), full),
        scratch_shapes=[pltpu.VMEM(shape, dtype) for shape, dtype in scratch]
        + [pltpu.SemaphoreType.DMA((n,)) for n in semaphores],
        compiler_params=params(59 * MIB),
        cost_estimate=cost(2 * 10**9, 10**7),
        name="mid_level",
    )(*scalars, *arrays)


def leaf_kernel(
    sizes, size, pair, arrived, wide, basis, back, out,
    arrived_held, wide_held, basis_held, back_held, parts, out_held,
    arrived_sem, wide_sem, basis_sem, back_sem, out_sem,
):
    chunk, group = sizes
    leaves, points, _ = basis.shape
    slots, _, ports = arrived.shape

    def fetch_arrived(index):
        source = arrived.at[pl.ds(index * chunk, chunk)]
        return pltpu.make_async_copy(source, arrived_held.at[index % 2], arrived_sem.at[index % 2])

    def fetch_leaves(index):
        some = pl.ds(index * group, group)
        return (
            pltpu.make_async_copy(wide.at[some], wide_held.at[some], wide_sem.at[index]),
            pltpu.make_async_copy(basis.at[some], basis_held.at[some], basis_sem.at[index]),
        )

    def send(index):
        rows = group * points
        target = out.at[pl.ds(index * rows, rows), :]
        return pltpu.make_async_copy(out_held.at[index % 2], target, out_sem.at[index % 2])

    fetch_back = pltpu.make_async_copy(back, back_held, back_sem)
    chunks = slots // chunk
    for index in range(min(2, chunks)):
        fetch_arrived(index).start()
    ahead = 3
    for index in range(ahead - 1):
        for copy in fetch_leaves(index):
            copy.start()
        if index == 0:
            fetch_back.start()

    parts[slots] = jnp.zeros(parts.shape[1:], jnp.bfloat16)
    for index in range(chunks):
        fetch_arrived(index).wait()

        @pl.loop(0, chunk, unroll=8)
        def _(slot):
            parts[index * chunk + slot] = lanes_of(arrived_held[index % 2, slot])

        if index + 2 < chunks:
            fetch_arrived(index + 2).start()

    point = lax.broadcasted_iota(jnp.int32, (points, ports), 0)
    fetch_back.wait()
    for index in range(leaves // group):
        if index + ahead - 1 < leaves // group:
            for copy in fetch_leaves(index + ahead - 1):
                copy.start()
        for copy in fetch_leaves(index):
            copy.wait()
        values = []
        for g in range(group):
            leaf = index * group + g
            stacked = jnp.concatenate([parts[pair[leaf, k]] for k in range(pair.shape[1])], axis=0)
            values.append(fold(dot(wide_held[leaf], stacked)) + back_held[leaf])
        if index >= 2:
            send(index - 2).wait()
        for g in range(group):
            far = deep_dot(basis_held[index * group + g], values[g])
            far = jnp.where(point < size[index * group + g], far, 0.0)
            out_held[index % 2, g * points : (g + 1) * points, :] = far
        send(index).start()
    for index in range(max(0, leaves // group - 2), leaves // group):
        send(index).wait()


def leaf_level(size, pair, arrived, wide, basis, back):
    leaves, points, _ = basis.shape
    slots, rank, ports = arrived.shape
    group, chunk = 4, min(slots, 32)
    full, half = jnp.float32, jnp.bfloat16
    scratch = [
        ((2, chunk, rank, ports), full),
        (wide.shape, half),
        (basis.shape, half),
        (back.shape, full),
        ((slots + 1, rank, 2 * ports), half),
        ((2, group * points, ports), full),
    ]
    semaphores = [(2,), (leaves // group,), (leaves // group,), (), (2,)]
    return pl.pallas_call(
        functools.partial(leaf_kernel, (chunk, group)),
        in_specs=[pl.BlockSpec(memory_space=pltpu.SMEM)] * 2 + [pl.BlockSpec(memory_space=pl.ANY)] * 4,
        out_specs=pl.BlockSpec(memory_space=pl.ANY),
        out_shape=jax.ShapeDtypeStruct((leaves * points, ports), full),
        scratch_shapes=[pltpu.VMEM(shape, dtype) for shape, dtype in scratch]
        + [pltpu.SemaphoreType.DMA(n) for n in semaphores],
        compiler_params=params(59 * MIB),
        cost_estimate=cost(4 * 10**9, 2 * 10**7),
        name="leaf_level",
    )(size, pair, arrived, wide, basis, back)


def body(
    charges, leaf_size, leaf_basis, leaf_transfer, mid_transfer, leaf_parent, send_leaf, pair_leaf,
    leaf_coupling, send_mid, pair_mid, mid_coupling, top_pairs, top_coupling,
):
    rank = leaf_basis.shape[1]
    ports = charges.shape[1]
    mids = mid_transfer.shape[0]
    slots = send_mid.shape[0]
    groups, per_cluster = lax.axis_size("group"), lax.axis_size("cluster")
    owners = groups * per_cluster
    lines = per_cluster // 2
    per_pair = slots // owners
    group, lane = lax.axis_index("group"), lax.axis_index("cluster")

    group_at, lane_at = group.astype(jnp.int32)[None], lane.astype(jnp.int32)[None]
    coef, lifted = up_sweep(
        charges, leaf_size, leaf_basis, leaf_transfer, mid_transfer, leaf_parent, send_mid
    )
    up_rows = lifted.shape[0]
    outgoing = spread(send_leaf, coef)

    received = [lifted] * lines
    for d in range(lines - 1, 0, -1):
        received[d] = lax.ppermute(lifted, "cluster", [(c, c ^ (2 * d)) for c in range(per_cluster)])
    wide, basis_t, transfer_t, mid_wide, mid_transfer_t = prepare(
        lifted, leaf_coupling, leaf_basis, leaf_transfer, mid_coupling, mid_transfer
    )

    def spot_of(sender):
        at_group, at_lane = sender // per_cluster, sender % per_cluster
        line = (at_lane // 2) ^ (lane // 2)
        return ((at_group ^ group) * 2 + ((at_lane ^ lane) & 1)) * lines + line

    spot = spot_of(pair_mid // per_pair) * per_pair + pair_mid % per_pair
    spot = jnp.where((pair_mid >= 0) & (pair_mid < slots), spot, slots)
    wanted = lax.dynamic_slice_in_dim(top_pairs, lane, 1, 0)[0]
    tops = jnp.where((wanted >= 0) & (wanted < owners), spot_of(wanted), owners)

    bounds = (0, 2, lines)
    swap = [(c, c ^ 1) for c in range(per_cluster)]
    near_side, far_side = [], []
    for low, high in zip(bounds[:-1], bounds[1:]):
        sizes = (high - low, per_cluster, up_rows, mids, rank, per_pair, groups)
        messages = select(sizes, group_at, lane_at, received[low:high])
        moved = [messages[0]]
        for d in range(1, groups):
            moved.append(lax.ppermute(messages[d], "group", [(g, g ^ d) for g in range(groups)]))
        if high < lines:
            near_side += moved
        if low == 0:
            outgoing, near_side, received[2:] = lax.optimization_barrier(
                (outgoing, near_side, received[2:])
            )
            arrived = lax.all_to_all(outgoing, AXES, split_axis=0, concat_axis=0, tiled=True)
            far_side = [lax.ppermute(m, "cluster", swap) for m in near_side]
        if high == lines:
            ready = (moved, far_side, mid_wide, spot, tops, pair_leaf)
            moved, far_side, mid_wide, spot, tops, pair_leaf = lax.optimization_barrier(ready)
            near_side += moved
            far_side += [lax.ppermute(m, "cluster", swap) for m in moved]

    back = mid_level(
        bounds, per_pair, groups, leaf_parent, spot, lane_at, tops, near_side, far_side, mid_wide,
        mid_transfer_t, transfer_t, top_coupling,
    )
    return leaf_level(leaf_size, pair_leaf, arrived, wide, basis_t, back)


def solution(mesh):
    both = P(AXES)
    in_specs = (
        P(AXES, None),
        both,
        P(AXES, None, None),
        P(AXES, None, None),
        P(AXES, None, None),
        both,
        both,
        P(AXES, None),
        P(AXES, None, None),
        both,
        P(AXES, None),
        P(AXES, None, None),
        P("group", None),
        P("group", None, None),
    )
    return jax.shard_map(
        body, mesh=mesh, in_specs=in_specs, out_specs=P(AXES, None), check_vma=False
    )
```

```python
import functools

import jax
import jax.numpy as jnp
from jax import lax
from jax.experimental import pallas as pl
from jax.experimental.pallas import tpu as pltpu
from jax.sharding import PartitionSpec as P

AXES = ("group", "cluster")
MIB = 1024 * 1024


def params(size):
    return pltpu.CompilerParams(vmem_limit_bytes=size)


def cost(flops, size):
    return pl.CostEstimate(flops=flops, bytes_accessed=size, transcendentals=0)


def whole(shape):
    return pl.BlockSpec(shape, lambda i, *_: (0,) * len(shape), pipeline_mode=pl.Buffered(1))


def first(group, *rest):
    return pl.BlockSpec((group,) + rest, lambda i, *_: (i,) + (0,) * len(rest))


def split(x):
    high = x.astype(jnp.bfloat16)
    low = (x - high.astype(jnp.float32)).astype(jnp.bfloat16)
    return high, low


def rows_of(x):
    return jnp.concatenate(split(x), axis=0)


def lanes_of(x):
    return jnp.concatenate(split(x), axis=1)


def dot(a, b):
    return lax.dot_general(a, b, (((1,), (0,)), ((), ())), preferred_element_type=jnp.float32)


def fold(product):
    m, n = product.shape[0] // 2, product.shape[1] // 2
    return product[:m, :n] + (product[:m, n:] + product[m:, :n] + product[m:, n:])


def deep_dot(a, b):
    high, low = split(b)
    return dot(jnp.concatenate([a, a], axis=1), jnp.concatenate([high, high, low, low], axis=0))


def up_kernel(
    sizes, size, parent, slots, group_at, lane_at, charges, basis, transfer, mid_transfer, send, coef, up,
    *messages
):
    step = pl.program_id(0)
    group, rank, points = basis.shape
    mids = mid_transfer.shape[0]
    ports = up.shape[1]

    @pl.when(step == 0)
    def _():
        up[: mids * rank, :] = jnp.zeros((mids * rank, ports), jnp.float32)
        up[(mids + 1) * rank :, :] = jnp.zeros((up.shape[0] - (mids + 1) * rank, ports), jnp.float32)
        for row in range(send.shape[0]):
            spot = (mids + 1) * rank + row
            up[spot : spot + 1, : send.shape[1]] = send[row : row + 1, :].astype(jnp.float32)

    point = lax.broadcasted_iota(jnp.int32, (points, ports), 0)
    values = []
    for g in range(group):
        block = jnp.where(
            point < size[step * group + g], charges[g * points : (g + 1) * points, :], 0.0
        )
        values.append(fold(dot(rows_of(basis[g]), lanes_of(block))))
    for g in range(group):
        coef[g] = values[g]
    moved = [fold(dot(rows_of(transfer[g]), lanes_of(values[g]))) for g in range(group)]
    for g in range(group):
        where = pl.ds(pl.multiple_of(parent[step * group + g] * rank, rank), rank)
        up[where, :] += moved[g]

    @pl.when(step == pl.num_programs(0) - 1)
    def _():
        terms = [
            fold(dot(rows_of(mid_transfer[c]), lanes_of(up[c * rank : (c + 1) * rank, :])))
            for c in range(mids)
        ]
        while len(terms) > 1:
            terms = [sum(terms[i : i + 2]) for i in range(0, len(terms), 2)]
        up[mids * rank : (mids + 1) * rank, :] = terms[0]
        per_cluster, per_pair = sizes
        for d, message in enumerate(messages):
            for side in range(2):
                receiver = (group_at[0] ^ d) * per_cluster + (lane_at[0] ^ side)
                for j in range(per_pair):
                    block = jnp.clip(slots[receiver * per_pair + j], 0, mids - 1)
                    source = pl.ds(pl.multiple_of(block * rank, rank), rank)
                    message[(1 - side) * (per_pair + 1) + j] = up[source, :]
            message[per_pair] = terms[0]


def up_sweep(
    sizes, groups, group_at, lane_at, charges, leaf_size, basis, transfer, mid_transfer, leaf_parent, slots
):
    leaves, rank, points = basis.shape
    ports = charges.shape[1]
    mids = mid_transfer.shape[0]
    group = 8
    send_mid = slots.reshape(-1, min(slots.shape[0], ports))
    up_rows = (mids + 1) * rank + -(-send_mid.shape[0] // 8) * 8
    message = (2 * sizes[1] + 1, rank, ports)
    return pl.pallas_call(
        functools.partial(up_kernel, sizes),
        grid_spec=pltpu.PrefetchScalarGridSpec(
            num_scalar_prefetch=5,
            grid=(leaves // group,),
            in_specs=[
                first(group * points, ports),
                first(group, rank, points),
                first(group, rank, rank),
                whole(mid_transfer.shape),
                whole(send_mid.shape),
            ],
            out_specs=[first(group, rank, ports), whole((up_rows, ports))] + [whole(message)] * groups,
        ),
        out_shape=[
            jax.ShapeDtypeStruct((leaves, rank, ports), jnp.float32),
            jax.ShapeDtypeStruct((up_rows, ports), jnp.float32),
        ]
        + [jax.ShapeDtypeStruct(message, jnp.float32)] * groups,
        compiler_params=params(60 * MIB),
        cost_estimate=cost(10**9, 10**7),
        name="up_sweep",
    )(
        leaf_size, leaf_parent, slots, group_at, lane_at, charges, basis, transfer, mid_transfer, send_mid
    )


def spread_kernel(send, coef, out):
    leaves = coef.shape[0]

    @pl.loop(0, out.shape[0], unroll=8)
    def _(slot):
        out[slot] = coef[jnp.minimum(send[slot], leaves - 1)]


def spread(send_leaf, coef):
    vmem = pl.BlockSpec(memory_space=pltpu.VMEM)
    shape = (send_leaf.shape[0],) + coef.shape[1:]
    return pl.pallas_call(
        spread_kernel,
        in_specs=[pl.BlockSpec(memory_space=pltpu.SMEM), vmem],
        out_specs=vmem,
        out_shape=jax.ShapeDtypeStruct(shape, jnp.float32),
        compiler_params=params(60 * MIB),
        cost_estimate=cost(0, 4 * 10**6),
        name="spread",
    )(send_leaf, coef)


def select_kernel(sizes, group_at, lane_at, *refs):
    lines, per_cluster, up_rows, mids, rank, per_pair, groups = sizes
    received, messages = refs[:lines], refs[lines : lines + groups]
    payloads, tables, sem, table_sem = refs[lines + groups :]
    group, lane = group_at[0], lane_at[0]
    table_rows = up_rows - (mids + 1) * rank
    ports = payloads.shape[2]
    copies = []
    for line, ref in enumerate(received):
        table = ref.at[pl.ds((mids + 1) * rank, table_rows), :]
        copies.append(pltpu.make_async_copy(table, tables.at[line], table_sem.at[line]))
        copies.append(pltpu.make_async_copy(ref, payloads.at[line], sem.at[line]))
    for copy in copies:
        copy.start()
    for copy in copies:
        copy.wait()
    for d, message in enumerate(messages):
        for side in range(2):
            receiver = (group ^ d) * per_cluster + (lane ^ side)

            @pl.loop(0, lines, unroll=min(lines, 4))
            def _(line):
                for j in range(per_pair):
                    entry = receiver * per_pair + j
                    listed = tables[line, lax.div(entry, ports), lax.rem(entry, ports)]
                    block = jnp.clip(listed.astype(jnp.int32), 0, mids - 1)
                    target = (1 - side) * (per_pair + 1) * lines + line * per_pair + j
                    message[target] = payloads[line, pl.ds(pl.multiple_of(block * rank, 8), rank), :]

        for line in range(lines):
            message[lines * per_pair + line] = payloads[line, mids * rank : (mids + 1) * rank, :]


def select(sizes, group_at, lane_at, received):
    lines, per_cluster, up_rows, mids, rank, per_pair, groups = sizes
    ports = received[0].shape[1]
    table_rows = up_rows - (mids + 1) * rank
    payloads = (lines, up_rows, ports)
    shape = jax.ShapeDtypeStruct((lines * (2 * per_pair + 1), rank, ports), jnp.float32)
    return pl.pallas_call(
        functools.partial(select_kernel, sizes),
        in_specs=[pl.BlockSpec(memory_space=pltpu.SMEM)] * 2
        + [pl.BlockSpec(memory_space=pl.ANY)] * len(received),
        out_specs=[pl.BlockSpec(memory_space=pltpu.VMEM)] * groups,
        out_shape=[shape] * groups,
        scratch_shapes=[
            pltpu.VMEM(payloads, jnp.float32),
            pltpu.SMEM((lines, table_rows, ports), jnp.float32),
            pltpu.SemaphoreType.DMA((lines,)),
            pltpu.SemaphoreType.DMA((lines,)),
        ],
        compiler_params=params(60 * MIB),
        cost_estimate=cost(0, 4 * 10**6),
        name="select",
    )(group_at, lane_at, *received)


def prepare_kernel(after, coupling, basis, transfer, mid_coupling, mid_transfer, wide, basis_t, mid_wide):
    for g in range(coupling.shape[0]):
        wide[g] = rows_of(jnp.concatenate([coupling[g], transfer[g].T], axis=1))
        basis_t[g] = rows_of(basis[g]).T
    for g in range(mid_coupling.shape[0]):
        mid_wide[g] = rows_of(jnp.concatenate([mid_coupling[g], mid_transfer[g].T], axis=1))


def prepare(after, coupling, basis, transfer, mid_coupling, mid_transfer):
    leaves, rank, width = coupling.shape
    points = basis.shape[2]
    mids, _, mid_width = mid_coupling.shape
    steps = mids
    group = leaves // steps
    shapes = [
        (leaves, 2 * rank, width + rank),
        (leaves, points, 2 * rank),
        (mids, 2 * rank, mid_width + rank),
    ]
    return pl.pallas_call(
        prepare_kernel,
        grid=(steps,),
        in_specs=[
            pl.BlockSpec(memory_space=pl.ANY),
            first(group, rank, width),
            first(group, rank, points),
            first(group, rank, rank),
            first(1, rank, mid_width),
            first(1, rank, rank),
        ],
        out_specs=[first(s[0] // steps, *s[1:]) for s in shapes],
        out_shape=[jax.ShapeDtypeStruct(s, jnp.bfloat16) for s in shapes],
        compiler_params=params(60 * MIB),
        cost_estimate=cost(0, 3 * 10**7),
        name="prepare",
    )(after, coupling, basis, transfer, mid_coupling, mid_transfer)


def tail_kernel(sizes, parent, pair, position, tops, size, pair_leaf, *refs):
    bounds, per_pair, groups, chunk, group, ahead = sizes
    lines, count = bounds[-1], (len(bounds) - 1) * groups
    messages = refs[: 2 * count]
    arrived, mid_wide, top_coupling, wide, basis, out = refs[2 * count : 2 * count + 6]
    scratch = refs[2 * count + 6 :]
    held_messages, scratch = scratch[: 2 * count], scratch[2 * count :]
    (
        arrived_held, mid_wide_held, top_held, wide_held, basis_held, parts, top_parts, leaf_parts, out_held,
        message_sem, arrived_sem, mid_sem, top_sem, wide_sem, basis_sem, out_sem,
    ) = scratch
    mids, leaves, points = mid_wide.shape[0], wide.shape[0], basis.shape[1]
    slots, top_count = arrived.shape[0], top_parts.shape[0] - 1
    ports = out.shape[1]
    steps, chunks = leaves // group, slots // chunk

    def fetch_message(index):
        held = held_messages[index]
        start = 0 if index >= count else messages[index].shape[0] - held.shape[0]
        source = messages[index].at[pl.ds(start, held.shape[0])]
        return pltpu.make_async_copy(source, held, message_sem.at[index])

    def fetch_arrived(index):
        source = arrived.at[pl.ds(index * chunk, chunk)]
        return pltpu.make_async_copy(source, arrived_held.at[index % 2], arrived_sem.at[index % 2])

    def fetch_mid(c):
        return pltpu.make_async_copy(mid_wide.at[c], mid_wide_held.at[c], mid_sem.at[c])

    def fetch_leaves(index):
        some = pl.ds(index * group, group)
        return (
            pltpu.make_async_copy(wide.at[some], wide_held.at[some], wide_sem.at[index]),
            pltpu.make_async_copy(basis.at[some], basis_held.at[some], basis_sem.at[index]),
        )

    fetch_top = pltpu.make_async_copy(top_coupling.at[position[0]], top_held, top_sem)
    for index in range(min(2, chunks)):
        fetch_arrived(index).start()
    for index in range(2 * count):
        fetch_message(index).start()
    fetch_top.start()

    leaf_parts[slots] = jnp.zeros(leaf_parts.shape[1:], jnp.bfloat16)
    parts[slots] = jnp.zeros(parts.shape[1:], jnp.bfloat16)
    top_parts[top_count] = jnp.zeros(top_parts.shape[1:], jnp.bfloat16)
    for index in range(chunks):
        fetch_arrived(index).wait()
        if index == min(1, chunks - 1):
            for c in range(mids):
                fetch_mid(c).start()

        @pl.loop(0, chunk, unroll=8)
        def _(slot):
            leaf_parts[index * chunk + slot] = lanes_of(arrived_held[index % 2, slot])

        if index + 2 < chunks:
            fetch_arrived(index + 2).start()

    for index in range(2 * count):
        side, message = divmod(index, count)
        batch, d = divmod(message, groups)
        lines_held = bounds[batch + 1] - bounds[batch]
        piece = lines_held * per_pair
        base = (d * 2 + side) * lines + bounds[batch]
        held = held_messages[index]
        first_slot, first_top = (lines_held, 0) if side == 0 else (0, piece)
        fetch_message(index).wait()

        @pl.loop(0, piece, unroll=min(piece, 6))
        def _(slot):
            parts[base * per_pair + slot] = lanes_of(held[first_slot + slot])

        for line in range(lines_held):
            top_parts[base + line] = lanes_of(held[first_top + line])

    for index in range(ahead):
        for copy in fetch_leaves(index):
            copy.start()
    fetch_top.wait()
    stacked = jnp.concatenate([top_parts[tops[k]] for k in range(tops.shape[0])], axis=0)
    parts[slots + 1] = lanes_of(fold(dot(rows_of(top_held[...]), stacked)))
    for c in range(mids):
        fetch_mid(c).wait()

    @pl.loop(0, mids, step=4)
    def _(start):
        values = []
        for g in range(4):
            blocks = [parts[pair[start + g, k]] for k in range(pair.shape[1])] + [parts[slots + 1]]
            values.append(fold(dot(mid_wide_held[start + g], jnp.concatenate(blocks, axis=0))))
        for g in range(4):
            leaf_parts[slots + 1 + start + g] = lanes_of(values[g])

    point = lax.broadcasted_iota(jnp.int32, (points, ports), 0)

    def send(index):
        rows = group * points
        target = out.at[pl.ds(index * rows, rows), :]
        return pltpu.make_async_copy(out_held.at[index % 2], target, out_sem.at[index % 2])

    for index in range(steps):
        if index + ahead < steps:
            for copy in fetch_leaves(index + ahead):
                copy.start()
        for copy in fetch_leaves(index):
            copy.wait()
        values = []
        for g in range(group):
            leaf = index * group + g
            blocks = [leaf_parts[pair_leaf[leaf, k]] for k in range(pair_leaf.shape[1])]
            blocks.append(leaf_parts[slots + 1 + parent[leaf]])
            values.append(fold(dot(wide_held[leaf], jnp.concatenate(blocks, axis=0))))
        if index >= 2:
            send(index - 2).wait()
        for g in range(group):
            far = deep_dot(basis_held[index * group + g], values[g])
            far = jnp.where(point < size[index * group + g], far, 0.0)
            out_held[index % 2, g * points : (g + 1) * points, :] = far
        send(index).start()
    for index in range(max(0, steps - 2), steps):
        send(index).wait()


def tail(
    bounds, per_pair, groups, parent, pair, position, tops, size, pair_leaf, near_side, far_side, arrived,
    mid_wide, top_coupling, wide, basis
):
    mids = mid_wide.shape[0]
    leaves, points, _ = basis.shape
    slots, rank, ports = arrived.shape
    owners = slots // per_pair
    group, chunk, ahead = 4, min(slots, 32), 3
    held = []
    for message in range(len(near_side)):
        batch = message // groups
        held.append((bounds[batch + 1] - bounds[batch]) * (per_pair + 1))
    full, half = jnp.float32, jnp.bfloat16
    scratch = [((h, rank, ports), full) for h in held + held] + [
        ((2, chunk, rank, ports), full),
        (mid_wide.shape, half),
        (top_coupling.shape[1:], full),
        (wide.shape, half),
        (basis.shape, half),
        ((slots + 2, rank, 2 * ports), half),
        ((owners + 1, rank, 2 * ports), half),
        ((slots + 1 + mids, rank, 2 * ports), half),
        ((2, group * points, ports), full),
    ]
    semaphores = [(2 * len(near_side),), (2,), (mids,), (), (leaves // group,), (leaves // group,), (2,)]
    scalars = (parent, pair, position, tops, size, pair_leaf)
    arrays = (*near_side, *far_side, arrived, mid_wide, top_coupling, wide, basis)
    return pl.pallas_call(
        functools.partial(tail_kernel, (bounds, per_pair, groups, chunk, group, ahead)),
        in_specs=[pl.BlockSpec(memory_space=pltpu.SMEM)] * len(scalars)
        + [pl.BlockSpec(memory_space=pl.ANY)] * len(arrays),
        out_specs=pl.BlockSpec(memory_space=pl.ANY),
        out_shape=jax.ShapeDtypeStruct((leaves * points, ports), full),
        scratch_shapes=[pltpu.VMEM(shape, dtype) for shape, dtype in scratch]
        + [pltpu.SemaphoreType.DMA(n) for n in semaphores],
        compiler_params=params(60 * MIB),
        cost_estimate=cost(6 * 10**9, 2 * 10**7),
        name="tail",
    )(*scalars, *arrays)


def body(
    charges, leaf_size, leaf_basis, leaf_transfer, mid_transfer, leaf_parent, send_leaf, pair_leaf,
    leaf_coupling, send_mid, pair_mid, mid_coupling, top_pairs, top_coupling,
):
    rank = leaf_basis.shape[1]
    ports = charges.shape[1]
    mids = mid_transfer.shape[0]
    slots = send_mid.shape[0]
    groups, per_cluster = lax.axis_size("group"), lax.axis_size("cluster")
    owners = groups * per_cluster
    lines = per_cluster // 2
    per_pair = slots // owners
    group, lane = lax.axis_index("group"), lax.axis_index("cluster")

    group_at, lane_at = group.astype(jnp.int32)[None], lane.astype(jnp.int32)[None]
    coef, lifted, *own_messages = up_sweep(
        (per_cluster, per_pair), groups, group_at, lane_at, charges, leaf_size, leaf_basis,
        leaf_transfer, mid_transfer, leaf_parent, send_mid,
    )
    up_rows = lifted.shape[0]
    outgoing = spread(send_leaf, coef)

    received = [lifted]
    for d in range(1, lines):
        received.append(
            lax.ppermute(lifted, "cluster", [(c, c ^ (2 * d)) for c in range(per_cluster)])
        )
    wide, basis_t, mid_wide = prepare(
        lifted, leaf_coupling, leaf_basis, leaf_transfer, mid_coupling, mid_transfer
    )

    def spot_of(sender):
        at_group, at_lane = sender // per_cluster, sender % per_cluster
        line = (at_lane // 2) ^ (lane // 2)
        return ((at_group ^ group) * 2 + ((at_lane ^ lane) & 1)) * lines + line

    spot = spot_of(pair_mid // per_pair) * per_pair + pair_mid % per_pair
    spot = jnp.where((pair_mid >= 0) & (pair_mid < slots), spot, slots)
    wanted = lax.dynamic_slice_in_dim(top_pairs, lane, 1, 0)[0]
    tops = jnp.where((wanted >= 0) & (wanted < owners), spot_of(wanted), owners)

    own_messages, received[1], spot, tops, pair_leaf, mid_wide = lax.optimization_barrier(
        (own_messages, received[1], spot, tops, pair_leaf, mid_wide)
    )
    bounds = (0, 1, lines)
    swap = [(c, c ^ 1) for c in range(per_cluster)]
    near_side, far_side = [], []
    for low, high in zip(bounds[:-1], bounds[1:]):
        sizes = (high - low, per_cluster, up_rows, mids, rank, per_pair, groups)
        messages = own_messages if low == 0 else select(sizes, group_at, lane_at, received[low:high])
        moved = [messages[0]]
        for d in range(1, groups):
            moved.append(lax.ppermute(messages[d], "group", [(g, g ^ d) for g in range(groups)]))
        if high < lines:
            near_side += moved
        if low == 0:
            outgoing, near_side, received[1:] = lax.optimization_barrier(
                (outgoing, near_side, received[1:])
            )
            arrived = lax.all_to_all(outgoing, AXES, split_axis=0, concat_axis=0, tiled=True)
            far_side = [lax.ppermute(m, "cluster", swap) for m in near_side]
        if high == lines:
            near_side += moved
            far_side += [lax.ppermute(m, "cluster", swap) for m in moved]

    return tail(
        bounds, per_pair, groups, leaf_parent, spot, lane_at, tops, leaf_size, pair_leaf, near_side,
        far_side, arrived, mid_wide, top_coupling, wide, basis_t,
    )


def solution(mesh):
    both = P(AXES)
    in_specs = (
        P(AXES, None),
        both,
        P(AXES, None, None),
        P(AXES, None, None),
        P(AXES, None, None),
        both,
        both,
        P(AXES, None),
        P(AXES, None, None),
        both,
        P(AXES, None),
        P(AXES, None, None),
        P("group", None),
        P("group", None, None),
    )
    return jax.shard_map(
        body, mesh=mesh, in_specs=in_specs, out_specs=P(AXES, None), check_vma=False
    )
```

```python
import functools
import math

import jax
import jax.numpy as jnp
from jax import lax
from jax.experimental import pallas as pl
from jax.experimental.pallas import tpu as pltpu
from jax.sharding import PartitionSpec as P

AXES = ("group", "cluster")
MIB = 1024 * 1024


def params(size):
    return pltpu.CompilerParams(vmem_limit_bytes=size)


def cost(flops, size):
    return pl.CostEstimate(flops=flops, bytes_accessed=size, transcendentals=0)


def whole(shape):
    return pl.BlockSpec(shape, lambda i, *_: (0,) * len(shape), pipeline_mode=pl.Buffered(1))


def first(group, *rest):
    return pl.BlockSpec((group,) + rest, lambda i, *_: (i,) + (0,) * len(rest))


def split(x):
    high = x.astype(jnp.bfloat16)
    low = (x - high.astype(jnp.float32)).astype(jnp.bfloat16)
    return high, low


def rows_of(x):
    return jnp.concatenate(split(x), axis=0)


def lanes_of(x):
    return jnp.concatenate(split(x), axis=1)


def dot(a, b):
    return lax.dot_general(a, b, (((1,), (0,)), ((), ())), preferred_element_type=jnp.float32)


def fold(product):
    m, n = product.shape[0] // 2, product.shape[1] // 2
    return product[:m, :n] + (product[:m, n:] + product[m:, :n] + product[m:, n:])


def deep_dot(a, b):
    high, low = split(b)
    return dot(jnp.concatenate([a, a], axis=1), jnp.concatenate([high, high, low, low], axis=0))


def up_kernel(
    sizes, size, parent, slots, group_at, lane_at, charges, basis, transfer, mid_transfer, send, coef, up,
    *messages
):
    step = pl.program_id(0)
    group, rank, points = basis.shape
    mids = mid_transfer.shape[0]
    ports = up.shape[1]

    @pl.when(step == 0)
    def _():
        up[: mids * rank, :] = jnp.zeros((mids * rank, ports), jnp.float32)
        up[(mids + 1) * rank :, :] = jnp.zeros((up.shape[0] - (mids + 1) * rank, ports), jnp.float32)
        for row in range(send.shape[0]):
            spot = (mids + 1) * rank + row
            up[spot : spot + 1, : send.shape[1]] = send[row : row + 1, :].astype(jnp.float32)

    point = lax.broadcasted_iota(jnp.int32, (points, ports), 0)
    values = []
    for g in range(group):
        block = jnp.where(
            point < size[step * group + g], charges[g * points : (g + 1) * points, :], 0.0
        )
        values.append(fold(dot(rows_of(basis[g]), lanes_of(block))))
    for g in range(group):
        coef[g] = values[g]
    moved = [fold(dot(rows_of(transfer[g]), lanes_of(values[g]))) for g in range(group)]
    for g in range(group):
        where = pl.ds(pl.multiple_of(parent[step * group + g] * rank, rank), rank)
        up[where, :] += moved[g]

    @pl.when(step == pl.num_programs(0) - 1)
    def _():
        terms = [
            fold(dot(rows_of(mid_transfer[c]), lanes_of(up[c * rank : (c + 1) * rank, :])))
            for c in range(mids)
        ]
        while len(terms) > 1:
            terms = [sum(terms[i : i + 2]) for i in range(0, len(terms), 2)]
        up[mids * rank : (mids + 1) * rank, :] = terms[0]
        per_cluster, per_pair = sizes
        for d, message in enumerate(messages):
            for side in range(2):
                receiver = (group_at[0] ^ d) * per_cluster + (lane_at[0] ^ side)
                for j in range(per_pair):
                    block = jnp.clip(slots[receiver * per_pair + j], 0, mids - 1)
                    source = pl.ds(pl.multiple_of(block * rank, rank), rank)
                    message[(1 - side) * (per_pair + 1) + j] = up[source, :]
            message[per_pair] = terms[0]


def up_sweep(
    sizes, groups, group_at, lane_at, charges, leaf_size, basis, transfer, mid_transfer, leaf_parent, slots
):
    leaves, rank, points = basis.shape
    ports = charges.shape[1]
    mids = mid_transfer.shape[0]
    group = 8
    send_mid = slots.reshape(-1, min(slots.shape[0], ports))
    up_rows = (mids + 1) * rank + -(-send_mid.shape[0] // 8) * 8
    message = (2 * sizes[1] + 1, rank, ports)
    return pl.pallas_call(
        functools.partial(up_kernel, sizes),
        grid_spec=pltpu.PrefetchScalarGridSpec(
            num_scalar_prefetch=5,
            grid=(leaves // group,),
            in_specs=[
                first(group * points, ports),
                first(group, rank, points),
                first(group, rank, rank),
                whole(mid_transfer.shape),
                whole(send_mid.shape),
            ],
            out_specs=[first(group, rank, ports), whole((up_rows, ports))] + [whole(message)] * groups,
        ),
        out_shape=[
            jax.ShapeDtypeStruct((leaves, rank, ports), jnp.float32),
            jax.ShapeDtypeStruct((up_rows, ports), jnp.float32),
        ]
        + [jax.ShapeDtypeStruct(message, jnp.float32)] * groups,
        compiler_params=params(60 * MIB),
        cost_estimate=cost(10**9, 10**7),
        name="up_sweep",
    )(
        leaf_size, leaf_parent, slots, group_at, lane_at, charges, basis, transfer, mid_transfer, send_mid
    )


def spread_kernel(send, coef, out):
    leaves = coef.shape[0]

    @pl.loop(0, out.shape[0], unroll=8)
    def _(slot):
        out[slot] = coef[jnp.minimum(send[slot], leaves - 1)]


def spread(send_leaf, coef):
    vmem = pl.BlockSpec(memory_space=pltpu.VMEM)
    shape = (send_leaf.shape[0],) + coef.shape[1:]
    return pl.pallas_call(
        spread_kernel,
        in_specs=[pl.BlockSpec(memory_space=pltpu.SMEM), vmem],
        out_specs=vmem,
        out_shape=jax.ShapeDtypeStruct(shape, jnp.float32),
        compiler_params=params(60 * MIB),
        cost_estimate=cost(0, 4 * 10**6),
        name="spread",
    )(send_leaf, coef)


def select_kernel(sizes, group_at, lane_at, *refs):
    lines, per_cluster, up_rows, mids, rank, per_pair, groups = sizes
    received, messages = refs[:lines], refs[lines : lines + groups]
    payloads, tables, sem, table_sem = refs[lines + groups :]
    group, lane = group_at[0], lane_at[0]
    table_rows = up_rows - (mids + 1) * rank
    ports = payloads.shape[2]
    copies = []
    for line, ref in enumerate(received):
        table = ref.at[pl.ds((mids + 1) * rank, table_rows), :]
        copies.append(pltpu.make_async_copy(table, tables.at[line], table_sem.at[line]))
        copies.append(pltpu.make_async_copy(ref, payloads.at[line], sem.at[line]))
    for copy in copies:
        copy.start()
    for copy in copies:
        copy.wait()
    for d, message in enumerate(messages):
        for side in range(2):
            receiver = (group ^ d) * per_cluster + (lane ^ side)

            @pl.loop(0, lines, unroll=min(lines, 4))
            def _(line):
                for j in range(per_pair):
                    entry = receiver * per_pair + j
                    listed = tables[line, lax.div(entry, ports), lax.rem(entry, ports)]
                    block = jnp.clip(listed.astype(jnp.int32), 0, mids - 1)
                    target = (1 - side) * (per_pair + 1) * lines + line * per_pair + j
                    message[target] = payloads[line, pl.ds(pl.multiple_of(block * rank, 8), rank), :]

        for line in range(lines):
            message[lines * per_pair + line] = payloads[line, mids * rank : (mids + 1) * rank, :]


def select(sizes, group_at, lane_at, received):
    lines, per_cluster, up_rows, mids, rank, per_pair, groups = sizes
    ports = received[0].shape[1]
    table_rows = up_rows - (mids + 1) * rank
    payloads = (lines, up_rows, ports)
    shape = jax.ShapeDtypeStruct((lines * (2 * per_pair + 1), rank, ports), jnp.float32)
    return pl.pallas_call(
        functools.partial(select_kernel, sizes),
        in_specs=[pl.BlockSpec(memory_space=pltpu.SMEM)] * 2
        + [pl.BlockSpec(memory_space=pl.ANY)] * len(received),
        out_specs=[pl.BlockSpec(memory_space=pltpu.VMEM)] * groups,
        out_shape=[shape] * groups,
        scratch_shapes=[
            pltpu.VMEM(payloads, jnp.float32),
            pltpu.SMEM((lines, table_rows, ports), jnp.float32),
            pltpu.SemaphoreType.DMA((lines,)),
            pltpu.SemaphoreType.DMA((lines,)),
        ],
        compiler_params=params(60 * MIB),
        cost_estimate=cost(0, 4 * 10**6),
        name="select",
    )(group_at, lane_at, *received)


def prepare_kernel(after, coupling, basis, transfer, mid_coupling, mid_transfer, wide, basis_t, mid_wide):
    for g in range(coupling.shape[0]):
        wide[g] = rows_of(jnp.concatenate([coupling[g], transfer[g].T], axis=1))
        basis_t[g] = rows_of(basis[g]).T
    for g in range(mid_coupling.shape[0]):
        mid_wide[g] = rows_of(jnp.concatenate([mid_coupling[g], mid_transfer[g].T], axis=1))


def prepare(after, coupling, basis, transfer, mid_coupling, mid_transfer):
    leaves, rank, width = coupling.shape
    points = basis.shape[2]
    mids, _, mid_width = mid_coupling.shape
    steps = mids
    group = leaves // steps
    shapes = [
        (leaves, 2 * rank, width + rank),
        (leaves, points, 2 * rank),
        (mids, 2 * rank, mid_width + rank),
    ]
    return pl.pallas_call(
        prepare_kernel,
        grid=(steps,),
        in_specs=[
            pl.BlockSpec(memory_space=pl.ANY),
            first(group, rank, width),
            first(group, rank, points),
            first(group, rank, rank),
            first(1, rank, mid_width),
            first(1, rank, rank),
        ],
        out_specs=[first(s[0] // steps, *s[1:]) for s in shapes],
        out_shape=[jax.ShapeDtypeStruct(s, jnp.bfloat16) for s in shapes],
        compiler_params=params(60 * MIB),
        cost_estimate=cost(0, 3 * 10**7),
        name="prepare",
    )(after, coupling, basis, transfer, mid_coupling, mid_transfer)


def tail_kernel(sizes, parent, pair, position, tops, size, pair_leaf, *refs):
    bounds, per_pair, groups, chunk, group, ahead = sizes
    lines, count = bounds[-1], (len(bounds) - 1) * groups
    messages = refs[: 2 * count]
    arrived, mid_wide, top_coupling, wide, basis, out = refs[2 * count : 2 * count + 6]
    scratch = refs[2 * count + 6 :]
    held_messages, scratch = scratch[: 2 * count], scratch[2 * count :]
    (
        arrived_held, mid_wide_held, top_held, wide_held, basis_held, parts, top_parts, leaf_parts, out_held,
        message_sem, arrived_sem, mid_sem, top_sem, wide_sem, basis_sem, out_sem,
    ) = scratch
    mids, leaves, points = mid_wide.shape[0], wide.shape[0], basis.shape[1]
    slots, top_count = arrived.shape[0], top_parts.shape[0] - 1
    ports = out.shape[1]
    steps, chunks = leaves // group, slots // chunk

    def fetch_message(index):
        held = held_messages[index]
        start = 0 if index >= count else messages[index].shape[0] - held.shape[0]
        source = messages[index].at[pl.ds(start, held.shape[0])]
        return pltpu.make_async_copy(source, held, message_sem.at[index])

    def fetch_arrived(index):
        source = arrived.at[pl.ds(index * chunk, chunk)]
        return pltpu.make_async_copy(source, arrived_held.at[index % 2], arrived_sem.at[index % 2])

    def fetch_mid(c):
        return pltpu.make_async_copy(mid_wide.at[c], mid_wide_held.at[c], mid_sem.at[c])

    def fetch_leaves(index):
        some = pl.ds(index * group, group)
        return (
            pltpu.make_async_copy(wide.at[some], wide_held.at[some], wide_sem.at[index]),
            pltpu.make_async_copy(basis.at[some], basis_held.at[some], basis_sem.at[index]),
        )

    fetch_top = pltpu.make_async_copy(top_coupling.at[position[0]], top_held, top_sem)
    for index in range(min(2, chunks)):
        fetch_arrived(index).start()
    for c in range(mids // 2):
        fetch_mid(c).start()
    for index in range(2 * count):
        fetch_message(index).start()
    fetch_top.start()
    for c in range(mids // 2, mids):
        fetch_mid(c).start()

    leaf_parts[slots] = jnp.zeros(leaf_parts.shape[1:], jnp.bfloat16)
    parts[slots] = jnp.zeros(parts.shape[1:], jnp.bfloat16)
    top_parts[top_count] = jnp.zeros(top_parts.shape[1:], jnp.bfloat16)
    for index in range(chunks):
        fetch_arrived(index).wait()
        @pl.loop(0, chunk, unroll=8)
        def _(slot):
            leaf_parts[index * chunk + slot] = lanes_of(arrived_held[index % 2, slot])

        if index + 2 < chunks:
            fetch_arrived(index + 2).start()

    for index in range(2 * count):
        side, message = divmod(index, count)
        batch, d = divmod(message, groups)
        lines_held = bounds[batch + 1] - bounds[batch]
        piece = lines_held * per_pair
        base = (d * 2 + side) * lines + bounds[batch]
        held = held_messages[index]
        first_slot, first_top = (lines_held, 0) if side == 0 else (0, piece)
        fetch_message(index).wait()

        @pl.loop(0, piece, unroll=min(piece, 6))
        def _(slot):
            parts[base * per_pair + slot] = lanes_of(held[first_slot + slot])

        for line in range(lines_held):
            top_parts[base + line] = lanes_of(held[first_top + line])

    for index in range(ahead):
        for copy in fetch_leaves(index):
            copy.start()
    fetch_top.wait()
    stacked = jnp.concatenate([top_parts[tops[k]] for k in range(tops.shape[0])], axis=0)
    parts[slots + 1] = lanes_of(fold(dot(rows_of(top_held[...]), stacked)))
    for c in range(mids):
        fetch_mid(c).wait()

    @pl.loop(0, mids, step=4)
    def _(start):
        values = []
        for g in range(4):
            blocks = [parts[pair[start + g, k]] for k in range(pair.shape[1])] + [parts[slots + 1]]
            values.append(fold(dot(mid_wide_held[start + g], jnp.concatenate(blocks, axis=0))))
        for g in range(4):
            leaf_parts[slots + 1 + start + g] = lanes_of(values[g])

    point = lax.broadcasted_iota(jnp.int32, (points, ports), 0)

    def send(index):
        rows = group * points
        target = out.at[pl.ds(index * rows, rows), :]
        return pltpu.make_async_copy(out_held.at[index % 2], target, out_sem.at[index % 2])

    for index in range(steps):
        if index + ahead < steps:
            for copy in fetch_leaves(index + ahead):
                copy.start()
        for copy in fetch_leaves(index):
            copy.wait()
        values = []
        for g in range(group):
            leaf = index * group + g
            blocks = [leaf_parts[pair_leaf[leaf, k]] for k in range(pair_leaf.shape[1])]
            blocks.append(leaf_parts[slots + 1 + parent[leaf]])
            values.append(fold(dot(wide_held[leaf], jnp.concatenate(blocks, axis=0))))
        if index >= 2:
            send(index - 2).wait()
        for g in range(group):
            far = deep_dot(basis_held[index * group + g], values[g])
            far = jnp.where(point < size[index * group + g], far, 0.0)
            out_held[index % 2, g * points : (g + 1) * points, :] = far
        send(index).start()
    for index in range(max(0, steps - 2), steps):
        send(index).wait()


def tail(
    bounds, per_pair, groups, parent, pair, position, tops, size, pair_leaf, near_side, far_side, arrived,
    mid_wide, top_coupling, wide, basis
):
    mids = mid_wide.shape[0]
    leaves, points, _ = basis.shape
    slots, rank, ports = arrived.shape
    owners = slots // per_pair
    group, chunk, ahead = 4, min(slots, 32), 3
    held = []
    for message in range(len(near_side)):
        batch = message // groups
        held.append((bounds[batch + 1] - bounds[batch]) * (per_pair + 1))
    full, half = jnp.float32, jnp.bfloat16
    scratch = [((h, rank, ports), full) for h in held + held] + [
        ((2, chunk, rank, ports), full),
        (mid_wide.shape, half),
        (top_coupling.shape[1:], full),
        (wide.shape, half),
        (basis.shape, half),
        ((slots + 2, rank, 2 * ports), half),
        ((owners + 1, rank, 2 * ports), half),
        ((slots + 1 + mids, rank, 2 * ports), half),
        ((2, group * points, ports), full),
    ]
    semaphores = [(2 * len(near_side),), (2,), (mids,), (), (leaves // group,), (leaves // group,), (2,)]
    scalars = (parent, pair, position, tops, size, pair_leaf)
    pinned = (pltpu.with_memory_space_constraint(x, pltpu.HBM) for x in (mid_wide, top_coupling, wide, basis))
    arrays = (*near_side, *far_side, arrived, *pinned)
    used = sum(jnp.dtype(dtype).itemsize * math.prod(shape) for shape, dtype in scratch)
    return pl.pallas_call(
        functools.partial(tail_kernel, (bounds, per_pair, groups, chunk, group, ahead)),
        in_specs=[pl.BlockSpec(memory_space=pltpu.SMEM)] * len(scalars)
        + [pl.BlockSpec(memory_space=pl.ANY)] * len(arrays),
        out_specs=pl.BlockSpec(memory_space=pl.ANY),
        out_shape=jax.ShapeDtypeStruct((leaves * points, ports), full),
        scratch_shapes=[pltpu.VMEM(shape, dtype) for shape, dtype in scratch]
        + [pltpu.SemaphoreType.DMA(n) for n in semaphores],
        compiler_params=params(min(60 * MIB, used + 6 * MIB)),
        cost_estimate=cost(6 * 10**9, 2 * 10**7),
        name="tail",
    )(*scalars, *arrays)


def body(
    charges, leaf_size, leaf_basis, leaf_transfer, mid_transfer, leaf_parent, send_leaf, pair_leaf,
    leaf_coupling, send_mid, pair_mid, mid_coupling, top_pairs, top_coupling,
):
    rank = leaf_basis.shape[1]
    ports = charges.shape[1]
    mids = mid_transfer.shape[0]
    slots = send_mid.shape[0]
    groups, per_cluster = lax.axis_size("group"), lax.axis_size("cluster")
    owners = groups * per_cluster
    lines = per_cluster // 2
    per_pair = slots // owners
    group, lane = lax.axis_index("group"), lax.axis_index("cluster")

    group_at, lane_at = group.astype(jnp.int32)[None], lane.astype(jnp.int32)[None]
    coef, lifted, *own_messages = up_sweep(
        (per_cluster, per_pair), groups, group_at, lane_at, charges, leaf_size, leaf_basis,
        leaf_transfer, mid_transfer, leaf_parent, send_mid,
    )
    up_rows = lifted.shape[0]
    outgoing = spread(send_leaf, coef)

    received = [lifted]
    for d in range(1, lines):
        received.append(
            lax.ppermute(lifted, "cluster", [(c, c ^ (2 * d)) for c in range(per_cluster)])
        )
    wide, basis_t, mid_wide = prepare(
        lifted, leaf_coupling, leaf_basis, leaf_transfer, mid_coupling, mid_transfer
    )

    def spot_of(sender):
        at_group, at_lane = sender // per_cluster, sender % per_cluster
        line = (at_lane // 2) ^ (lane // 2)
        return ((at_group ^ group) * 2 + ((at_lane ^ lane) & 1)) * lines + line

    spot = spot_of(pair_mid // per_pair) * per_pair + pair_mid % per_pair
    spot = jnp.where((pair_mid >= 0) & (pair_mid < slots), spot, slots)
    wanted = lax.dynamic_slice_in_dim(top_pairs, lane, 1, 0)[0]
    tops = jnp.where((wanted >= 0) & (wanted < owners), spot_of(wanted), owners)

    own_messages, spot, tops, pair_leaf, mid_wide = lax.optimization_barrier(
        (own_messages, spot, tops, pair_leaf, mid_wide)
    )
    bounds = (0, 1, lines)
    swap = [(c, c ^ 1) for c in range(per_cluster)]
    near_side, far_side = [], []
    for low, high in zip(bounds[:-1], bounds[1:]):
        sizes = (high - low, per_cluster, up_rows, mids, rank, per_pair, groups)
        messages = own_messages if low == 0 else select(sizes, group_at, lane_at, received[low:high])
        moved = [messages[0]]
        for d in range(1, groups):
            moved.append(lax.ppermute(messages[d], "group", [(g, g ^ d) for g in range(groups)]))
        if high < lines:
            near_side += moved
        if low == 0:
            outgoing, near_side, received[1:] = lax.optimization_barrier(
                (outgoing, near_side, received[1:])
            )
            arrived = lax.all_to_all(outgoing, AXES, split_axis=0, concat_axis=0, tiled=True)
            far_side = [lax.ppermute(m, "cluster", swap) for m in near_side]
        if high == lines:
            near_side += moved
            far_side += [lax.ppermute(m, "cluster", swap) for m in moved]

    return tail(
        bounds, per_pair, groups, leaf_parent, spot, lane_at, tops, leaf_size, pair_leaf, near_side,
        far_side, arrived, mid_wide, top_coupling, wide, basis_t,
    )


def solution(mesh):
    both = P(AXES)
    in_specs = (
        P(AXES, None),
        both,
        P(AXES, None, None),
        P(AXES, None, None),
        P(AXES, None, None),
        both,
        both,
        P(AXES, None),
        P(AXES, None, None),
        both,
        P(AXES, None),
        P(AXES, None, None),
        P("group", None),
        P("group", None, None),
    )
    return jax.shard_map(
        body, mesh=mesh, in_specs=in_specs, out_specs=P(AXES, None), check_vma=False
    )
```

```python
import functools

import jax
import jax.numpy as jnp
from jax import lax
from jax.experimental import pallas as pl
from jax.experimental.pallas import tpu as pltpu
from jax.sharding import PartitionSpec as P

AXES = ("group", "cluster")
MIB = 1024 * 1024


def params(size):
    return pltpu.CompilerParams(vmem_limit_bytes=size)


def cost(flops, size):
    return pl.CostEstimate(flops=flops, bytes_accessed=size, transcendentals=0)


def whole(shape):
    return pl.BlockSpec(shape, lambda i, *_: (0,) * len(shape), pipeline_mode=pl.Buffered(1))


def first(group, *rest):
    return pl.BlockSpec((group,) + rest, lambda i, *_: (i,) + (0,) * len(rest))


def split(x):
    high = x.astype(jnp.bfloat16)
    low = (x - high.astype(jnp.float32)).astype(jnp.bfloat16)
    return high, low


def rows_of(x):
    return jnp.concatenate(split(x), axis=0)


def lanes_of(x):
    return jnp.concatenate(split(x), axis=1)


def dot(a, b):
    return lax.dot_general(a, b, (((1,), (0,)), ((), ())), preferred_element_type=jnp.float32)


def fold(product):
    m, n = product.shape[0] // 2, product.shape[1] // 2
    return product[:m, :n] + (product[:m, n:] + product[m:, :n] + product[m:, n:])


def deep_dot(a, b):
    high, low = split(b)
    return dot(jnp.concatenate([a, a], axis=1), jnp.concatenate([high, high, low, low], axis=0))


def up_kernel(
    sizes, size, parent, slots, group_at, lane_at, charges, basis, transfer, mid_transfer, send, coef, up,
    *messages
):
    step = pl.program_id(0)
    group, rank, points = basis.shape
    mids = mid_transfer.shape[0]
    ports = up.shape[1]

    @pl.when(step == 0)
    def _():
        up[: mids * rank, :] = jnp.zeros((mids * rank, ports), jnp.float32)
        up[(mids + 1) * rank :, :] = jnp.zeros((up.shape[0] - (mids + 1) * rank, ports), jnp.float32)
        for row in range(send.shape[0]):
            spot = (mids + 1) * rank + row
            up[spot : spot + 1, : send.shape[1]] = send[row : row + 1, :].astype(jnp.float32)

    point = lax.broadcasted_iota(jnp.int32, (points, ports), 0)
    values = []
    for g in range(group):
        block = jnp.where(
            point < size[step * group + g], charges[g * points : (g + 1) * points, :], 0.0
        )
        values.append(fold(dot(rows_of(basis[g]), lanes_of(block))))
    for g in range(group):
        coef[g] = values[g]
    moved = [fold(dot(rows_of(transfer[g]), lanes_of(values[g]))) for g in range(group)]
    for g in range(group):
        where = pl.ds(pl.multiple_of(parent[step * group + g] * rank, rank), rank)
        up[where, :] += moved[g]

    @pl.when(step == pl.num_programs(0) - 1)
    def _():
        terms = [
            fold(dot(rows_of(mid_transfer[c]), lanes_of(up[c * rank : (c + 1) * rank, :])))
            for c in range(mids)
        ]
        while len(terms) > 1:
            terms = [sum(terms[i : i + 2]) for i in range(0, len(terms), 2)]
        up[mids * rank : (mids + 1) * rank, :] = terms[0]
        per_cluster, per_pair = sizes
        for d, message in enumerate(messages):
            for side in range(2):
                receiver = (group_at[0] ^ d) * per_cluster + (lane_at[0] ^ side)
                for j in range(per_pair):
                    block = jnp.clip(slots[receiver * per_pair + j], 0, mids - 1)
                    source = pl.ds(pl.multiple_of(block * rank, rank), rank)
                    message[(1 - side) * (per_pair + 1) + j] = up[source, :]
            message[per_pair] = terms[0]


def up_sweep(
    sizes, groups, group_at, lane_at, charges, leaf_size, basis, transfer, mid_transfer, leaf_parent, slots
):
    leaves, rank, points = basis.shape
    ports = charges.shape[1]
    mids = mid_transfer.shape[0]
    group = 8
    send_mid = slots.reshape(-1, min(slots.shape[0], ports))
    up_rows = (mids + 1) * rank + -(-send_mid.shape[0] // 8) * 8
    message = (2 * sizes[1] + 1, rank, ports)
    return pl.pallas_call(
        functools.partial(up_kernel, sizes),
        grid_spec=pltpu.PrefetchScalarGridSpec(
            num_scalar_prefetch=5,
            grid=(leaves // group,),
            in_specs=[
                first(group * points, ports),
                first(group, rank, points),
                first(group, rank, rank),
                whole(mid_transfer.shape),
                whole(send_mid.shape),
            ],
            out_specs=[first(group, rank, ports), whole((up_rows, ports))] + [whole(message)] * groups,
        ),
        out_shape=[
            jax.ShapeDtypeStruct((leaves, rank, ports), jnp.float32),
            jax.ShapeDtypeStruct((up_rows, ports), jnp.float32),
        ]
        + [jax.ShapeDtypeStruct(message, jnp.float32)] * groups,
        compiler_params=params(60 * MIB),
        cost_estimate=cost(10**9, 10**7),
        name="up_sweep",
    )(
        leaf_size, leaf_parent, slots, group_at, lane_at, charges, basis, transfer, mid_transfer, send_mid
    )


def spread_kernel(send, coef, out):
    leaves = coef.shape[0]

    @pl.loop(0, out.shape[0], unroll=8)
    def _(slot):
        out[slot] = coef[jnp.minimum(send[slot], leaves - 1)]


def spread(send_leaf, coef):
    vmem = pl.BlockSpec(memory_space=pltpu.VMEM)
    shape = (send_leaf.shape[0],) + coef.shape[1:]
    return pl.pallas_call(
        spread_kernel,
        in_specs=[pl.BlockSpec(memory_space=pltpu.SMEM), vmem],
        out_specs=vmem,
        out_shape=jax.ShapeDtypeStruct(shape, jnp.float32),
        compiler_params=params(60 * MIB),
        cost_estimate=cost(0, 4 * 10**6),
        name="spread",
    )(send_leaf, coef)


def select_kernel(sizes, group_at, lane_at, *refs):
    lines, per_cluster, up_rows, mids, rank, per_pair, groups = sizes
    received, messages = refs[:lines], refs[lines : lines + groups]
    payloads, tables, sem, table_sem = refs[lines + groups :]
    group, lane = group_at[0], lane_at[0]
    table_rows = up_rows - (mids + 1) * rank
    ports = payloads.shape[2]
    copies = []
    for line, ref in enumerate(received):
        table = ref.at[pl.ds((mids + 1) * rank, table_rows), :]
        copies.append(pltpu.make_async_copy(table, tables.at[line], table_sem.at[line]))
        copies.append(pltpu.make_async_copy(ref, payloads.at[line], sem.at[line]))
    for copy in copies:
        copy.start()
    for copy in copies:
        copy.wait()
    for d, message in enumerate(messages):
        for side in range(2):
            receiver = (group ^ d) * per_cluster + (lane ^ side)

            @pl.loop(0, lines, unroll=min(lines, 4))
            def _(line):
                for j in range(per_pair):
                    entry = receiver * per_pair + j
                    listed = tables[line, lax.div(entry, ports), lax.rem(entry, ports)]
                    block = jnp.clip(listed.astype(jnp.int32), 0, mids - 1)
                    target = (1 - side) * (per_pair + 1) * lines + line * per_pair + j
                    message[target] = payloads[line, pl.ds(pl.multiple_of(block * rank, 8), rank), :]

        for line in range(lines):
            message[lines * per_pair + line] = payloads[line, mids * rank : (mids + 1) * rank, :]


def select(sizes, group_at, lane_at, received):
    lines, per_cluster, up_rows, mids, rank, per_pair, groups = sizes
    ports = received[0].shape[1]
    table_rows = up_rows - (mids + 1) * rank
    payloads = (lines, up_rows, ports)
    shape = jax.ShapeDtypeStruct((lines * (2 * per_pair + 1), rank, ports), jnp.float32)
    return pl.pallas_call(
        functools.partial(select_kernel, sizes),
        in_specs=[pl.BlockSpec(memory_space=pltpu.SMEM)] * 2
        + [pl.BlockSpec(memory_space=pl.ANY)] * len(received),
        out_specs=[pl.BlockSpec(memory_space=pltpu.VMEM)] * groups,
        out_shape=[shape] * groups,
        scratch_shapes=[
            pltpu.VMEM(payloads, jnp.float32),
            pltpu.SMEM((lines, table_rows, ports), jnp.float32),
            pltpu.SemaphoreType.DMA((lines,)),
            pltpu.SemaphoreType.DMA((lines,)),
        ],
        compiler_params=params(60 * MIB),
        cost_estimate=cost(0, 4 * 10**6),
        name="select",
    )(group_at, lane_at, *received)


def prepare_kernel(after, coupling, basis, transfer, mid_coupling, mid_transfer, wide, basis_t, mid_wide):
    for g in range(coupling.shape[0]):
        wide[g] = rows_of(jnp.concatenate([coupling[g], transfer[g].T], axis=1))
        basis_t[g] = rows_of(basis[g]).T
    for g in range(mid_coupling.shape[0]):
        mid_wide[g] = rows_of(jnp.concatenate([mid_coupling[g], mid_transfer[g].T], axis=1))


def prepare(after, coupling, basis, transfer, mid_coupling, mid_transfer):
    leaves, rank, width = coupling.shape
    points = basis.shape[2]
    mids, _, mid_width = mid_coupling.shape
    steps = mids
    group = leaves // steps
    shapes = [
        (leaves, 2 * rank, width + rank),
        (leaves, points, 2 * rank),
        (mids, 2 * rank, mid_width + rank),
    ]
    return pl.pallas_call(
        prepare_kernel,
        grid=(steps,),
        in_specs=[
            pl.BlockSpec(memory_space=pl.ANY),
            first(group, rank, width),
            first(group, rank, points),
            first(group, rank, rank),
            first(1, rank, mid_width),
            first(1, rank, rank),
        ],
        out_specs=[first(s[0] // steps, *s[1:]) for s in shapes],
        out_shape=[jax.ShapeDtypeStruct(s, jnp.bfloat16) for s in shapes],
        compiler_params=params(60 * MIB),
        cost_estimate=cost(0, 3 * 10**7),
        name="prepare",
    )(after, coupling, basis, transfer, mid_coupling, mid_transfer)


def mid_kernel(sizes, pair, position, tops, *refs):
    bounds, per_pair, groups = sizes
    lines, count = bounds[-1], (len(bounds) - 1) * groups
    messages = refs[: 2 * count]
    mid_wide, top_coupling, out = refs[2 * count : 2 * count + 3]
    scratch = refs[2 * count + 3 :]
    held_messages, scratch = scratch[: 2 * count], scratch[2 * count :]
    mid_wide_held, top_held, parts, top_parts, message_sem, mid_sem, top_sem = scratch
    mids = mid_wide.shape[0]
    slots, top_count = parts.shape[0] - 2, top_parts.shape[0] - 1

    def fetch_message(index):
        held = held_messages[index]
        start = 0 if index >= count else messages[index].shape[0] - held.shape[0]
        source = messages[index].at[pl.ds(start, held.shape[0])]
        return pltpu.make_async_copy(source, held, message_sem.at[index])

    def fetch_mid(c):
        return pltpu.make_async_copy(mid_wide.at[c], mid_wide_held.at[c], mid_sem.at[c])

    fetch_top = pltpu.make_async_copy(top_coupling.at[position[0]], top_held, top_sem)
    for index in range(2 * count):
        fetch_message(index).start()
    fetch_top.start()
    for c in range(mids):
        fetch_mid(c).start()

    parts[slots] = jnp.zeros(parts.shape[1:], jnp.bfloat16)
    top_parts[top_count] = jnp.zeros(top_parts.shape[1:], jnp.bfloat16)
    for index in range(2 * count):
        side, message = divmod(index, count)
        batch, d = divmod(message, groups)
        lines_held = bounds[batch + 1] - bounds[batch]
        piece = lines_held * per_pair
        base = (d * 2 + side) * lines + bounds[batch]
        held = held_messages[index]
        first_slot, first_top = (lines_held, 0) if side == 0 else (0, piece)
        fetch_message(index).wait()

        @pl.loop(0, piece, unroll=min(piece, 6))
        def _(slot):
            parts[base * per_pair + slot] = lanes_of(held[first_slot + slot])

        for line in range(lines_held):
            top_parts[base + line] = lanes_of(held[first_top + line])

    fetch_top.wait()
    stacked = jnp.concatenate([top_parts[tops[k]] for k in range(tops.shape[0])], axis=0)
    parts[slots + 1] = lanes_of(fold(dot(rows_of(top_held[...]), stacked)))
    for c in range(mids):
        fetch_mid(c).wait()

    @pl.loop(0, mids, step=4)
    def _(start):
        values = []
        for g in range(4):
            blocks = [parts[pair[start + g, k]] for k in range(pair.shape[1])] + [parts[slots + 1]]
            values.append(fold(dot(mid_wide_held[start + g], jnp.concatenate(blocks, axis=0))))
        for g in range(4):
            out[start + g] = values[g]


def mid_level(
    bounds, per_pair, groups, pair, position, tops, near_side, far_side, mid_wide, top_coupling
):
    mids = mid_wide.shape[0]
    rank, ports = near_side[0].shape[1:]
    owners = 2 * bounds[-1] * groups
    held = []
    for message in range(len(near_side)):
        batch = message // groups
        held.append((bounds[batch + 1] - bounds[batch]) * (per_pair + 1))
    full, half = jnp.float32, jnp.bfloat16
    scratch = [((h, rank, ports), full) for h in held + held] + [
        (mid_wide.shape, half),
        (top_coupling.shape[1:], full),
        ((owners * per_pair + 2, rank, 2 * ports), half),
        ((owners + 1, rank, 2 * ports), half),
    ]
    semaphores = [(2 * len(near_side),), (mids,), ()]
    scalars = (pair, position, tops)
    arrays = (*near_side, *far_side, mid_wide, top_coupling)
    return pl.pallas_call(
        functools.partial(mid_kernel, (bounds, per_pair, groups)),
        in_specs=[pl.BlockSpec(memory_space=pltpu.SMEM)] * len(scalars)
        + [pl.BlockSpec(memory_space=pl.ANY)] * len(arrays),
        out_specs=pl.BlockSpec(memory_space=pltpu.VMEM),
        out_shape=jax.ShapeDtypeStruct((mids, rank, ports), full),
        scratch_shapes=[pltpu.VMEM(shape, dtype) for shape, dtype in scratch]
        + [pltpu.SemaphoreType.DMA(n) for n in semaphores],
        compiler_params=params(60 * MIB),
        cost_estimate=cost(2 * 10**9, 10**7),
        name="mid_level",
    )(*scalars, *arrays)


def leaf_kernel(
    sizes, parent, size, pair, arrived, wide, basis, down, out,
    arrived_held, wide_held, basis_held, down_held, parts, out_held,
    arrived_sem, wide_sem, basis_sem, down_sem, out_sem,
):
    chunk, group, ahead = sizes
    leaves, points, _ = basis.shape
    slots, _, ports = arrived.shape
    steps, chunks = leaves // group, slots // chunk

    def fetch_arrived(index):
        source = arrived.at[pl.ds(index * chunk, chunk)]
        return pltpu.make_async_copy(source, arrived_held.at[index % 2], arrived_sem.at[index % 2])

    def fetch_leaves(index):
        some = pl.ds(index * group, group)
        return (
            pltpu.make_async_copy(wide.at[some], wide_held.at[some], wide_sem.at[index]),
            pltpu.make_async_copy(basis.at[some], basis_held.at[some], basis_sem.at[index]),
        )

    def send(index):
        rows = group * points
        target = out.at[pl.ds(index * rows, rows), :]
        return pltpu.make_async_copy(out_held.at[index % 2], target, out_sem.at[index % 2])

    fetch_down = pltpu.make_async_copy(down, down_held, down_sem)
    for index in range(min(2, chunks)):
        fetch_arrived(index).start()
    fetch_down.start()
    for index in range(ahead):
        for copy in fetch_leaves(index):
            copy.start()

    parts[slots] = jnp.zeros(parts.shape[1:], jnp.bfloat16)
    for index in range(chunks):
        fetch_arrived(index).wait()

        @pl.loop(0, chunk, unroll=8)
        def _(slot):
            parts[index * chunk + slot] = lanes_of(arrived_held[index % 2, slot])

        if index + 2 < chunks:
            fetch_arrived(index + 2).start()

    fetch_down.wait()
    for c in range(down.shape[0]):
        parts[slots + 1 + c] = lanes_of(down_held[c])

    point = lax.broadcasted_iota(jnp.int32, (points, ports), 0)
    for index in range(steps):
        if index + ahead < steps:
            for copy in fetch_leaves(index + ahead):
                copy.start()
        for copy in fetch_leaves(index):
            copy.wait()
        values = []
        for g in range(group):
            leaf = index * group + g
            blocks = [parts[pair[leaf, k]] for k in range(pair.shape[1])]
            blocks.append(parts[slots + 1 + parent[leaf]])
            values.append(fold(dot(wide_held[leaf], jnp.concatenate(blocks, axis=0))))
        if index >= 2:
            send(index - 2).wait()
        for g in range(group):
            far = deep_dot(basis_held[index * group + g], values[g])
            far = jnp.where(point < size[index * group + g], far, 0.0)
            out_held[index % 2, g * points : (g + 1) * points, :] = far
        send(index).start()
    for index in range(max(0, steps - 2), steps):
        send(index).wait()


def leaf_level(parent, size, pair, arrived, wide, basis, down):
    leaves, points, _ = basis.shape
    slots, rank, ports = arrived.shape
    group, chunk, ahead = 4, min(slots, 32), 3
    full, half = jnp.float32, jnp.bfloat16
    scratch = [
        ((2, chunk, rank, ports), full),
        (wide.shape, half),
        (basis.shape, half),
        (down.shape, full),
        ((slots + 1 + down.shape[0], rank, 2 * ports), half),
        ((2, group * points, ports), full),
    ]
    semaphores = [(2,), (leaves // group,), (leaves // group,), (), (2,)]
    return pl.pallas_call(
        functools.partial(leaf_kernel, (chunk, group, ahead)),
        in_specs=[pl.BlockSpec(memory_space=pltpu.SMEM)] * 3 + [pl.BlockSpec(memory_space=pl.ANY)] * 4,
        out_specs=pl.BlockSpec(memory_space=pl.ANY),
        out_shape=jax.ShapeDtypeStruct((leaves * points, ports), full),
        scratch_shapes=[pltpu.VMEM(shape, dtype) for shape, dtype in scratch]
        + [pltpu.SemaphoreType.DMA(n) for n in semaphores],
        compiler_params=params(60 * MIB),
        cost_estimate=cost(4 * 10**9, 2 * 10**7),
        name="leaf_level",
    )(parent, size, pair, arrived, wide, basis, down)


def body(
    charges, leaf_size, leaf_basis, leaf_transfer, mid_transfer, leaf_parent, send_leaf, pair_leaf,
    leaf_coupling, send_mid, pair_mid, mid_coupling, top_pairs, top_coupling,
):
    rank = leaf_basis.shape[1]
    ports = charges.shape[1]
    mids = mid_transfer.shape[0]
    slots = send_mid.shape[0]
    groups, per_cluster = lax.axis_size("group"), lax.axis_size("cluster")
    owners = groups * per_cluster
    lines = per_cluster // 2
    per_pair = slots // owners
    group, lane = lax.axis_index("group"), lax.axis_index("cluster")

    group_at, lane_at = group.astype(jnp.int32)[None], lane.astype(jnp.int32)[None]
    coef, lifted, *own_messages = up_sweep(
        (per_cluster, per_pair), groups, group_at, lane_at, charges, leaf_size, leaf_basis,
        leaf_transfer, mid_transfer, leaf_parent, send_mid,
    )
    up_rows = lifted.shape[0]
    outgoing = spread(send_leaf, coef)

    received = [lifted]
    for d in range(1, lines):
        received.append(
            lax.ppermute(lifted, "cluster", [(c, c ^ (2 * d)) for c in range(per_cluster)])
        )
    wide, basis_t, mid_wide = prepare(
        lifted, leaf_coupling, leaf_basis, leaf_transfer, mid_coupling, mid_transfer
    )

    def spot_of(sender):
        at_group, at_lane = sender // per_cluster, sender % per_cluster
        line = (at_lane // 2) ^ (lane // 2)
        return ((at_group ^ group) * 2 + ((at_lane ^ lane) & 1)) * lines + line

    spot = spot_of(pair_mid // per_pair) * per_pair + pair_mid % per_pair
    spot = jnp.where((pair_mid >= 0) & (pair_mid < slots), spot, slots)
    wanted = lax.dynamic_slice_in_dim(top_pairs, lane, 1, 0)[0]
    tops = jnp.where((wanted >= 0) & (wanted < owners), spot_of(wanted), owners)

    own_messages, received[1] = lax.optimization_barrier((own_messages, received[1]))
    bounds = (0, 1, 2, lines)
    swap = [(c, c ^ 1) for c in range(per_cluster)]
    near_side, far_side = [], []
    for low, high in zip(bounds[:-1], bounds[1:]):
        sizes = (high - low, per_cluster, up_rows, mids, rank, per_pair, groups)
        messages = own_messages if low == 0 else select(sizes, group_at, lane_at, received[low:high])
        moved = [messages[0]]
        for d in range(1, groups):
            moved.append(lax.ppermute(messages[d], "group", [(g, g ^ d) for g in range(groups)]))
        if high < lines:
            near_side += moved
        if low == 1:
            outgoing, near_side, received[2:] = lax.optimization_barrier(
                (outgoing, near_side, received[2:])
            )
            arrived = lax.all_to_all(outgoing, AXES, split_axis=0, concat_axis=0, tiled=True)
            far_side = [lax.ppermute(m, "cluster", swap) for m in near_side]
        if high == lines:
            ready = (moved, far_side, mid_wide, spot, tops, pair_leaf)
            moved, far_side, mid_wide, spot, tops, pair_leaf = lax.optimization_barrier(ready)
            near_side += moved
            far_side += [lax.ppermute(m, "cluster", swap) for m in moved]

    down = mid_level(
        bounds, per_pair, groups, spot, lane_at, tops, near_side, far_side, mid_wide, top_coupling
    )
    return leaf_level(leaf_parent, leaf_size, pair_leaf, arrived, wide, basis_t, down)


def solution(mesh):
    both = P(AXES)
    in_specs = (
        P(AXES, None),
        both,
        P(AXES, None, None),
        P(AXES, None, None),
        P(AXES, None, None),
        both,
        both,
        P(AXES, None),
        P(AXES, None, None),
        both,
        P(AXES, None),
        P(AXES, None, None),
        P("group", None),
        P("group", None, None),
    )
    return jax.shard_map(
        body, mesh=mesh, in_specs=in_specs, out_specs=P(AXES, None), check_vma=False
    )
```

```python
import functools
import math

import jax
import jax.numpy as jnp
from jax import lax
from jax.experimental import pallas as pl
from jax.experimental.pallas import tpu as pltpu
from jax.sharding import PartitionSpec as P

AXES = ("group", "cluster")
MIB = 1024 * 1024


def params(size):
    return pltpu.CompilerParams(vmem_limit_bytes=size)


def cost(flops, size):
    return pl.CostEstimate(flops=flops, bytes_accessed=size, transcendentals=0)


def whole(shape):
    return pl.BlockSpec(shape, lambda i, *_: (0,) * len(shape), pipeline_mode=pl.Buffered(1))


def first(group, *rest):
    return pl.BlockSpec((group,) + rest, lambda i, *_: (i,) + (0,) * len(rest))


def split(x):
    high = x.astype(jnp.bfloat16)
    low = (x - high.astype(jnp.float32)).astype(jnp.bfloat16)
    return high, low


def rows_of(x):
    return jnp.concatenate(split(x), axis=0)


def lanes_of(x):
    return jnp.concatenate(split(x), axis=1)


def dot(a, b):
    return lax.dot_general(a, b, (((1,), (0,)), ((), ())), preferred_element_type=jnp.float32)


def fold(product):
    m, n = product.shape[0] // 2, product.shape[1] // 2
    return product[:m, :n] + (product[:m, n:] + product[m:, :n] + product[m:, n:])


def deep_dot(a, b):
    high, low = split(b)
    return dot(jnp.concatenate([a, a], axis=1), jnp.concatenate([high, high, low, low], axis=0))


def up_kernel(
    sizes, size, parent, slots, group_at, lane_at, charges, basis, transfer, mid_transfer, send, coef, up,
    *messages
):
    step = pl.program_id(0)
    group, rank, points = basis.shape
    mids = mid_transfer.shape[0]
    ports = up.shape[1]

    @pl.when(step == 0)
    def _():
        up[: mids * rank, :] = jnp.zeros((mids * rank, ports), jnp.float32)
        up[(mids + 1) * rank :, :] = jnp.zeros((up.shape[0] - (mids + 1) * rank, ports), jnp.float32)
        for row in range(send.shape[0]):
            spot = (mids + 1) * rank + row
            up[spot : spot + 1, : send.shape[1]] = send[row : row + 1, :].astype(jnp.float32)

    point = lax.broadcasted_iota(jnp.int32, (points, ports), 0)
    values = []
    for g in range(group):
        block = jnp.where(
            point < size[step * group + g], charges[g * points : (g + 1) * points, :], 0.0
        )
        values.append(fold(dot(rows_of(basis[g]), lanes_of(block))))
    for g in range(group):
        coef[g] = values[g]
    moved = [fold(dot(rows_of(transfer[g]), lanes_of(values[g]))) for g in range(group)]
    for g in range(group):
        where = pl.ds(pl.multiple_of(parent[step * group + g] * rank, rank), rank)
        up[where, :] += moved[g]

    @pl.when(step == pl.num_programs(0) - 1)
    def _():
        terms = [
            fold(dot(rows_of(mid_transfer[c]), lanes_of(up[c * rank : (c + 1) * rank, :])))
            for c in range(mids)
        ]
        while len(terms) > 1:
            terms = [sum(terms[i : i + 2]) for i in range(0, len(terms), 2)]
        up[mids * rank : (mids + 1) * rank, :] = terms[0]
        per_cluster, per_pair = sizes
        for d, message in enumerate(messages):
            for side in range(2):
                receiver = (group_at[0] ^ d) * per_cluster + (lane_at[0] ^ side)
                for j in range(per_pair):
                    block = jnp.clip(slots[receiver * per_pair + j], 0, mids - 1)
                    source = pl.ds(pl.multiple_of(block * rank, rank), rank)
                    message[(1 - side) * (per_pair + 1) + j] = up[source, :]
            message[per_pair] = terms[0]


def up_sweep(
    sizes, groups, group_at, lane_at, charges, leaf_size, basis, transfer, mid_transfer, leaf_parent, slots
):
    leaves, rank, points = basis.shape
    ports = charges.shape[1]
    mids = mid_transfer.shape[0]
    group = 8
    send_mid = slots.reshape(-1, min(slots.shape[0], ports))
    up_rows = (mids + 1) * rank + -(-send_mid.shape[0] // 8) * 8
    message = (2 * sizes[1] + 1, rank, ports)
    return pl.pallas_call(
        functools.partial(up_kernel, sizes),
        grid_spec=pltpu.PrefetchScalarGridSpec(
            num_scalar_prefetch=5,
            grid=(leaves // group,),
            in_specs=[
                first(group * points, ports),
                first(group, rank, points),
                first(group, rank, rank),
                whole(mid_transfer.shape),
                whole(send_mid.shape),
            ],
            out_specs=[first(group, rank, ports), whole((up_rows, ports))] + [whole(message)] * groups,
        ),
        out_shape=[
            jax.ShapeDtypeStruct((leaves, rank, ports), jnp.float32),
            jax.ShapeDtypeStruct((up_rows, ports), jnp.float32),
        ]
        + [jax.ShapeDtypeStruct(message, jnp.float32)] * groups,
        compiler_params=params(60 * MIB),
        cost_estimate=cost(10**9, 10**7),
        name="up_sweep",
    )(
        leaf_size, leaf_parent, slots, group_at, lane_at, charges, basis, transfer, mid_transfer, send_mid
    )


def spread_kernel(send, coef, out):
    leaves = coef.shape[0]

    @pl.loop(0, out.shape[0], unroll=8)
    def _(slot):
        out[slot] = coef[jnp.minimum(send[slot], leaves - 1)]


def spread(send_leaf, coef):
    vmem = pl.BlockSpec(memory_space=pltpu.VMEM)
    shape = (send_leaf.shape[0],) + coef.shape[1:]
    return pl.pallas_call(
        spread_kernel,
        in_specs=[pl.BlockSpec(memory_space=pltpu.SMEM), vmem],
        out_specs=vmem,
        out_shape=jax.ShapeDtypeStruct(shape, jnp.float32),
        compiler_params=params(60 * MIB),
        cost_estimate=cost(0, 4 * 10**6),
        name="spread",
    )(send_leaf, coef)


def select_kernel(sizes, group_at, lane_at, *refs):
    lines, per_cluster, up_rows, mids, rank, per_pair, groups = sizes
    received, messages = refs[:lines], refs[lines : lines + groups]
    payloads, tables, sem, table_sem = refs[lines + groups :]
    group, lane = group_at[0], lane_at[0]
    table_rows = up_rows - (mids + 1) * rank
    ports = payloads.shape[2]
    copies = []
    for line, ref in enumerate(received):
        table = ref.at[pl.ds((mids + 1) * rank, table_rows), :]
        copies.append(pltpu.make_async_copy(table, tables.at[line], table_sem.at[line]))
        copies.append(pltpu.make_async_copy(ref, payloads.at[line], sem.at[line]))
    for copy in copies:
        copy.start()
    for copy in copies:
        copy.wait()
    for d, message in enumerate(messages):
        for side in range(2):
            receiver = (group ^ d) * per_cluster + (lane ^ side)

            @pl.loop(0, lines, unroll=min(lines, 4))
            def _(line):
                for j in range(per_pair):
                    entry = receiver * per_pair + j
                    listed = tables[line, lax.div(entry, ports), lax.rem(entry, ports)]
                    block = jnp.clip(listed.astype(jnp.int32), 0, mids - 1)
                    target = (1 - side) * (per_pair + 1) * lines + line * per_pair + j
                    message[target] = payloads[line, pl.ds(pl.multiple_of(block * rank, 8), rank), :]

        for line in range(lines):
            message[lines * per_pair + line] = payloads[line, mids * rank : (mids + 1) * rank, :]


def select(sizes, group_at, lane_at, received):
    lines, per_cluster, up_rows, mids, rank, per_pair, groups = sizes
    ports = received[0].shape[1]
    table_rows = up_rows - (mids + 1) * rank
    payloads = (lines, up_rows, ports)
    shape = jax.ShapeDtypeStruct((lines * (2 * per_pair + 1), rank, ports), jnp.float32)
    return pl.pallas_call(
        functools.partial(select_kernel, sizes),
        in_specs=[pl.BlockSpec(memory_space=pltpu.SMEM)] * 2
        + [pl.BlockSpec(memory_space=pl.ANY)] * len(received),
        out_specs=[pl.BlockSpec(memory_space=pltpu.VMEM)] * groups,
        out_shape=[shape] * groups,
        scratch_shapes=[
            pltpu.VMEM(payloads, jnp.float32),
            pltpu.SMEM((lines, table_rows, ports), jnp.float32),
            pltpu.SemaphoreType.DMA((lines,)),
            pltpu.SemaphoreType.DMA((lines,)),
        ],
        compiler_params=params(60 * MIB),
        cost_estimate=cost(0, 4 * 10**6),
        name="select",
    )(group_at, lane_at, *received)


def prepare_kernel(after, coupling, basis, transfer, mid_coupling, mid_transfer, wide, basis_t, mid_wide):
    for g in range(coupling.shape[0]):
        wide[g] = rows_of(jnp.concatenate([coupling[g], transfer[g].T], axis=1))
        basis_t[g] = rows_of(basis[g]).T
    for g in range(mid_coupling.shape[0]):
        mid_wide[g] = rows_of(jnp.concatenate([mid_coupling[g], mid_transfer[g].T], axis=1))


def prepare(after, coupling, basis, transfer, mid_coupling, mid_transfer):
    leaves, rank, width = coupling.shape
    points = basis.shape[2]
    mids, _, mid_width = mid_coupling.shape
    steps = mids
    group = leaves // steps
    shapes = [
        (leaves, 2 * rank, width + rank),
        (leaves, points, 2 * rank),
        (mids, 2 * rank, mid_width + rank),
    ]
    return pl.pallas_call(
        prepare_kernel,
        grid=(steps,),
        in_specs=[
            pl.BlockSpec(memory_space=pl.ANY),
            first(group, rank, width),
            first(group, rank, points),
            first(group, rank, rank),
            first(1, rank, mid_width),
            first(1, rank, rank),
        ],
        out_specs=[first(s[0] // steps, *s[1:]) for s in shapes],
        out_shape=[jax.ShapeDtypeStruct(s, jnp.bfloat16) for s in shapes],
        compiler_params=params(60 * MIB),
        cost_estimate=cost(0, 3 * 10**7),
        name="prepare",
    )(after, coupling, basis, transfer, mid_coupling, mid_transfer)


def tail_kernel(sizes, parent, pair, position, tops, size, pair_leaf, *refs):
    bounds, per_pair, groups, chunk, group, ahead = sizes
    lines, count = bounds[-1], (len(bounds) - 1) * groups
    messages = refs[: 2 * count]
    arrived, mid_wide, top_coupling, wide, basis, out = refs[2 * count : 2 * count + 6]
    scratch = refs[2 * count + 6 :]
    held_messages, scratch = scratch[: 2 * count], scratch[2 * count :]
    (
        arrived_held, mid_wide_held, top_held, wide_held, basis_held, parts, top_parts, leaf_parts, out_held,
        message_sem, arrived_sem, mid_sem, top_sem, wide_sem, basis_sem, out_sem,
    ) = scratch
    mids, leaves, points = mid_wide.shape[0], wide.shape[0], basis.shape[1]
    slots, top_count = arrived.shape[0], top_parts.shape[0] - 1
    ports = out.shape[1]
    steps, chunks = leaves // group, slots // chunk

    def fetch_message(index):
        held = held_messages[index]
        start = 0 if index >= count else messages[index].shape[0] - held.shape[0]
        source = messages[index].at[pl.ds(start, held.shape[0])]
        return pltpu.make_async_copy(source, held, message_sem.at[index])

    def fetch_arrived(index):
        source = arrived.at[pl.ds(index * chunk, chunk)]
        return pltpu.make_async_copy(source, arrived_held.at[index % 2], arrived_sem.at[index % 2])

    def fetch_mid(c):
        return pltpu.make_async_copy(mid_wide.at[c], mid_wide_held.at[c], mid_sem.at[c])

    def fetch_leaves(index):
        some = pl.ds(index * group, group)
        return (
            pltpu.make_async_copy(wide.at[some], wide_held.at[some], wide_sem.at[index]),
            pltpu.make_async_copy(basis.at[some], basis_held.at[some], basis_sem.at[index]),
        )

    fetch_top = pltpu.make_async_copy(top_coupling.at[position[0]], top_held, top_sem)
    for index in range(min(2, chunks)):
        fetch_arrived(index).start()
    for c in range(mids // 2):
        fetch_mid(c).start()
    for index in range(2 * count):
        fetch_message(index).start()
    fetch_top.start()
    for c in range(mids // 2, mids):
        fetch_mid(c).start()

    leaf_parts[slots] = jnp.zeros(leaf_parts.shape[1:], jnp.bfloat16)
    parts[slots] = jnp.zeros(parts.shape[1:], jnp.bfloat16)
    top_parts[top_count] = jnp.zeros(top_parts.shape[1:], jnp.bfloat16)
    for index in range(chunks):
        fetch_arrived(index).wait()
        @pl.loop(0, chunk, unroll=8)
        def _(slot):
            leaf_parts[index * chunk + slot] = lanes_of(arrived_held[index % 2, slot])

        if index + 2 < chunks:
            fetch_arrived(index + 2).start()

    for index in range(2 * count):
        side, message = divmod(index, count)
        batch, d = divmod(message, groups)
        lines_held = bounds[batch + 1] - bounds[batch]
        piece = lines_held * per_pair
        base = (d * 2 + side) * lines + bounds[batch]
        held = held_messages[index]
        first_slot, first_top = (lines_held, 0) if side == 0 else (0, piece)
        fetch_message(index).wait()

        @pl.loop(0, piece, unroll=min(piece, 6))
        def _(slot):
            parts[base * per_pair + slot] = lanes_of(held[first_slot + slot])

        for line in range(lines_held):
            top_parts[base + line] = lanes_of(held[first_top + line])

    for index in range(ahead):
        for copy in fetch_leaves(index):
            copy.start()
    fetch_top.wait()
    stacked = jnp.concatenate([top_parts[tops[k]] for k in range(tops.shape[0])], axis=0)
    parts[slots + 1] = lanes_of(fold(dot(rows_of(top_held[...]), stacked)))
    for c in range(mids):
        fetch_mid(c).wait()

    @pl.loop(0, mids, step=4)
    def _(start):
        values = []
        for g in range(4):
            blocks = [parts[pair[start + g, k]] for k in range(pair.shape[1])] + [parts[slots + 1]]
            values.append(fold(dot(mid_wide_held[start + g], jnp.concatenate(blocks, axis=0))))
        for g in range(4):
            leaf_parts[slots + 1 + start + g] = lanes_of(values[g])

    point = lax.broadcasted_iota(jnp.int32, (points, ports), 0)

    def send(index):
        rows = group * points
        target = out.at[pl.ds(index * rows, rows), :]
        return pltpu.make_async_copy(out_held.at[index % 2], target, out_sem.at[index % 2])

    for index in range(steps):
        if index + ahead < steps:
            for copy in fetch_leaves(index + ahead):
                copy.start()
        for copy in fetch_leaves(index):
            copy.wait()
        values = []
        for g in range(group):
            leaf = index * group + g
            blocks = [leaf_parts[pair_leaf[leaf, k]] for k in range(pair_leaf.shape[1])]
            blocks.append(leaf_parts[slots + 1 + parent[leaf]])
            values.append(fold(dot(wide_held[leaf], jnp.concatenate(blocks, axis=0))))
        if index >= 2:
            send(index - 2).wait()
        for g in range(group):
            far = deep_dot(basis_held[index * group + g], values[g])
            far = jnp.where(point < size[index * group + g], far, 0.0)
            out_held[index % 2, g * points : (g + 1) * points, :] = far
        send(index).start()
    for index in range(max(0, steps - 2), steps):
        send(index).wait()


def tail(
    bounds, per_pair, groups, parent, pair, position, tops, size, pair_leaf, near_side, far_side, arrived,
    mid_wide, top_coupling, wide, basis
):
    mids = mid_wide.shape[0]
    leaves, points, _ = basis.shape
    slots, rank, ports = arrived.shape
    owners = slots // per_pair
    group, chunk, ahead = 4, min(slots, 32), 3
    held = []
    for message in range(len(near_side)):
        batch = message // groups
        held.append((bounds[batch + 1] - bounds[batch]) * (per_pair + 1))
    full, half = jnp.float32, jnp.bfloat16
    scratch = [((h, rank, ports), full) for h in held + held] + [
        ((2, chunk, rank, ports), full),
        (mid_wide.shape, half),
        (top_coupling.shape[1:], full),
        (wide.shape, half),
        (basis.shape, half),
        ((slots + 2, rank, 2 * ports), half),
        ((owners + 1, rank, 2 * ports), half),
        ((slots + 1 + mids, rank, 2 * ports), half),
        ((2, group * points, ports), full),
    ]
    semaphores = [(2 * len(near_side),), (2,), (mids,), (), (leaves // group,), (leaves // group,), (2,)]
    scalars = (parent, pair, position, tops, size, pair_leaf)
    pin = functools.partial(pltpu.with_memory_space_constraint, memory_space=pltpu.HBM)
    matrices = (mid_wide, top_coupling, wide, basis)
    arrays = (*map(pin, near_side), *map(pin, far_side), arrived, *map(pin, matrices))
    used = sum(jnp.dtype(dtype).itemsize * math.prod(shape) for shape, dtype in scratch)
    return pl.pallas_call(
        functools.partial(tail_kernel, (bounds, per_pair, groups, chunk, group, ahead)),
        in_specs=[pl.BlockSpec(memory_space=pltpu.SMEM)] * len(scalars)
        + [pl.BlockSpec(memory_space=pl.ANY)] * len(arrays),
        out_specs=pl.BlockSpec(memory_space=pl.ANY),
        out_shape=jax.ShapeDtypeStruct((leaves * points, ports), full),
        scratch_shapes=[pltpu.VMEM(shape, dtype) for shape, dtype in scratch]
        + [pltpu.SemaphoreType.DMA(n) for n in semaphores],
        compiler_params=params(min(60 * MIB, used + 6 * MIB)),
        cost_estimate=cost(6 * 10**9, 2 * 10**7),
        name="tail",
    )(*scalars, *arrays)


def body(
    charges, leaf_size, leaf_basis, leaf_transfer, mid_transfer, leaf_parent, send_leaf, pair_leaf,
    leaf_coupling, send_mid, pair_mid, mid_coupling, top_pairs, top_coupling,
):
    rank = leaf_basis.shape[1]
    ports = charges.shape[1]
    mids = mid_transfer.shape[0]
    slots = send_mid.shape[0]
    groups, per_cluster = lax.axis_size("group"), lax.axis_size("cluster")
    owners = groups * per_cluster
    lines = per_cluster // 2
    per_pair = slots // owners
    group, lane = lax.axis_index("group"), lax.axis_index("cluster")

    group_at, lane_at = group.astype(jnp.int32)[None], lane.astype(jnp.int32)[None]
    coef, lifted, *own_messages = up_sweep(
        (per_cluster, per_pair), groups, group_at, lane_at, charges, leaf_size, leaf_basis,
        leaf_transfer, mid_transfer, leaf_parent, send_mid,
    )
    up_rows = lifted.shape[0]
    outgoing = spread(send_leaf, coef)

    received = [lifted] * lines
    for d in range(lines - 1, 0, -1):
        received[d] = lax.ppermute(lifted, "cluster", [(c, c ^ (2 * d)) for c in range(per_cluster)])
    wide, basis_t, mid_wide = prepare(
        lifted, leaf_coupling, leaf_basis, leaf_transfer, mid_coupling, mid_transfer
    )

    def spot_of(sender):
        at_group, at_lane = sender // per_cluster, sender % per_cluster
        line = (at_lane // 2) ^ (lane // 2)
        return ((at_group ^ group) * 2 + ((at_lane ^ lane) & 1)) * lines + line

    spot = spot_of(pair_mid // per_pair) * per_pair + pair_mid % per_pair
    spot = jnp.where((pair_mid >= 0) & (pair_mid < slots), spot, slots)
    wanted = lax.dynamic_slice_in_dim(top_pairs, lane, 1, 0)[0]
    tops = jnp.where((wanted >= 0) & (wanted < owners), spot_of(wanted), owners)

    own_messages, received[-1] = lax.optimization_barrier((own_messages, received[-1]))
    bounds = (0, 1, lines)
    swap = [(c, c ^ 1) for c in range(per_cluster)]
    near_side, far_side = [], []
    for low, high in zip(bounds[:-1], bounds[1:]):
        sizes = (high - low, per_cluster, up_rows, mids, rank, per_pair, groups)
        messages = own_messages if low == 0 else select(sizes, group_at, lane_at, received[low:high])
        moved = [messages[0]]
        for d in range(1, groups):
            moved.append(lax.ppermute(messages[d], "group", [(g, g ^ d) for g in range(groups)]))
        if high < lines:
            near_side += moved
        if low == 0:
            outgoing, near_side, received[1:] = lax.optimization_barrier(
                (outgoing, near_side, received[1:])
            )
            arrived = lax.all_to_all(outgoing, AXES, split_axis=0, concat_axis=0, tiled=True)
            far_side = [lax.ppermute(m, "cluster", swap) for m in near_side]
        if high == lines:
            ready = (moved, far_side, mid_wide, spot, tops, pair_leaf)
            moved, far_side, mid_wide, spot, tops, pair_leaf = lax.optimization_barrier(ready)
            near_side += moved
            far_side += [lax.ppermute(m, "cluster", swap) for m in moved]

    return tail(
        bounds, per_pair, groups, leaf_parent, spot, lane_at, tops, leaf_size, pair_leaf, near_side,
        far_side, arrived, mid_wide, top_coupling, wide, basis_t,
    )


def solution(mesh):
    both = P(AXES)
    in_specs = (
        P(AXES, None),
        both,
        P(AXES, None, None),
        P(AXES, None, None),
        P(AXES, None, None),
        both,
        both,
        P(AXES, None),
        P(AXES, None, None),
        both,
        P(AXES, None),
        P(AXES, None, None),
        P("group", None),
        P("group", None, None),
    )
    return jax.shard_map(
        body, mesh=mesh, in_specs=in_specs, out_specs=P(AXES, None), check_vma=False
    )
```

```python
import functools
import math

import jax
import jax.numpy as jnp
from jax import lax
from jax.experimental import pallas as pl
from jax.experimental.pallas import tpu as pltpu
from jax.sharding import PartitionSpec as P

AXES = ("group", "cluster")
MIB = 1024 * 1024


def params(size):
    return pltpu.CompilerParams(vmem_limit_bytes=size)


def cost(flops, size):
    return pl.CostEstimate(flops=flops, bytes_accessed=size, transcendentals=0)


def whole(shape):
    return pl.BlockSpec(shape, lambda i, *_: (0,) * len(shape), pipeline_mode=pl.Buffered(1))


def first(group, *rest):
    return pl.BlockSpec((group,) + rest, lambda i, *_: (i,) + (0,) * len(rest))


def split(x):
    high = x.astype(jnp.bfloat16)
    low = (x - high.astype(jnp.float32)).astype(jnp.bfloat16)
    return high, low


def rows_of(x):
    return jnp.concatenate(split(x), axis=0)


def lanes_of(x):
    return jnp.concatenate(split(x), axis=1)


def dot(a, b):
    return lax.dot_general(a, b, (((1,), (0,)), ((), ())), preferred_element_type=jnp.float32)


def fold(product):
    m, n = product.shape[0] // 2, product.shape[1] // 2
    return product[:m, :n] + (product[:m, n:] + product[m:, :n] + product[m:, n:])


def deep_dot(a, b):
    high, low = split(b)
    return dot(jnp.concatenate([a, a], axis=1), jnp.concatenate([high, high, low, low], axis=0))


def up_kernel(
    sizes, size, parent, slots, group_at, lane_at, charges, basis, transfer, mid_transfer, send, coef, up,
    *messages
):
    step = pl.program_id(0)
    group, rank, points = basis.shape
    mids = mid_transfer.shape[0]
    ports = up.shape[1]

    @pl.when(step == 0)
    def _():
        up[: mids * rank, :] = jnp.zeros((mids * rank, ports), jnp.float32)
        up[(mids + 1) * rank :, :] = jnp.zeros((up.shape[0] - (mids + 1) * rank, ports), jnp.float32)
        for row in range(send.shape[0]):
            spot = (mids + 1) * rank + row
            up[spot : spot + 1, : send.shape[1]] = send[row : row + 1, :].astype(jnp.float32)

    point = lax.broadcasted_iota(jnp.int32, (points, ports), 0)
    values = []
    for g in range(group):
        block = jnp.where(
            point < size[step * group + g], charges[g * points : (g + 1) * points, :], 0.0
        )
        values.append(fold(dot(rows_of(basis[g]), lanes_of(block))))
    for g in range(group):
        coef[g] = values[g]
    moved = [fold(dot(rows_of(transfer[g]), lanes_of(values[g]))) for g in range(group)]
    for g in range(group):
        where = pl.ds(pl.multiple_of(parent[step * group + g] * rank, rank), rank)
        up[where, :] += moved[g]

    @pl.when(step == pl.num_programs(0) - 1)
    def _():
        terms = [
            fold(dot(rows_of(mid_transfer[c]), lanes_of(up[c * rank : (c + 1) * rank, :])))
            for c in range(mids)
        ]
        while len(terms) > 1:
            terms = [sum(terms[i : i + 2]) for i in range(0, len(terms), 2)]
        up[mids * rank : (mids + 1) * rank, :] = terms[0]
        per_cluster, per_pair = sizes
        for d, message in enumerate(messages):
            for side in range(2):
                receiver = (group_at[0] ^ d) * per_cluster + (lane_at[0] ^ side)
                for j in range(per_pair):
                    block = jnp.clip(slots[receiver * per_pair + j], 0, mids - 1)
                    source = pl.ds(pl.multiple_of(block * rank, rank), rank)
                    message[(1 - side) * (per_pair + 1) + j] = up[source, :]
            message[per_pair] = terms[0]


def up_sweep(
    sizes, groups, group_at, lane_at, charges, leaf_size, basis, transfer, mid_transfer, leaf_parent, slots
):
    leaves, rank, points = basis.shape
    ports = charges.shape[1]
    mids = mid_transfer.shape[0]
    group = 8
    send_mid = slots.reshape(-1, min(slots.shape[0], ports))
    up_rows = (mids + 1) * rank + -(-send_mid.shape[0] // 8) * 8
    message = (2 * sizes[1] + 1, rank, ports)
    return pl.pallas_call(
        functools.partial(up_kernel, sizes),
        grid_spec=pltpu.PrefetchScalarGridSpec(
            num_scalar_prefetch=5,
            grid=(leaves // group,),
            in_specs=[
                first(group * points, ports),
                first(group, rank, points),
                first(group, rank, rank),
                whole(mid_transfer.shape),
                whole(send_mid.shape),
            ],
            out_specs=[first(group, rank, ports), whole((up_rows, ports))] + [whole(message)] * groups,
        ),
        out_shape=[
            jax.ShapeDtypeStruct((leaves, rank, ports), jnp.float32),
            jax.ShapeDtypeStruct((up_rows, ports), jnp.float32),
        ]
        + [jax.ShapeDtypeStruct(message, jnp.float32)] * groups,
        compiler_params=params(60 * MIB),
        cost_estimate=cost(10**9, 10**7),
        name="up_sweep",
    )(
        leaf_size, leaf_parent, slots, group_at, lane_at, charges, basis, transfer, mid_transfer, send_mid
    )


def spread_kernel(send, coef, out):
    leaves = coef.shape[0]

    @pl.loop(0, out.shape[0], unroll=8)
    def _(slot):
        out[slot] = coef[jnp.minimum(send[slot], leaves - 1)]


def spread(send_leaf, coef):
    vmem = pl.BlockSpec(memory_space=pltpu.VMEM)
    shape = (send_leaf.shape[0],) + coef.shape[1:]
    return pl.pallas_call(
        spread_kernel,
        in_specs=[pl.BlockSpec(memory_space=pltpu.SMEM), vmem],
        out_specs=vmem,
        out_shape=jax.ShapeDtypeStruct(shape, jnp.float32),
        compiler_params=params(60 * MIB),
        cost_estimate=cost(0, 4 * 10**6),
        name="spread",
    )(send_leaf, coef)


def select_kernel(sizes, group_at, lane_at, *refs):
    lines, per_cluster, up_rows, mids, rank, per_pair, groups = sizes
    received, messages = refs[:lines], refs[lines : lines + groups]
    payloads, tables, sem, table_sem = refs[lines + groups :]
    group, lane = group_at[0], lane_at[0]
    table_rows = up_rows - (mids + 1) * rank
    ports = payloads.shape[2]
    copies = []
    for line, ref in enumerate(received):
        table = ref.at[pl.ds((mids + 1) * rank, table_rows), :]
        copies.append(pltpu.make_async_copy(table, tables.at[line], table_sem.at[line]))
        copies.append(pltpu.make_async_copy(ref, payloads.at[line], sem.at[line]))
    for copy in copies:
        copy.start()
    for copy in copies:
        copy.wait()
    for d, message in enumerate(messages):
        for side in range(2):
            receiver = (group ^ d) * per_cluster + (lane ^ side)

            @pl.loop(0, lines, unroll=min(lines, 4))
            def _(line):
                for j in range(per_pair):
                    entry = receiver * per_pair + j
                    listed = tables[line, lax.div(entry, ports), lax.rem(entry, ports)]
                    block = jnp.clip(listed.astype(jnp.int32), 0, mids - 1)
                    target = (1 - side) * (per_pair + 1) * lines + line * per_pair + j
                    message[target] = payloads[line, pl.ds(pl.multiple_of(block * rank, 8), rank), :]

        for line in range(lines):
            message[lines * per_pair + line] = payloads[line, mids * rank : (mids + 1) * rank, :]


def select(sizes, group_at, lane_at, received):
    lines, per_cluster, up_rows, mids, rank, per_pair, groups = sizes
    ports = received[0].shape[1]
    table_rows = up_rows - (mids + 1) * rank
    payloads = (lines, up_rows, ports)
    shape = jax.ShapeDtypeStruct((lines * (2 * per_pair + 1), rank, ports), jnp.float32)
    return pl.pallas_call(
        functools.partial(select_kernel, sizes),
        in_specs=[pl.BlockSpec(memory_space=pltpu.SMEM)] * 2
        + [pl.BlockSpec(memory_space=pl.ANY)] * len(received),
        out_specs=[pl.BlockSpec(memory_space=pltpu.VMEM)] * groups,
        out_shape=[shape] * groups,
        scratch_shapes=[
            pltpu.VMEM(payloads, jnp.float32),
            pltpu.SMEM((lines, table_rows, ports), jnp.float32),
            pltpu.SemaphoreType.DMA((lines,)),
            pltpu.SemaphoreType.DMA((lines,)),
        ],
        compiler_params=params(60 * MIB),
        cost_estimate=cost(0, 4 * 10**6),
        name="select",
    )(group_at, lane_at, *received)


def prepare_kernel(after, coupling, basis, transfer, mid_coupling, mid_transfer, wide, basis_t, mid_wide):
    for g in range(coupling.shape[0]):
        wide[g] = rows_of(jnp.concatenate([coupling[g], transfer[g].T], axis=1))
        basis_t[g] = rows_of(basis[g]).T
    for g in range(mid_coupling.shape[0]):
        mid_wide[g] = rows_of(jnp.concatenate([mid_coupling[g], mid_transfer[g].T], axis=1))


def prepare(after, coupling, basis, transfer, mid_coupling, mid_transfer):
    leaves, rank, width = coupling.shape
    points = basis.shape[2]
    mids, _, mid_width = mid_coupling.shape
    steps = mids
    group = leaves // steps
    shapes = [
        (leaves, 2 * rank, width + rank),
        (leaves, points, 2 * rank),
        (mids, 2 * rank, mid_width + rank),
    ]
    return pl.pallas_call(
        prepare_kernel,
        grid=(steps,),
        in_specs=[
            pl.BlockSpec(memory_space=pl.ANY),
            first(group, rank, width),
            first(group, rank, points),
            first(group, rank, rank),
            first(1, rank, mid_width),
            first(1, rank, rank),
        ],
        out_specs=[first(s[0] // steps, *s[1:]) for s in shapes],
        out_shape=[jax.ShapeDtypeStruct(s, jnp.bfloat16) for s in shapes],
        compiler_params=params(60 * MIB),
        cost_estimate=cost(0, 3 * 10**7),
        name="prepare",
    )(after, coupling, basis, transfer, mid_coupling, mid_transfer)


def tail_kernel(sizes, parent, pair, position, tops, size, pair_leaf, *refs):
    bounds, per_pair, groups, chunk, group, ahead = sizes
    lines, count = bounds[-1], (len(bounds) - 1) * groups
    messages = refs[: 2 * count]
    arrived, mid_wide, top_coupling, wide, basis, out = refs[2 * count : 2 * count + 6]
    scratch = refs[2 * count + 6 :]
    held_messages, scratch = scratch[: 2 * count], scratch[2 * count :]
    (
        arrived_held, mid_wide_held, top_held, wide_held, basis_held, parts, top_parts, leaf_parts, out_held,
        message_sem, arrived_sem, mid_sem, top_sem, wide_sem, basis_sem, out_sem,
    ) = scratch
    mids, leaves, points = mid_wide.shape[0], wide.shape[0], basis.shape[1]
    slots, top_count = arrived.shape[0], top_parts.shape[0] - 1
    ports = out.shape[1]
    steps, chunks = leaves // group, slots // chunk

    def fetch_message(index):
        held = held_messages[index]
        start = 0 if index >= count else messages[index].shape[0] - held.shape[0]
        source = messages[index].at[pl.ds(start, held.shape[0])]
        return pltpu.make_async_copy(source, held, message_sem.at[index])

    def fetch_arrived(index):
        source = arrived.at[pl.ds(index * chunk, chunk)]
        return pltpu.make_async_copy(source, arrived_held.at[index % 2], arrived_sem.at[index % 2])

    def fetch_mid(c):
        return pltpu.make_async_copy(mid_wide.at[c], mid_wide_held.at[c], mid_sem.at[c])

    def fetch_leaves(index):
        some = pl.ds(index * group, group)
        return (
            pltpu.make_async_copy(wide.at[some], wide_held.at[some], wide_sem.at[index]),
            pltpu.make_async_copy(basis.at[some], basis_held.at[some], basis_sem.at[index]),
        )

    fetch_top = pltpu.make_async_copy(top_coupling.at[position[0]], top_held, top_sem)
    for index in range(min(2, chunks)):
        fetch_arrived(index).start()
    for c in range(mids // 2):
        fetch_mid(c).start()
    for index in range(2 * count):
        fetch_message(index).start()
    fetch_top.start()
    for c in range(mids // 2, mids):
        fetch_mid(c).start()

    leaf_parts[slots] = jnp.zeros(leaf_parts.shape[1:], jnp.bfloat16)
    parts[slots] = jnp.zeros(parts.shape[1:], jnp.bfloat16)
    top_parts[top_count] = jnp.zeros(top_parts.shape[1:], jnp.bfloat16)
    for index in range(chunks):
        fetch_arrived(index).wait()
        @pl.loop(0, chunk, unroll=8)
        def _(slot):
            leaf_parts[index * chunk + slot] = lanes_of(arrived_held[index % 2, slot])

        if index + 2 < chunks:
            fetch_arrived(index + 2).start()

    for index in range(2 * count):
        side, message = divmod(index, count)
        batch, d = divmod(message, groups)
        lines_held = bounds[batch + 1] - bounds[batch]
        piece = lines_held * per_pair
        base = (d * 2 + side) * lines + bounds[batch]
        held = held_messages[index]
        first_slot, first_top = (lines_held, 0) if side == 0 else (0, piece)
        fetch_message(index).wait()

        @pl.loop(0, piece, unroll=min(piece, 6))
        def _(slot):
            parts[base * per_pair + slot] = lanes_of(held[first_slot + slot])

        for line in range(lines_held):
            top_parts[base + line] = lanes_of(held[first_top + line])

    for index in range(ahead):
        for copy in fetch_leaves(index):
            copy.start()
    fetch_top.wait()
    stacked = jnp.concatenate([top_parts[tops[k]] for k in range(tops.shape[0])], axis=0)
    parts[slots + 1] = lanes_of(fold(dot(rows_of(top_held[...]), stacked)))
    for c in range(mids):
        fetch_mid(c).wait()

    @pl.loop(0, mids, step=4)
    def _(start):
        values = []
        for g in range(4):
            blocks = [parts[pair[start + g, k]] for k in range(pair.shape[1])] + [parts[slots + 1]]
            values.append(fold(dot(mid_wide_held[start + g], jnp.concatenate(blocks, axis=0))))
        for g in range(4):
            leaf_parts[slots + 1 + start + g] = lanes_of(values[g])

    point = lax.broadcasted_iota(jnp.int32, (points, ports), 0)

    def send(index):
        rows = group * points
        target = out.at[pl.ds(index * rows, rows), :]
        return pltpu.make_async_copy(out_held.at[index % 2], target, out_sem.at[index % 2])

    for index in range(steps):
        if index + ahead < steps:
            for copy in fetch_leaves(index + ahead):
                copy.start()
        for copy in fetch_leaves(index):
            copy.wait()
        values = []
        for g in range(group):
            leaf = index * group + g
            blocks = [leaf_parts[pair_leaf[leaf, k]] for k in range(pair_leaf.shape[1])]
            blocks.append(leaf_parts[slots + 1 + parent[leaf]])
            values.append(fold(dot(wide_held[leaf], jnp.concatenate(blocks, axis=0))))
        if index >= 2:
            send(index - 2).wait()
        for g in range(group):
            far = deep_dot(basis_held[index * group + g], values[g])
            far = jnp.where(point < size[index * group + g], far, 0.0)
            out_held[index % 2, g * points : (g + 1) * points, :] = far
        send(index).start()
    for index in range(max(0, steps - 2), steps):
        send(index).wait()


def tail(
    bounds, per_pair, groups, parent, pair, position, tops, size, pair_leaf, near_side, far_side, arrived,
    mid_wide, top_coupling, wide, basis
):
    mids = mid_wide.shape[0]
    leaves, points, _ = basis.shape
    slots, rank, ports = arrived.shape
    owners = slots // per_pair
    group, chunk, ahead = 4, min(slots, 32), 3
    held = []
    for message in range(len(near_side)):
        batch = message // groups
        held.append((bounds[batch + 1] - bounds[batch]) * (per_pair + 1))
    full, half = jnp.float32, jnp.bfloat16
    scratch = [((h, rank, ports), full) for h in held + held] + [
        ((2, chunk, rank, ports), full),
        (mid_wide.shape, half),
        (top_coupling.shape[1:], full),
        (wide.shape, half),
        (basis.shape, half),
        ((slots + 2, rank, 2 * ports), half),
        ((owners + 1, rank, 2 * ports), half),
        ((slots + 1 + mids, rank, 2 * ports), half),
        ((2, group * points, ports), full),
    ]
    semaphores = [(2 * len(near_side),), (2,), (mids,), (), (leaves // group,), (leaves // group,), (2,)]
    scalars = (parent, pair, position, tops, size, pair_leaf)
    pin = functools.partial(pltpu.with_memory_space_constraint, memory_space=pltpu.HBM)
    matrices = (mid_wide, top_coupling, wide, basis)
    arrays = (*map(pin, near_side), *map(pin, far_side), arrived, *map(pin, matrices))
    used = sum(jnp.dtype(dtype).itemsize * math.prod(shape) for shape, dtype in scratch)
    return pl.pallas_call(
        functools.partial(tail_kernel, (bounds, per_pair, groups, chunk, group, ahead)),
        in_specs=[pl.BlockSpec(memory_space=pltpu.SMEM)] * len(scalars)
        + [pl.BlockSpec(memory_space=pl.ANY)] * len(arrays),
        out_specs=pl.BlockSpec(memory_space=pl.ANY),
        out_shape=jax.ShapeDtypeStruct((leaves * points, ports), full),
        scratch_shapes=[pltpu.VMEM(shape, dtype) for shape, dtype in scratch]
        + [pltpu.SemaphoreType.DMA(n) for n in semaphores],
        compiler_params=params(min(60 * MIB, used + 6 * MIB)),
        cost_estimate=cost(6 * 10**9, 2 * 10**7),
        name="tail",
    )(*scalars, *arrays)


def body(
    charges, leaf_size, leaf_basis, leaf_transfer, mid_transfer, leaf_parent, send_leaf, pair_leaf,
    leaf_coupling, send_mid, pair_mid, mid_coupling, top_pairs, top_coupling,
):
    rank = leaf_basis.shape[1]
    ports = charges.shape[1]
    mids = mid_transfer.shape[0]
    slots = send_mid.shape[0]
    groups, per_cluster = lax.axis_size("group"), lax.axis_size("cluster")
    owners = groups * per_cluster
    lines = per_cluster // 2
    per_pair = slots // owners
    group, lane = lax.axis_index("group"), lax.axis_index("cluster")

    group_at, lane_at = group.astype(jnp.int32)[None], lane.astype(jnp.int32)[None]
    coef, lifted, *own_messages = up_sweep(
        (per_cluster, per_pair), groups, group_at, lane_at, charges, leaf_size, leaf_basis,
        leaf_transfer, mid_transfer, leaf_parent, send_mid,
    )
    up_rows = lifted.shape[0]
    outgoing = spread(send_leaf, coef)

    received = [lifted] * lines
    for d in range(1, lines):
        received[d] = lax.ppermute(lifted, "cluster", [(c, c ^ (2 * d)) for c in range(per_cluster)])
    wide, basis_t, mid_wide = prepare(
        lifted, leaf_coupling, leaf_basis, leaf_transfer, mid_coupling, mid_transfer
    )

    def spot_of(sender):
        at_group, at_lane = sender // per_cluster, sender % per_cluster
        line = (at_lane // 2) ^ (lane // 2)
        return ((at_group ^ group) * 2 + ((at_lane ^ lane) & 1)) * lines + line

    spot = spot_of(pair_mid // per_pair) * per_pair + pair_mid % per_pair
    spot = jnp.where((pair_mid >= 0) & (pair_mid < slots), spot, slots)
    wanted = lax.dynamic_slice_in_dim(top_pairs, lane, 1, 0)[0]
    tops = jnp.where((wanted >= 0) & (wanted < owners), spot_of(wanted), owners)

    own_messages, received[1] = lax.optimization_barrier((own_messages, received[1]))
    bounds = (0, 1, lines)
    swap = [(c, c ^ 1) for c in range(per_cluster)]
    near_side, far_side = [], []
    for low, high in zip(bounds[:-1], bounds[1:]):
        sizes = (high - low, per_cluster, up_rows, mids, rank, per_pair, groups)
        messages = own_messages if low == 0 else select(sizes, group_at, lane_at, received[low:high])
        moved = [messages[0]]
        for d in range(1, groups):
            moved.append(lax.ppermute(messages[d], "group", [(g, g ^ d) for g in range(groups)]))
        if high < lines:
            near_side += moved
        if low == 0:
            outgoing, near_side, received[1:] = lax.optimization_barrier(
                (outgoing, near_side, received[1:])
            )
            arrived = lax.all_to_all(outgoing, AXES, split_axis=0, concat_axis=0, tiled=True)
            far_side = [lax.ppermute(m, "cluster", swap) for m in near_side]
        if high == lines:
            ready = (moved[1], far_side, mid_wide, spot, tops, pair_leaf)
            moved[1], far_side, mid_wide, spot, tops, pair_leaf = lax.optimization_barrier(ready)
            near_side += moved
            far_side += [lax.ppermute(m, "cluster", swap) for m in moved]

    return tail(
        bounds, per_pair, groups, leaf_parent, spot, lane_at, tops, leaf_size, pair_leaf, near_side,
        far_side, arrived, mid_wide, top_coupling, wide, basis_t,
    )


def solution(mesh):
    both = P(AXES)
    in_specs = (
        P(AXES, None),
        both,
        P(AXES, None, None),
        P(AXES, None, None),
        P(AXES, None, None),
        both,
        both,
        P(AXES, None),
        P(AXES, None, None),
        both,
        P(AXES, None),
        P(AXES, None, None),
        P("group", None),
        P("group", None, None),
    )
    return jax.shard_map(
        body, mesh=mesh, in_specs=in_specs, out_specs=P(AXES, None), check_vma=False
    )
```

```python
import functools
import math

import jax
import jax.numpy as jnp
from jax import lax
from jax.experimental import pallas as pl
from jax.experimental.pallas import tpu as pltpu
from jax.sharding import PartitionSpec as P

AXES = ("group", "cluster")
MIB = 1024 * 1024


def params(size):
    return pltpu.CompilerParams(vmem_limit_bytes=size)


def cost(flops, size):
    return pl.CostEstimate(flops=flops, bytes_accessed=size, transcendentals=0)


def whole(shape):
    return pl.BlockSpec(shape, lambda i, *_: (0,) * len(shape), pipeline_mode=pl.Buffered(1))


def first(group, *rest):
    return pl.BlockSpec((group,) + rest, lambda i, *_: (i,) + (0,) * len(rest))


def split(x):
    high = x.astype(jnp.bfloat16)
    low = (x - high.astype(jnp.float32)).astype(jnp.bfloat16)
    return high, low


def rows_of(x):
    return jnp.concatenate(split(x), axis=0)


def lanes_of(x):
    return jnp.concatenate(split(x), axis=1)


def dot(a, b):
    return lax.dot_general(a, b, (((1,), (0,)), ((), ())), preferred_element_type=jnp.float32)


def fold(product):
    m, n = product.shape[0] // 2, product.shape[1] // 2
    return product[:m, :n] + (product[:m, n:] + product[m:, :n] + product[m:, n:])


def deep_dot(a, b):
    high, low = split(b)
    return dot(jnp.concatenate([a, a], axis=1), jnp.concatenate([high, high, low, low], axis=0))


def up_kernel(
    sizes, size, parent, slots, group_at, lane_at, charges, basis, transfer, mid_transfer, send, coef, up,
    *messages
):
    step = pl.program_id(0)
    group, rank, points = basis.shape
    mids = mid_transfer.shape[0]
    ports = up.shape[1]

    @pl.when(step == 0)
    def _():
        up[: mids * rank, :] = jnp.zeros((mids * rank, ports), jnp.float32)
        up[(mids + 1) * rank :, :] = jnp.zeros((up.shape[0] - (mids + 1) * rank, ports), jnp.float32)
        for row in range(send.shape[0]):
            spot = (mids + 1) * rank + row
            up[spot : spot + 1, : send.shape[1]] = send[row : row + 1, :].astype(jnp.float32)

    point = lax.broadcasted_iota(jnp.int32, (points, ports), 0)
    values = []
    for g in range(group):
        block = jnp.where(
            point < size[step * group + g], charges[g * points : (g + 1) * points, :], 0.0
        )
        values.append(fold(dot(rows_of(basis[g]), lanes_of(block))))
    for g in range(group):
        coef[g] = values[g]
    moved = [fold(dot(rows_of(transfer[g]), lanes_of(values[g]))) for g in range(group)]
    for g in range(group):
        where = pl.ds(pl.multiple_of(parent[step * group + g] * rank, rank), rank)
        up[where, :] += moved[g]

    @pl.when(step == pl.num_programs(0) - 1)
    def _():
        terms = [
            fold(dot(rows_of(mid_transfer[c]), lanes_of(up[c * rank : (c + 1) * rank, :])))
            for c in range(mids)
        ]
        while len(terms) > 1:
            terms = [sum(terms[i : i + 2]) for i in range(0, len(terms), 2)]
        up[mids * rank : (mids + 1) * rank, :] = terms[0]
        per_cluster, per_pair = sizes
        for d, message in enumerate(messages):
            for side in range(2):
                receiver = (group_at[0] ^ d) * per_cluster + (lane_at[0] ^ side)
                for j in range(per_pair):
                    block = jnp.clip(slots[receiver * per_pair + j], 0, mids - 1)
                    source = pl.ds(pl.multiple_of(block * rank, rank), rank)
                    message[(1 - side) * (per_pair + 1) + j] = up[source, :]
            message[per_pair] = terms[0]


def up_sweep(
    sizes, groups, group_at, lane_at, charges, leaf_size, basis, transfer, mid_transfer, leaf_parent, slots
):
    leaves, rank, points = basis.shape
    ports = charges.shape[1]
    mids = mid_transfer.shape[0]
    group = 8
    send_mid = slots.reshape(-1, min(slots.shape[0], ports))
    up_rows = (mids + 1) * rank + -(-send_mid.shape[0] // 8) * 8
    message = (2 * sizes[1] + 1, rank, ports)
    return pl.pallas_call(
        functools.partial(up_kernel, sizes),
        grid_spec=pltpu.PrefetchScalarGridSpec(
            num_scalar_prefetch=5,
            grid=(leaves // group,),
            in_specs=[
                first(group * points, ports),
                first(group, rank, points),
                first(group, rank, rank),
                whole(mid_transfer.shape),
                whole(send_mid.shape),
            ],
            out_specs=[first(group, rank, ports), whole((up_rows, ports))] + [whole(message)] * groups,
        ),
        out_shape=[
            jax.ShapeDtypeStruct((leaves, rank, ports), jnp.float32),
            jax.ShapeDtypeStruct((up_rows, ports), jnp.float32),
        ]
        + [jax.ShapeDtypeStruct(message, jnp.float32)] * groups,
        compiler_params=params(60 * MIB),
        cost_estimate=cost(10**9, 10**7),
        name="up_sweep",
    )(
        leaf_size, leaf_parent, slots, group_at, lane_at, charges, basis, transfer, mid_transfer, send_mid
    )


def spread_kernel(send, coef, out):
    leaves = coef.shape[0]

    @pl.loop(0, out.shape[0], unroll=8)
    def _(slot):
        out[slot] = coef[jnp.minimum(send[slot], leaves - 1)]


def spread(send_leaf, coef):
    vmem = pl.BlockSpec(memory_space=pltpu.VMEM)
    shape = (send_leaf.shape[0],) + coef.shape[1:]
    return pl.pallas_call(
        spread_kernel,
        in_specs=[pl.BlockSpec(memory_space=pltpu.SMEM), vmem],
        out_specs=vmem,
        out_shape=jax.ShapeDtypeStruct(shape, jnp.float32),
        compiler_params=params(60 * MIB),
        cost_estimate=cost(0, 4 * 10**6),
        name="spread",
    )(send_leaf, coef)


def select_kernel(sizes, group_at, lane_at, *refs):
    lines, per_cluster, up_rows, mids, rank, per_pair, groups = sizes
    received, messages = refs[:lines], refs[lines : lines + groups]
    payloads, tables, sem, table_sem = refs[lines + groups :]
    group, lane = group_at[0], lane_at[0]
    table_rows = up_rows - (mids + 1) * rank
    ports = payloads.shape[2]
    copies = []
    for line, ref in enumerate(received):
        table = ref.at[pl.ds((mids + 1) * rank, table_rows), :]
        copies.append(pltpu.make_async_copy(table, tables.at[line], table_sem.at[line]))
        copies.append(pltpu.make_async_copy(ref, payloads.at[line], sem.at[line]))
    for copy in copies:
        copy.start()
    for copy in copies:
        copy.wait()
    for d, message in enumerate(messages):
        for side in range(2):
            receiver = (group ^ d) * per_cluster + (lane ^ side)

            @pl.loop(0, lines, unroll=min(lines, 4))
            def _(line):
                for j in range(per_pair):
                    entry = receiver * per_pair + j
                    listed = tables[line, lax.div(entry, ports), lax.rem(entry, ports)]
                    block = jnp.clip(listed.astype(jnp.int32), 0, mids - 1)
                    target = (1 - side) * (per_pair + 1) * lines + line * per_pair + j
                    message[target] = payloads[line, pl.ds(pl.multiple_of(block * rank, 8), rank), :]

        for line in range(lines):
            message[lines * per_pair + line] = payloads[line, mids * rank : (mids + 1) * rank, :]


def select(sizes, group_at, lane_at, received):
    lines, per_cluster, up_rows, mids, rank, per_pair, groups = sizes
    ports = received[0].shape[1]
    table_rows = up_rows - (mids + 1) * rank
    payloads = (lines, up_rows, ports)
    shape = jax.ShapeDtypeStruct((lines * (2 * per_pair + 1), rank, ports), jnp.float32)
    return pl.pallas_call(
        functools.partial(select_kernel, sizes),
        in_specs=[pl.BlockSpec(memory_space=pltpu.SMEM)] * 2
        + [pl.BlockSpec(memory_space=pl.ANY)] * len(received),
        out_specs=[pl.BlockSpec(memory_space=pltpu.VMEM)] * groups,
        out_shape=[shape] * groups,
        scratch_shapes=[
            pltpu.VMEM(payloads, jnp.float32),
            pltpu.SMEM((lines, table_rows, ports), jnp.float32),
            pltpu.SemaphoreType.DMA((lines,)),
            pltpu.SemaphoreType.DMA((lines,)),
        ],
        compiler_params=params(60 * MIB),
        cost_estimate=cost(0, 4 * 10**6),
        name="select",
    )(group_at, lane_at, *received)


def prepare_kernel(after, coupling, basis, transfer, mid_coupling, mid_transfer, wide, basis_t, mid_wide):
    for g in range(coupling.shape[0]):
        wide[g] = rows_of(jnp.concatenate([coupling[g], transfer[g].T], axis=1))
        basis_t[g] = rows_of(basis[g]).T
    for g in range(mid_coupling.shape[0]):
        mid_wide[g] = rows_of(jnp.concatenate([mid_coupling[g], mid_transfer[g].T], axis=1))


def prepare(after, coupling, basis, transfer, mid_coupling, mid_transfer):
    leaves, rank, width = coupling.shape
    points = basis.shape[2]
    mids, _, mid_width = mid_coupling.shape
    steps = mids
    group = leaves // steps
    shapes = [
        (leaves, 2 * rank, width + rank),
        (leaves, points, 2 * rank),
        (mids, 2 * rank, mid_width + rank),
    ]
    return pl.pallas_call(
        prepare_kernel,
        grid=(steps,),
        in_specs=[
            pl.BlockSpec(memory_space=pl.ANY),
            first(group, rank, width),
            first(group, rank, points),
            first(group, rank, rank),
            first(1, rank, mid_width),
            first(1, rank, rank),
        ],
        out_specs=[first(s[0] // steps, *s[1:]) for s in shapes],
        out_shape=[jax.ShapeDtypeStruct(s, jnp.bfloat16) for s in shapes],
        compiler_params=params(60 * MIB),
        cost_estimate=cost(0, 3 * 10**7),
        name="prepare",
    )(after, coupling, basis, transfer, mid_coupling, mid_transfer)


def tail_kernel(sizes, parent, pair, position, tops, size, pair_leaf, *refs):
    bounds, per_pair, groups, chunk, group, ahead = sizes
    lines, count = bounds[-1], (len(bounds) - 1) * groups
    messages = refs[: 2 * count]
    arrived, mid_wide, top_coupling, wide, basis, out = refs[2 * count : 2 * count + 6]
    scratch = refs[2 * count + 6 :]
    held_messages, scratch = scratch[: 2 * count], scratch[2 * count :]
    (
        arrived_held, mid_wide_held, top_held, wide_held, basis_held, parts, top_parts, leaf_parts, near_top, out_held,
        message_sem, arrived_sem, mid_sem, top_sem, wide_sem, basis_sem, out_sem,
    ) = scratch
    mids, leaves, points = mid_wide.shape[0], wide.shape[0], basis.shape[1]
    slots, top_count = arrived.shape[0], top_parts.shape[0] - 1
    ports = out.shape[1]
    steps, chunks = leaves // group, slots // chunk

    def fetch_message(index):
        held = held_messages[index]
        start = 0 if index >= count else messages[index].shape[0] - held.shape[0]
        source = messages[index].at[pl.ds(start, held.shape[0])]
        return pltpu.make_async_copy(source, held, message_sem.at[index])

    def fetch_arrived(index):
        source = arrived.at[pl.ds(index * chunk, chunk)]
        return pltpu.make_async_copy(source, arrived_held.at[index % 2], arrived_sem.at[index % 2])

    def fetch_mid(c):
        return pltpu.make_async_copy(mid_wide.at[c], mid_wide_held.at[c], mid_sem.at[c])

    def fetch_leaves(index):
        some = pl.ds(index * group, group)
        return (
            pltpu.make_async_copy(wide.at[some], wide_held.at[some], wide_sem.at[index]),
            pltpu.make_async_copy(basis.at[some], basis_held.at[some], basis_sem.at[index]),
        )

    fetch_top = pltpu.make_async_copy(top_coupling.at[position[0]], top_held, top_sem)
    for index in range(min(2, chunks)):
        fetch_arrived(index).start()
    for c in range(mids // 2):
        fetch_mid(c).start()
    for index in range(2 * count):
        fetch_message(index).start()
    fetch_top.start()
    for c in range(mids // 2, mids):
        fetch_mid(c).start()

    leaf_parts[slots] = jnp.zeros(leaf_parts.shape[1:], jnp.bfloat16)
    parts[slots] = jnp.zeros(parts.shape[1:], jnp.bfloat16)
    top_parts[top_count] = jnp.zeros(top_parts.shape[1:], jnp.bfloat16)
    for index in range(chunks):
        fetch_arrived(index).wait()
        @pl.loop(0, chunk, unroll=8)
        def _(slot):
            leaf_parts[index * chunk + slot] = lanes_of(arrived_held[index % 2, slot])

        if index + 2 < chunks:
            fetch_arrived(index + 2).start()

    for index in range(2 * count):
        side, message = divmod(index, count)
        batch, d = divmod(message, groups)
        lines_held = bounds[batch + 1] - bounds[batch]
        piece = lines_held * per_pair
        base = (d * 2 + side) * lines + bounds[batch]
        held = held_messages[index]
        first_slot, first_top = (lines_held, 0) if side == 0 else (0, piece)
        fetch_message(index).wait()

        @pl.loop(0, piece, unroll=min(piece, 6))
        def _(slot):
            parts[base * per_pair + slot] = lanes_of(held[first_slot + slot])

        for line in range(lines_held):
            top_parts[base + line] = lanes_of(held[first_top + line])

    for index in range(ahead):
        for copy in fetch_leaves(index):
            copy.start()
    fetch_top.wait()
    stacked = jnp.concatenate([top_parts[tops[k]] for k in range(tops.shape[0])], axis=0)
    near_top[...] = lanes_of(fold(dot(rows_of(top_held[...]), stacked)))
    for c in range(mids):
        fetch_mid(c).wait()

    for c in range(mids):
        blocks = [parts[pair[c, k]] for k in range(pair.shape[1])] + [near_top[...]]
        value = fold(dot(mid_wide_held[c], jnp.concatenate(blocks, axis=0)))
        leaf_parts[slots + 1 + c] = lanes_of(value)

    point = lax.broadcasted_iota(jnp.int32, (points, ports), 0)

    def send(index):
        rows = group * points
        target = out.at[pl.ds(index * rows, rows), :]
        return pltpu.make_async_copy(out_held.at[index % 2], target, out_sem.at[index % 2])

    before = None
    for index in range(steps + 1):
        values = []
        if index < steps:
            if index + ahead < steps:
                for copy in fetch_leaves(index + ahead):
                    copy.start()
            for copy in fetch_leaves(index):
                copy.wait()
        if index >= 3:
            send(index - 3).wait()
        if index < steps:
            for g in range(group):
                leaf = index * group + g
                blocks = [leaf_parts[pair_leaf[leaf, k]] for k in range(pair_leaf.shape[1])]
                blocks.append(leaf_parts[slots + 1 + parent[leaf]])
                values.append(fold(dot(wide_held[leaf], jnp.concatenate(blocks, axis=0))))
        if before is not None:
            for g in range(group):
                leaf = (index - 1) * group + g
                far = jnp.where(point < size[leaf], deep_dot(basis_held[leaf], before[g]), 0.0)
                out_held[(index - 1) % 2, g * points : (g + 1) * points, :] = far
            send(index - 1).start()
        before = values
    for index in range(max(0, steps - 2), steps):
        send(index).wait()


def tail(
    bounds, per_pair, groups, parent, pair, position, tops, size, pair_leaf, near_side, far_side, arrived,
    mid_wide, top_coupling, wide, basis
):
    mids = mid_wide.shape[0]
    leaves, points, _ = basis.shape
    slots, rank, ports = arrived.shape
    owners = slots // per_pair
    group, chunk, ahead = 4, min(slots, 32), 3
    held = []
    for message in range(len(near_side)):
        batch = message // groups
        held.append((bounds[batch + 1] - bounds[batch]) * (per_pair + 1))
    full, half = jnp.float32, jnp.bfloat16
    scratch = [((h, rank, ports), full) for h in held + held] + [
        ((2, chunk, rank, ports), full),
        (mid_wide.shape, half),
        (top_coupling.shape[1:], full),
        (wide.shape, half),
        (basis.shape, half),
        ((slots + 1, rank, 2 * ports), half),
        ((owners + 1, rank, 2 * ports), half),
        ((slots + 1 + mids, rank, 2 * ports), half),
        ((rank, 2 * ports), half),
        ((2, group * points, ports), full),
    ]
    semaphores = [(2 * len(near_side),), (2,), (mids,), (), (leaves // group,), (leaves // group,), (2,)]
    scalars = (parent, pair, position, tops, size, pair_leaf)
    pin = functools.partial(pltpu.with_memory_space_constraint, memory_space=pltpu.HBM)
    matrices = (mid_wide, top_coupling, wide, basis)
    arrays = (*map(pin, near_side), *map(pin, far_side), arrived, *map(pin, matrices))
    used = sum(jnp.dtype(dtype).itemsize * math.prod(shape) for shape, dtype in scratch)
    return pl.pallas_call(
        functools.partial(tail_kernel, (bounds, per_pair, groups, chunk, group, ahead)),
        in_specs=[pl.BlockSpec(memory_space=pltpu.SMEM)] * len(scalars)
        + [pl.BlockSpec(memory_space=pl.ANY)] * len(arrays),
        out_specs=pl.BlockSpec(memory_space=pl.ANY),
        out_shape=jax.ShapeDtypeStruct((leaves * points, ports), full),
        scratch_shapes=[pltpu.VMEM(shape, dtype) for shape, dtype in scratch]
        + [pltpu.SemaphoreType.DMA(n) for n in semaphores],
        compiler_params=params(min(60 * MIB, used + 6 * MIB)),
        cost_estimate=cost(6 * 10**9, 2 * 10**7),
        name="tail",
    )(*scalars, *arrays)


def body(
    charges, leaf_size, leaf_basis, leaf_transfer, mid_transfer, leaf_parent, send_leaf, pair_leaf,
    leaf_coupling, send_mid, pair_mid, mid_coupling, top_pairs, top_coupling,
):
    rank = leaf_basis.shape[1]
    ports = charges.shape[1]
    mids = mid_transfer.shape[0]
    slots = send_mid.shape[0]
    groups, per_cluster = lax.axis_size("group"), lax.axis_size("cluster")
    owners = groups * per_cluster
    lines = per_cluster // 2
    per_pair = slots // owners
    group, lane = lax.axis_index("group"), lax.axis_index("cluster")

    group_at, lane_at = group.astype(jnp.int32)[None], lane.astype(jnp.int32)[None]
    coef, lifted, *own_messages = up_sweep(
        (per_cluster, per_pair), groups, group_at, lane_at, charges, leaf_size, leaf_basis,
        leaf_transfer, mid_transfer, leaf_parent, send_mid,
    )
    up_rows = lifted.shape[0]
    outgoing = spread(send_leaf, coef)

    received = [lifted] * lines
    for d in range(1, lines):
        received[d] = lax.ppermute(lifted, "cluster", [(c, c ^ (2 * d)) for c in range(per_cluster)])
    wide, basis_t, mid_wide = prepare(
        lifted, leaf_coupling, leaf_basis, leaf_transfer, mid_coupling, mid_transfer
    )

    def spot_of(sender):
        at_group, at_lane = sender // per_cluster, sender % per_cluster
        line = (at_lane // 2) ^ (lane // 2)
        return ((at_group ^ group) * 2 + ((at_lane ^ lane) & 1)) * lines + line

    spot = spot_of(pair_mid // per_pair) * per_pair + pair_mid % per_pair
    spot = jnp.where((pair_mid >= 0) & (pair_mid < slots), spot, slots)
    wanted = lax.dynamic_slice_in_dim(top_pairs, lane, 1, 0)[0]
    tops = jnp.where((wanted >= 0) & (wanted < owners), spot_of(wanted), owners)

    own_messages, received[1] = lax.optimization_barrier((own_messages, received[1]))
    bounds = (0, 1, lines)
    swap = [(c, c ^ 1) for c in range(per_cluster)]
    near_side, far_side = [], []
    for low, high in zip(bounds[:-1], bounds[1:]):
        sizes = (high - low, per_cluster, up_rows, mids, rank, per_pair, groups)
        messages = own_messages if low == 0 else select(sizes, group_at, lane_at, received[low:high])
        moved = [messages[0]]
        for d in range(1, groups):
            moved.append(lax.ppermute(messages[d], "group", [(g, g ^ d) for g in range(groups)]))
        if high < lines:
            near_side += moved
        if low == 0:
            outgoing, near_side, received[1:] = lax.optimization_barrier(
                (outgoing, near_side, received[1:])
            )
            arrived = lax.all_to_all(outgoing, AXES, split_axis=0, concat_axis=0, tiled=True)
            far_side = [lax.ppermute(m, "cluster", swap) for m in near_side]
        if high == lines:
            ready = (moved[1], far_side, mid_wide, spot, tops, pair_leaf)
            moved[1], far_side, mid_wide, spot, tops, pair_leaf = lax.optimization_barrier(ready)
            near_side += moved
            far_side += [lax.ppermute(m, "cluster", swap) for m in moved]

    return tail(
        bounds, per_pair, groups, leaf_parent, spot, lane_at, tops, leaf_size, pair_leaf, near_side,
        far_side, arrived, mid_wide, top_coupling, wide, basis_t,
    )


def solution(mesh):
    both = P(AXES)
    in_specs = (
        P(AXES, None),
        both,
        P(AXES, None, None),
        P(AXES, None, None),
        P(AXES, None, None),
        both,
        both,
        P(AXES, None),
        P(AXES, None, None),
        both,
        P(AXES, None),
        P(AXES, None, None),
        P("group", None),
        P("group", None, None),
    )
    return jax.shard_map(
        body, mesh=mesh, in_specs=in_specs, out_specs=P(AXES, None), check_vma=False
    )
```

```python
import functools
import math

import jax
import jax.numpy as jnp
from jax import lax
from jax.experimental import pallas as pl
from jax.experimental.pallas import tpu as pltpu
from jax.sharding import PartitionSpec as P

AXES = ("group", "cluster")
MIB = 1024 * 1024


def params(size):
    return pltpu.CompilerParams(vmem_limit_bytes=size)


def cost(flops, size):
    return pl.CostEstimate(flops=flops, bytes_accessed=size, transcendentals=0)


def whole(shape):
    return pl.BlockSpec(shape, lambda i, *_: (0,) * len(shape), pipeline_mode=pl.Buffered(1))


def first(group, *rest):
    return pl.BlockSpec((group,) + rest, lambda i, *_: (i,) + (0,) * len(rest))


def split(x):
    high = x.astype(jnp.bfloat16)
    low = (x - high.astype(jnp.float32)).astype(jnp.bfloat16)
    return high, low


def rows_of(x):
    return jnp.concatenate(split(x), axis=0)


def lanes_of(x):
    return jnp.concatenate(split(x), axis=1)


def dot(a, b):
    return lax.dot_general(a, b, (((1,), (0,)), ((), ())), preferred_element_type=jnp.float32)


def fold(product):
    m, n = product.shape[0] // 2, product.shape[1] // 2
    return product[:m, :n] + (product[:m, n:] + product[m:, :n] + product[m:, n:])


def deep_dot(a, b):
    high, low = split(b)
    return dot(jnp.concatenate([a, a], axis=1), jnp.concatenate([high, high, low, low], axis=0))


def up_kernel(
    sizes, size, parent, slots, group_at, lane_at, charges, basis, transfer, mid_transfer, send, coef, up,
    *messages
):
    step = pl.program_id(0)
    group, rank, points = basis.shape
    mids = mid_transfer.shape[0]
    ports = up.shape[1]

    @pl.when(step == 0)
    def _():
        up[: mids * rank, :] = jnp.zeros((mids * rank, ports), jnp.float32)
        up[(mids + 1) * rank :, :] = jnp.zeros((up.shape[0] - (mids + 1) * rank, ports), jnp.float32)
        for row in range(send.shape[0]):
            spot = (mids + 1) * rank + row
            up[spot : spot + 1, : send.shape[1]] = send[row : row + 1, :].astype(jnp.float32)

    point = lax.broadcasted_iota(jnp.int32, (points, ports), 0)
    values = []
    for g in range(group):
        block = jnp.where(
            point < size[step * group + g], charges[g * points : (g + 1) * points, :], 0.0
        )
        values.append(fold(dot(rows_of(basis[g]), lanes_of(block))))
    for g in range(group):
        coef[g] = values[g]
    moved = [fold(dot(rows_of(transfer[g]), lanes_of(values[g]))) for g in range(group)]
    for g in range(group):
        where = pl.ds(pl.multiple_of(parent[step * group + g] * rank, rank), rank)
        up[where, :] += moved[g]

    @pl.when(step == pl.num_programs(0) - 1)
    def _():
        terms = [
            fold(dot(rows_of(mid_transfer[c]), lanes_of(up[c * rank : (c + 1) * rank, :])))
            for c in range(mids)
        ]
        while len(terms) > 1:
            terms = [sum(terms[i : i + 2]) for i in range(0, len(terms), 2)]
        up[mids * rank : (mids + 1) * rank, :] = terms[0]
        per_cluster, per_pair = sizes
        for d, message in enumerate(messages):
            for side in range(2):
                receiver = (group_at[0] ^ d) * per_cluster + (lane_at[0] ^ side)
                for j in range(per_pair):
                    block = jnp.clip(slots[receiver * per_pair + j], 0, mids - 1)
                    source = pl.ds(pl.multiple_of(block * rank, rank), rank)
                    message[(1 - side) * (per_pair + 1) + j] = up[source, :]
            message[per_pair] = terms[0]


def up_sweep(
    sizes, groups, group_at, lane_at, charges, leaf_size, basis, transfer, mid_transfer, leaf_parent, slots
):
    leaves, rank, points = basis.shape
    ports = charges.shape[1]
    mids = mid_transfer.shape[0]
    group = 4
    send_mid = slots.reshape(-1, min(slots.shape[0], ports))
    up_rows = (mids + 1) * rank + -(-send_mid.shape[0] // 8) * 8
    message = (2 * sizes[1] + 1, rank, ports)
    return pl.pallas_call(
        functools.partial(up_kernel, sizes),
        grid_spec=pltpu.PrefetchScalarGridSpec(
            num_scalar_prefetch=5,
            grid=(leaves // group,),
            in_specs=[
                first(group * points, ports),
                first(group, rank, points),
                first(group, rank, rank),
                whole(mid_transfer.shape),
                whole(send_mid.shape),
            ],
            out_specs=[first(group, rank, ports), whole((up_rows, ports))] + [whole(message)] * groups,
        ),
        out_shape=[
            jax.ShapeDtypeStruct((leaves, rank, ports), jnp.float32),
            jax.ShapeDtypeStruct((up_rows, ports), jnp.float32),
        ]
        + [jax.ShapeDtypeStruct(message, jnp.float32)] * groups,
        compiler_params=params(60 * MIB),
        cost_estimate=cost(10**9, 10**7),
        name="up_sweep",
    )(
        leaf_size, leaf_parent, slots, group_at, lane_at, charges, basis, transfer, mid_transfer, send_mid
    )


def spread_kernel(send, coef, out):
    leaves = coef.shape[0]

    @pl.loop(0, out.shape[0], unroll=8)
    def _(slot):
        out[slot] = coef[jnp.minimum(send[slot], leaves - 1)]


def spread(send_leaf, coef):
    vmem = pl.BlockSpec(memory_space=pltpu.VMEM)
    shape = (send_leaf.shape[0],) + coef.shape[1:]
    return pl.pallas_call(
        spread_kernel,
        in_specs=[pl.BlockSpec(memory_space=pltpu.SMEM), vmem],
        out_specs=vmem,
        out_shape=jax.ShapeDtypeStruct(shape, jnp.float32),
        compiler_params=params(60 * MIB),
        cost_estimate=cost(0, 4 * 10**6),
        name="spread",
    )(send_leaf, coef)


def select_kernel(sizes, group_at, lane_at, *refs):
    lines, per_cluster, up_rows, mids, rank, per_pair, groups = sizes
    received, messages = refs[:lines], refs[lines : lines + groups]
    payloads, tables, sem, table_sem = refs[lines + groups :]
    group, lane = group_at[0], lane_at[0]
    table_rows = up_rows - (mids + 1) * rank
    ports = payloads.shape[2]
    copies = []
    for line, ref in enumerate(received):
        table = ref.at[pl.ds((mids + 1) * rank, table_rows), :]
        copies.append(pltpu.make_async_copy(table, tables.at[line], table_sem.at[line]))
        copies.append(pltpu.make_async_copy(ref, payloads.at[line], sem.at[line]))
    for copy in copies:
        copy.start()
    for copy in copies:
        copy.wait()
    for d, message in enumerate(messages):
        for side in range(2):
            receiver = (group ^ d) * per_cluster + (lane ^ side)

            @pl.loop(0, lines, unroll=min(lines, 4))
            def _(line):
                for j in range(per_pair):
                    entry = receiver * per_pair + j
                    listed = tables[line, lax.div(entry, ports), lax.rem(entry, ports)]
                    block = jnp.clip(listed.astype(jnp.int32), 0, mids - 1)
                    target = (1 - side) * (per_pair + 1) * lines + line * per_pair + j
                    message[target] = payloads[line, pl.ds(pl.multiple_of(block * rank, 8), rank), :]

        for line in range(lines):
            message[lines * per_pair + line] = payloads[line, mids * rank : (mids + 1) * rank, :]


def select(sizes, group_at, lane_at, received):
    lines, per_cluster, up_rows, mids, rank, per_pair, groups = sizes
    ports = received[0].shape[1]
    table_rows = up_rows - (mids + 1) * rank
    payloads = (lines, up_rows, ports)
    shape = jax.ShapeDtypeStruct((lines * (2 * per_pair + 1), rank, ports), jnp.float32)
    return pl.pallas_call(
        functools.partial(select_kernel, sizes),
        in_specs=[pl.BlockSpec(memory_space=pltpu.SMEM)] * 2
        + [pl.BlockSpec(memory_space=pl.ANY)] * len(received),
        out_specs=[pl.BlockSpec(memory_space=pltpu.VMEM)] * groups,
        out_shape=[shape] * groups,
        scratch_shapes=[
            pltpu.VMEM(payloads, jnp.float32),
            pltpu.SMEM((lines, table_rows, ports), jnp.float32),
            pltpu.SemaphoreType.DMA((lines,)),
            pltpu.SemaphoreType.DMA((lines,)),
        ],
        compiler_params=params(60 * MIB),
        cost_estimate=cost(0, 4 * 10**6),
        name="select",
    )(group_at, lane_at, *received)


def prepare_kernel(after, coupling, basis, transfer, mid_coupling, mid_transfer, wide, basis_t, mid_wide):
    for g in range(coupling.shape[0]):
        wide[g] = rows_of(jnp.concatenate([coupling[g], transfer[g].T], axis=1))
        basis_t[g] = rows_of(basis[g]).T
    for g in range(mid_coupling.shape[0]):
        mid_wide[g] = rows_of(jnp.concatenate([mid_coupling[g], mid_transfer[g].T], axis=1))


def prepare(after, coupling, basis, transfer, mid_coupling, mid_transfer):
    leaves, rank, width = coupling.shape
    points = basis.shape[2]
    mids, _, mid_width = mid_coupling.shape
    steps = mids
    group = leaves // steps
    shapes = [
        (leaves, 2 * rank, width + rank),
        (leaves, points, 2 * rank),
        (mids, 2 * rank, mid_width + rank),
    ]
    return pl.pallas_call(
        prepare_kernel,
        grid=(steps,),
        in_specs=[
            pl.BlockSpec(memory_space=pl.ANY),
            first(group, rank, width),
            first(group, rank, points),
            first(group, rank, rank),
            first(1, rank, mid_width),
            first(1, rank, rank),
        ],
        out_specs=[first(s[0] // steps, *s[1:]) for s in shapes],
        out_shape=[jax.ShapeDtypeStruct(s, jnp.bfloat16) for s in shapes],
        compiler_params=params(60 * MIB),
        cost_estimate=cost(0, 3 * 10**7),
        name="prepare",
    )(after, coupling, basis, transfer, mid_coupling, mid_transfer)


def tail_kernel(sizes, parent, pair, position, tops, size, pair_leaf, *refs):
    bounds, per_pair, groups, chunk, group, ahead = sizes
    lines, count = bounds[-1], (len(bounds) - 1) * groups
    messages = refs[: 2 * count]
    arrived, mid_wide, top_coupling, wide, basis, out = refs[2 * count : 2 * count + 6]
    scratch = refs[2 * count + 6 :]
    held_messages, scratch = scratch[: 2 * count], scratch[2 * count :]
    (
        arrived_held, mid_wide_held, top_held, wide_held, basis_held, parts, top_parts, leaf_parts, near_top, out_held,
        message_sem, arrived_sem, mid_sem, top_sem, wide_sem, basis_sem, out_sem,
    ) = scratch
    mids, leaves, points = mid_wide.shape[0], wide.shape[0], basis.shape[1]
    slots, top_count = arrived.shape[0], top_parts.shape[0] - 1
    ports = out.shape[1]
    steps, chunks = leaves // group, slots // chunk

    def fetch_message(index):
        held = held_messages[index]
        start = 0 if index >= count else messages[index].shape[0] - held.shape[0]
        source = messages[index].at[pl.ds(start, held.shape[0])]
        return pltpu.make_async_copy(source, held, message_sem.at[index])

    def fetch_arrived(index):
        source = arrived.at[pl.ds(index * chunk, chunk)]
        return pltpu.make_async_copy(source, arrived_held.at[index % 2], arrived_sem.at[index % 2])

    def fetch_mid(c):
        return pltpu.make_async_copy(mid_wide.at[c], mid_wide_held.at[c], mid_sem.at[c])

    def fetch_leaves(index):
        some = pl.ds(index * group, group)
        return (
            pltpu.make_async_copy(wide.at[some], wide_held.at[some], wide_sem.at[index]),
            pltpu.make_async_copy(basis.at[some], basis_held.at[some], basis_sem.at[index]),
        )

    fetch_top = pltpu.make_async_copy(top_coupling.at[position[0]], top_held, top_sem)
    for index in range(min(2, chunks)):
        fetch_arrived(index).start()
    for c in range(mids // 2):
        fetch_mid(c).start()
    for index in range(2 * count):
        fetch_message(index).start()
    fetch_top.start()
    for c in range(mids // 2, mids):
        fetch_mid(c).start()

    leaf_parts[slots] = jnp.zeros(leaf_parts.shape[1:], jnp.bfloat16)
    parts[slots] = jnp.zeros(parts.shape[1:], jnp.bfloat16)
    top_parts[top_count] = jnp.zeros(top_parts.shape[1:], jnp.bfloat16)
    for index in range(chunks):
        fetch_arrived(index).wait()
        @pl.loop(0, chunk, unroll=8)
        def _(slot):
            leaf_parts[index * chunk + slot] = lanes_of(arrived_held[index % 2, slot])

        if index + 2 < chunks:
            fetch_arrived(index + 2).start()

    for index in range(2 * count):
        side, message = divmod(index, count)
        batch, d = divmod(message, groups)
        lines_held = bounds[batch + 1] - bounds[batch]
        piece = lines_held * per_pair
        base = (d * 2 + side) * lines + bounds[batch]
        held = held_messages[index]
        first_slot, first_top = (lines_held, 0) if side == 0 else (0, piece)
        fetch_message(index).wait()
        if index == count:
            for step in range(ahead):
                for copy in fetch_leaves(step):
                    copy.start()

        @pl.loop(0, piece, unroll=min(piece, 6))
        def _(slot):
            parts[base * per_pair + slot] = lanes_of(held[first_slot + slot])

        for line in range(lines_held):
            top_parts[base + line] = lanes_of(held[first_top + line])

    fetch_top.wait()
    stacked = jnp.concatenate([top_parts[tops[k]] for k in range(tops.shape[0])], axis=0)
    near_top[...] = lanes_of(fold(dot(rows_of(top_held[...]), stacked)))
    for c in range(mids):
        fetch_mid(c).wait()

    for c in range(mids):
        blocks = [parts[pair[c, k]] for k in range(pair.shape[1])] + [near_top[...]]
        value = fold(dot(mid_wide_held[c], jnp.concatenate(blocks, axis=0)))
        leaf_parts[slots + 1 + c] = lanes_of(value)

    point = lax.broadcasted_iota(jnp.int32, (points, ports), 0)

    def send(index):
        rows = group * points
        target = out.at[pl.ds(index * rows, rows), :]
        return pltpu.make_async_copy(out_held.at[index % 2], target, out_sem.at[index % 2])

    before = None
    for index in range(steps + 1):
        values = []
        if index < steps:
            if index + ahead < steps:
                for copy in fetch_leaves(index + ahead):
                    copy.start()
            for copy in fetch_leaves(index):
                copy.wait()
        if index >= 3:
            send(index - 3).wait()
        if index < steps:
            for g in range(group):
                leaf = index * group + g
                blocks = [leaf_parts[pair_leaf[leaf, k]] for k in range(pair_leaf.shape[1])]
                blocks.append(leaf_parts[slots + 1 + parent[leaf]])
                values.append(fold(dot(wide_held[leaf], jnp.concatenate(blocks, axis=0))))
        if before is not None:
            for g in range(group):
                leaf = (index - 1) * group + g
                far = jnp.where(point < size[leaf], deep_dot(basis_held[leaf], before[g]), 0.0)
                out_held[(index - 1) % 2, g * points : (g + 1) * points, :] = far
            send(index - 1).start()
        before = values
    for index in range(max(0, steps - 2), steps):
        send(index).wait()


def tail(
    bounds, per_pair, groups, parent, pair, position, tops, size, pair_leaf, near_side, far_side, arrived,
    mid_wide, top_coupling, wide, basis
):
    mids = mid_wide.shape[0]
    leaves, points, _ = basis.shape
    slots, rank, ports = arrived.shape
    owners = slots // per_pair
    group, chunk, ahead = 4, min(slots, 32), 6
    held = []
    for message in range(len(near_side)):
        batch = message // groups
        held.append((bounds[batch + 1] - bounds[batch]) * (per_pair + 1))
    full, half = jnp.float32, jnp.bfloat16
    scratch = [((h, rank, ports), full) for h in held + held] + [
        ((2, chunk, rank, ports), full),
        (mid_wide.shape, half),
        (top_coupling.shape[1:], full),
        (wide.shape, half),
        (basis.shape, half),
        ((slots + 1, rank, 2 * ports), half),
        ((owners + 1, rank, 2 * ports), half),
        ((slots + 1 + mids, rank, 2 * ports), half),
        ((rank, 2 * ports), half),
        ((2, group * points, ports), full),
    ]
    semaphores = [(2 * len(near_side),), (2,), (mids,), (), (leaves // group,), (leaves // group,), (2,)]
    scalars = (parent, pair, position, tops, size, pair_leaf)
    pin = functools.partial(pltpu.with_memory_space_constraint, memory_space=pltpu.HBM)
    matrices = (mid_wide, top_coupling, wide, basis)
    arrays = (*map(pin, near_side), *map(pin, far_side), arrived, *map(pin, matrices))
    used = sum(jnp.dtype(dtype).itemsize * math.prod(shape) for shape, dtype in scratch)
    return pl.pallas_call(
        functools.partial(tail_kernel, (bounds, per_pair, groups, chunk, group, ahead)),
        in_specs=[pl.BlockSpec(memory_space=pltpu.SMEM)] * len(scalars)
        + [pl.BlockSpec(memory_space=pl.ANY)] * len(arrays),
        out_specs=pl.BlockSpec(memory_space=pl.ANY),
        out_shape=jax.ShapeDtypeStruct((leaves * points, ports), full),
        scratch_shapes=[pltpu.VMEM(shape, dtype) for shape, dtype in scratch]
        + [pltpu.SemaphoreType.DMA(n) for n in semaphores],
        compiler_params=params(min(60 * MIB, used + 6 * MIB)),
        cost_estimate=cost(6 * 10**9, 2 * 10**7),
        name="tail",
    )(*scalars, *arrays)


def body(
    charges, leaf_size, leaf_basis, leaf_transfer, mid_transfer, leaf_parent, send_leaf, pair_leaf,
    leaf_coupling, send_mid, pair_mid, mid_coupling, top_pairs, top_coupling,
):
    rank = leaf_basis.shape[1]
    ports = charges.shape[1]
    mids = mid_transfer.shape[0]
    slots = send_mid.shape[0]
    groups, per_cluster = lax.axis_size("group"), lax.axis_size("cluster")
    owners = groups * per_cluster
    lines = per_cluster // 2
    per_pair = slots // owners
    group, lane = lax.axis_index("group"), lax.axis_index("cluster")

    group_at, lane_at = group.astype(jnp.int32)[None], lane.astype(jnp.int32)[None]
    coef, lifted, *own_messages = up_sweep(
        (per_cluster, per_pair), groups, group_at, lane_at, charges, leaf_size, leaf_basis,
        leaf_transfer, mid_transfer, leaf_parent, send_mid,
    )
    up_rows = lifted.shape[0]
    outgoing = spread(send_leaf, coef)

    received = [lifted] * lines
    for d in range(1, lines):
        received[d] = lax.ppermute(lifted, "cluster", [(c, c ^ (2 * d)) for c in range(per_cluster)])
    wide, basis_t, mid_wide = prepare(
        lifted, leaf_coupling, leaf_basis, leaf_transfer, mid_coupling, mid_transfer
    )

    def spot_of(sender):
        at_group, at_lane = sender // per_cluster, sender % per_cluster
        line = (at_lane // 2) ^ (lane // 2)
        return ((at_group ^ group) * 2 + ((at_lane ^ lane) & 1)) * lines + line

    spot = spot_of(pair_mid // per_pair) * per_pair + pair_mid % per_pair
    spot = jnp.where((pair_mid >= 0) & (pair_mid < slots), spot, slots)
    wanted = lax.dynamic_slice_in_dim(top_pairs, lane, 1, 0)[0]
    tops = jnp.where((wanted >= 0) & (wanted < owners), spot_of(wanted), owners)

    own_messages, received[1] = lax.optimization_barrier((own_messages, received[1]))
    bounds = (0, 1, lines)
    swap = [(c, c ^ 1) for c in range(per_cluster)]
    near_side, far_side = [], []
    for low, high in zip(bounds[:-1], bounds[1:]):
        sizes = (high - low, per_cluster, up_rows, mids, rank, per_pair, groups)
        messages = own_messages if low == 0 else select(sizes, group_at, lane_at, received[low:high])
        moved = [messages[0]]
        for d in range(1, groups):
            moved.append(lax.ppermute(messages[d], "group", [(g, g ^ d) for g in range(groups)]))
        if high < lines:
            near_side += moved
        if low == 0:
            outgoing, near_side, received[1:] = lax.optimization_barrier(
                (outgoing, near_side, received[1:])
            )
            arrived = lax.all_to_all(outgoing, AXES, split_axis=0, concat_axis=0, tiled=True)
            far_side = [lax.ppermute(m, "cluster", swap) for m in near_side]
        if high == lines:
            ready = (moved[1], far_side, mid_wide, spot, tops, pair_leaf)
            moved[1], far_side, mid_wide, spot, tops, pair_leaf = lax.optimization_barrier(ready)
            near_side += moved
            far_side += [lax.ppermute(m, "cluster", swap) for m in moved]

    return tail(
        bounds, per_pair, groups, leaf_parent, spot, lane_at, tops, leaf_size, pair_leaf, near_side,
        far_side, arrived, mid_wide, top_coupling, wide, basis_t,
    )


def solution(mesh):
    both = P(AXES)
    in_specs = (
        P(AXES, None),
        both,
        P(AXES, None, None),
        P(AXES, None, None),
        P(AXES, None, None),
        both,
        both,
        P(AXES, None),
        P(AXES, None, None),
        both,
        P(AXES, None),
        P(AXES, None, None),
        P("group", None),
        P("group", None, None),
    )
    return jax.shard_map(
        body, mesh=mesh, in_specs=in_specs, out_specs=P(AXES, None), check_vma=False
    )
```

```python
import functools
import math

import jax
import jax.numpy as jnp
from jax import lax
from jax.experimental import pallas as pl
from jax.experimental.pallas import tpu as pltpu
from jax.sharding import PartitionSpec as P

AXES = ("group", "cluster")
MIB = 1024 * 1024


def params(size):
    return pltpu.CompilerParams(vmem_limit_bytes=size)


def cost(flops, size):
    return pl.CostEstimate(flops=flops, bytes_accessed=size, transcendentals=0)


def whole(shape):
    return pl.BlockSpec(shape, lambda i, *_: (0,) * len(shape), pipeline_mode=pl.Buffered(1))


def first(group, *rest):
    return pl.BlockSpec((group,) + rest, lambda i, *_: (i,) + (0,) * len(rest))


def split(x):
    high = x.astype(jnp.bfloat16)
    low = (x - high.astype(jnp.float32)).astype(jnp.bfloat16)
    return high, low


def rows_of(x):
    return jnp.concatenate(split(x), axis=0)


def lanes_of(x):
    return jnp.concatenate(split(x), axis=1)


def dot(a, b):
    return lax.dot_general(a, b, (((1,), (0,)), ((), ())), preferred_element_type=jnp.float32)


def fold(product):
    m, n = product.shape[0] // 2, product.shape[1] // 2
    return product[:m, :n] + (product[:m, n:] + product[m:, :n] + product[m:, n:])


def deep_dot(a, b):
    high, low = split(b)
    return dot(jnp.concatenate([a, a], axis=1), jnp.concatenate([high, high, low, low], axis=0))


def up_kernel(
    sizes, size, parent, slots, group_at, lane_at, charges, basis, transfer, mid_transfer, send, coef, up,
    *messages
):
    step = pl.program_id(0)
    group, rank, points = basis.shape
    mids = mid_transfer.shape[0]
    ports = up.shape[1]

    @pl.when(step == 0)
    def _():
        up[: mids * rank, :] = jnp.zeros((mids * rank, ports), jnp.float32)
        up[(mids + 1) * rank :, :] = jnp.zeros((up.shape[0] - (mids + 1) * rank, ports), jnp.float32)
        for row in range(send.shape[0]):
            spot = (mids + 1) * rank + row
            up[spot : spot + 1, : send.shape[1]] = send[row : row + 1, :].astype(jnp.float32)

    point = lax.broadcasted_iota(jnp.int32, (points, ports), 0)
    values = []
    for g in range(group):
        block = jnp.where(
            point < size[step * group + g], charges[g * points : (g + 1) * points, :], 0.0
        )
        values.append(fold(dot(rows_of(basis[g]), lanes_of(block))))
    for g in range(group):
        coef[g] = values[g]
    moved = [fold(dot(rows_of(transfer[g]), lanes_of(values[g]))) for g in range(group)]
    for g in range(group):
        where = pl.ds(pl.multiple_of(parent[step * group + g] * rank, rank), rank)
        up[where, :] += moved[g]

    @pl.when(step == pl.num_programs(0) - 1)
    def _():
        terms = [
            fold(dot(rows_of(mid_transfer[c]), lanes_of(up[c * rank : (c + 1) * rank, :])))
            for c in range(mids)
        ]
        while len(terms) > 1:
            terms = [sum(terms[i : i + 2]) for i in range(0, len(terms), 2)]
        up[mids * rank : (mids + 1) * rank, :] = terms[0]
        per_cluster, per_pair = sizes
        for d, message in enumerate(messages):
            for side in range(2):
                receiver = (group_at[0] ^ d) * per_cluster + (lane_at[0] ^ side)
                for j in range(per_pair):
                    block = jnp.clip(slots[receiver * per_pair + j], 0, mids - 1)
                    source = pl.ds(pl.multiple_of(block * rank, rank), rank)
                    message[(1 - side) * (per_pair + 1) + j] = up[source, :]
            message[per_pair] = terms[0]


def up_sweep(
    sizes, groups, group_at, lane_at, charges, leaf_size, basis, transfer, mid_transfer, leaf_parent, slots
):
    leaves, rank, points = basis.shape
    ports = charges.shape[1]
    mids = mid_transfer.shape[0]
    group = 16
    send_mid = slots.reshape(-1, min(slots.shape[0], ports))
    up_rows = (mids + 1) * rank + -(-send_mid.shape[0] // 8) * 8
    message = (2 * sizes[1] + 1, rank, ports)
    return pl.pallas_call(
        functools.partial(up_kernel, sizes),
        grid_spec=pltpu.PrefetchScalarGridSpec(
            num_scalar_prefetch=5,
            grid=(leaves // group,),
            in_specs=[
                first(group * points, ports),
                first(group, rank, points),
                first(group, rank, rank),
                whole(mid_transfer.shape),
                whole(send_mid.shape),
            ],
            out_specs=[first(group, rank, ports), whole((up_rows, ports))] + [whole(message)] * groups,
        ),
        out_shape=[
            jax.ShapeDtypeStruct((leaves, rank, ports), jnp.float32),
            jax.ShapeDtypeStruct((up_rows, ports), jnp.float32),
        ]
        + [jax.ShapeDtypeStruct(message, jnp.float32)] * groups,
        compiler_params=params(60 * MIB),
        cost_estimate=cost(10**9, 10**7),
        name="up_sweep",
    )(
        leaf_size, leaf_parent, slots, group_at, lane_at, charges, basis, transfer, mid_transfer, send_mid
    )


def spread_kernel(send, coef, out):
    leaves = coef.shape[0]

    @pl.loop(0, out.shape[0], unroll=8)
    def _(slot):
        out[slot] = coef[jnp.minimum(send[slot], leaves - 1)]


def spread(send_leaf, coef):
    vmem = pl.BlockSpec(memory_space=pltpu.VMEM)
    shape = (send_leaf.shape[0],) + coef.shape[1:]
    return pl.pallas_call(
        spread_kernel,
        in_specs=[pl.BlockSpec(memory_space=pltpu.SMEM), vmem],
        out_specs=vmem,
        out_shape=jax.ShapeDtypeStruct(shape, jnp.float32),
        compiler_params=params(60 * MIB),
        cost_estimate=cost(0, 4 * 10**6),
        name="spread",
    )(send_leaf, coef)


def select_kernel(sizes, group_at, lane_at, *refs):
    lines, per_cluster, up_rows, mids, rank, per_pair, groups = sizes
    received, messages = refs[:lines], refs[lines : lines + groups]
    payloads, tables, sem, table_sem = refs[lines + groups :]
    group, lane = group_at[0], lane_at[0]
    table_rows = up_rows - (mids + 1) * rank
    ports = payloads.shape[2]
    copies = []
    for line, ref in enumerate(received):
        table = ref.at[pl.ds((mids + 1) * rank, table_rows), :]
        copies.append(pltpu.make_async_copy(table, tables.at[line], table_sem.at[line]))
        copies.append(pltpu.make_async_copy(ref, payloads.at[line], sem.at[line]))
    for copy in copies:
        copy.start()
    for copy in copies:
        copy.wait()
    for d, message in enumerate(messages):
        for side in range(2):
            receiver = (group ^ d) * per_cluster + (lane ^ side)

            @pl.loop(0, lines, unroll=min(lines, 4))
            def _(line):
                for j in range(per_pair):
                    entry = receiver * per_pair + j
                    listed = tables[line, lax.div(entry, ports), lax.rem(entry, ports)]
                    block = jnp.clip(listed.astype(jnp.int32), 0, mids - 1)
                    target = (1 - side) * (per_pair + 1) * lines + line * per_pair + j
                    message[target] = payloads[line, pl.ds(pl.multiple_of(block * rank, 8), rank), :]

        for line in range(lines):
            message[lines * per_pair + line] = payloads[line, mids * rank : (mids + 1) * rank, :]


def select(sizes, group_at, lane_at, received):
    lines, per_cluster, up_rows, mids, rank, per_pair, groups = sizes
    ports = received[0].shape[1]
    table_rows = up_rows - (mids + 1) * rank
    payloads = (lines, up_rows, ports)
    shape = jax.ShapeDtypeStruct((lines * (2 * per_pair + 1), rank, ports), jnp.float32)
    return pl.pallas_call(
        functools.partial(select_kernel, sizes),
        in_specs=[pl.BlockSpec(memory_space=pltpu.SMEM)] * 2
        + [pl.BlockSpec(memory_space=pl.ANY)] * len(received),
        out_specs=[pl.BlockSpec(memory_space=pltpu.VMEM)] * groups,
        out_shape=[shape] * groups,
        scratch_shapes=[
            pltpu.VMEM(payloads, jnp.float32),
            pltpu.SMEM((lines, table_rows, ports), jnp.float32),
            pltpu.SemaphoreType.DMA((lines,)),
            pltpu.SemaphoreType.DMA((lines,)),
        ],
        compiler_params=params(60 * MIB),
        cost_estimate=cost(0, 4 * 10**6),
        name="select",
    )(group_at, lane_at, *received)


def prepare_kernel(after, coupling, basis, transfer, mid_coupling, mid_transfer, wide, basis_t, mid_wide):
    for g in range(coupling.shape[0]):
        wide[g] = rows_of(jnp.concatenate([coupling[g], transfer[g].T], axis=1))
        basis_t[g] = rows_of(basis[g]).T
    for g in range(mid_coupling.shape[0]):
        mid_wide[g] = rows_of(jnp.concatenate([mid_coupling[g], mid_transfer[g].T], axis=1))


def prepare(after, coupling, basis, transfer, mid_coupling, mid_transfer):
    leaves, rank, width = coupling.shape
    points = basis.shape[2]
    mids, _, mid_width = mid_coupling.shape
    steps = mids
    group = leaves // steps
    shapes = [
        (leaves, 2 * rank, width + rank),
        (leaves, points, 2 * rank),
        (mids, 2 * rank, mid_width + rank),
    ]
    return pl.pallas_call(
        prepare_kernel,
        grid=(steps,),
        in_specs=[
            pl.BlockSpec(memory_space=pl.ANY),
            first(group, rank, width),
            first(group, rank, points),
            first(group, rank, rank),
            first(1, rank, mid_width),
            first(1, rank, rank),
        ],
        out_specs=[first(s[0] // steps, *s[1:]) for s in shapes],
        out_shape=[jax.ShapeDtypeStruct(s, jnp.bfloat16) for s in shapes],
        compiler_params=params(60 * MIB),
        cost_estimate=cost(0, 3 * 10**7),
        name="prepare",
    )(after, coupling, basis, transfer, mid_coupling, mid_transfer)


def tail_kernel(sizes, parent, pair, position, tops, size, pair_leaf, *refs):
    bounds, per_pair, groups, chunk, group, ahead = sizes
    lines, count = bounds[-1], (len(bounds) - 1) * groups
    messages = refs[: 2 * count]
    arrived, mid_wide, top_coupling, wide, basis, out = refs[2 * count : 2 * count + 6]
    scratch = refs[2 * count + 6 :]
    held_messages, scratch = scratch[: 2 * count], scratch[2 * count :]
    (
        arrived_held, mid_wide_held, top_held, wide_held, basis_held, parts, top_parts, leaf_parts, near_top, out_held,
        message_sem, arrived_sem, mid_sem, top_sem, wide_sem, basis_sem, out_sem,
    ) = scratch
    mids, leaves, points = mid_wide.shape[0], wide.shape[0], basis.shape[1]
    slots, top_count = arrived.shape[0], top_parts.shape[0] - 1
    ports = out.shape[1]
    steps, chunks = leaves // group, slots // chunk

    def fetch_message(index):
        held = held_messages[index]
        start = 0 if index >= count else messages[index].shape[0] - held.shape[0]
        source = messages[index].at[pl.ds(start, held.shape[0])]
        return pltpu.make_async_copy(source, held, message_sem.at[index])

    def fetch_arrived(index):
        source = arrived.at[pl.ds(index * chunk, chunk)]
        return pltpu.make_async_copy(source, arrived_held.at[index % 2], arrived_sem.at[index % 2])

    def fetch_mid(c):
        return pltpu.make_async_copy(mid_wide.at[c], mid_wide_held.at[c], mid_sem.at[c])

    def fetch_leaves(index):
        some = pl.ds(index * group, group)
        return (
            pltpu.make_async_copy(wide.at[some], wide_held.at[some], wide_sem.at[index]),
            pltpu.make_async_copy(basis.at[some], basis_held.at[some], basis_sem.at[index]),
        )

    fetch_top = pltpu.make_async_copy(top_coupling.at[position[0]], top_held, top_sem)
    for index in range(min(2, chunks)):
        fetch_arrived(index).start()
    for c in range(mids // 2):
        fetch_mid(c).start()
    for index in range(2 * count):
        fetch_message(index).start()
    fetch_top.start()
    for c in range(mids // 2, mids):
        fetch_mid(c).start()

    leaf_parts[slots] = jnp.zeros(leaf_parts.shape[1:], jnp.bfloat16)
    parts[slots] = jnp.zeros(parts.shape[1:], jnp.bfloat16)
    top_parts[top_count] = jnp.zeros(top_parts.shape[1:], jnp.bfloat16)
    for index in range(chunks):
        fetch_arrived(index).wait()
        @pl.loop(0, chunk, unroll=8)
        def _(slot):
            leaf_parts[index * chunk + slot] = lanes_of(arrived_held[index % 2, slot])

        if index + 2 < chunks:
            fetch_arrived(index + 2).start()

    for index in range(2 * count):
        side, message = divmod(index, count)
        batch, d = divmod(message, groups)
        lines_held = bounds[batch + 1] - bounds[batch]
        piece = lines_held * per_pair
        base = (d * 2 + side) * lines + bounds[batch]
        held = held_messages[index]
        first_slot, first_top = (lines_held, 0) if side == 0 else (0, piece)
        fetch_message(index).wait()
        if index == count:
            for step in range(ahead):
                for copy in fetch_leaves(step):
                    copy.start()

        @pl.loop(0, piece, unroll=min(piece, 6))
        def _(slot):
            parts[base * per_pair + slot] = lanes_of(held[first_slot + slot])

        for line in range(lines_held):
            top_parts[base + line] = lanes_of(held[first_top + line])

    fetch_top.wait()
    stacked = jnp.concatenate([top_parts[tops[k]] for k in range(tops.shape[0])], axis=0)
    near_top[...] = lanes_of(fold(dot(rows_of(top_held[...]), stacked)))
    for c in range(mids):
        fetch_mid(c).wait()

    for c in range(mids):
        blocks = [parts[pair[c, k]] for k in range(pair.shape[1])] + [near_top[...]]
        value = fold(dot(mid_wide_held[c], jnp.concatenate(blocks, axis=0)))
        leaf_parts[slots + 1 + c] = lanes_of(value)

    point = lax.broadcasted_iota(jnp.int32, (points, ports), 0)

    def send(index):
        rows = group * points
        target = out.at[pl.ds(index * rows, rows), :]
        return pltpu.make_async_copy(out_held.at[index % 2], target, out_sem.at[index % 2])

    before = None
    for index in range(steps + 1):
        values = []
        if index < steps:
            if index + ahead < steps:
                for copy in fetch_leaves(index + ahead):
                    copy.start()
            for copy in fetch_leaves(index):
                copy.wait()
        if index >= 3:
            send(index - 3).wait()
        if index < steps:
            for g in range(group):
                leaf = index * group + g
                blocks = [leaf_parts[pair_leaf[leaf, k]] for k in range(pair_leaf.shape[1])]
                blocks.append(leaf_parts[slots + 1 + parent[leaf]])
                values.append(fold(dot(wide_held[leaf], jnp.concatenate(blocks, axis=0))))
        if before is not None:
            for g in range(group):
                leaf = (index - 1) * group + g
                far = jnp.where(point < size[leaf], deep_dot(basis_held[leaf], before[g]), 0.0)
                out_held[(index - 1) % 2, g * points : (g + 1) * points, :] = far
            send(index - 1).start()
        before = values
    for index in range(max(0, steps - 2), steps):
        send(index).wait()


def tail(
    bounds, per_pair, groups, parent, pair, position, tops, size, pair_leaf, near_side, far_side, arrived,
    mid_wide, top_coupling, wide, basis
):
    mids = mid_wide.shape[0]
    leaves, points, _ = basis.shape
    slots, rank, ports = arrived.shape
    owners = slots // per_pair
    group, chunk, ahead = 4, min(slots, 32), 6
    held = []
    for message in range(len(near_side)):
        batch = message // groups
        held.append((bounds[batch + 1] - bounds[batch]) * (per_pair + 1))
    full, half = jnp.float32, jnp.bfloat16
    scratch = [((h, rank, ports), full) for h in held + held] + [
        ((2, chunk, rank, ports), full),
        (mid_wide.shape, half),
        (top_coupling.shape[1:], full),
        (wide.shape, half),
        (basis.shape, half),
        ((slots + 1, rank, 2 * ports), half),
        ((owners + 1, rank, 2 * ports), half),
        ((slots + 1 + mids, rank, 2 * ports), half),
        ((rank, 2 * ports), half),
        ((2, group * points, ports), full),
    ]
    semaphores = [(2 * len(near_side),), (2,), (mids,), (), (leaves // group,), (leaves // group,), (2,)]
    scalars = (parent, pair, position, tops, size, pair_leaf)
    pin = functools.partial(pltpu.with_memory_space_constraint, memory_space=pltpu.HBM)
    matrices = (mid_wide, top_coupling, wide, basis)
    arrays = (*map(pin, near_side), *map(pin, far_side), arrived, *map(pin, matrices))
    used = sum(jnp.dtype(dtype).itemsize * math.prod(shape) for shape, dtype in scratch)
    return pl.pallas_call(
        functools.partial(tail_kernel, (bounds, per_pair, groups, chunk, group, ahead)),
        in_specs=[pl.BlockSpec(memory_space=pltpu.SMEM)] * len(scalars)
        + [pl.BlockSpec(memory_space=pl.ANY)] * len(arrays),
        out_specs=pl.BlockSpec(memory_space=pl.ANY),
        out_shape=jax.ShapeDtypeStruct((leaves * points, ports), full),
        scratch_shapes=[pltpu.VMEM(shape, dtype) for shape, dtype in scratch]
        + [pltpu.SemaphoreType.DMA(n) for n in semaphores],
        compiler_params=params(min(60 * MIB, used + 6 * MIB)),
        cost_estimate=cost(6 * 10**9, 2 * 10**7),
        name="tail",
    )(*scalars, *arrays)


def body(
    charges, leaf_size, leaf_basis, leaf_transfer, mid_transfer, leaf_parent, send_leaf, pair_leaf,
    leaf_coupling, send_mid, pair_mid, mid_coupling, top_pairs, top_coupling,
):
    rank = leaf_basis.shape[1]
    ports = charges.shape[1]
    mids = mid_transfer.shape[0]
    slots = send_mid.shape[0]
    groups, per_cluster = lax.axis_size("group"), lax.axis_size("cluster")
    owners = groups * per_cluster
    lines = per_cluster // 2
    per_pair = slots // owners
    group, lane = lax.axis_index("group"), lax.axis_index("cluster")

    group_at, lane_at = group.astype(jnp.int32)[None], lane.astype(jnp.int32)[None]
    coef, lifted, *own_messages = up_sweep(
        (per_cluster, per_pair), groups, group_at, lane_at, charges, leaf_size, leaf_basis,
        leaf_transfer, mid_transfer, leaf_parent, send_mid,
    )
    up_rows = lifted.shape[0]
    outgoing = spread(send_leaf, coef)

    received = [lifted] * lines
    for d in range(1, lines):
        received[d] = lax.ppermute(lifted, "cluster", [(c, c ^ (2 * d)) for c in range(per_cluster)])
    wide, basis_t, mid_wide = prepare(
        lifted, leaf_coupling, leaf_basis, leaf_transfer, mid_coupling, mid_transfer
    )

    def spot_of(sender):
        at_group, at_lane = sender // per_cluster, sender % per_cluster
        line = (at_lane // 2) ^ (lane // 2)
        return ((at_group ^ group) * 2 + ((at_lane ^ lane) & 1)) * lines + line

    spot = spot_of(pair_mid // per_pair) * per_pair + pair_mid % per_pair
    spot = jnp.where((pair_mid >= 0) & (pair_mid < slots), spot, slots)
    wanted = lax.dynamic_slice_in_dim(top_pairs, lane, 1, 0)[0]
    tops = jnp.where((wanted >= 0) & (wanted < owners), spot_of(wanted), owners)

    own_messages, received[1] = lax.optimization_barrier((own_messages, received[1]))
    bounds = (0, 1, lines)
    swap = [(c, c ^ 1) for c in range(per_cluster)]
    near_side, far_side = [], []
    for low, high in zip(bounds[:-1], bounds[1:]):
        sizes = (high - low, per_cluster, up_rows, mids, rank, per_pair, groups)
        messages = own_messages if low == 0 else select(sizes, group_at, lane_at, received[low:high])
        moved = [messages[0]]
        for d in range(1, groups):
            moved.append(lax.ppermute(messages[d], "group", [(g, g ^ d) for g in range(groups)]))
        if high < lines:
            near_side += moved
        if low == 0:
            outgoing, near_side, received[1:] = lax.optimization_barrier(
                (outgoing, near_side, received[1:])
            )
            arrived = lax.all_to_all(outgoing, AXES, split_axis=0, concat_axis=0, tiled=True)
            far_side = [lax.ppermute(m, "cluster", swap) for m in near_side]
        if high == lines:
            ready = (moved[1], far_side, mid_wide, spot, tops, pair_leaf)
            moved[1], far_side, mid_wide, spot, tops, pair_leaf = lax.optimization_barrier(ready)
            near_side += moved
            far_side += [lax.ppermute(m, "cluster", swap) for m in moved]

    return tail(
        bounds, per_pair, groups, leaf_parent, spot, lane_at, tops, leaf_size, pair_leaf, near_side,
        far_side, arrived, mid_wide, top_coupling, wide, basis_t,
    )


def solution(mesh):
    both = P(AXES)
    in_specs = (
        P(AXES, None),
        both,
        P(AXES, None, None),
        P(AXES, None, None),
        P(AXES, None, None),
        both,
        both,
        P(AXES, None),
        P(AXES, None, None),
        both,
        P(AXES, None),
        P(AXES, None, None),
        P("group", None),
        P("group", None, None),
    )
    return jax.shard_map(
        body, mesh=mesh, in_specs=in_specs, out_specs=P(AXES, None), check_vma=False
    )
```
